32 devices in a mesh: dp: 8 (over y, x, core), ctx: 4 (over z).
Axes of the slice: x: 2, y: 2, z: 4, core: 2. Of those that a mesh axis runs over, the one named last changes fastest.
Arguments:
- tokens: bfloat16 [8192, 2048], P(('dp', 'ctx')), may hold values from -6 to 6
- cotangent: bfloat16 [8192, 2048], P(('dp', 'ctx')), may hold values from -6 to 6
- segments: int32 [8192], P(('dp', 'ctx')), may hold values from 0 to 1023, as said below
- attn_weight: float32 [2048, 4, 2048], P(('dp', 'ctx'))
- attn_first: float32 [2048, 4, 2048], P(('dp', 'ctx'))
- attn_second: float32 [2048, 4, 2048], P(('dp', 'ctx'))
- mlp_weight: float32 [8192, 3, 2048], P(('dp', 'ctx'))
- mlp_first: float32 [8192, 3, 2048], P(('dp', 'ctx'))
- mlp_second: float32 [8192, 3, 2048], P(('dp', 'ctx'))
- gain_weight: float32 [2, 2048], P(None, ('dp', 'ctx')), may hold values from 0.5 to 1.5
- gain_first: float32 [2, 2048], P(None, ('dp', 'ctx'))
- gain_second: float32 [2, 2048], P(None, ('dp', 'ctx'))
Outputs:
- output: bfloat16 [8192, 2048], P(('dp', 'ctx'))
- grad_input: float32 [8192, 2048], P(('dp', 'ctx'))
- attn_first_new: float32 [2048, 4, 2048], P(('dp', 'ctx'))
- attn_second_new: float32 [2048, 3, 2048], P(('dp', 'ctx'))
- projection_second: float32 [2048, 2048], P(('dp', 'ctx'))
- attn_weight_new: float32 [2048, 4, 2048], P(('dp', 'ctx'))
- mlp_first_new: float32 [8192, 3, 2048], P(('dp', 'ctx'))
- mlp_second_new: float32 [8192, 3, 2048], P(('dp', 'ctx'))
- mlp_weight_new: float32 [8192, 3, 2048], P(('dp', 'ctx'))
- gain_first_new: float32 [2, 2048], P(None, ('dp', 'ctx'))
- gain_second_new: float32 [2, 2048], P(None, ('dp', 'ctx'))
- gain_weight_new: float32 [2, 2048], P(None, ('dp', 'ctx'))
The draws below stay inside these ranges and needn't reach their ends.
Inputs may be any that keep to these rules, and one draw needn't show every extreme that they name: `segments`: within each sequence of 1024 tokens the numbers start at 0, never fall, and the last document is numbered 1024 - 1; equal numbers mark one document. In every sequence one document begins within the first 256 tokens and ends within the last 256 tokens.
All inputs are finite; a program needn't handle non-finite values.
Results may differ from the reference program's by a relative error of at most 0.014.
Values may be sent and summed in bfloat16 or wider, within the bound.
A program may use at most 1.125 GiB of HBM per device.

```python
import jax
import jax.numpy as jnp
from jax import lax

D = 2048
HEADS = 32
HD = 64
FF = 8192
TOK_DEV = 256
STEP = 10
SEQ = 1024
TOKENS = 8192


def slot_normal(key, shape, factors):
    scales = jnp.asarray(factors, jnp.float32).reshape(1, len(factors), 1)
    return jax.random.normal(key, shape, jnp.float32) * scales


def slot_second(key, shape, factors):
    scales = jnp.asarray(factors, jnp.float32).reshape(1, len(factors), 1)
    spread = jax.random.uniform(key, shape, jnp.float32, jnp.log(0.03), jnp.log(0.4))
    return jnp.exp(spread) * scales * scales


def attn_grad_scale():
    root = TOKENS ** 0.5
    return [0.6 * root, 0.6 * root, 0.7 * root, 0.1 * root]


def mlp_grad_scale():
    root = TOKENS ** 0.5
    return [0.25 * root, 0.25 * root, 0.4 * root]


def draw_attn_weight(key, part):
    key = jax.random.fold_in(key, 1)
    base = D ** (-0.5)
    return slot_normal(key, (D, 4, D), [base, base, base, 12.0 * base])


def draw_attn_first(key, part):
    key = jax.random.fold_in(key, 2)
    return slot_normal(key, (D, 4, D), [0.11 * value for value in attn_grad_scale()])


def draw_attn_second(key, part):
    key = jax.random.fold_in(key, 3)
    return slot_second(key, (D, 4, D), attn_grad_scale())


def draw_mlp_weight(key, part):
    key = jax.random.fold_in(key, 4)
    return slot_normal(key, (FF, 3, D), [D ** (-0.5), D ** (-0.5), FF ** (-0.5)])


def draw_mlp_first(key, part):
    key = jax.random.fold_in(key, 5)
    return slot_normal(key, (FF, 3, D), [0.11 * value for value in mlp_grad_scale()])


def draw_mlp_second(key, part):
    key = jax.random.fold_in(key, 6)
    return slot_second(key, (FF, 3, D), mlp_grad_scale())


def draw_gain_first(key, part):
    key = jax.random.fold_in(key, 7)
    return jax.random.normal(key, (2, D), jnp.float32) * (0.11 * 0.5 * TOKENS ** 0.5)


def draw_gain_second(key, part):
    key = jax.random.fold_in(key, 8)
    spread = jax.random.uniform(key, (2, D), jnp.float32, jnp.log(0.03), jnp.log(0.4))
    return jnp.exp(spread) * (0.25 * TOKENS)


def draw_segments(key, part):
    key = jax.random.fold_in(key, 9)
    first_key, last_key, cut_key = jax.random.split(key, 3)
    count_seq = TOKENS // SEQ
    opening = jax.random.randint(first_key, (count_seq, 1), 1, TOK_DEV)
    closing = SEQ - jax.random.randint(last_key, (count_seq, 1), 1, TOK_DEV)
    place = jnp.arange(SEQ, dtype=jnp.int32)[None, :]
    cuts = jax.random.randint(cut_key, (count_seq, SEQ), 0, 24) == 0
    outside = (place < opening) | (place > closing)
    marks = cuts & outside & (place > 0) | (place == opening) | (place == closing)
    counted = jnp.cumsum(marks.astype(jnp.int32), axis=1).astype(jnp.int32)
    total = counted[:, -1:]
    numbered = jnp.where(counted == total, jnp.int32(SEQ - 1), counted)
    return numbered.astype(jnp.int32).reshape(TOKENS)


def shard_levels(own_key, dims, cuts, low, top_value):
    def one(dim, parts):
        heights = jax.random.uniform(jax.random.fold_in(jax.random.fold_in(own_key, 6), dim), (parts,), jnp.float32, low / len(cuts), top_value / len(cuts))
        return jnp.repeat(jnp.exp(heights), dims[dim] // parts).reshape((-1,) + (1,) * (len(dims) - dim - 1))

    gain = one(*cuts[0])
    for cut in cuts[1:]:
        gain = gain * one(*cut)
    return gain


def normal_values(own_key, extent, width, most, pieces=(), kind=jnp.bfloat16):
    drawn = jax.random.normal(own_key, extent, jnp.float32) * width
    if len(pieces) > 0:
        drawn = shard_levels(own_key, extent, pieces, -0.22, 0.18) * drawn
    return jnp.clip(drawn, min=-most, max=most).astype(kind)


def setup_inputs(seed: int = 0) -> dict:
    key_of = jax.random.split(jax.random.key(seed), 13)
    return {
        "tokens": normal_values(key_of[0], (TOKENS, D), 1.0, 6.0, ((0, 32),)),
        "cotangent": normal_values(key_of[1], (TOKENS, D), 1.0, 6.0, ((0, 32),)),
        "segments": draw_segments(jax.random.fold_in(key_of[12], 71), 0),
        "attn_weight": draw_attn_weight(jax.random.fold_in(key_of[12], 71), 0),
        "attn_first": draw_attn_first(jax.random.fold_in(key_of[12], 71), 0),
        "attn_second": draw_attn_second(jax.random.fold_in(key_of[12], 71), 0),
        "mlp_weight": draw_mlp_weight(jax.random.fold_in(key_of[12], 71), 0),
        "mlp_first": draw_mlp_first(jax.random.fold_in(key_of[12], 71), 0),
        "mlp_second": draw_mlp_second(jax.random.fold_in(key_of[12], 71), 0),
        "gain_weight": jnp.clip(1.0 + 0.1 * jax.random.normal(key_of[9], (2, D), jnp.float32), 0.5, 1.5),
        "gain_first": draw_gain_first(jax.random.fold_in(key_of[12], 71), 0),
        "gain_second": draw_gain_second(jax.random.fold_in(key_of[12], 71), 0),
    }


NORM_EPS = 1e-05
ROPE_BASE = 130000.0
BETA_ONE = 0.9
BETA_TWO = 0.95
ADAM_EPS = 1e-08
WEIGHT_DECAY = 0.1
RATE_FACTOR = 1.5
GAIN_RATE = 0.6
OUTPUT_BOOST = 12.0
MASKED = -1e+30
HIGH = lax.Precision.HIGHEST

@jax.custom_vjp
def low(v):
    return lax.optimization_barrier(v.astype(jnp.bfloat16)).astype(jnp.float32)

@jax.custom_vjp
def low_back(v):
    return v

def low_keep(v):
    return (low(v), None)

def low_pass(kept, grad):
    return (grad,)

def back_keep(v):
    return (v, None)

def back_low(kept, grad):
    return (low(grad),)
low.defvjp(low_keep, low_pass)
low_back.defvjp(back_keep, back_low)

def rope_tables(position):
    halved = HD // 2
    frequency = ROPE_BASE ** (-(jnp.arange(halved, dtype=jnp.float32) * 2.0 / HD))
    angle = position.astype(jnp.float32)[:, None] * frequency[None, :]
    return (jnp.concatenate([jnp.cos(angle), jnp.cos(angle)], -1), jnp.concatenate([jnp.sin(angle), jnp.sin(angle)], -1))

def rotate(values, cosine, sine, direction):
    halved = HD // 2
    turned = jnp.concatenate([-values[..., halved:], values[..., :halved]], -1)
    return values * cosine[:, None, :] + direction * turned * sine[:, None, :]

def norm_scale(values):
    return lax.rsqrt(lax.optimization_barrier(jnp.mean(values * values, -1, keepdims=True)) + NORM_EPS)

def rounded_copy(values):
    return lax.optimization_barrier(values.astype(jnp.bfloat16)).astype(jnp.float32)

def adam_update(master, first, second, grad, rate, decay):
    first_new = BETA_ONE * first + (1.0 - BETA_ONE) * grad
    second_new = BETA_TWO * second + (1.0 - BETA_TWO) * grad * grad
    direction = first_new / (1.0 - BETA_ONE ** STEP) / (jnp.sqrt(second_new / (1.0 - BETA_TWO ** STEP)) + ADAM_EPS)
    return (first_new, second_new, master - rate * (direction + decay * master))

def sequence_forward(source, segment, attn_w, mlp_w, gains):
    length = source.shape[0]
    position = jnp.arange(length, dtype=jnp.int32)
    cosine, sine = rope_tables(position)
    normed = low(source * norm_scale(source) * gains[0])
    projected = low_back(jnp.einsum('td,fkd->tkf', normed, attn_w[:, :3, :], precision=HIGH))
    query = low(rotate(projected[:, 0].reshape(length, HEADS, HD), cosine, sine, 1.0))
    key_all = low(rotate(projected[:, 1].reshape(length, HEADS, HD), cosine, sine, 1.0))
    value_all = low(projected[:, 2].reshape(length, HEADS, HD))
    rows_block = min(512, length)

    def attend(block_index):
        first_row = block_index * rows_block
        query_block = lax.dynamic_slice_in_dim(query, first_row, rows_block, 0)
        segment_block = lax.dynamic_slice_in_dim(segment, first_row, rows_block, 0)
        query_place = first_row + jnp.arange(rows_block, dtype=jnp.int32)
        allowed = (position[None, :] <= query_place[:, None]) & (segment[None, :] == segment_block[:, None])
        scores = low_back(jnp.einsum('qhe,khe->hqk', query_block, key_all, precision=HIGH) * HD ** (-0.5))
        scores = jnp.where(allowed[None], scores, MASKED)
        probs = jax.nn.softmax(scores, axis=-1)
        return jnp.einsum('hqk,khe->qhe', low(probs), value_all, precision=HIGH)
    attended = lax.map(jax.checkpoint(attend), jnp.arange(length // rows_block, dtype=jnp.int32))
    attended = low(low_back(attended.reshape(length, HEADS * HD)))
    branch = low_back(jnp.dot(attended, attn_w[:, 3, :], precision=HIGH))
    middle = source + branch
    normed_two = low(middle * norm_scale(middle) * gains[1])
    gate_up = low_back(jnp.einsum('td,fkd->tkf', normed_two, mlp_w[:, :2, :], precision=HIGH))
    hidden = low(jax.nn.silu(gate_up[:, 0]) * gate_up[:, 1])
    return middle + low_back(jnp.dot(hidden, mlp_w[:, 2, :], precision=HIGH))

def layer_forward(source, attn_w, mlp_w, gains, segment):
    count_seq = source.shape[0] // SEQ
    blocks = source.reshape(count_seq, SEQ, D)
    segment_rows = segment.reshape(count_seq, SEQ)
    checked = jax.checkpoint(sequence_forward)

    def one_sequence(carry, item):
        return (carry, checked(item[0], item[1], attn_w, mlp_w, gains))
    _, result = lax.scan(one_sequence, None, (blocks, segment_rows))
    return result.reshape(count_seq * SEQ, D)

def reference(tokens, cotangent, segments, attn_weight, attn_first, attn_second, mlp_weight, mlp_first, mlp_second, gain_weight, gain_first, gain_second):
    attn_low = rounded_copy(attn_weight)
    mlp_low = rounded_copy(mlp_weight)
    gain_low = rounded_copy(gain_weight)
    source = tokens.astype(jnp.float32)

    def forward(source_in, attn_in, mlp_in, gain_in):
        return layer_forward(source_in, attn_in, mlp_in, gain_in, segments)
    result, pullback = jax.vjp(forward, source, attn_low, mlp_low, gain_low)
    grad_input, attn_grad, mlp_grad, gain_grad = pullback(cotangent.astype(jnp.float32))
    attn_rate = RATE_FACTOR * D ** (-0.5) * jnp.array([1.0, 1.0, 1.0, OUTPUT_BOOST], jnp.float32).reshape(1, 4, 1)
    mlp_rate = RATE_FACTOR * jnp.array([D ** (-0.5), D ** (-0.5), FF ** (-0.5)], jnp.float32).reshape(1, 3, 1)
    attn_new = adam_update(attn_weight, attn_first, attn_second, attn_grad, attn_rate, WEIGHT_DECAY)
    mlp_new = adam_update(mlp_weight, mlp_first, mlp_second, mlp_grad, mlp_rate, WEIGHT_DECAY)
    gain_new = adam_update(gain_weight, gain_first, gain_second, gain_grad, GAIN_RATE, 0.0)
    return (result.astype(jnp.bfloat16), grad_input, attn_new[0], attn_new[1][:, :3, :], attn_new[1][:, 3, :], attn_new[2], mlp_new[0], mlp_new[1], mlp_new[2], gain_new[0], gain_new[1], gain_new[2])
```

```python
import functools

import jax
import jax.numpy as jnp
import numpy as np
from jax import lax
from jax.experimental import pallas as pl
from jax.experimental.pallas import tpu as pltpu
from jax.sharding import Mesh
from jax.sharding import PartitionSpec as P

D = 2048
HEADS = 32
HD = 64
FF = 8192
STEP = 10


NORM_EPS = 1e-05
ROPE_BASE = 130000.0
BETA_ONE = 0.9
BETA_TWO = 0.95
ADAM_EPS = 1e-08
WEIGHT_DECAY = 0.1
RATE_FACTOR = 1.5
GAIN_RATE = 0.6
OUTPUT_BOOST = 12.0
MASKED = -1e30
BF = jnp.bfloat16
F32 = jnp.float32
ALL = ("plane", "core", "ctx")
TEAM = ("core", "ctx")


BLOCK = 256
CHUNKS = 2
VMEM_LIMIT = 60 * 1024 * 1024
MESH_ID = pl.DeviceIdType.MESH


def params(semantics=1, **more):
    return pltpu.CompilerParams(
        dimension_semantics=("arbitrary",) * semantics, vmem_limit_bytes=VMEM_LIMIT, **more
    )


def rope_tables(length):
    halved = HD // 2
    frequency = (ROPE_BASE ** (-(np.arange(halved) * 2.0 / HD))).astype(np.float32)
    angle = np.arange(length, dtype=np.float32)[:, None] * frequency[None, :]
    cosine, sine = np.cos(angle).astype(np.float32), np.sin(angle).astype(np.float32)
    zero = np.zeros_like(sine)
    return (
        jnp.asarray(np.concatenate([cosine] * 4, 1)),
        jnp.asarray(np.concatenate([-sine, zero] * 2, 1)),
        jnp.asarray(np.concatenate([zero, sine] * 2, 1)),
    )


def widen(table, feats):
    return jnp.concatenate([table] * (feats // 128), 1) if feats > 128 else table


def rope(values, cosine, low_sine, high_sine):
    width = values.shape[-1]
    ahead = pltpu.roll(values, width - HD // 2, 1)
    behind = pltpu.roll(values, HD // 2, 1)
    return values * cosine + ahead * low_sine + behind * high_sine


def rope_back(values, cosine, low_sine, high_sine):
    width = values.shape[-1]
    ahead = pltpu.roll(values, width - HD // 2, 1)
    behind = pltpu.roll(values, HD // 2, 1)
    return values * cosine - ahead * low_sine - behind * high_sine


def mm(a, b, ca, cb):
    return lax.dot_general(a, b, (((ca,), (cb,)), ((), ())), preferred_element_type=F32)


def norm_scale(values):
    return lax.rsqrt(jnp.mean(values * values, -1, keepdims=True) + NORM_EPS)


def norm_back(grad_normed, values, scale, gain):
    weighted = grad_normed * gain
    grad_values = scale * (
        weighted - values * scale * scale * jnp.mean(weighted * values, -1, keepdims=True)
    )
    return (grad_values, jnp.sum(grad_normed * values * scale, 0))


def adam_update(master, first, second, grad, rate, decay):
    first_new = BETA_ONE * first + (1.0 - BETA_ONE) * grad
    second_new = BETA_TWO * second + (1.0 - BETA_TWO) * grad * grad
    direction = (
        first_new
        / (1.0 - BETA_ONE**STEP)
        / (jnp.sqrt(second_new / (1.0 - BETA_TWO**STEP)) + ADAM_EPS)
    )
    return (first_new, second_new, master - rate * (direction + decay * master))


def greet_all(peers):
    barrier = pltpu.get_barrier_semaphore()
    for peer in peers:
        pl.semaphore_signal(barrier, inc=1, device_id=peer, device_id_type=MESH_ID)
    pl.semaphore_wait(barrier, len(peers))


def neighbours(planes, ctxs):
    plane, core, ctx = lax.axis_index("plane"), lax.axis_index("core"), lax.axis_index("ctx")
    column = [lax.rem(plane + k, planes) for k in range(1, planes)]
    group = [
        (core if dc == 0 else 1 - core, lax.rem(ctx + dz, ctxs))
        for dc in range(2)
        for dz in range(ctxs)
        if dc + dz > 0
    ]
    return plane, core, ctx, column, group


def gather_kernel(planes, ctxs, lines, boards, inputs, refs):
    ins, outs = refs[:inputs], refs[inputs : inputs + len(lines) + len(boards)]
    line_send, line_recv, side_send, side_recv, board_send, board_recv, pass_send, pass_recv, here = refs[
        inputs + len(lines) + len(boards) :
    ]
    plane, core, ctx = lax.axis_index("plane"), lax.axis_index("core"), lax.axis_index("ctx")
    last = ctxs - 1
    column = [lax.rem(plane + k, planes) for k in range(1, planes)]
    greet_all(
        [(p, core, ctx) for p in column]
        + [(plane, core, lax.rem(ctx + k, ctxs)) for k in range(1, ctxs)]
        + [(plane, 1 - core, ctx)]
    )
    other = (plane, 1 - core, ctx)
    pieces = []
    for source, target, chunks in lines:
        rows = ins[source].shape[0] // chunks
        for chunk in range(chunks):
            pieces.append((ins[source], outs[target], pl.ds(chunk * rows, rows)))

    def remote(source, target, send, recv, peer):
        return pltpu.make_async_remote_copy(
            src_ref=source,
            dst_ref=target,
            send_sem=send,
            recv_sem=recv,
            device_id=peer,
            device_id_type=MESH_ID,
        )

    def line(index, way, hop, block, peer_ctx, own):
        value, out, rows = pieces[index]
        slot = out.at[core * ctxs + block, rows]
        return remote(
            value.at[rows] if own else slot,
            slot,
            line_send.at[index, way, hop],
            line_recv.at[index, way, hop],
            (plane, core, peer_ctx),
        )

    def side(index, order, side_core, block, own):
        value, out, rows = pieces[index]
        slot = out.at[side_core * ctxs + block, rows]
        return remote(
            value.at[rows] if own else slot,
            slot,
            side_send.at[index, order],
            side_recv.at[index, order],
            other,
        )

    square = planes == 4
    near_x = plane + 1 - 2 * lax.rem(plane, 2)
    near_y = lax.rem(plane + 2, 4)
    far = 3 - plane

    def board_refs(index, home, half=None, own=True):
        kind, source, target = boards[index]
        value, out = source(ins, outs), outs[target]
        if kind in ("block", "late"):
            size = value.shape[0]
            part = pl.ds(0, size) if half is None else pl.ds(half * (size // 2), size // 2)
            slot = out.at[home, part]
            return (value.at[part] if own else slot), slot
        if kind == "slots":
            size = value.shape[1]
            part = pl.ds(0, size) if half is None else pl.ds(half * (size // 2), size // 2)
            slot = out.at[:, home, part]
            return (value.at[:, part] if own else slot), slot
        size = ctxs if half is None else ctxs // 2
        part = pl.ds(core * ctxs + (0 if half is None else half * size), size)
        slot = out.at[part, home]
        return (value.at[part] if own else slot), slot

    def board(index, k, home, peer):
        value, slot = board_refs(index, home)
        return remote(
            value, slot, board_send.at[index, k], board_recv.at[index, k], (peer, core, ctx)
        )

    sent = [(plane, 0, near_x), (plane, 1, near_x), (plane, 0, near_y), (plane, 1, near_y)]
    sent += [(near_y, 0, near_x), (near_x, 1, near_y)]
    landed = [near_x, near_x, near_y, near_y, far, far]

    def relay(index, k, arriving=False):
        home, half, peer = sent[k]
        value, slot = board_refs(index, landed[k] if arriving else home, half, k < 4)
        return remote(
            value, slot, board_send.at[index, k], board_recv.at[index, k], (peer, core, ctx)
        )

    def relayed(index):
        return square and boards[index][0] != "late"

    def board_start(index):
        if relayed(index):
            for k in (1, 2, 0, 3):
                relay(index, k).start()
            return
        for k, peer in enumerate(column):
            board(index, k, plane, peer).start()

    def board_pass(index):
        if relayed(index):
            relay(index, 2, True).wait_recv()
            relay(index, 4).start()
            relay(index, 1, True).wait_recv()
            relay(index, 5).start()

    def sources(index):
        if relayed(index):
            return [near_x, near_y, far]
        return [lax.rem(plane + planes - 1 - k, planes) for k in range(planes - 1)]

    def share(index, k, home):
        _, slot = board_refs(index, home)
        return remote(slot, slot, pass_send.at[index, k], pass_recv.at[index, k], other)

    def board_finish(index):
        if relayed(index):
            for k in (0, 3, 4, 5):
                relay(index, k, True).wait_recv()
        for k, home in enumerate(sources(index)):
            if not relayed(index):
                board(index, k, home, home).wait_recv()
            if boards[index][0] == "half":
                share(index, k, home).start()

    def board_close(index):
        if relayed(index):
            for k in range(6):
                relay(index, k).wait_send()
        else:
            for k, peer in enumerate(column):
                board(index, k, plane, peer).wait_send()
        if boards[index][0] == "half":
            out = outs[boards[index][2]]
            for k, home in enumerate(sources(index)):
                share(index, k, home).wait_send()
                slot = out.at[pl.ds((1 - core) * ctxs, ctxs), home]
                remote(
                    slot, slot, pass_send.at[index, k], pass_recv.at[index, k], other
                ).wait_recv()

    count = len(pieces)
    late = [i for i in range(len(boards)) if boards[i][0] == "late"]
    early = [i for i in range(len(boards)) if boards[i][0] != "late"]
    board_start(early[0]) if early else None

    @pl.when(ctx < last)
    def _():
        for i in range(count):
            line(i, 0, 1, ctx, ctx + 1, True).start()

    @pl.when(ctx > 0)
    def _():
        for i in range(count):
            line(i, 1, 1, ctx, ctx - 1, True).start()

    for i in range(count):
        side(i, 0, core, ctx, True).start()
    copies = []
    for i, (value, out, rows) in enumerate(pieces):
        copies.append(
            pltpu.make_async_copy(value.at[rows], out.at[core * ctxs + ctx, rows], here.at[i])
        )
    for i in early:
        kind, source, target = boards[i]
        slot = outs[target].at[plane] if kind == "block" else outs[target].at[:, plane]
        copies.append(pltpu.make_async_copy(source(ins, outs), slot, here.at[count + i]))
    for copy in copies:
        copy.start()

    passed = 0
    board_pass(early[0])
    if len(early) > 1:
        board_start(early[1])
    for hop in range(1, ctxs):

        @pl.when(ctx >= hop)
        def _():
            block = ctx - hop
            for i in range(count):
                line(i, 0, hop, block, ctx - 1, False).wait_recv()

                @pl.when(ctx < last)
                def _():
                    line(i, 0, hop + 1, block, ctx + 1, False).start()

                side(i, hop, core, block, False).start()

        @pl.when(ctx + hop <= last)
        def _():
            block = ctx + hop
            for i in range(count):
                line(i, 1, hop, block, ctx + 1, False).wait_recv()

                @pl.when(ctx > 0)
                def _():
                    line(i, 1, hop + 1, block, ctx - 1, False).start()

                side(i, last + hop, core, block, False).start()

        if passed + 1 < len(early):
            passed += 1
            board_pass(early[passed])
            if passed + 1 < len(early):
                board_start(early[passed + 1])
    for i in early:
        board_finish(i)

    for i in range(count):
        side(i, 0, 1 - core, ctx, False).wait_recv()
    for hop in range(1, ctxs):

        @pl.when(ctx >= hop)
        def _():
            for i in range(count):
                side(i, hop, 1 - core, ctx - hop, False).wait_recv()

        @pl.when(ctx + hop <= last)
        def _():
            for i in range(count):
                side(i, last + hop, 1 - core, ctx + hop, False).wait_recv()

    for copy in copies:
        copy.wait()
    for i in late:
        board_start(i)
        kind, source, target = boards[i]
        copy = pltpu.make_async_copy(source(ins, outs), outs[target].at[plane], here.at[count + i])
        copy.start()
        copy.wait()
    for i in late:
        board_finish(i)

    for i in range(len(boards)):
        board_close(i)
    for i in range(count):
        side(i, 0, core, ctx, True).wait_send()
    for hop in range(1, ctxs):

        @pl.when(ctx >= hop)
        def _():
            for i in range(count):
                side(i, hop, core, ctx - hop, False).wait_send()

        @pl.when(ctx + hop <= last)
        def _():
            for i in range(count):
                side(i, last + hop, core, ctx + hop, False).wait_send()

        @pl.when((ctx < last) & (ctx >= hop - 1))
        def _():
            for i in range(count):
                line(i, 0, hop, ctx - hop + 1, ctx + 1, False).wait_send()

        @pl.when((ctx > 0) & (ctx + hop - 1 <= last))
        def _():
            for i in range(count):
                line(i, 1, hop, ctx + hop - 1, ctx - 1, False).wait_send()


def gather_call(planes, ctxs, number, inputs, lines, boards, shapes, name):
    pieces = sum(chunks for _, _, chunks in lines)
    dma = pltpu.SemaphoreType.DMA

    def kernel(*refs):
        gather_kernel(planes, ctxs, lines, boards, len(inputs), refs)

    return pl.pallas_call(
        kernel,
        out_shape=tuple(jax.ShapeDtypeStruct(shape, dtype) for shape, dtype in shapes),
        in_specs=[pl.BlockSpec(memory_space=pl.ANY)] * len(inputs),
        out_specs=tuple(pl.BlockSpec(memory_space=pl.ANY) for _ in shapes),
        scratch_shapes=[
            dma((pieces, 2, ctxs + 1)),
            dma((pieces, 2, ctxs + 1)),
            dma((pieces, 2 * ctxs)),
            dma((pieces, 2 * ctxs)),
            dma((len(boards), max(planes, 6))),
            dma((len(boards), max(planes, 6))),
            dma((len(boards), planes)),
            dma((len(boards), planes)),
            dma((pieces + len(boards),)),
        ],
        compiler_params=pltpu.CompilerParams(collective_id=number, has_side_effects=True),
        name=name,
    )(*inputs)


def small_sum_kernel(planes, ctxs, value_ref, out_ref, got_one, middle, got_two, sems):
    plane, core, ctx, column, group = neighbours(planes, ctxs)
    greet_all([(p, core, ctx) for p in column] + [(plane, c, z) for c, z in group])

    def hop(index, source, target, peer):
        return pltpu.make_async_remote_copy(
            src_ref=source,
            dst_ref=target,
            send_sem=sems.at[0, index],
            recv_sem=sems.at[1, index],
            device_id=peer,
            device_id_type=MESH_ID,
        )

    first = [
        hop(i, value_ref.at[p], got_one.at[i], (p, core, ctx)) for i, p in enumerate(column)
    ]
    for copy in first:
        copy.start()
    total = value_ref[plane]
    for i, copy in enumerate(first):
        copy.wait_recv()
        total = total + got_one[i]
    middle[...] = total
    base = len(column)
    second = [
        hop(base + i, middle.at[c * ctxs + z], got_two.at[i], (plane, c, z))
        for i, (c, z) in enumerate(group)
    ]
    for copy in second:
        copy.start()
    total = middle[core * ctxs + ctx]
    for i, copy in enumerate(second):
        copy.wait_recv()
        total = total + got_two[i]
    out_ref[...] = total
    for copy in first + second:
        copy.wait_send()


def small_sum(planes, ctxs, value):
    hops = planes + 2 * ctxs - 2
    tile = value.shape[2:]
    return pl.pallas_call(
        functools.partial(small_sum_kernel, planes, ctxs),
        out_shape=jax.ShapeDtypeStruct(tile, F32),
        in_specs=[pl.BlockSpec(memory_space=pltpu.VMEM)],
        out_specs=pl.BlockSpec(memory_space=pltpu.VMEM),
        scratch_shapes=[
            pltpu.VMEM((planes - 1, 2 * ctxs) + tile, F32),
            pltpu.VMEM((2 * ctxs,) + tile, F32),
            pltpu.VMEM((2 * ctxs - 1,) + tile, F32),
            pltpu.SemaphoreType.DMA((2, hops)),
        ],
        compiler_params=pltpu.CompilerParams(collective_id=1, has_side_effects=True),
        name="small_sum",
    )(value)


class Gather:
    def __init__(self, ctxs, pieces, boards, sems):
        self.ctxs, self.pieces, self.boards = ctxs, pieces, boards
        self.line_sem, self.side_sem, self.board_sem, self.pass_sem = sems
        self.plane, self.core, self.ctx = (
            lax.axis_index("plane"),
            lax.axis_index("core"),
            lax.axis_index("ctx"),
        )
        self.last = ctxs - 1
        self.near_x = self.plane + 1 - 2 * lax.rem(self.plane, 2)
        self.near_y = lax.rem(self.plane + 2, 4)
        self.far = 3 - self.plane

    @staticmethod
    def scratch(ctxs, pieces, boards):
        dma = pltpu.SemaphoreType.DMA
        return [
            dma((2, pieces, 2, ctxs + 1)),
            dma((2, pieces, 2 * ctxs)),
            dma((2, boards, 6)),
            dma((2, boards, 3)),
        ]

    def peers(self):
        plane, core, ctx, ctxs = self.plane, self.core, self.ctx, self.ctxs
        return (
            [(plane, core, lax.rem(ctx + k, ctxs)) for k in range(1, ctxs)]
            + [(plane, 1 - core, ctx)]
            + [(near, core, ctx) for near in (self.near_x, self.near_y)]
        )

    def remote(self, slot, sem, index, peer):
        return pltpu.make_async_remote_copy(
            src_ref=slot,
            dst_ref=slot,
            send_sem=sem.at[(0,) + index],
            recv_sem=sem.at[(1,) + index],
            device_id=peer,
            device_id_type=MESH_ID,
        )

    def line(self, i, way, hop, block):
        buffer, rows = self.pieces[i]
        slot = buffer.at[self.core * self.ctxs + block, rows]
        peer = (self.plane, self.core, self.ctx + (1 if way == 0 else -1))
        return self.remote(slot, self.line_sem, (i, way, hop), peer)

    def side(self, i, order, core, block):
        buffer, rows = self.pieces[i]
        slot = buffer.at[core * self.ctxs + block, rows]
        return self.remote(slot, self.side_sem, (i, order), (self.plane, 1 - self.core, self.ctx))

    def send_own(self, items):
        @pl.when(self.ctx < self.last)
        def _():
            for i in items:
                self.line(i, 0, 1, self.ctx).start()

        @pl.when(self.ctx > 0)
        def _():
            for i in items:
                self.line(i, 1, 1, self.ctx).start()

        for i in items:
            self.side(i, 0, self.core, self.ctx).start()

    def hop(self, k, items):
        ctx, last = self.ctx, self.last

        for i in items:

            @pl.when(ctx >= k)
            def _():
                self.line(i, 0, k, ctx - k).wait_recv()

                @pl.when(ctx < last)
                def _():
                    self.line(i, 0, k + 1, ctx - k).start()

                self.side(i, k, self.core, ctx - k).start()

            @pl.when(ctx + k <= last)
            def _():
                self.line(i, 1, k, ctx + k).wait_recv()

                @pl.when(ctx > 0)
                def _():
                    self.line(i, 1, k + 1, ctx + k).start()

                self.side(i, last + k, self.core, ctx + k).start()

    def side_arrive(self, k, items):
        ctx, last = self.ctx, self.last
        if k == 0:
            for i in items:
                self.side(i, 0, 1 - self.core, ctx).wait_recv()
            return

        @pl.when(ctx >= k)
        def _():
            for i in items:
                self.side(i, k, 1 - self.core, ctx - k).wait_recv()

        @pl.when(ctx + k <= last)
        def _():
            for i in items:
                self.side(i, last + k, 1 - self.core, ctx + k).wait_recv()

    def distant(self, k, action):
        ctx, last = self.ctx, self.last
        behind = (ctx >= k).astype(jnp.int32)
        ahead = (ctx + k <= last).astype(jnp.int32)

        def body(i, carry):
            action(jnp.where((behind == 1) & (i == 0), ctx - k, ctx + k))
            return carry

        lax.fori_loop(0, behind + ahead, body, 0)

    def board_slot(self, index, home, half):
        kind, buffer = self.boards[index]
        if kind == "block":
            size = buffer.shape[1] // 2
            return buffer.at[home, pl.ds(half * size, size)]
        if kind == "slots":
            size = buffer.shape[2] // 2
            return buffer.at[:, home, pl.ds(half * size, size)]
        size = self.ctxs // 2
        return buffer.at[pl.ds(self.core * self.ctxs + half * size, size), home]

    def relay(self, index, k, arriving=False):
        plane, near_x, near_y, far = self.plane, self.near_x, self.near_y, self.far
        sent = [(plane, 0, near_x), (plane, 1, near_x), (plane, 0, near_y), (plane, 1, near_y)]
        home, half, peer = (sent + [(near_y, 0, near_x), (near_x, 1, near_y)])[k]
        if arriving:
            home = [near_x, near_x, near_y, near_y, far, far][k]
        slot = self.board_slot(index, home, half)
        return self.remote(slot, self.board_sem, (index, k), (peer, self.core, self.ctx))

    def board_start(self, index):
        for k in (1, 2, 0, 3):
            self.relay(index, k).start()

    def board_pass(self, index):
        self.relay(index, 2, True).wait_recv()
        self.relay(index, 4).start()
        self.relay(index, 1, True).wait_recv()
        self.relay(index, 5).start()

    def share(self, index, k, core):
        buffer = self.boards[index][1]
        home = [self.near_x, self.near_y, self.far][k]
        slot = buffer.at[pl.ds(core * self.ctxs, self.ctxs), home]
        return self.remote(
            slot, self.pass_sem, (index, k), (self.plane, 1 - self.core, self.ctx)
        )

    def board_finish(self, index):
        for k in (0, 3, 4, 5):
            self.relay(index, k, True).wait_recv()
        if self.boards[index][0] == "half":
            for k in range(3):
                self.share(index, k, self.core).start()

    def board_shared(self, index):
        for k in range(3):
            self.share(index, k, 1 - self.core).wait_recv()

    def close(self):
        ctx, last = self.ctx, self.last
        items = range(len(self.pieces))
        for index in range(len(self.boards)):
            for k in range(6):
                self.relay(index, k).wait_send()
            if self.boards[index][0] == "half":
                for k in range(3):
                    self.share(index, k, self.core).wait_send()
        for i in items:
            self.side(i, 0, self.core, ctx).wait_send()
        for k in range(1, self.ctxs):

            @pl.when(ctx >= k)
            def _():
                for i in items:
                    self.side(i, k, self.core, ctx - k).wait_send()

            @pl.when(ctx + k <= last)
            def _():
                for i in items:
                    self.side(i, last + k, self.core, ctx + k).wait_send()

            @pl.when((ctx < last) & (ctx >= k - 1))
            def _():
                for i in items:
                    self.line(i, 0, k, ctx - k + 1).wait_send()

            @pl.when((ctx > 0) & (ctx + k - 1 <= last))
            def _():
                for i in items:
                    self.line(i, 1, k, ctx + k - 1).wait_send()


def front_kernel(ctxs, refs):
    tokens, qkv, mlp, packed, c_ref, a_ref, b_ref = refs[:7]
    x_out, n_out, q_out, k_out, v_out, w_out, g_out, small = refs[7:15]
    xs, ns, qs, ks, vs, ws, gs, wide, load, store, small_sem = refs[15:26]
    own = tokens.shape[0]
    half = own // 2
    pieces = [(xs, pl.ds(0, half)), (xs, pl.ds(half, half))]
    boards = [("slots", ws), ("block", gs)]
    net = Gather(ctxs, pieces, boards, refs[26:])
    plane, core, ctx = net.plane, net.core, net.ctx
    me = core * ctxs + ctx
    loads = [
        pltpu.make_async_copy(qkv, ws.at[:, plane], load.at[0]),
        pltpu.make_async_copy(tokens, xs.at[me], load.at[1]),
        pltpu.make_async_copy(mlp.at[0], wide, load.at[2]),
    ]
    for copy in loads:
        copy.start()
    others = [
        (core if dc == 0 else 1 - core, lax.rem(ctx + dz, ctxs))
        for dc in range(2)
        for dz in range(ctxs)
        if dc + dz > 0
    ]
    column = [lax.rem(plane + k, 4) for k in range(1, 4)]
    greet_all([(plane, c, z) for c, z in others] + [(p, core, ctx) for p in column])

    def tiny(index, source, target, peer):
        return pltpu.make_async_remote_copy(
            src_ref=source,
            dst_ref=target,
            send_sem=small_sem.at[0, index],
            recv_sem=small_sem.at[1, index],
            device_id=peer,
            device_id_type=MESH_ID,
        )

    small[plane, me] = packed[...]
    one = [
        tiny(i, packed, small.at[plane, me], (plane, c, z)) for i, (c, z) in enumerate(others)
    ]
    for copy in one:
        copy.start()
    for copy in loads[:2]:
        copy.wait()
    net.board_start(0)
    net.send_own([0, 1])
    i = 0
    for dc in range(2):
        for dz in range(ctxs):
            if dc + dz > 0:
                c, z = core if dc == 0 else 1 - core, lax.rem(ctx + ctxs - dz, ctxs)
                tiny(i, packed, small.at[plane, c * ctxs + z], (plane, c, z)).wait_recv()
                i += 1
    two = [
        tiny(i + k, small.at[plane], small.at[plane], (p, core, ctx))
        for k, p in enumerate(column)
    ]
    for copy in two:
        copy.start()
    loads[2].wait()

    def narrow(g, carry):
        part = pl.ds(pl.multiple_of(g * 16, 16), 16)
        gs[plane, part, :] = wide[part, :].astype(BF)
        return carry

    lax.fori_loop(0, wide.shape[0] // 16, narrow, 0)
    net.board_pass(0)
    net.board_start(1)
    for k in range(3):
        home = lax.rem(plane + 3 - k, 4)
        tiny(i + k, small.at[plane], small.at[home], (home, core, ctx)).wait_recv()
    tiles = [
        small[p, 2 * j][0:1] + small[p, 2 * j + 1][0:1] for p in range(4) for j in range(ctxs)
    ]
    gain = jnp.concatenate(tiles, 1)
    feats = q_out.shape[-1]
    stores = []

    blocks = [(xs, x_out), (ns, n_out), (qs, q_out), (ks, k_out), (vs, v_out)]

    def put(source, target, index):
        return pltpu.make_async_copy(source, target, store.at[index])

    def compute(side_core):
        def action(block):
            b = side_core * ctxs + block
            values = xs[b].astype(F32)
            normed = (values * norm_scale(values) * gain).astype(BF)
            ns[b] = normed
            rows = pl.ds(pl.multiple_of(block * own, own), own)
            cosine, low_sine, high_sine = [
                widen(ref[rows, :], feats) for ref in (c_ref, a_ref, b_ref)
            ]
            q = mm(normed, ws[0].reshape(feats, D), 1, 1)
            qs[b] = rope(q, cosine, low_sine, high_sine).astype(BF)
            k = mm(normed, ws[1].reshape(feats, D), 1, 1)
            ks[b] = rope(k, cosine, low_sine, high_sine).astype(BF)
            vs[b] = mm(normed, ws[2].reshape(feats, D), 1, 1).astype(BF)
            for i, (source, target) in enumerate(blocks):
                put(source.at[b], target.at[b], 5 * b + i).start()

        return action

    base = 10 * ctxs
    parts = [0, 1]
    stores = [put(s, t, base + i) for i, (s, t) in enumerate([(ws, w_out), (gs, g_out)])]
    net.hop(1, parts)
    net.board_finish(0)
    stores[0].start()
    compute(core)(ctx)
    net.side_arrive(0, parts)
    compute(1 - core)(ctx)
    net.board_pass(1)
    for k in range(1, ctxs):
        net.distant(k, compute(core))
        if k + 1 < ctxs:
            net.hop(k + 1, parts)
        net.side_arrive(k, parts)
        net.distant(k, compute(1 - core))
        if k == min(2, ctxs - 1):
            net.board_finish(1)
            stores[1].start()
    net.close()
    for copy in one + two:
        copy.wait_send()
    for copy in stores:
        copy.wait()
    for b in range(2 * ctxs):
        for i, (source, target) in enumerate(blocks):
            put(source.at[b], target.at[b], 5 * b + i).wait()


def front_call(ctxs, tokens, qkv, mlp, packed, tables):
    team = 2 * ctxs
    own, arows, frows = tokens.shape[0], qkv.shape[1], mlp.shape[1]
    feats = 4 * arows
    block, part = (team, own, D), (team, own, feats)
    shapes = [block, block, part, part, part, (3, 4, arows, D)]
    shapes += [(4, frows, D)]
    dma = pltpu.SemaphoreType.DMA
    hbm, vmem = pl.BlockSpec(memory_space=pl.ANY), pl.BlockSpec(memory_space=pltpu.VMEM)

    def kernel(*refs):
        front_kernel(ctxs, refs)

    return pl.pallas_call(
        kernel,
        out_shape=[jax.ShapeDtypeStruct(shape, BF) for shape in shapes]
        + [jax.ShapeDtypeStruct((4, team, 8, 128), F32)],
        in_specs=[hbm] * 3 + [vmem] * 4,
        out_specs=[hbm] * len(shapes) + [vmem],
        scratch_shapes=[pltpu.VMEM(shape, BF) for shape in shapes]
        + [pltpu.VMEM((frows, D), F32)]
        + [dma((3,)), dma((5 * team + 2,)), dma((2, team + 2))]
        + Gather.scratch(ctxs, 2, 2),
        compiler_params=pltpu.CompilerParams(
            collective_id=0, has_side_effects=True, vmem_limit_bytes=VMEM_LIMIT
        ),
        cost_estimate=pl.CostEstimate(
            flops=6 * team * own * D * feats, bytes_accessed=40 * own * D, transcendentals=0
        ),
        name="front",
    )(tokens, qkv, mlp, packed, *tables)


def attend_part(q_ref, k_ref, v_ref, col_ref, row_ref, l_ref, put, start, length, pair, unit):
    lanes = pl.ds(pl.multiple_of(pair * 128, 128), 128)
    for first in range(0, length, BLOCK):
        keys = first + BLOCK
        rows = pl.ds(pl.multiple_of(start + first, BLOCK), BLOCK)
        past = pl.ds(pl.multiple_of(start, BLOCK), keys)
        same = col_ref[rows, :] == row_ref[:, 0:keys]
        query_place = first + lax.broadcasted_iota(jnp.int32, (BLOCK, keys), 0)
        key_place = lax.broadcasted_iota(jnp.int32, (BLOCK, keys), 1)
        allowed = same & (key_place <= query_place)
        query, key, value = q_ref[rows, lanes], k_ref[past, lanes], v_ref[past, lanes]
        parts = []
        for head in range(128 // HD):
            cut = slice(head * HD, (head + 1) * HD)
            scores = mm(query[:, cut] * HD ** (-0.5), key[:, cut], 1, 1)
            scores = jnp.where(allowed, scores, MASKED)
            highest = jnp.max(scores, -1, keepdims=True)
            shifted = jnp.exp(scores - highest)
            totals = jnp.sum(shifted, -1, keepdims=True)
            weights = (shifted * (1.0 / totals)).astype(BF)
            parts.append(mm(weights, value[:, cut], 1, 0))
            l_ref[unit + head, first:keys, :] = highest + jnp.log(totals)
        put(rows, lanes, jnp.concatenate(parts, 1).astype(BF))


def second_kernel(ctxs, refs):
    q_ref, k_ref, v_ref, col_ref, row_ref, proj, mlp = refs[:7]
    o_out, p_out, d_out, l_ref = refs[7:11]
    outs, ps, ds_, wide, load, store = refs[11:17]
    count, feats = q_ref.shape
    seq = count // 2
    pairs = feats // 128
    plane = lax.axis_index("plane")
    pieces = [(outs, pl.ds(0, seq)), (outs, pl.ds(seq, seq)), (ps, plane)]
    net = Gather(ctxs, pieces, [("block", ds_), ("half", ps)], refs[17:])
    core, ctx = net.core, net.ctx
    me = core * ctxs + ctx
    loads = [
        pltpu.make_async_copy(proj, ps.at[me, plane], load.at[0]),
        pltpu.make_async_copy(mlp.at[1], wide, load.at[1]),
    ]
    for copy in loads:
        copy.start()
    greet_all(net.peers())
    loads[0].wait()
    net.send_own([2])
    loads[1].wait()

    def narrow(g, carry):
        part = pl.ds(pl.multiple_of(g * 16, 16), 16)
        ds_[plane, part, :] = wide[part, :].astype(BF)
        return carry

    lax.fori_loop(0, wide.shape[0] // 16, narrow, 0)
    net.board_start(0)

    def put(rows, lanes, values):
        outs[me, rows, lanes] = values

    hops = list(range(1, ctxs))
    for s in range(2):
        for pair in range(pairs):
            attend_part(
                q_ref, k_ref, v_ref, col_ref, row_ref.at[s], l_ref, put,
                s * seq, seq, pair, (s * pairs + pair) * (128 // HD),
            )
            if s * pairs + pair == 2 * pairs - 1:
                net.send_own([1])
            if hops:
                net.hop(hops.pop(0), [2])
                if not hops:
                    net.board_start(1)
            if s * pairs + pair == pairs - 1:
                net.send_own([0])
                net.board_pass(0)
    for k in hops:
        net.hop(k, [2])
    if hops:
        net.board_start(1)

    def copy_out(b):
        return pltpu.make_async_copy(outs.at[b], o_out.at[b], store.at[b])

    copy_out(me).start()
    for k in range(1, ctxs):
        net.hop(k, [0])
        if k == 2 or ctxs == 2:
            net.board_pass(1)
        net.hop(k, [1])
        net.distant(k, lambda block: copy_out(core * ctxs + block).start())
        net.side_arrive(k - 1, [0, 1])
        if k == 1:
            copy_out((1 - core) * ctxs + ctx).start()
            net.board_finish(0)
        else:
            net.distant(k - 1, lambda block: copy_out((1 - core) * ctxs + block).start())
    tail = [
        pltpu.make_async_copy(ds_, d_out, store.at[2 * ctxs]),
        pltpu.make_async_copy(ps, p_out, store.at[2 * ctxs + 1]),
    ]
    tail[0].start()
    for k in range(ctxs):
        net.side_arrive(k, [2])
    net.board_finish(1)
    net.board_shared(1)
    tail[1].start()
    net.side_arrive(ctxs - 1, [0, 1])
    net.distant(ctxs - 1, lambda block: copy_out((1 - core) * ctxs + block).start())
    net.close()
    for copy in tail:
        copy.wait()
    for b in range(2 * ctxs):
        copy_out(b).wait()


def second_call(ctxs, query, key, value, col, row, proj, mlp):
    team = 2 * ctxs
    count, feats = query.shape
    seq = count // 2
    arows, frows = proj.shape[0], mlp.shape[1]
    shapes = [(team, count, feats), (team, 4, arows, D), (4, frows, D)]
    dma = pltpu.SemaphoreType.DMA
    hbm, vmem = pl.BlockSpec(memory_space=pl.ANY), pl.BlockSpec(memory_space=pltpu.VMEM)

    def kernel(*refs):
        second_kernel(ctxs, refs)

    return pl.pallas_call(
        kernel,
        out_shape=[jax.ShapeDtypeStruct(shape, BF) for shape in shapes]
        + [jax.ShapeDtypeStruct((2 * feats // HD, seq, 1), F32)],
        in_specs=[vmem] * 5 + [hbm] * 2,
        out_specs=[hbm] * 3 + [vmem],
        scratch_shapes=[pltpu.VMEM(shape, BF) for shape in shapes]
        + [pltpu.VMEM((frows, D), F32)]
        + [dma((2,)), dma((team + 2,))]
        + Gather.scratch(ctxs, 3, 2),
        compiler_params=pltpu.CompilerParams(
            collective_id=2, has_side_effects=True, vmem_limit_bytes=VMEM_LIMIT
        ),
        cost_estimate=pl.CostEstimate(
            flops=4 * count * seq * feats, bytes_accessed=24 * count * feats, transcendentals=0
        ),
        name="second",
    )(query, key, value, col, row, proj, mlp)


def third_kernel(ctxs, refs):
    att, proj, x_all, gain, gate, up, down, dy = refs[:8]
    m_out, a_out, n_out, o_out, g_out, u_out, d_out = refs[8:15]
    pv, gv, uv, dv, ys, hs, gs, us, ob, xb, nb, sb = refs[15:27]
    load, block_sem, store, late = refs[27:31]
    team, own = ys.shape[0], ys.shape[1]
    wide = gv.shape[0]
    pieces = [(ys, pl.ds(0, own // 2)), (ys, pl.ds(own // 2, own // 2))]
    net = Gather(ctxs, pieces, [("block", dv)], refs[31:])
    plane, core, ctx = net.plane, net.core, net.ctx
    me = core * ctxs + ctx
    loads = [
        pltpu.make_async_copy(dy, ys.at[me], load.at[0]),
        pltpu.make_async_copy(down, dv.at[plane], load.at[1]),
        pltpu.make_async_copy(proj, pv, load.at[2]),
        pltpu.make_async_copy(gate, gv, load.at[3]),
        pltpu.make_async_copy(up, uv, load.at[4]),
    ]

    def fetch(i):
        slot = lax.rem(i, 2)
        rows = pl.ds(pl.multiple_of(i * own, own), own)
        return (
            pltpu.make_async_copy(att.at[:, rows], ob.at[slot], block_sem.at[0, slot]),
            pltpu.make_async_copy(x_all.at[i], xb.at[slot], block_sem.at[1, slot]),
        )

    def n_store(i):
        return pltpu.make_async_copy(nb.at[lax.rem(i, 2)], n_out.at[i], store.at[0, lax.rem(i, 2)])

    def s_store(i, out):
        return pltpu.make_async_copy(sb.at[lax.rem(i, 2)], out.at[i], store.at[1, lax.rem(i, 2)])

    for copy in loads:
        copy.start()
    for copy in fetch(0):
        copy.start()
    greet_all(net.peers())
    loads[0].wait()
    net.send_own([0, 1])
    loads[1].wait()
    net.board_start(0)
    for copy in loads[2:]:
        copy.wait()

    steps = [(hop, chunk) for hop in range(1, ctxs) for chunk in range(2)]
    stages = []
    for i, step in enumerate(steps[: 2 * (ctxs - 2)] if ctxs > 2 else []):
        stages.append((min(2 * i + 1, team - 1), step))

    def forward(i, carry):
        slot = lax.rem(i, 2)
        for copy in fetch(i):
            copy.wait()

        @pl.when(i + 1 < team)
        def _():
            for copy in fetch(i + 1):
                copy.start()

        total = xb[slot].astype(F32)
        for t in range(team):
            total = total + mm(ob[slot, t], pv[t], 1, 0)

        @pl.when(i >= 2)
        def _():
            n_store(i - 2).wait()

        nb[slot] = (total * norm_scale(total) * gain[...]).astype(BF)
        n_store(i).start()

        @pl.when(i == me)
        def _():
            m_out[...] = total
            keep = pltpu.make_async_copy(ob.at[slot], a_out, late.at[0])
            keep.start()
            keep.wait()

        normed = nb[slot]
        for first in range(0, wide, 512):
            part = slice(first, first + 512)
            g = mm(normed, gv[part, :], 1, 1)
            u = mm(normed, uv[part, :], 1, 1)
            sig = 1.0 / (1.0 + jnp.exp(-g))
            lit = g * sig
            hs[i, :, part] = (lit * u).astype(BF)
            gs[i, :, part] = (u * sig * (1.0 + g * (1.0 - sig))).astype(BF)
            us[i, :, part] = lit.astype(BF)
        for at, (hop, chunk) in stages:

            @pl.when(i == at)
            def _():
                net.hop(hop, [chunk])

        @pl.when(i == 1)
        def _():
            net.board_pass(0)

        return carry

    lax.fori_loop(0, team, forward, 0)
    n_store(team - 2).wait()
    n_store(team - 1).wait()
    net.board_finish(0)

    def outward(i, carry):
        @pl.when(i >= 2)
        def _():
            s_store(i - 2, o_out).wait()

        sb[lax.rem(i, 2)] = mm(hs[i], dv[...].reshape(wide, D), 1, 0).astype(BF)
        s_store(i, o_out).start()

        @pl.when(i == team // 2)
        def _():
            net.hop(ctxs - 1, [0])

        return carry

    def backward(side_core):
        def action(block):
            b = side_core * ctxs + block
            for p in range(4):
                cols = slice(p * (wide // 4), (p + 1) * (wide // 4))
                dh = mm(ys[b], dv[p], 1, 1)
                gs[b, :, cols] = (dh * gs[b, :, cols].astype(F32)).astype(BF)
                us[b, :, cols] = (dh * us[b, :, cols].astype(F32)).astype(BF)
            pltpu.make_async_copy(gs.at[b], g_out.at[b], late.at[1 + b]).start()
            pltpu.make_async_copy(us.at[b], u_out.at[b], late.at[1 + team + b]).start()

        return action

    if ctxs == 2:
        lax.fori_loop(0, team, outward, 0)
    else:
        lax.fori_loop(0, team, outward, 0)
    s_store(team - 2, o_out).wait()
    s_store(team - 1, o_out).wait()
    backward(core)(ctx)
    net.side_arrive(0, [0, 1])
    backward(1 - core)(ctx)
    net.hop(ctxs - 1, [1])
    for k in range(1, ctxs):
        net.distant(k, backward(core))
        net.side_arrive(k, [0, 1])
        net.distant(k, backward(1 - core))
    for p in range(4):
        if p >= 2:
            s_store(p - 2, d_out).wait()
        hidden = hs[:, :, p * (wide // 4) : (p + 1) * (wide // 4)].reshape(team * own, wide // 4)
        sb[p % 2] = mm(hidden, ys[...].reshape(team * own, D), 0, 0).astype(BF)
        s_store(p, d_out).start()
    s_store(2, d_out).wait()
    s_store(3, d_out).wait()
    net.close()
    for b in range(team):
        pltpu.make_async_copy(gs.at[b], g_out.at[b], late.at[1 + b]).wait()
        pltpu.make_async_copy(us.at[b], u_out.at[b], late.at[1 + team + b]).wait()


def third_call(ctxs, att, proj, x_all, gain, gate, up, down, dy):
    team, own, wide = 2 * ctxs, dy.shape[0], gate.shape[0]
    feats = proj.shape[1]
    block, hidden = (team, own, D), (team, own, wide)
    shapes = [(team, own, feats), block, block, hidden, hidden, (4, wide // 4, D)]
    dma = pltpu.SemaphoreType.DMA
    hbm, vmem = pl.BlockSpec(memory_space=pl.ANY), pl.BlockSpec(memory_space=pltpu.VMEM)
    held = [proj.shape, gate.shape, up.shape, (4, wide // 4, D), block, hidden, hidden, hidden]
    held += [(2, team, own, feats), (2, own, D), (2, own, D), (2, own, D)]

    def kernel(*refs):
        third_kernel(ctxs, refs)

    return pl.pallas_call(
        kernel,
        out_shape=[jax.ShapeDtypeStruct((own, D), F32)]
        + [jax.ShapeDtypeStruct(shape, BF) for shape in shapes],
        in_specs=[hbm] * 3 + [vmem] + [hbm] * 4,
        out_specs=[vmem] + [hbm] * len(shapes),
        scratch_shapes=[pltpu.VMEM(shape, BF) for shape in held]
        + [dma((5,)), dma((2, 2)), dma((2, 2)), dma((2 * team + 1,))]
        + Gather.scratch(ctxs, 2, 1),
        compiler_params=pltpu.CompilerParams(
            collective_id=6, has_side_effects=True, vmem_limit_bytes=VMEM_LIMIT
        ),
        cost_estimate=pl.CostEstimate(
            flops=2 * team * own * D * (D + 5 * wide),
            bytes_accessed=30 * own * D,
            transcendentals=0,
        ),
        name="third",
    )(att, proj, x_all, gain, gate, up, down, dy)


class Cargo:
    def __init__(self, arrays, refs):
        refs = list(refs)
        self.parts = []
        for array in arrays:
            ref = None if Cargo.made(array) else refs.pop(0)
            self.parts += [None if ref is None else ref.at[i] for i in range(array.shape[0])]
        count = len(self.parts)
        self.sums, refs = refs[:count], refs[count:]
        self.kept, refs = refs[:count], refs[count:]
        self.got, refs = refs[:count], refs[count:]
        self.last, refs = refs[:count], refs[count:]
        self.load, self.one, self.two = refs
        self.plane, self.core, self.ctx = (
            lax.axis_index("plane"),
            lax.axis_index("core"),
            lax.axis_index("ctx"),
        )
        self.near = (
            self.plane + 1 - 2 * lax.rem(self.plane, 2),
            lax.rem(self.plane + 2, 4),
        )

    @staticmethod
    def made(array):
        return isinstance(array, jax.ShapeDtypeStruct)

    @staticmethod
    def given(arrays):
        return [array for array in arrays if not Cargo.made(array)]

    def peers(self):
        return [(near, self.core, self.ctx) for near in self.near]

    def rows(self, s, half):
        size = self.kept[s].shape[1] // 2
        return pl.ds(half * size, size)

    def remote(self, source, target, sems, index, near):
        return pltpu.make_async_remote_copy(
            src_ref=source,
            dst_ref=target,
            send_sem=sems.at[(0,) + index],
            recv_sem=sems.at[(1,) + index],
            device_id=(near, self.core, self.ctx),
            device_id_type=MESH_ID,
        )

    def first(self, half, s, b):
        block = self.near[half] if b == 0 else 3 - self.plane
        source = self.kept[s].at[block, self.rows(s, half)]
        target = self.got[s].at[half, b]
        return self.remote(source, target, self.one, (half, s, b), self.near[half])

    def fetch(self, s):
        return pltpu.make_async_copy(self.parts[s], self.kept[s], self.load.at[s])

    def second(self, half, s):
        source = self.kept[s].at[self.near[1 - half], self.rows(s, half)]
        target = self.last[s].at[half]
        return self.remote(source, target, self.two, (half, s), self.near[1 - half])

    def begin(self):
        for s in range(len(self.parts)):
            if self.parts[s] is not None:
                self.fetch(s).start()

    def start(self, slots=None):
        for s in range(len(self.parts)) if slots is None else slots:
            if self.parts[s] is not None:
                self.fetch(s).wait()
            for b in (1, 0):
                for half in range(2):
                    self.first(half, s, b).start()

    def middle(self, s):
        kept, got = self.kept[s], self.got[s]
        size = got.shape[2]
        for half in range(2):
            block = self.near[1 - half]
            self.first(half, s, 1).wait_recv()

            def group(g, carry):
                part = pl.ds(pl.multiple_of(g * 16, 16), 16)
                rows = pl.ds(pl.multiple_of(half * size + g * 16, 16), 16)
                total = kept[block, rows, :].astype(F32) + got[half, 1, part, :].astype(F32)
                kept[block, rows, :] = total.astype(BF)
                return carry

            lax.fori_loop(0, size // 16, group, 0)
            self.second(half, s).start()

    def end(self):
        for s in range(len(self.parts)):
            kept, got, last, sums = self.kept[s], self.got[s], self.last[s], self.sums[s]
            size = got.shape[2]
            for half in range(2):
                self.first(half, s, 0).wait_recv()
                self.second(half, s).wait_recv()

                def group(g, carry):
                    part = pl.ds(pl.multiple_of(g * 16, 16), 16)
                    rows = pl.ds(pl.multiple_of(half * size + g * 16, 16), 16)
                    total = kept[self.plane, rows, :].astype(F32)
                    total = total + got[half, 0, part, :].astype(F32)
                    total = total + last[half, part, :].astype(F32)
                    sums[rows, :] = total
                    return carry

                lax.fori_loop(0, size // 16, group, 0)
        for s in range(len(self.parts)):
            for half in range(2):
                self.first(half, s, 0).wait_send()
                self.first(half, s, 1).wait_send()
                self.second(half, s).wait_send()

    @staticmethod
    def rows_of(arrays):
        return [array.shape[2] for array in arrays for _ in range(array.shape[0])]

    @staticmethod
    def out_shapes(arrays):
        return [jax.ShapeDtypeStruct((rows, D), F32) for rows in Cargo.rows_of(arrays)]

    @staticmethod
    def scratch(arrays):
        rows = Cargo.rows_of(arrays)
        if not rows:
            return []
        dma = pltpu.SemaphoreType.DMA
        return (
            [pltpu.VMEM((4, r, D), BF) for r in rows]
            + [pltpu.VMEM((2, 2, r // 2, D), BF) for r in rows]
            + [pltpu.VMEM((2, r // 2, D), BF) for r in rows]
            + [dma((len(rows),)), dma((2, 2, len(rows), 2)), dma((2, 2, len(rows)))]
        )


def team_sum_kernel(ctxs, pairs, refs, cargo, more):
    lhs, rhs, out_ref = refs[:pairs], refs[pairs : 2 * pairs], refs[2 * pairs]
    refs = refs[2 * pairs + 1 :]
    lhs_v, rhs_v = refs[:pairs], refs[pairs : 2 * pairs]
    staged, theirs, mine, from_left, from_right, load, side, hops = refs[2 * pairs :]
    plane, core, ctx = lax.axis_index("plane"), lax.axis_index("core"), lax.axis_index("ctx")
    last = ctxs - 1
    away = last - ctx
    own = out_ref.shape[0]
    rows = own // CHUNKS
    other = (plane, 1 - core, ctx)
    loads = []
    for i in range(pairs):
        loads.append(pltpu.make_async_copy(rhs[i], rhs_v[i], load.at[0, i]))
        loads.append(pltpu.make_async_copy(lhs[i], lhs_v[i], load.at[1, i]))
    for copy in loads:
        copy.start()
    if cargo:
        cargo.begin()
    greet_all(
        [other]
        + [(plane, core, lax.rem(ctx + k, ctxs)) for k in range(1, ctxs)]
        + (cargo.peers() if cargo else [])
    )
    pending = list(range(len(cargo.parts))) if cargo else []
    ready = [i for i in pending if cargo.parts[i] is not None]
    if cargo:
        cargo.start(ready)
    for copy in loads:
        copy.wait()
    fills = []
    if more:
        other_in, other_v, made, tiles, sems = more
        other_copy = pltpu.make_async_copy(other_in, other_v, sems.at[2])
        other_copy.start()
        if made:

            def store(i, p):
                slot = (4 * i + p) % 2
                return pltpu.make_async_copy(tiles.at[slot], made[i].at[0, p], sems.at[slot])

            def tile(i, p):
                size = lhs_v[i].shape[1] // 4
                index = 4 * i + p
                if index >= 2:
                    store((index - 2) // 4, (index - 2) % 4).wait()
                part = lhs_v[i][:, p * size : (p + 1) * size]
                tiles[index % 2] = mm(part, other_v[...], 0, 0).astype(BF)
                store(i, p).start()

            fills = [functools.partial(tile, i, p) for i in range(len(made)) for p in range(4)]

    def produce(block, target):
        where = pl.ds(pl.multiple_of(block * own, own), own)

        def tile(t, carry):
            cols = pl.ds(pl.multiple_of(t * 512, 512), 512)
            total = mm(lhs_v[0][where, :], rhs_v[0][:, cols], 1, 0)
            for i in range(1, pairs):
                total = total + mm(lhs_v[i][where, :], rhs_v[i][:, cols], 1, 0)
            target[:, cols] = total.astype(BF)
            return carry

        lax.fori_loop(0, D // 512, tile, 0)

    def add(index, chunk, extra, slot):
        def group(g, carry):
            part = pl.ds(pl.multiple_of(chunk * rows + g * 16, 16), 16)
            total = mine[index, part, :].astype(F32) + theirs[index, part, :].astype(F32)
            if extra is not None:
                total = total + extra[slot, part, :].astype(F32)
            mine[index, part, :] = total.astype(BF)
            return carry

        lax.fori_loop(0, rows // 16, group, 0)

    def share(index):
        return pltpu.make_async_remote_copy(
            src_ref=staged.at[index],
            dst_ref=theirs.at[index],
            send_sem=side.at[0, index],
            recv_sem=side.at[1, index],
            device_id=other,
            device_id_type=MESH_ID,
        )

    def hop(way, slot, chunk, index):
        part = pl.ds(chunk * rows, rows)
        inbox = from_left if way == 0 else from_right
        return pltpu.make_async_remote_copy(
            src_ref=mine.at[index, part],
            dst_ref=inbox.at[slot, part],
            send_sem=hops.at[0, way, slot, chunk],
            recv_sem=hops.at[1, way, slot, chunk],
            device_id=(plane, core, ctx + 1 if way == 0 else ctx - 1),
            device_id_type=MESH_ID,
        )

    order = []
    for i in range((ctxs + 1) // 2):
        order += [last - i, i] if last - i != i else [i]
    for place in order:
        index = jnp.where(2 * ctx >= ctxs, last - place, place)
        produce((1 - core) * ctxs + index, staged.at[index])
        share(index).start()
        produce(core * ctxs + index, mine.at[index])

        if place > 0:

            @pl.when(ctx == 0)
            def _():
                share(place).wait_recv()
                for chunk in range(CHUNKS):
                    add(place, chunk, None, 0)
                    hop(0, ctxs - place, chunk, place).start()

            @pl.when(ctx == last)
            def _():
                share(last - place).wait_recv()
                for chunk in range(CHUNKS):
                    add(last - place, chunk, None, 0)
                    hop(1, ctxs - place, chunk, last - place).start()

    if more:
        other_copy.wait()
        if not made:
            fresh = [i for i in pending if cargo.parts[i] is None]
            for i, slot in enumerate(fresh):
                size = lhs_v[i].shape[1]
                product = mm(lhs_v[i][...], other_v[...], 0, 0).astype(BF)
                cargo.kept[slot][...] = product.reshape(4, size // 4, D)
                cargo.start([slot])

    for step in range(1, last):

        @pl.when((ctx > 0) & (step >= ctx))
        def _():
            index = last + ctx - step
            share(index).wait_recv()
            for chunk in range(CHUNKS):
                hop(0, step, chunk, index).wait_recv()
                add(index, chunk, from_left, step)

                @pl.when(ctx < last)
                def _():
                    hop(0, step + 1, chunk, index).start()

        @pl.when((away > 0) & (step >= away))
        def _():
            index = step - away
            share(index).wait_recv()
            for chunk in range(CHUNKS):
                hop(1, step, chunk, index).wait_recv()
                add(index, chunk, from_right, step)

                @pl.when(ctx > 0)
                def _():
                    hop(1, step + 1, chunk, index).start()

        for fill in fills[:3]:
            fill()
        fills = fills[3:]
        if pending:
            cargo.middle(pending.pop(0))
    for fill in fills:
        fill()
    for s in pending:
        cargo.middle(s)

    share(ctx).wait_recv()

    def close(way):
        for chunk in range(CHUNKS):
            hop(way, last, chunk, ctx).wait_recv()

    def finish(inboxes):
        def group(g, carry):
            part = pl.ds(pl.multiple_of(g * 16, 16), 16)
            total = mine[ctx, part, :].astype(F32) + theirs[ctx, part, :].astype(F32)
            for inbox in inboxes:
                total = total + inbox[last, part, :].astype(F32)
            out_ref[part, :] = total
            return carry

        lax.fori_loop(0, own // 16, group, 0)

    @pl.when(ctx == 0)
    def _():
        close(1)
        finish([from_right])

    @pl.when(ctx == last)
    def _():
        close(0)
        finish([from_left])

    @pl.when((ctx > 0) & (ctx < last))
    def _():
        close(0)
        close(1)
        finish([from_left, from_right])

    for index in range(ctxs):
        share(index).wait_send()
    for slot in range(1, ctxs):

        @pl.when((ctx < last) & (slot >= ctx + 1))
        def _():
            for chunk in range(CHUNKS):
                hop(0, slot, chunk, ctxs + ctx - slot).wait_send()

        @pl.when((ctx > 0) & (slot >= away + 1))
        def _():
            for chunk in range(CHUNKS):
                hop(1, slot, chunk, slot - 1 - away).wait_send()

    if more and made:
        store(len(made) - 1, 2).wait()
        store(len(made) - 1, 3).wait()
    if cargo:
        cargo.end()


def team_sum(ctxs, number, pairs, name, freight=(), other=None, outer=False):
    count = pairs[0][0].shape[0]
    own = count // (2 * ctxs)
    lhs, rhs = [a for a, _ in pairs], [b for _, b in pairs]
    dma = pltpu.SemaphoreType.DMA

    inputs = 2 * len(pairs)
    given = Cargo.given(freight)
    outputs = 1 + len(Cargo.rows_of(freight))
    scratch = [pltpu.VMEM(a.shape, BF) for a in lhs + rhs]
    scratch += [pltpu.VMEM((ctxs, own, D), BF)] * 5
    scratch += [dma((2, len(pairs))), dma((2, ctxs)), dma((2, 2, ctxs, CHUNKS))]
    made = [(1, 4, a.shape[1] // 4, D) for a in lhs] if outer else []
    extra = [other] if other is not None else []
    held = [pltpu.VMEM(a.shape, BF) for a in extra]
    held += [pltpu.VMEM((2,) + made[0][2:], BF)] if made else []
    held += [dma((3,))] if extra else []

    def kernel(*refs):
        ins, refs = refs[:inputs], refs[inputs:]
        parts, refs = refs[: len(given)], refs[len(given) :]
        more, refs = refs[: len(extra)], refs[len(extra) :]
        outs, refs = refs[:outputs], refs[outputs:]
        products, refs = refs[: len(made)], refs[len(made) :]
        mine, refs = refs[: len(scratch)], refs[len(scratch) :]
        spare, buffers = refs[: len(refs) - len(held)], refs[len(refs) - len(held) :]
        cargo = Cargo(freight, parts + outs[1:] + spare) if freight else None
        if more:
            tiles = buffers[1] if made else None
            more = (more[0], buffers[0], products, tiles, buffers[-1])
        team_sum_kernel(ctxs, len(pairs), ins + outs[:1] + mine, cargo, more)

    depth = sum(b.shape[0] for b in rhs)
    return pl.pallas_call(
        kernel,
        out_shape=[jax.ShapeDtypeStruct((own, D), F32)]
        + Cargo.out_shapes(freight)
        + [jax.ShapeDtypeStruct(shape, BF) for shape in made],
        in_specs=[pl.BlockSpec(memory_space=pl.ANY)] * (inputs + len(given) + len(extra)),
        out_specs=[pl.BlockSpec(memory_space=pltpu.VMEM)] * outputs
        + [pl.BlockSpec(memory_space=pl.ANY)] * len(made),
        scratch_shapes=scratch + Cargo.scratch(freight) + held,
        compiler_params=pltpu.CompilerParams(
            collective_id=number, has_side_effects=True, vmem_limit_bytes=VMEM_LIMIT
        ),
        cost_estimate=pl.CostEstimate(
            flops=2 * count * depth * D,
            bytes_accessed=2 * (count + D) * depth + 4 * own * D,
            transcendentals=0,
        ),
        name=name,
    )(*lhs, *rhs, *given, *extra)


def middle_kernel(ctxs, refs, freight):
    da, att, proj, out_part = refs[:4]
    refs = refs[4:]
    part, grad, joined, outs = refs[0], refs[1], refs[2], refs[3 : 3 + ctxs]
    first, sums, refs = refs[3 + ctxs], refs[4 + ctxs], refs[5 + ctxs :]
    pv, ov, sent, staged, mine, theirs, others, load, swap, side, shift = refs[:11]
    cargo = Cargo(freight, [part, sums] + list(refs[11:]))
    plane, core, ctx = cargo.plane, cargo.core, cargo.ctx
    me = core * ctxs + ctx
    loads = [
        pltpu.make_async_copy(proj, pv, load.at[0]),
        pltpu.make_async_copy(out_part, ov, load.at[1]),
    ]
    for copy in loads:
        copy.start()
    cargo.begin()
    partners = [
        (dc, dz) for dz in range(ctxs - 1, -1, -1) for dc in range(2) if dc + dz > 0
    ]

    def partner(dc, dz):
        return (core if dc == 0 else 1 - core, lax.rem(ctx + dz, ctxs))

    greet_all([(plane,) + partner(*step) for step in partners] + cargo.peers())
    cargo.start()
    loads[0].wait()

    def remote(source, target, sems, index, peer):
        return pltpu.make_async_remote_copy(
            src_ref=source,
            dst_ref=target,
            send_sem=sems.at[(0,) + index],
            recv_sem=sems.at[(1,) + index],
            device_id=(plane,) + peer,
            device_id_type=MESH_ID,
        )

    def piece(i, c, z, home):
        return remote(sent.at[c * ctxs + z], grad.at[home], swap, (i,), (c, z))

    for i, step in enumerate(partners):
        c, z = partner(*step)
        sent[c * ctxs + z] = mm(da[...], pv[c * ctxs + z], 1, 1).astype(BF)
        piece(i, c, z, me).start()
    grad[me] = mm(da[...], pv[me], 1, 1).astype(BF)
    loads[1].wait()

    def share(kind, z):
        source = ov.at[(1 - core) * ctxs + z] if kind == 0 else staged.at[z]
        target = others.at[z] if kind == 0 else theirs.at[z]
        return remote(source, target, side, (kind, z), (1 - core, ctx))

    for z in range(ctxs):
        share(0, z).start()
    for z in range(ctxs):
        staged[z] = mm(att[(1 - core) * ctxs + z], da[...], 0, 0).astype(BF)
        share(1, z).start()
    for z in range(ctxs):
        mine[z] = mm(att[core * ctxs + z], da[...], 0, 0).astype(BF)
    size = pv.shape[1]
    for k in list(range(1, ctxs)) + [0]:
        z = lax.rem(ctx + k, ctxs)
        share(0, z).wait_recv()
        target = outs[k - 1]

        def group(g, carry):
            part_ = pl.ds(pl.multiple_of(g * 16, 16), 16)
            total = ov[core * ctxs + z, part_, :].astype(F32) + others[z, part_, :].astype(F32)
            target[part_, :] = total.astype(BF)
            return carry

        lax.fori_loop(0, target.shape[0] // 16, group, 0)
        if k == 1:
            pass_on = remote(outs[0], first, shift, (0,), (core, z))
            pass_on.start()
    cargo.middle(0)
    for z in range(ctxs):
        share(1, z).wait_recv()
        for p in range(4):

            def group(g, carry):
                rows = pl.ds(pl.multiple_of(p * (size // 4) + g * 16, 16), 16)
                total = mine[z, rows, :].astype(F32) + theirs[z, rows, :].astype(F32)
                joined[p, z, pl.ds(pl.multiple_of(g * 16, 16), 16), :] = total.astype(BF)
                return carry

            lax.fori_loop(0, size // 64, group, 0)
    for i, (dc, dz) in enumerate(partners):
        c, z = core if dc == 0 else 1 - core, lax.rem(ctx + ctxs - dz, ctxs)
        piece(i, c, z, c * ctxs + z).wait_recv()
    cargo.end()
    pass_on.wait()
    for i, step in enumerate(partners):
        c, z = partner(*step)
        piece(i, c, z, me).wait_send()
    for z in range(ctxs):
        share(0, z).wait_send()
        share(1, z).wait_send()


def middle_call(ctxs, da, att, proj, out_part, part):
    team, own = 2 * ctxs, da.shape[0]
    feats = proj.shape[1]
    freight = (part,)
    dma = pltpu.SemaphoreType.DMA
    hbm, vmem = pl.BlockSpec(memory_space=pl.ANY), pl.BlockSpec(memory_space=pltpu.VMEM)
    block = (ctxs, own, D)

    def kernel(*refs):
        middle_kernel(ctxs, refs, freight)

    return pl.pallas_call(
        kernel,
        out_shape=[
            jax.ShapeDtypeStruct((team, own, feats), BF),
            jax.ShapeDtypeStruct((4, ctxs, feats // 4, D), BF),
        ]
        + [jax.ShapeDtypeStruct((own, D), BF)] * (ctxs + 1)
        + Cargo.out_shapes(freight),
        in_specs=[vmem, vmem, hbm, hbm, hbm],
        out_specs=[vmem] * (4 + ctxs),
        scratch_shapes=[
            pltpu.VMEM(proj.shape, BF),
            pltpu.VMEM(out_part.shape, BF),
            pltpu.VMEM((team, own, feats), BF),
            pltpu.VMEM((ctxs, feats, D), BF),
            pltpu.VMEM((ctxs, feats, D), BF),
            pltpu.VMEM((ctxs, feats, D), BF),
            pltpu.VMEM(block, BF),
            dma((2,)),
            dma((2, team - 1)),
            dma((2, 2, ctxs)),
            dma((2, 1)),
        ]
        + Cargo.scratch(freight),
        compiler_params=pltpu.CompilerParams(
            collective_id=7, has_side_effects=True, vmem_limit_bytes=VMEM_LIMIT
        ),
        cost_estimate=pl.CostEstimate(
            flops=4 * own * D * D, bytes_accessed=60 * own * D, transcendentals=0
        ),
        name="middle",
    )(da, att, proj, out_part, part)


def qkv_kernel(feats, x_ref, gain_ref, w_ref, c_ref, a_ref, b_ref, n_ref, q_ref, k_ref, v_ref):
    values = x_ref[...].astype(F32)
    normed = (values * norm_scale(values) * gain_ref[...]).astype(BF)
    n_ref[...] = normed
    cosine, low_sine, high_sine = [widen(ref[...], feats) for ref in (c_ref, a_ref, b_ref)]
    q = mm(normed, w_ref[0:feats], 1, 1)
    q_ref[...] = rope(q, cosine, low_sine, high_sine).astype(BF)
    k = mm(normed, w_ref[feats : 2 * feats], 1, 1)
    k_ref[...] = rope(k, cosine, low_sine, high_sine).astype(BF)
    v_ref[...] = mm(normed, w_ref[2 * feats :], 1, 1).astype(BF)


def qkv_call(x_all, gain, weights, tables):
    count = x_all.shape[0]
    feats = weights.shape[0] // 3
    turns = tables[0].shape[0] // BLOCK
    rows = pl.BlockSpec((BLOCK, D), lambda i: (i, 0))
    part = pl.BlockSpec((BLOCK, feats), lambda i: (i, 0))
    table = pl.BlockSpec((BLOCK, 128), lambda i: (i % turns, 0))
    out = jax.ShapeDtypeStruct((count, feats), BF)
    return pl.pallas_call(
        functools.partial(qkv_kernel, feats),
        grid=(count // BLOCK,),
        out_shape=(jax.ShapeDtypeStruct((count, D), BF), out, out, out),
        in_specs=[
            rows,
            pl.BlockSpec((1, D), lambda i: (0, 0)),
            pl.BlockSpec((3 * feats, D), lambda i: (0, 0)),
            table,
            table,
            table,
        ],
        out_specs=(rows, part, part, part),
        compiler_params=params(),
        cost_estimate=pl.CostEstimate(
            flops=6 * count * D * feats, bytes_accessed=4 * count * D, transcendentals=0
        ),
        name="qkv",
    )(x_all, gain, weights, *tables)


def allowed_keys(col_ref, row_ref, first, size, keys):
    same = col_ref[first : first + size, :] == row_ref[:, 0:keys]
    query_place = first + lax.broadcasted_iota(jnp.int32, (size, keys), 0)
    key_place = lax.broadcasted_iota(jnp.int32, (size, keys), 1)
    return same & (key_place <= query_place)


def attend_kernel(q_ref, k_ref, v_ref, col_ref, row_ref, o_ref, l_ref):
    length = q_ref.shape[0]
    for first in range(0, length, BLOCK):
        keys = first + BLOCK
        allowed = allowed_keys(col_ref, row_ref, first, BLOCK, keys)
        parts = []
        for head in range(q_ref.shape[1] // HD):
            lanes = slice(head * HD, (head + 1) * HD)
            query = q_ref[first:keys, lanes] * HD ** (-0.5)
            scores = jnp.where(allowed, mm(query, k_ref[0:keys, lanes], 1, 1), MASKED)
            highest = jnp.max(scores, -1, keepdims=True)
            shifted = jnp.exp(scores - highest)
            totals = jnp.sum(shifted, -1, keepdims=True)
            weights = (shifted * (1.0 / totals)).astype(BF)
            parts.append(mm(weights, v_ref[0:keys, lanes], 1, 0))
            l_ref[head, first:keys, :] = highest + jnp.log(totals)
        o_ref[first:keys, :] = jnp.concatenate(parts, 1).astype(BF)


def attend_call(query, key, value, col, row, seq):
    count, feats = query.shape
    pairs = feats // 128
    part = pl.BlockSpec((seq, 128), lambda s, h: (s, h))
    each = 128 // HD
    return pl.pallas_call(
        attend_kernel,
        grid=(2, pairs),
        out_shape=(
            jax.ShapeDtypeStruct((count, feats), BF),
            jax.ShapeDtypeStruct((2 * pairs * each, seq, 1), F32),
        ),
        in_specs=[
            part,
            part,
            part,
            pl.BlockSpec((seq, 1), lambda s, h: (s, 0)),
            pl.BlockSpec((None, 1, seq), lambda s, h: (s, 0, 0)),
        ],
        out_specs=(part, pl.BlockSpec((each, seq, 1), lambda s, h: (s * pairs + h, 0, 0))),
        compiler_params=params(2),
        cost_estimate=pl.CostEstimate(
            flops=4 * count * seq * feats, bytes_accessed=8 * count * feats, transcendentals=0
        ),
        name="attend",
    )(query, key, value, col, row)


def attend_back_kernel(
    q_ref, k_ref, v_ref, g_ref, l_ref, col_ref, row_ref, c_ref, a_ref, b_ref,
    dq_ref, dk_ref, dv_ref, key_total, value_total, query_total,
):
    length = q_ref.shape[0]
    scale = HD ** (-0.5)
    key_total[...] = jnp.zeros_like(key_total)
    value_total[...] = jnp.zeros_like(value_total)
    for first in range(0, length, BLOCK):
        keys = first + BLOCK
        allowed = allowed_keys(col_ref, row_ref, first, BLOCK, keys)
        dq_parts, dk_parts, dv_parts = [], [], []
        for head in range(q_ref.shape[1] // HD):
            lanes = slice(head * HD, (head + 1) * HD)
            query = q_ref[first:keys, lanes] * scale
            key = k_ref[0:keys, lanes]
            grad = g_ref[first:keys, lanes]
            scores = jnp.where(allowed, mm(query, key, 1, 1), MASKED)
            probs = jnp.exp(scores - l_ref[head, first:keys, :])
            grad_probs = mm(grad, v_ref[0:keys, lanes], 1, 1)
            inner = jnp.sum(probs * grad_probs, -1, keepdims=True)
            grad_scores = (probs * (grad_probs - inner)).astype(BF)
            dq_parts.append(mm(grad_scores, key, 1, 0) * scale)
            dk_parts.append(mm(grad_scores, query, 0, 0))
            dv_parts.append(mm(probs.astype(BF), grad, 0, 0))
        query_total[first:keys, :] = jnp.concatenate(dq_parts, 1)
        key_total[0:keys, :] += jnp.concatenate(dk_parts, 1)
        value_total[0:keys, :] += jnp.concatenate(dv_parts, 1)
    cosine, low_sine, high_sine = c_ref[...], a_ref[...], b_ref[...]
    dq_ref[...] = rope_back(query_total[...], cosine, low_sine, high_sine).astype(BF)
    dk_ref[...] = rope_back(key_total[...], cosine, low_sine, high_sine).astype(BF)
    dv_ref[...] = value_total[...].astype(BF)


def attend_back_call(
    query, key, value, grad, log_sums, col, row, tables, seq, freight=(), rider=(), number=None
):
    count, feats = query.shape
    pairs = feats // 128
    part = pl.BlockSpec((seq, 128), lambda s, h: (s, h))
    table = pl.BlockSpec((seq, 128), lambda s, h: (0, 0))
    each = 128 // HD
    out = jax.ShapeDtypeStruct((count, feats), BF)
    outputs = len(Cargo.rows_of(freight))

    def kernel(*refs):
        ins, refs = refs[:10], refs[10:]
        parts, refs = refs[: len(freight)], refs[len(freight) :]
        riders, refs = refs[: len(rider)], refs[len(rider) :]
        outs, refs = refs[:3], refs[3:]
        sums, refs = refs[:outputs], refs[outputs:]
        landed, refs = refs[: len(rider)], refs[len(rider) :]
        mine, spare = refs[:3], refs[3:]
        step = pl.program_id(0) * pairs + pl.program_id(1)
        if rider:
            held, got, sems = spare[-3:]
            spare = spare[:-3]
            plane, core, ctx = [lax.axis_index(name) for name in ALL]
            across = (plane, core, lax.rem(ctx + 2, 4))
            fetch = pltpu.make_async_copy(riders[0], held, sems.at[0])
            ride = pltpu.make_async_remote_copy(
                src_ref=held,
                dst_ref=got,
                send_sem=sems.at[1],
                recv_sem=sems.at[2],
                device_id=across,
                device_id_type=MESH_ID,
            )
        cargo = Cargo(freight, parts + sums + spare) if freight else None
        if freight:

            @pl.when(step == 0)
            def _():
                cargo.begin()
                if rider:
                    fetch.start()
                greet_all(cargo.peers() + ([across] if rider else []))
                if rider:
                    fetch.wait()
                    ride.start()
                cargo.start()

            @pl.when(step == 2 * pairs - 1)
            def _():
                for s in range(outputs):
                    cargo.middle(s)

        attend_back_kernel(*ins, *outs, *mine)
        if freight:

            @pl.when(step == 2 * pairs - 1)
            def _():
                cargo.end()
                if rider:
                    ride.wait()
                    landed[0][...] = got[...]

    more = dict(collective_id=number, has_side_effects=True) if freight else {}
    return pl.pallas_call(
        kernel,
        grid=(2, pairs),
        out_shape=[out, out, out]
        + Cargo.out_shapes(freight)
        + [jax.ShapeDtypeStruct(array.shape, BF) for array in rider],
        in_specs=[
            part,
            part,
            part,
            part,
            pl.BlockSpec((each, seq, 1), lambda s, h: (s * pairs + h, 0, 0)),
            pl.BlockSpec((seq, 1), lambda s, h: (s, 0)),
            pl.BlockSpec((None, 1, seq), lambda s, h: (s, 0, 0)),
            table,
            table,
            table,
        ]
        + [pl.BlockSpec(memory_space=pl.ANY)] * (len(freight) + len(rider)),
        out_specs=[part, part, part]
        + [pl.BlockSpec((rows, D), lambda s, h: (0, 0)) for rows in Cargo.rows_of(freight)]
        + [pl.BlockSpec(array.shape, lambda s, h: (0, 0)) for array in rider],
        scratch_shapes=[pltpu.VMEM((seq, 128), F32)] * 3
        + Cargo.scratch(freight)
        + ([pltpu.VMEM(rider[0].shape, BF)] * 2 + [pltpu.SemaphoreType.DMA((3,))] if rider else []),
        compiler_params=params(2, **more),
        cost_estimate=pl.CostEstimate(
            flops=10 * count * seq * feats, bytes_accessed=14 * count * feats, transcendentals=0
        ),
        name="attend_back",
    )(query, key, value, grad, log_sums, col, row, *tables, *freight, *rider)


def project_kernel(o_ref, w_ref, x_ref, gain_ref, m_ref, n_ref):
    total = x_ref[...].astype(F32)
    for index in range(o_ref.shape[0]):
        total = total + mm(o_ref[index], w_ref[index], 1, 0)
    m_ref[...] = total
    n_ref[...] = (total * norm_scale(total) * gain_ref[...]).astype(BF)


def project_call(attended, weights, x_all, gain):
    team, count, feats = attended.shape
    rows = pl.BlockSpec((BLOCK, D), lambda i: (i, 0))
    return pl.pallas_call(
        project_kernel,
        grid=(count // BLOCK,),
        out_shape=(
            jax.ShapeDtypeStruct((count, D), F32),
            jax.ShapeDtypeStruct((count, D), BF),
        ),
        in_specs=[
            pl.BlockSpec((team, BLOCK, feats), lambda i: (0, i, 0)),
            pl.BlockSpec((team, feats, D), lambda i: (0, 0, 0), pipeline_mode=pl.Buffered(1)),
            rows,
            pl.BlockSpec((1, D), lambda i: (0, 0)),
        ],
        out_specs=(rows, rows),
        compiler_params=params(),
        cost_estimate=pl.CostEstimate(
            flops=2 * count * D * D, bytes_accessed=10 * count * D, transcendentals=0
        ),
        name="project",
    )(attended, weights, x_all, gain)


def shifted(value, axis, size, step):
    return lax.ppermute(value, axis, [(i, (i + step) % size) for i in range(size)])


def plane_reduce(parts, planes):
    home = lax.axis_index("plane")
    rows = parts[0].shape[1]

    def block(index, first, size):
        return jnp.stack(
            [
                lax.dynamic_slice(part, (index, first, 0), (1, size, D))[0].astype(BF)
                for part in parts
            ],
            0,
        )

    if planes != 4:
        total = block(home, 0, rows).astype(F32)
        for k in range(1, planes):
            part = block(lax.rem(home + k, planes), 0, rows)
            total = total + shifted(part, "plane", planes, k).astype(F32)
        return total
    near_x, near_y = home + 1 - 2 * lax.rem(home, 2), lax.rem(home + 2, 4)
    far = 3 - home
    along = ([(0, 1), (1, 0), (2, 3), (3, 2)], [(0, 2), (2, 0), (1, 3), (3, 1)])
    size = rows // 2
    sums = []
    for half in range(2):
        one, two = (near_x, near_y) if half == 0 else (near_y, near_x)
        first = half * size
        sent = jnp.stack([block(one, first, size), block(far, first, size)], 0)
        got = lax.ppermute(sent, "plane", along[half]).astype(F32)
        kept = block(home, first, size).astype(F32) + got[0]
        passed = (block(two, first, size).astype(F32) + got[1]).astype(BF)
        sums.append(kept + lax.ppermute(passed, "plane", along[1 - half]).astype(F32))
    return jnp.concatenate(sums, 1)


def core_join(parts, ctxs):
    core = lax.axis_index("core")
    parts = parts.reshape((2, ctxs) + parts.shape[1:])
    got = shifted(lax.dynamic_index_in_dim(parts, 1 - core, 0, False), "core", 2, 1)
    kept = lax.dynamic_index_in_dim(parts, core, 0, False)
    joined = (kept.astype(F32) + got.astype(F32)).astype(BF)
    return jnp.moveaxis(joined, 1, 0)


def line_reduce(parts, ctxs):
    ctx = lax.axis_index("ctx")
    total = lax.dynamic_index_in_dim(parts, ctx, 0, False)
    for k in range(1, ctxs):
        part = lax.dynamic_index_in_dim(parts, lax.rem(ctx + k, ctxs), 0, False)
        total = total + shifted(part.astype(BF), "ctx", ctxs, k).astype(F32)
    return total


def after(value, *others):
    return lax.optimization_barrier((value,) + others)[0]


def team_join(parts, ctxs):
    core, ctx = lax.axis_index("core"), lax.axis_index("ctx")
    own = parts.shape[0] // (2 * ctxs)
    parts = parts.reshape(2 * ctxs, own, D)

    def block(which, k):
        return lax.dynamic_index_in_dim(parts, which * ctxs + (ctx + k) % ctxs, 0, False)

    joined = []
    for k in list(range(1, ctxs)) + [0]:
        got = shifted(block(1 - core, k), "core", 2, 1)
        both = block(core, k).astype(F32) + got.astype(F32)
        joined.append(both.astype(BF) if k > 0 else both)
    return joined


def team_finish(joined, ctxs):
    total = joined[-1].astype(F32)
    for k in range(1, ctxs):
        total = total + shifted(joined[k - 1], "ctx", ctxs, k).astype(F32)
    return total


def local(
    planes,
    ctxs,
    tokens,
    cotangent,
    segments,
    attn_weight,
    attn_first,
    attn_second,
    mlp_weight,
    mlp_first,
    mlp_second,
    gain_weight,
    gain_first,
    gain_second,
):
    team = 2 * ctxs
    devices = planes * team
    own = tokens.shape[0]
    seq = ctxs * own
    count = 2 * seq
    arows = attn_weight.shape[0]
    frows = mlp_weight.shape[0]
    gcols = gain_weight.shape[1]
    feats = planes * arows
    hidden_count = planes * frows
    whole_heads = arows % HD == 0
    me = lax.axis_index(TEAM)

    lines_seg = own // 128
    square = planes == 4 and ctxs == 4 and whole_heads and gcols == 64
    packed = jnp.zeros((8, 128), F32)
    own_gain = lax.reduce_precision(gain_weight, 8, 7)
    if square:
        side = lax.rem(lax.axis_index("ctx"), 2)
        packed = lax.dynamic_update_slice(packed, own_gain, (0, side * gcols))
    else:
        packed = packed.at[0:2, 0:gcols].set(own_gain)
    packed = packed.at[2 : 2 + lines_seg].set(segments.astype(F32).reshape(lines_seg, 128))
    attn_low = attn_weight.astype(BF)
    qkv_low = jnp.moveaxis(attn_low[:, :3], 1, 0)
    proj_low = attn_low[:, 3]
    gate_low, up_low, down_low = [mlp_weight[:, i].astype(BF) for i in range(3)]
    tables = rope_tables(seq)
    if square:
        mlp_slots = jnp.moveaxis(mlp_weight, 1, 0)
        x_all, normed, query, key, value, qkv, gate_w, small = front_call(
            ctxs, tokens, qkv_low, mlp_slots, packed, tables
        )
        normed = normed.reshape(count, D)
        query, key, value = [part.reshape(count, feats) for part in (query, key, value)]
        qkv = qkv.reshape(3 * feats, D)
        gate_w = gate_w.reshape(hidden_count, D)
        gains = small.reshape(planes, ctxs, 2, 8, 128)[:, :, :, 0:2].sum(2)
        gains = gains.transpose(2, 0, 1, 3).reshape(2, D)
        team_small = lax.dynamic_index_in_dim(small, lax.axis_index("plane"), 0, False)
        seg = team_small[:, 2 : 2 + lines_seg].reshape(count)
        seg_col, seg_row = seg.reshape(count, 1), seg.reshape(2, 1, seq)
        att_all, proj, up_w, log_sums = second_call(
            ctxs, query, key, value, seg_col, seg_row, proj_low, mlp_slots
        )
        proj = proj.reshape(team, feats, D)
        up_w = up_w.reshape(hidden_count, D)
        middle_own, att_own, normed_two, out_part, dgate, dup, down_part = third_call(
            ctxs, att_all, proj, x_all, gains[1:2], gate_w, up_w, down_low, cotangent
        )
        normed_two, out_part = normed_two.reshape(count, D), out_part.reshape(count, D)
        dgate, dup = dgate.reshape(count, hidden_count), dup.reshape(count, hidden_count)
        down_part = down_part.reshape(1, planes, frows, D)
    else:
        inputs = [tokens, packed, gate_low, up_low]
        lines = [(0, 0, 2), (1, 1, 1)]
        shapes = [((team, own, D), BF), ((team, 8, 128), F32)]
        boards = []
        if whole_heads:
            inputs += [proj_low, qkv_low]
            lines.append((4, 2, 1))
            shapes.append(((team, arows, D), BF))
            boards.append(("slots", lambda ins, outs: ins[5], len(shapes)))
            shapes.append(((3, planes, arows, D), BF))
        boards.append(("block", lambda ins, outs: ins[2], len(shapes)))
        shapes.append(((planes, frows, D), BF))
        boards.append(("block", lambda ins, outs: ins[3], len(shapes)))
        shapes.append(((planes, frows, D), BF))
        boards.append(("late", lambda ins, outs: outs[1], len(shapes)))
        shapes.append(((planes, team, 8, 128), F32))
        gathered = gather_call(planes, ctxs, 0, inputs, lines, boards, shapes, "gather_first")
        x_all = gathered[0].reshape(count, D)
        small = gathered[-1]
        gate_w = gathered[-3].reshape(hidden_count, D)
        up_w = gathered[-2].reshape(hidden_count, D)
        gains = small[:, :, 0:2, 0:gcols].transpose(2, 0, 1, 3).reshape(2, D)
        seg = gathered[1][:, 2 : 2 + lines_seg].reshape(count)
        seg_col, seg_row = seg.reshape(count, 1), seg.reshape(2, 1, seq)
        if whole_heads:
            qkv = gathered[3].reshape(3 * feats, D)
        else:
            qkv = lax.all_gather(qkv_low, ALL, axis=1, tiled=True)
            qkv = lax.dynamic_slice_in_dim(qkv, me * feats, feats, 1).reshape(3 * feats, D)
            proj = lax.all_gather(proj_low, ALL, axis=0, tiled=True).reshape(team, feats, D)

        normed, query, key, value = qkv_call(x_all, gains[0:1], qkv, tables)
        attended, log_sums = attend_call(query, key, value, seg_col, seg_row, seq)

        inputs = [attended, down_low]
        lines = [(0, 0, 2)]
        shapes = [((team, count, feats), BF)]
        boards = []
        if whole_heads:
            inputs.append(gathered[2])
            boards.append(("half", lambda ins, outs: ins[2], len(shapes)))
            shapes.append(((team, planes, arows, D), BF))
        boards.append(("block", lambda ins, outs: ins[1], len(shapes)))
        shapes.append(((planes, frows, D), BF))
        gathered = gather_call(planes, ctxs, 2, inputs, lines, boards, shapes, "gather_second")
        att_all = gathered[0]
        down_w = gathered[-1].reshape(hidden_count, D)
        if whole_heads:
            proj = gathered[1].reshape(team, feats, D)
        dy_all = lax.all_gather(after(cotangent, att_all), TEAM, axis=0, tiled=True)
        middle, normed_two = project_call(att_all, proj, x_all, gains[1:2])
        mlp_w = (gate_w, up_w, down_w)

        gate = mm(normed_two, mlp_w[0], 1, 1)
        up = mm(normed_two, mlp_w[1], 1, 1)
        hidden = (jax.nn.silu(gate) * up).astype(BF)
        out_part = mm(hidden, mlp_w[2], 1, 0).astype(BF)
        grad_hidden = mm(after(dy_all, out_part), mlp_w[2], 1, 1)
        sig = jax.nn.sigmoid(gate)
        dgate = (grad_hidden * up * sig * (1.0 + gate * (1.0 - sig))).astype(BF)
        dup = (grad_hidden * gate * sig).astype(BF)
        down_part = mm(hidden, dy_all, 0, 0).astype(BF).reshape(1, planes, frows, D)
        middle_own = lax.dynamic_slice_in_dim(middle, me * own, own, 0)
        att_own = lax.dynamic_slice_in_dim(att_all, me * own, own, 1)
    if square:
        dn2, *down_sum, gate_part, up_part = team_sum(
            ctxs,
            3,
            [(dgate, gate_w), (dup, up_w)],
            "sum_two",
            (down_part,),
            normed_two,
            True,
        )
    else:
        (dn2,) = team_sum(ctxs, 3, [(dgate, gate_w), (dup, up_w)], "sum_two")
        gate_part = mm(dgate, normed_two, 0, 0).astype(BF).reshape(1, planes, frows, D)
        up_part = mm(dup, normed_two, 0, 0).astype(BF).reshape(1, planes, frows, D)

    middle_part, gain_two_grad = norm_back(dn2, middle_own, norm_scale(middle_own), gains[1])
    grad_middle = cotangent.astype(F32) + middle_part
    grad_branch = grad_middle.astype(BF)
    freight, rider = (), ()
    if square:
        grad_att, proj_part, *rest = middle_call(
            ctxs, grad_branch, att_own, proj, out_part.reshape(team, own, D), gate_part
        )
        joined, first_out, gate_sum = rest[:ctxs], rest[ctxs], rest[ctxs + 1]
        rider = (joined[1],)
        freight = (proj_part.reshape(1, planes, ctxs * arows, D),)
    else:
        grad_att = jnp.einsum("td,sfd->stf", grad_branch, proj, preferred_element_type=F32)
        grad_att = lax.all_to_all(
            grad_att.astype(BF), TEAM, split_axis=0, concat_axis=0, tiled=True
        )
        output = (middle_own + team_finish(team_join(out_part, ctxs), ctxs)).astype(BF)
        proj_part = jnp.einsum("tsf,sd->tfd", att_own, grad_branch, preferred_element_type=F32)
        proj_part = proj_part.astype(BF)
        if whole_heads:
            proj_part = core_join(proj_part.reshape(team, planes, arows, D), ctxs)
            proj_part = proj_part.reshape(1, planes, ctxs * arows, D)
        else:
            proj_grad = lax.psum_scatter(
                proj_part.reshape(D, D), ALL, scatter_dimension=0, tiled=True
            ).astype(F32)

    dq, dk, dv, *proj_sum = attend_back_call(
        query,
        key,
        value,
        grad_att.reshape(count, feats),
        log_sums,
        seg_col,
        seg_row,
        tables,
        seq,
        freight,
        rider,
        5,
    )
    pairs = [(dq, qkv[0:feats]), (dk, qkv[feats : 2 * feats]), (dv, qkv[2 * feats :])]
    if square:
        freight = (up_part, jax.ShapeDtypeStruct((3, planes, arows, D), BF))
        dn1, up_sum, *attn_sums = team_sum(ctxs, 4, pairs, "sum_one", freight, normed)
        proj_sum, second_out = proj_sum
        mlp_grad = jnp.stack([gate_sum, up_sum, down_sum[0]], 1)
    else:
        (dn1,) = team_sum(ctxs, 4, pairs, "sum_one")
        dqkv = jnp.concatenate([dq, dk, dv], 1)
        qkv_part = mm(dqkv, normed, 0, 0).astype(BF)
        mlp_grad = [plane_reduce([p[0]], planes)[0] for p in (gate_part, up_part, down_part)]
        mlp_grad = jnp.stack(mlp_grad, 1)
        if whole_heads:
            attn_part = qkv_part.reshape(3, planes, arows, D)
            attn_grad = plane_reduce([attn_part[i] for i in range(3)], planes)
            proj_grad = plane_reduce([proj_part[0]], planes)[0].reshape(ctxs, arows, D)
            proj_grad = line_reduce(proj_grad, ctxs)
        else:
            padded = lax.dynamic_update_slice_in_dim(
                jnp.zeros((3, D, D), BF), qkv_part.reshape(3, feats, D), me * feats, 1
            )
            attn_grad = lax.psum_scatter(padded, ALL, scatter_dimension=1, tiled=True)
            attn_grad = attn_grad.astype(F32)
            proj_grad = lax.psum_scatter(
                proj_part.reshape(D, D), ALL, scatter_dimension=0, tiled=True
            ).astype(F32)
        attn_grad = jnp.moveaxis(jnp.concatenate([attn_grad, proj_grad[None]], 0), 0, 1)

    source = tokens.astype(F32)
    source_part, gain_one_grad = norm_back(dn1, source, norm_scale(source), gains[0])
    grad_input = grad_middle + source_part
    gain_part = jnp.stack([gain_one_grad, gain_two_grad], 0).reshape(2, planes, team, gcols)
    gain_part = gain_part.transpose(1, 2, 0, 3)
    gain_part = jnp.pad(gain_part, ((0, 0), (0, 0), (0, 6), (0, 128 - gcols)))
    gain_grad = small_sum(planes, ctxs, gain_part)
    if square:
        gain_grad, last_out, proj_sum = lax.optimization_barrier((gain_grad, joined[2], proj_sum))
        output = middle_own + joined[3].astype(F32) + first_out.astype(F32)
        output = output + second_out.astype(F32) + shifted(last_out, "ctx", 4, 3).astype(F32)
        output = output.astype(BF)
        proj_sum = line_reduce(proj_sum.reshape(ctxs, arows, D), ctxs)
        attn_grad = jnp.stack(attn_sums + [proj_sum], 1)
    gain_grad = gain_grad[0:2, 0:gcols]

    attn_rate = (
        RATE_FACTOR
        * D ** (-0.5)
        * jnp.array([1.0, 1.0, 1.0, OUTPUT_BOOST], jnp.float32).reshape(1, 4, 1)
    )
    mlp_rate = RATE_FACTOR * jnp.array(
        [D ** (-0.5), D ** (-0.5), FF ** (-0.5)], jnp.float32
    ).reshape(1, 3, 1)
    attn_new = adam_update(attn_weight, attn_first, attn_second, attn_grad, attn_rate, WEIGHT_DECAY)
    mlp_new = adam_update(mlp_weight, mlp_first, mlp_second, mlp_grad, mlp_rate, WEIGHT_DECAY)
    gain_new = adam_update(gain_weight, gain_first, gain_second, gain_grad, GAIN_RATE, 0.0)
    return (
        output,
        grad_input,
        attn_new[0],
        attn_new[1][:, :3, :],
        attn_new[1][:, 3, :],
        attn_new[2],
        mlp_new[0],
        mlp_new[1],
        mlp_new[2],
        gain_new[0],
        gain_new[1],
        gain_new[2],
    )


def solution(mesh):
    dp, ctxs = mesh.shape["dp"], mesh.shape["ctx"]
    planes = dp // 2
    inner = Mesh(mesh.devices.reshape(planes, 2, ctxs), ALL)
    rows = P(ALL, None)
    cube = P(ALL, None, None)
    gain = P(None, ALL)

    def step(*args):
        return local(planes, ctxs, *args)

    return jax.shard_map(
        step,
        mesh=inner,
        in_specs=(rows, rows, P(ALL)) + (cube,) * 6 + (gain,) * 3,
        out_specs=(rows, rows, cube, cube, rows) + (cube,) * 4 + (gain,) * 3,
        check_vma=False,
    )
```

```python
import functools

import jax
import jax.numpy as jnp
import numpy as np
from jax import lax
from jax.experimental import pallas as pl
from jax.experimental.pallas import tpu as pltpu
from jax.sharding import Mesh
from jax.sharding import PartitionSpec as P

D = 2048
HEADS = 32
HD = 64
FF = 8192
STEP = 10


NORM_EPS = 1e-05
ROPE_BASE = 130000.0
BETA_ONE = 0.9
BETA_TWO = 0.95
ADAM_EPS = 1e-08
WEIGHT_DECAY = 0.1
RATE_FACTOR = 1.5
GAIN_RATE = 0.6
OUTPUT_BOOST = 12.0
MASKED = -1e30
BF = jnp.bfloat16
F32 = jnp.float32
ALL = ("plane", "core", "ctx")
TEAM = ("core", "ctx")


BLOCK = 256
CHUNKS = 2
VMEM_LIMIT = 60 * 1024 * 1024
MESH_ID = pl.DeviceIdType.MESH


def params(semantics=1, **more):
    return pltpu.CompilerParams(
        dimension_semantics=("arbitrary",) * semantics, vmem_limit_bytes=VMEM_LIMIT, **more
    )


def rope_tables(length):
    halved = HD // 2
    frequency = (ROPE_BASE ** (-(np.arange(halved) * 2.0 / HD))).astype(np.float32)
    angle = np.arange(length, dtype=np.float32)[:, None] * frequency[None, :]
    cosine, sine = np.cos(angle).astype(np.float32), np.sin(angle).astype(np.float32)
    zero = np.zeros_like(sine)
    return (
        jnp.asarray(np.concatenate([cosine] * 4, 1)),
        jnp.asarray(np.concatenate([-sine, zero] * 2, 1)),
        jnp.asarray(np.concatenate([zero, sine] * 2, 1)),
    )


def widen(table, feats):
    return jnp.concatenate([table] * (feats // 128), 1) if feats > 128 else table


def rope(values, cosine, low_sine, high_sine):
    width = values.shape[-1]
    ahead = pltpu.roll(values, width - HD // 2, 1)
    behind = pltpu.roll(values, HD // 2, 1)
    return values * cosine + ahead * low_sine + behind * high_sine


def rope_back(values, cosine, low_sine, high_sine):
    width = values.shape[-1]
    ahead = pltpu.roll(values, width - HD // 2, 1)
    behind = pltpu.roll(values, HD // 2, 1)
    return values * cosine - ahead * low_sine - behind * high_sine


def mm(a, b, ca, cb):
    return lax.dot_general(a, b, (((ca,), (cb,)), ((), ())), preferred_element_type=F32)


def norm_scale(values):
    return lax.rsqrt(jnp.mean(values * values, -1, keepdims=True) + NORM_EPS)


def norm_back(grad_normed, values, scale, gain):
    weighted = grad_normed * gain
    grad_values = scale * (
        weighted - values * scale * scale * jnp.mean(weighted * values, -1, keepdims=True)
    )
    return (grad_values, jnp.sum(grad_normed * values * scale, 0))


def adam_update(master, first, second, grad, rate, decay):
    first_new = BETA_ONE * first + (1.0 - BETA_ONE) * grad
    second_new = BETA_TWO * second + (1.0 - BETA_TWO) * grad * grad
    direction = (
        first_new
        / (1.0 - BETA_ONE**STEP)
        / (jnp.sqrt(second_new / (1.0 - BETA_TWO**STEP)) + ADAM_EPS)
    )
    return (first_new, second_new, master - rate * (direction + decay * master))


def greet_all(peers):
    barrier = pltpu.get_barrier_semaphore()
    for peer in peers:
        pl.semaphore_signal(barrier, inc=1, device_id=peer, device_id_type=MESH_ID)
    pl.semaphore_wait(barrier, len(peers))


def neighbours(planes, ctxs):
    plane, core, ctx = lax.axis_index("plane"), lax.axis_index("core"), lax.axis_index("ctx")
    column = [lax.rem(plane + k, planes) for k in range(1, planes)]
    group = [
        (core if dc == 0 else 1 - core, lax.rem(ctx + dz, ctxs))
        for dc in range(2)
        for dz in range(ctxs)
        if dc + dz > 0
    ]
    return plane, core, ctx, column, group


def gather_kernel(planes, ctxs, lines, boards, inputs, refs):
    ins, outs = refs[:inputs], refs[inputs : inputs + len(lines) + len(boards)]
    line_send, line_recv, side_send, side_recv, board_send, board_recv, pass_send, pass_recv, here = refs[
        inputs + len(lines) + len(boards) :
    ]
    plane, core, ctx = lax.axis_index("plane"), lax.axis_index("core"), lax.axis_index("ctx")
    last = ctxs - 1
    column = [lax.rem(plane + k, planes) for k in range(1, planes)]
    greet_all(
        [(p, core, ctx) for p in column]
        + [(plane, core, lax.rem(ctx + k, ctxs)) for k in range(1, ctxs)]
        + [(plane, 1 - core, ctx)]
    )
    other = (plane, 1 - core, ctx)
    pieces = []
    for source, target, chunks in lines:
        rows = ins[source].shape[0] // chunks
        for chunk in range(chunks):
            pieces.append((ins[source], outs[target], pl.ds(chunk * rows, rows)))

    def remote(source, target, send, recv, peer):
        return pltpu.make_async_remote_copy(
            src_ref=source,
            dst_ref=target,
            send_sem=send,
            recv_sem=recv,
            device_id=peer,
            device_id_type=MESH_ID,
        )

    def line(index, way, hop, block, peer_ctx, own):
        value, out, rows = pieces[index]
        slot = out.at[core * ctxs + block, rows]
        return remote(
            value.at[rows] if own else slot,
            slot,
            line_send.at[index, way, hop],
            line_recv.at[index, way, hop],
            (plane, core, peer_ctx),
        )

    def side(index, order, side_core, block, own):
        value, out, rows = pieces[index]
        slot = out.at[side_core * ctxs + block, rows]
        return remote(
            value.at[rows] if own else slot,
            slot,
            side_send.at[index, order],
            side_recv.at[index, order],
            other,
        )

    square = planes == 4
    near_x = plane + 1 - 2 * lax.rem(plane, 2)
    near_y = lax.rem(plane + 2, 4)
    far = 3 - plane

    def board_refs(index, home, half=None, own=True):
        kind, source, target = boards[index]
        value, out = source(ins, outs), outs[target]
        if kind in ("block", "late"):
            size = value.shape[0]
            part = pl.ds(0, size) if half is None else pl.ds(half * (size // 2), size // 2)
            slot = out.at[home, part]
            return (value.at[part] if own else slot), slot
        if kind == "slots":
            size = value.shape[1]
            part = pl.ds(0, size) if half is None else pl.ds(half * (size // 2), size // 2)
            slot = out.at[:, home, part]
            return (value.at[:, part] if own else slot), slot
        size = ctxs if half is None else ctxs // 2
        part = pl.ds(core * ctxs + (0 if half is None else half * size), size)
        slot = out.at[part, home]
        return (value.at[part] if own else slot), slot

    def board(index, k, home, peer):
        value, slot = board_refs(index, home)
        return remote(
            value, slot, board_send.at[index, k], board_recv.at[index, k], (peer, core, ctx)
        )

    sent = [(plane, 0, near_x), (plane, 1, near_x), (plane, 0, near_y), (plane, 1, near_y)]
    sent += [(near_y, 0, near_x), (near_x, 1, near_y)]
    landed = [near_x, near_x, near_y, near_y, far, far]

    def relay(index, k, arriving=False):
        home, half, peer = sent[k]
        value, slot = board_refs(index, landed[k] if arriving else home, half, k < 4)
        return remote(
            value, slot, board_send.at[index, k], board_recv.at[index, k], (peer, core, ctx)
        )

    def relayed(index):
        return square and boards[index][0] != "late"

    def board_start(index):
        if relayed(index):
            for k in (1, 2, 0, 3):
                relay(index, k).start()
            return
        for k, peer in enumerate(column):
            board(index, k, plane, peer).start()

    def board_pass(index):
        if relayed(index):
            relay(index, 2, True).wait_recv()
            relay(index, 4).start()
            relay(index, 1, True).wait_recv()
            relay(index, 5).start()

    def sources(index):
        if relayed(index):
            return [near_x, near_y, far]
        return [lax.rem(plane + planes - 1 - k, planes) for k in range(planes - 1)]

    def share(index, k, home):
        _, slot = board_refs(index, home)
        return remote(slot, slot, pass_send.at[index, k], pass_recv.at[index, k], other)

    def board_finish(index):
        if relayed(index):
            for k in (0, 3, 4, 5):
                relay(index, k, True).wait_recv()
        for k, home in enumerate(sources(index)):
            if not relayed(index):
                board(index, k, home, home).wait_recv()
            if boards[index][0] == "half":
                share(index, k, home).start()

    def board_close(index):
        if relayed(index):
            for k in range(6):
                relay(index, k).wait_send()
        else:
            for k, peer in enumerate(column):
                board(index, k, plane, peer).wait_send()
        if boards[index][0] == "half":
            out = outs[boards[index][2]]
            for k, home in enumerate(sources(index)):
                share(index, k, home).wait_send()
                slot = out.at[pl.ds((1 - core) * ctxs, ctxs), home]
                remote(
                    slot, slot, pass_send.at[index, k], pass_recv.at[index, k], other
                ).wait_recv()

    count = len(pieces)
    late = [i for i in range(len(boards)) if boards[i][0] == "late"]
    early = [i for i in range(len(boards)) if boards[i][0] != "late"]
    board_start(early[0]) if early else None

    @pl.when(ctx < last)
    def _():
        for i in range(count):
            line(i, 0, 1, ctx, ctx + 1, True).start()

    @pl.when(ctx > 0)
    def _():
        for i in range(count):
            line(i, 1, 1, ctx, ctx - 1, True).start()

    for i in range(count):
        side(i, 0, core, ctx, True).start()
    copies = []
    for i, (value, out, rows) in enumerate(pieces):
        copies.append(
            pltpu.make_async_copy(value.at[rows], out.at[core * ctxs + ctx, rows], here.at[i])
        )
    for i in early:
        kind, source, target = boards[i]
        slot = outs[target].at[plane] if kind == "block" else outs[target].at[:, plane]
        copies.append(pltpu.make_async_copy(source(ins, outs), slot, here.at[count + i]))
    for copy in copies:
        copy.start()

    passed = 0
    board_pass(early[0])
    if len(early) > 1:
        board_start(early[1])
    for hop in range(1, ctxs):

        @pl.when(ctx >= hop)
        def _():
            block = ctx - hop
            for i in range(count):
                line(i, 0, hop, block, ctx - 1, False).wait_recv()

                @pl.when(ctx < last)
                def _():
                    line(i, 0, hop + 1, block, ctx + 1, False).start()

                side(i, hop, core, block, False).start()

        @pl.when(ctx + hop <= last)
        def _():
            block = ctx + hop
            for i in range(count):
                line(i, 1, hop, block, ctx + 1, False).wait_recv()

                @pl.when(ctx > 0)
                def _():
                    line(i, 1, hop + 1, block, ctx - 1, False).start()

                side(i, last + hop, core, block, False).start()

        if passed + 1 < len(early):
            passed += 1
            board_pass(early[passed])
            if passed + 1 < len(early):
                board_start(early[passed + 1])
    for i in early:
        board_finish(i)

    for i in range(count):
        side(i, 0, 1 - core, ctx, False).wait_recv()
    for hop in range(1, ctxs):

        @pl.when(ctx >= hop)
        def _():
            for i in range(count):
                side(i, hop, 1 - core, ctx - hop, False).wait_recv()

        @pl.when(ctx + hop <= last)
        def _():
            for i in range(count):
                side(i, last + hop, 1 - core, ctx + hop, False).wait_recv()

    for copy in copies:
        copy.wait()
    for i in late:
        board_start(i)
        kind, source, target = boards[i]
        copy = pltpu.make_async_copy(source(ins, outs), outs[target].at[plane], here.at[count + i])
        copy.start()
        copy.wait()
    for i in late:
        board_finish(i)

    for i in range(len(boards)):
        board_close(i)
    for i in range(count):
        side(i, 0, core, ctx, True).wait_send()
    for hop in range(1, ctxs):

        @pl.when(ctx >= hop)
        def _():
            for i in range(count):
                side(i, hop, core, ctx - hop, False).wait_send()

        @pl.when(ctx + hop <= last)
        def _():
            for i in range(count):
                side(i, last + hop, core, ctx + hop, False).wait_send()

        @pl.when((ctx < last) & (ctx >= hop - 1))
        def _():
            for i in range(count):
                line(i, 0, hop, ctx - hop + 1, ctx + 1, False).wait_send()

        @pl.when((ctx > 0) & (ctx + hop - 1 <= last))
        def _():
            for i in range(count):
                line(i, 1, hop, ctx + hop - 1, ctx - 1, False).wait_send()


def gather_call(planes, ctxs, number, inputs, lines, boards, shapes, name):
    pieces = sum(chunks for _, _, chunks in lines)
    dma = pltpu.SemaphoreType.DMA

    def kernel(*refs):
        gather_kernel(planes, ctxs, lines, boards, len(inputs), refs)

    return pl.pallas_call(
        kernel,
        out_shape=tuple(jax.ShapeDtypeStruct(shape, dtype) for shape, dtype in shapes),
        in_specs=[pl.BlockSpec(memory_space=pl.ANY)] * len(inputs),
        out_specs=tuple(pl.BlockSpec(memory_space=pl.ANY) for _ in shapes),
        scratch_shapes=[
            dma((pieces, 2, ctxs + 1)),
            dma((pieces, 2, ctxs + 1)),
            dma((pieces, 2 * ctxs)),
            dma((pieces, 2 * ctxs)),
            dma((len(boards), max(planes, 6))),
            dma((len(boards), max(planes, 6))),
            dma((len(boards), planes)),
            dma((len(boards), planes)),
            dma((pieces + len(boards),)),
        ],
        compiler_params=pltpu.CompilerParams(collective_id=number, has_side_effects=True),
        name=name,
    )(*inputs)


def small_sum_kernel(planes, ctxs, value_ref, out_ref, got_one, middle, got_two, sems):
    plane, core, ctx, column, group = neighbours(planes, ctxs)
    greet_all([(p, core, ctx) for p in column] + [(plane, c, z) for c, z in group])

    def hop(index, source, target, peer):
        return pltpu.make_async_remote_copy(
            src_ref=source,
            dst_ref=target,
            send_sem=sems.at[0, index],
            recv_sem=sems.at[1, index],
            device_id=peer,
            device_id_type=MESH_ID,
        )

    first = [
        hop(i, value_ref.at[p], got_one.at[i], (p, core, ctx)) for i, p in enumerate(column)
    ]
    for copy in first:
        copy.start()
    total = value_ref[plane]
    for i, copy in enumerate(first):
        copy.wait_recv()
        total = total + got_one[i]
    middle[...] = total
    base = len(column)
    second = [
        hop(base + i, middle.at[c * ctxs + z], got_two.at[i], (plane, c, z))
        for i, (c, z) in enumerate(group)
    ]
    for copy in second:
        copy.start()
    total = middle[core * ctxs + ctx]
    for i, copy in enumerate(second):
        copy.wait_recv()
        total = total + got_two[i]
    out_ref[...] = total
    for copy in first + second:
        copy.wait_send()


def small_sum(planes, ctxs, value):
    hops = planes + 2 * ctxs - 2
    tile = value.shape[2:]
    return pl.pallas_call(
        functools.partial(small_sum_kernel, planes, ctxs),
        out_shape=jax.ShapeDtypeStruct(tile, F32),
        in_specs=[pl.BlockSpec(memory_space=pltpu.VMEM)],
        out_specs=pl.BlockSpec(memory_space=pltpu.VMEM),
        scratch_shapes=[
            pltpu.VMEM((planes - 1, 2 * ctxs) + tile, F32),
            pltpu.VMEM((2 * ctxs,) + tile, F32),
            pltpu.VMEM((2 * ctxs - 1,) + tile, F32),
            pltpu.SemaphoreType.DMA((2, hops)),
        ],
        compiler_params=pltpu.CompilerParams(collective_id=1, has_side_effects=True),
        name="small_sum",
    )(value)


class Gather:
    def __init__(self, ctxs, pieces, boards, sems):
        self.ctxs, self.pieces, self.boards = ctxs, pieces, boards
        self.line_sem, self.side_sem, self.board_sem, self.pass_sem = sems
        self.plane, self.core, self.ctx = (
            lax.axis_index("plane"),
            lax.axis_index("core"),
            lax.axis_index("ctx"),
        )
        self.last = ctxs - 1
        self.near_x = self.plane + 1 - 2 * lax.rem(self.plane, 2)
        self.near_y = lax.rem(self.plane + 2, 4)
        self.far = 3 - self.plane

    @staticmethod
    def scratch(ctxs, pieces, boards):
        dma = pltpu.SemaphoreType.DMA
        return [
            dma((2, pieces, 2, ctxs + 1)),
            dma((2, pieces, 2 * ctxs)),
            dma((2, boards, 6)),
            dma((2, boards, 3)),
        ]

    def peers(self):
        plane, core, ctx, ctxs = self.plane, self.core, self.ctx, self.ctxs
        return (
            [(plane, core, lax.rem(ctx + k, ctxs)) for k in range(1, ctxs)]
            + [(plane, 1 - core, ctx)]
            + [(near, core, ctx) for near in (self.near_x, self.near_y)]
        )

    def remote(self, slot, sem, index, peer):
        return pltpu.make_async_remote_copy(
            src_ref=slot,
            dst_ref=slot,
            send_sem=sem.at[(0,) + index],
            recv_sem=sem.at[(1,) + index],
            device_id=peer,
            device_id_type=MESH_ID,
        )

    def line(self, i, way, hop, block):
        buffer, rows = self.pieces[i]
        slot = buffer.at[self.core * self.ctxs + block, rows]
        away = 1 if way == 0 else self.ctxs - 1
        peer = (self.plane, self.core, lax.rem(self.ctx + away, self.ctxs))
        return self.remote(slot, self.line_sem, (i, way, hop), peer)

    def side(self, i, order, core, block):
        buffer, rows = self.pieces[i]
        slot = buffer.at[core * self.ctxs + block, rows]
        return self.remote(slot, self.side_sem, (i, order), (self.plane, 1 - self.core, self.ctx))

    def send_own(self, items):
        @pl.when(self.ctx < self.last)
        def _():
            for i in items:
                self.line(i, 0, 1, self.ctx).start()

        @pl.when(self.ctx > 0)
        def _():
            for i in items:
                self.line(i, 1, 1, self.ctx).start()

        for i in items:
            self.side(i, 0, self.core, self.ctx).start()

    def hop(self, k, items):
        ctx, last = self.ctx, self.last

        for i in items:

            @pl.when(ctx >= k)
            def _():
                self.line(i, 0, k, ctx - k).wait_recv()

                @pl.when(ctx < last)
                def _():
                    self.line(i, 0, k + 1, ctx - k).start()

                self.side(i, k, self.core, ctx - k).start()

            @pl.when(ctx + k <= last)
            def _():
                self.line(i, 1, k, ctx + k).wait_recv()

                @pl.when(ctx > 0)
                def _():
                    self.line(i, 1, k + 1, ctx + k).start()

                self.side(i, last + k, self.core, ctx + k).start()

    def side_arrive(self, k, items):
        ctx, last = self.ctx, self.last
        if k == 0:
            for i in items:
                self.side(i, 0, 1 - self.core, ctx).wait_recv()
            return

        @pl.when(ctx >= k)
        def _():
            for i in items:
                self.side(i, k, 1 - self.core, ctx - k).wait_recv()

        @pl.when(ctx + k <= last)
        def _():
            for i in items:
                self.side(i, last + k, 1 - self.core, ctx + k).wait_recv()

    def distant(self, k, action):
        ctx, last = self.ctx, self.last
        behind = (ctx >= k).astype(jnp.int32)
        ahead = (ctx + k <= last).astype(jnp.int32)

        def body(i, carry):
            action(jnp.where((behind == 1) & (i == 0), ctx - k, ctx + k))
            return carry

        lax.fori_loop(0, behind + ahead, body, 0)

    def board_slot(self, index, home, half):
        kind, buffer = self.boards[index]
        if kind == "block":
            size = buffer.shape[1] // 2
            return buffer.at[home, pl.ds(half * size, size)]
        if kind == "slots":
            size = buffer.shape[2] // 2
            return buffer.at[:, home, pl.ds(half * size, size)]
        size = self.ctxs // 2
        return buffer.at[pl.ds(self.core * self.ctxs + half * size, size), home]

    def relay(self, index, k, arriving=False):
        plane, near_x, near_y, far = self.plane, self.near_x, self.near_y, self.far
        sent = [(plane, 0, near_x), (plane, 1, near_x), (plane, 0, near_y), (plane, 1, near_y)]
        home, half, peer = (sent + [(near_y, 0, near_x), (near_x, 1, near_y)])[k]
        if arriving:
            home = [near_x, near_x, near_y, near_y, far, far][k]
        slot = self.board_slot(index, home, half)
        return self.remote(slot, self.board_sem, (index, k), (peer, self.core, self.ctx))

    def board_start(self, index):
        for k in (1, 2, 0, 3):
            self.relay(index, k).start()

    def board_pass(self, index):
        self.relay(index, 2, True).wait_recv()
        self.relay(index, 4).start()
        self.relay(index, 1, True).wait_recv()
        self.relay(index, 5).start()

    def share(self, index, k, core):
        buffer = self.boards[index][1]
        home = [self.near_x, self.near_y, self.far][k]
        slot = buffer.at[pl.ds(core * self.ctxs, self.ctxs), home]
        return self.remote(
            slot, self.pass_sem, (index, k), (self.plane, 1 - self.core, self.ctx)
        )

    def board_finish(self, index):
        for k in (0, 3, 4, 5):
            self.relay(index, k, True).wait_recv()
        if self.boards[index][0] == "half":
            for k in range(3):
                self.share(index, k, self.core).start()

    def board_shared(self, index):
        for k in range(3):
            self.share(index, k, 1 - self.core).wait_recv()

    def close(self):
        ctx, last = self.ctx, self.last
        items = range(len(self.pieces))
        for index in range(len(self.boards)):
            for k in range(6):
                self.relay(index, k).wait_send()
            if self.boards[index][0] == "half":
                for k in range(3):
                    self.share(index, k, self.core).wait_send()
        for i in items:
            self.side(i, 0, self.core, ctx).wait_send()
        for k in range(1, self.ctxs):

            @pl.when(ctx >= k)
            def _():
                for i in items:
                    self.side(i, k, self.core, ctx - k).wait_send()

            @pl.when(ctx + k <= last)
            def _():
                for i in items:
                    self.side(i, last + k, self.core, ctx + k).wait_send()

            @pl.when((ctx < last) & (ctx >= k - 1))
            def _():
                for i in items:
                    self.line(i, 0, k, ctx - k + 1).wait_send()

            @pl.when((ctx > 0) & (ctx + k - 1 <= last))
            def _():
                for i in items:
                    self.line(i, 1, k, ctx + k - 1).wait_send()


def front_kernel(ctxs, refs):
    tokens, qkv, mlp, packed, c_ref, a_ref, b_ref = refs[:7]
    x_out, n_out, q_out, k_out, v_out, w_out, g_out, small = refs[7:15]
    xs, ns, qs, ks, vs, ws, gs, wide, load, store, small_sem = refs[15:26]
    own = tokens.shape[0]
    half = own // 2
    pieces = [(xs, pl.ds(0, half)), (xs, pl.ds(half, half))]
    boards = [("slots", ws), ("block", gs)]
    net = Gather(ctxs, pieces, boards, refs[26:])
    plane, core, ctx = net.plane, net.core, net.ctx
    me = core * ctxs + ctx
    loads = [
        pltpu.make_async_copy(qkv, ws.at[:, plane], load.at[0]),
        pltpu.make_async_copy(tokens, xs.at[me], load.at[1]),
        pltpu.make_async_copy(mlp.at[0], wide, load.at[2]),
    ]
    for copy in loads:
        copy.start()
    others = [
        (core if dc == 0 else 1 - core, lax.rem(ctx + dz, ctxs))
        for dc in range(2)
        for dz in range(ctxs)
        if dc + dz > 0
    ]
    column = [lax.rem(plane + k, 4) for k in range(1, 4)]
    greet_all([(plane, c, z) for c, z in others] + [(p, core, ctx) for p in column])

    def tiny(index, source, target, peer):
        return pltpu.make_async_remote_copy(
            src_ref=source,
            dst_ref=target,
            send_sem=small_sem.at[0, index],
            recv_sem=small_sem.at[1, index],
            device_id=peer,
            device_id_type=MESH_ID,
        )

    small[plane, me] = packed[...]
    one = [
        tiny(i, packed, small.at[plane, me], (plane, c, z)) for i, (c, z) in enumerate(others)
    ]
    for copy in one:
        copy.start()
    for copy in loads[:2]:
        copy.wait()
    net.board_start(0)
    net.send_own([0, 1])
    i = 0
    for dc in range(2):
        for dz in range(ctxs):
            if dc + dz > 0:
                c, z = core if dc == 0 else 1 - core, lax.rem(ctx + ctxs - dz, ctxs)
                tiny(i, packed, small.at[plane, c * ctxs + z], (plane, c, z)).wait_recv()
                i += 1
    two = [
        tiny(i + k, small.at[plane], small.at[plane], (p, core, ctx))
        for k, p in enumerate(column)
    ]
    for copy in two:
        copy.start()
    loads[2].wait()

    def narrow(g, carry):
        part = pl.ds(pl.multiple_of(g * 16, 16), 16)
        gs[plane, part, :] = wide[part, :].astype(BF)
        return carry

    lax.fori_loop(0, wide.shape[0] // 16, narrow, 0)
    net.board_pass(0)
    net.board_start(1)
    for k in range(3):
        home = lax.rem(plane + 3 - k, 4)
        tiny(i + k, small.at[plane], small.at[home], (home, core, ctx)).wait_recv()
    tiles = [
        small[p, 2 * j][0:1] + small[p, 2 * j + 1][0:1] for p in range(4) for j in range(ctxs)
    ]
    gain = jnp.concatenate(tiles, 1)
    feats = q_out.shape[-1]
    stores = []

    blocks = [(xs, x_out), (ns, n_out), (qs, q_out), (ks, k_out), (vs, v_out)]

    def put(source, target, index):
        return pltpu.make_async_copy(source, target, store.at[index])

    def compute(side_core):
        def action(block):
            b = side_core * ctxs + block
            values = xs[b].astype(F32)
            normed = (values * norm_scale(values) * gain).astype(BF)
            ns[b] = normed
            rows = pl.ds(pl.multiple_of(block * own, own), own)
            cosine, low_sine, high_sine = [
                widen(ref[rows, :], feats) for ref in (c_ref, a_ref, b_ref)
            ]
            q = mm(normed, ws[0].reshape(feats, D), 1, 1)
            qs[b] = rope(q, cosine, low_sine, high_sine).astype(BF)
            k = mm(normed, ws[1].reshape(feats, D), 1, 1)
            ks[b] = rope(k, cosine, low_sine, high_sine).astype(BF)
            vs[b] = mm(normed, ws[2].reshape(feats, D), 1, 1).astype(BF)
            for i, (source, target) in enumerate(blocks):
                put(source.at[b], target.at[b], 5 * b + i).start()

        return action

    base = 10 * ctxs
    parts = [0, 1]
    stores = [put(s, t, base + i) for i, (s, t) in enumerate([(ws, w_out), (gs, g_out)])]
    net.hop(1, parts)
    net.board_finish(0)
    stores[0].start()
    compute(core)(ctx)
    net.side_arrive(0, parts)
    compute(1 - core)(ctx)
    net.board_pass(1)
    for k in range(1, ctxs):
        net.distant(k, compute(core))
        if k + 1 < ctxs:
            net.hop(k + 1, parts)
        net.side_arrive(k, parts)
        net.distant(k, compute(1 - core))
        if k == min(2, ctxs - 1):
            net.board_finish(1)
            stores[1].start()
    net.close()
    for copy in one + two:
        copy.wait_send()
    for copy in stores:
        copy.wait()
    for b in range(2 * ctxs):
        for i, (source, target) in enumerate(blocks):
            put(source.at[b], target.at[b], 5 * b + i).wait()


def front_call(ctxs, tokens, qkv, mlp, packed, tables):
    team = 2 * ctxs
    own, arows, frows = tokens.shape[0], qkv.shape[1], mlp.shape[1]
    feats = 4 * arows
    block, part = (team, own, D), (team, own, feats)
    shapes = [block, block, part, part, part, (3, 4, arows, D)]
    shapes += [(4, frows, D)]
    dma = pltpu.SemaphoreType.DMA
    hbm, vmem = pl.BlockSpec(memory_space=pl.ANY), pl.BlockSpec(memory_space=pltpu.VMEM)

    def kernel(*refs):
        front_kernel(ctxs, refs)

    return pl.pallas_call(
        kernel,
        out_shape=[jax.ShapeDtypeStruct(shape, BF) for shape in shapes]
        + [jax.ShapeDtypeStruct((4, team, 8, 128), F32)],
        in_specs=[hbm] * 3 + [vmem] * 4,
        out_specs=[hbm] * len(shapes) + [vmem],
        scratch_shapes=[pltpu.VMEM(shape, BF) for shape in shapes]
        + [pltpu.VMEM((frows, D), F32)]
        + [dma((3,)), dma((5 * team + 2,)), dma((2, team + 2))]
        + Gather.scratch(ctxs, 2, 2),
        compiler_params=pltpu.CompilerParams(
            collective_id=0, has_side_effects=True, vmem_limit_bytes=VMEM_LIMIT
        ),
        cost_estimate=pl.CostEstimate(
            flops=6 * team * own * D * feats, bytes_accessed=40 * own * D, transcendentals=0
        ),
        name="front",
    )(tokens, qkv, mlp, packed, *tables)


def attend_part(q_ref, k_ref, v_ref, col_ref, row_ref, l_ref, put, start, length, pair, unit):
    lanes = pl.ds(pl.multiple_of(pair * 128, 128), 128)
    for first in range(0, length, BLOCK):
        keys = first + BLOCK
        rows = pl.ds(pl.multiple_of(start + first, BLOCK), BLOCK)
        past = pl.ds(pl.multiple_of(start, BLOCK), keys)
        same = col_ref[rows, :] == row_ref[:, 0:keys]
        query_place = first + lax.broadcasted_iota(jnp.int32, (BLOCK, keys), 0)
        key_place = lax.broadcasted_iota(jnp.int32, (BLOCK, keys), 1)
        allowed = same & (key_place <= query_place)
        query, key, value = q_ref[rows, lanes], k_ref[past, lanes], v_ref[past, lanes]
        parts = []
        for head in range(128 // HD):
            cut = slice(head * HD, (head + 1) * HD)
            scores = mm(query[:, cut] * HD ** (-0.5), key[:, cut], 1, 1)
            scores = jnp.where(allowed, scores, MASKED)
            highest = jnp.max(scores, -1, keepdims=True)
            shifted = jnp.exp(scores - highest)
            totals = jnp.sum(shifted, -1, keepdims=True)
            weights = (shifted * (1.0 / totals)).astype(BF)
            parts.append(mm(weights, value[:, cut], 1, 0))
            l_ref[unit + head, first:keys, :] = highest + jnp.log(totals)
        put(rows, lanes, jnp.concatenate(parts, 1).astype(BF))


def second_kernel(ctxs, refs):
    q_ref, k_ref, v_ref, col_ref, row_ref, proj, mlp = refs[:7]
    o_out, p_out, d_out, l_ref = refs[7:11]
    outs, ps, ds_, wide, load, store = refs[11:17]
    count, feats = q_ref.shape
    seq = count // 2
    pairs = feats // 128
    plane = lax.axis_index("plane")
    pieces = [(outs, pl.ds(0, seq)), (outs, pl.ds(seq, seq)), (ps, plane)]
    net = Gather(ctxs, pieces, [("block", ds_), ("half", ps)], refs[17:])
    core, ctx = net.core, net.ctx
    me = core * ctxs + ctx
    loads = [
        pltpu.make_async_copy(proj, ps.at[me, plane], load.at[0]),
        pltpu.make_async_copy(mlp.at[1], wide, load.at[1]),
    ]
    for copy in loads:
        copy.start()
    greet_all(net.peers())
    loads[0].wait()
    net.send_own([2])
    loads[1].wait()

    def narrow(g, carry):
        part = pl.ds(pl.multiple_of(g * 16, 16), 16)
        ds_[plane, part, :] = wide[part, :].astype(BF)
        return carry

    lax.fori_loop(0, wide.shape[0] // 16, narrow, 0)
    net.board_start(0)

    def put(rows, lanes, values):
        outs[me, rows, lanes] = values

    hops = list(range(1, ctxs))
    for s in range(2):
        for pair in range(pairs):
            attend_part(
                q_ref, k_ref, v_ref, col_ref, row_ref.at[s], l_ref, put,
                s * seq, seq, pair, (s * pairs + pair) * (128 // HD),
            )
            if s * pairs + pair == 2 * pairs - 1:
                net.send_own([1])
            if hops:
                net.hop(hops.pop(0), [2])
                if not hops:
                    net.board_start(1)
            if s * pairs + pair == pairs - 1:
                net.send_own([0])
                net.board_pass(0)
    for k in hops:
        net.hop(k, [2])
    if hops:
        net.board_start(1)

    def copy_out(b):
        return pltpu.make_async_copy(outs.at[b], o_out.at[b], store.at[b])

    copy_out(me).start()
    for k in range(1, ctxs):
        net.hop(k, [0])
        if k == 2 or ctxs == 2:
            net.board_pass(1)
        net.hop(k, [1])
        net.distant(k, lambda block: copy_out(core * ctxs + block).start())
        net.side_arrive(k - 1, [0, 1])
        if k == 1:
            copy_out((1 - core) * ctxs + ctx).start()
            net.board_finish(0)
        else:
            net.distant(k - 1, lambda block: copy_out((1 - core) * ctxs + block).start())
    tail = [
        pltpu.make_async_copy(ds_, d_out, store.at[2 * ctxs]),
        pltpu.make_async_copy(ps, p_out, store.at[2 * ctxs + 1]),
    ]
    tail[0].start()
    for k in range(ctxs):
        net.side_arrive(k, [2])
    net.board_finish(1)
    net.board_shared(1)
    tail[1].start()
    net.side_arrive(ctxs - 1, [0, 1])
    net.distant(ctxs - 1, lambda block: copy_out((1 - core) * ctxs + block).start())
    net.close()
    for copy in tail:
        copy.wait()
    for b in range(2 * ctxs):
        copy_out(b).wait()


def second_call(ctxs, query, key, value, col, row, proj, mlp):
    team = 2 * ctxs
    count, feats = query.shape
    seq = count // 2
    arows, frows = proj.shape[0], mlp.shape[1]
    shapes = [(team, count, feats), (team, 4, arows, D), (4, frows, D)]
    dma = pltpu.SemaphoreType.DMA
    hbm, vmem = pl.BlockSpec(memory_space=pl.ANY), pl.BlockSpec(memory_space=pltpu.VMEM)

    def kernel(*refs):
        second_kernel(ctxs, refs)

    return pl.pallas_call(
        kernel,
        out_shape=[jax.ShapeDtypeStruct(shape, BF) for shape in shapes]
        + [jax.ShapeDtypeStruct((2 * feats // HD, seq, 1), F32)],
        in_specs=[vmem] * 5 + [hbm] * 2,
        out_specs=[hbm] * 3 + [vmem],
        scratch_shapes=[pltpu.VMEM(shape, BF) for shape in shapes]
        + [pltpu.VMEM((frows, D), F32)]
        + [dma((2,)), dma((team + 2,))]
        + Gather.scratch(ctxs, 3, 2),
        compiler_params=pltpu.CompilerParams(
            collective_id=2, has_side_effects=True, vmem_limit_bytes=VMEM_LIMIT
        ),
        cost_estimate=pl.CostEstimate(
            flops=4 * count * seq * feats, bytes_accessed=24 * count * feats, transcendentals=0
        ),
        name="second",
    )(query, key, value, col, row, proj, mlp)


def third_kernel(ctxs, refs):
    att, proj, x_all, gain, gate, up, mlp, dy = refs[:8]
    m_out, a_out, n_out, o_out, g_out, u_out, d_out = refs[8:15]
    pv, gv, uv, dv, ys, hs, gs, us, ob, xb, nb, sb, narrowed = refs[15:28]
    load, block_sem, store, late = refs[28:32]
    team, own = ys.shape[0], ys.shape[1]
    wide = gv.shape[0]
    pieces = [(ys, pl.ds(0, own // 2)), (ys, pl.ds(own // 2, own // 2))]
    net = Gather(ctxs, pieces, [("block", dv)], refs[32:])
    plane, core, ctx = net.plane, net.core, net.ctx
    me = core * ctxs + ctx
    loads = [
        pltpu.make_async_copy(dy, ys.at[me], load.at[0]),
        pltpu.make_async_copy(mlp.at[2], narrowed, load.at[1]),
        pltpu.make_async_copy(proj, pv, load.at[2]),
        pltpu.make_async_copy(gate, gv, load.at[3]),
        pltpu.make_async_copy(up, uv, load.at[4]),
    ]

    def fetch(i):
        slot = lax.rem(i, 2)
        rows = pl.ds(pl.multiple_of(i * own, own), own)
        size = att.shape[2]
        copies = [
            pltpu.make_async_copy(
                att.at[t, rows], ob.at[slot, :, pl.ds(t * size, size)], block_sem.at[t, slot]
            )
            for t in range(team)
        ]
        return copies + [pltpu.make_async_copy(x_all.at[i], xb.at[slot], block_sem.at[team, slot])]

    def n_store(i):
        return pltpu.make_async_copy(nb.at[lax.rem(i, 2)], n_out.at[i], store.at[0, lax.rem(i, 2)])

    def s_store(i, out):
        return pltpu.make_async_copy(sb.at[lax.rem(i, 2)], out.at[i], store.at[1, lax.rem(i, 2)])

    for copy in loads:
        copy.start()
    for copy in fetch(0):
        copy.start()
    greet_all(net.peers())
    loads[0].wait()
    net.send_own([0, 1])
    loads[1].wait()

    def narrow(g, carry):
        part = pl.ds(pl.multiple_of(g * 16, 16), 16)
        dv[plane, part, :] = narrowed[part, :].astype(BF)
        return carry

    lax.fori_loop(0, narrowed.shape[0] // 16, narrow, 0)
    net.board_start(0)
    for copy in loads[2:]:
        copy.wait()

    steps = [(hop, chunk) for hop in range(1, ctxs) for chunk in range(2)]
    stages = []
    for i, step in enumerate(steps[: 2 * (ctxs - 2)] if ctxs > 2 else []):
        stages.append((min(2 * i + 1, team - 1), step))

    def forward(i, carry):
        slot = lax.rem(i, 2)
        for copy in fetch(i):
            copy.wait()

        @pl.when(i + 1 < team)
        def _():
            for copy in fetch(i + 1):
                copy.start()

        total = xb[slot].astype(F32)
        total = total + mm(ob[slot], pv[...].reshape(ob.shape[2], D), 1, 0)

        @pl.when(i >= 2)
        def _():
            n_store(i - 2).wait()

        nb[slot] = (total * norm_scale(total) * gain[...]).astype(BF)
        n_store(i).start()

        @pl.when(i == me)
        def _():
            m_out[...] = total
            keep = pltpu.make_async_copy(ob.at[slot], a_out, late.at[0])
            keep.start()
            keep.wait()

        normed = nb[slot]
        for first in range(0, wide, 512):
            part = slice(first, first + 512)
            g = mm(normed, gv[part, :], 1, 1)
            u = mm(normed, uv[part, :], 1, 1)
            sig = 1.0 / (1.0 + jnp.exp(-g))
            lit = g * sig
            hs[i, :, part] = (lit * u).astype(BF)
            gs[i, :, part] = (u * sig * (1.0 + g * (1.0 - sig))).astype(BF)
            us[i, :, part] = lit.astype(BF)
        for at, (hop, chunk) in stages:

            @pl.when(i == at)
            def _():
                net.hop(hop, [chunk])

        @pl.when(i == 1)
        def _():
            net.board_pass(0)

        return carry

    lax.fori_loop(0, team, forward, 0)
    n_store(team - 2).wait()
    n_store(team - 1).wait()
    net.board_finish(0)

    def outward(i, carry):
        @pl.when(i >= 2)
        def _():
            s_store(i - 2, o_out).wait()

        sb[lax.rem(i, 2)] = mm(hs[i], dv[...].reshape(wide, D), 1, 0).astype(BF)
        s_store(i, o_out).start()

        @pl.when(i == team // 2)
        def _():
            net.hop(ctxs - 1, [0])

        return carry

    def backward(side_core):
        def action(block):
            b = side_core * ctxs + block
            for p in range(4):
                cols = slice(p * (wide // 4), (p + 1) * (wide // 4))
                dh = mm(ys[b], dv[p], 1, 1)
                gs[b, :, cols] = (dh * gs[b, :, cols].astype(F32)).astype(BF)
                us[b, :, cols] = (dh * us[b, :, cols].astype(F32)).astype(BF)
            pltpu.make_async_copy(gs.at[b], g_out.at[b], late.at[1 + b]).start()
            pltpu.make_async_copy(us.at[b], u_out.at[b], late.at[1 + team + b]).start()

        return action

    if ctxs == 2:
        lax.fori_loop(0, team, outward, 0)
    else:
        lax.fori_loop(0, team, outward, 0)
    s_store(team - 2, o_out).wait()
    s_store(team - 1, o_out).wait()
    backward(core)(ctx)
    net.side_arrive(0, [0, 1])
    backward(1 - core)(ctx)
    net.hop(ctxs - 1, [1])
    for k in range(1, ctxs):
        net.distant(k, backward(core))
        net.side_arrive(k, [0, 1])
        net.distant(k, backward(1 - core))
    for p in range(4):
        if p >= 2:
            s_store(p - 2, d_out).wait()
        hidden = hs[:, :, p * (wide // 4) : (p + 1) * (wide // 4)].reshape(team * own, wide // 4)
        sb[p % 2] = mm(hidden, ys[...].reshape(team * own, D), 0, 0).astype(BF)
        s_store(p, d_out).start()
    s_store(2, d_out).wait()
    s_store(3, d_out).wait()
    net.close()
    for b in range(team):
        pltpu.make_async_copy(gs.at[b], g_out.at[b], late.at[1 + b]).wait()
        pltpu.make_async_copy(us.at[b], u_out.at[b], late.at[1 + team + b]).wait()


def third_call(ctxs, att, proj, x_all, gain, gate, up, mlp, dy):
    team, own, wide = 2 * ctxs, dy.shape[0], gate.shape[0]
    feats = proj.shape[1]
    block, hidden = (team, own, D), (team, own, wide)
    shapes = [(own, team * feats), block, block, hidden, hidden, (4, wide // 4, D)]
    dma = pltpu.SemaphoreType.DMA
    hbm, vmem = pl.BlockSpec(memory_space=pl.ANY), pl.BlockSpec(memory_space=pltpu.VMEM)
    held = [proj.shape, gate.shape, up.shape, (4, wide // 4, D), block, hidden, hidden, hidden]
    held += [(2, own, team * feats), (2, own, D), (2, own, D), (2, own, D)]

    def kernel(*refs):
        third_kernel(ctxs, refs)

    return pl.pallas_call(
        kernel,
        out_shape=[jax.ShapeDtypeStruct((own, D), F32)]
        + [jax.ShapeDtypeStruct(shape, BF) for shape in shapes],
        in_specs=[hbm] * 3 + [vmem] + [hbm] * 4,
        out_specs=[vmem] + [hbm] * len(shapes),
        scratch_shapes=[pltpu.VMEM(shape, BF) for shape in held]
        + [pltpu.VMEM((wide // 4, D), F32)]
        + [dma((5,)), dma((team + 1, 2)), dma((2, 2)), dma((2 * team + 1,))]
        + Gather.scratch(ctxs, 2, 1),
        compiler_params=pltpu.CompilerParams(
            collective_id=6, has_side_effects=True, vmem_limit_bytes=VMEM_LIMIT
        ),
        cost_estimate=pl.CostEstimate(
            flops=2 * team * own * D * (D + 5 * wide),
            bytes_accessed=30 * own * D,
            transcendentals=0,
        ),
        name="third",
    )(att, proj, x_all, gain, gate, up, mlp, dy)


class Cargo:
    def __init__(self, arrays, refs):
        refs = list(refs)
        self.parts = []
        for array in arrays:
            ref = None if Cargo.made(array) else refs.pop(0)
            self.parts += [None if ref is None else ref.at[i] for i in range(array.shape[0])]
        count = len(self.parts)
        self.sums, refs = refs[:count], refs[count:]
        self.kept, refs = refs[:count], refs[count:]
        self.got, refs = refs[:count], refs[count:]
        self.last, refs = refs[:count], refs[count:]
        self.load, self.one, self.two = refs
        self.plane, self.core, self.ctx = (
            lax.axis_index("plane"),
            lax.axis_index("core"),
            lax.axis_index("ctx"),
        )
        self.near = (
            self.plane + 1 - 2 * lax.rem(self.plane, 2),
            lax.rem(self.plane + 2, 4),
        )

    @staticmethod
    def made(array):
        return isinstance(array, jax.ShapeDtypeStruct)

    @staticmethod
    def given(arrays):
        return [array for array in arrays if not Cargo.made(array)]

    def peers(self):
        return [(near, self.core, self.ctx) for near in self.near]

    def rows(self, s, half):
        size = self.kept[s].shape[1] // 2
        return pl.ds(half * size, size)

    def remote(self, source, target, sems, index, near):
        return pltpu.make_async_remote_copy(
            src_ref=source,
            dst_ref=target,
            send_sem=sems.at[(0,) + index],
            recv_sem=sems.at[(1,) + index],
            device_id=(near, self.core, self.ctx),
            device_id_type=MESH_ID,
        )

    def first(self, half, s, b):
        block = self.near[half] if b == 0 else 3 - self.plane
        source = self.kept[s].at[block, self.rows(s, half)]
        target = self.got[s].at[half, b]
        return self.remote(source, target, self.one, (half, s, b), self.near[half])

    def fetch(self, s):
        return pltpu.make_async_copy(self.parts[s], self.kept[s], self.load.at[s])

    def second(self, half, s):
        source = self.kept[s].at[self.near[1 - half], self.rows(s, half)]
        target = self.last[s].at[half]
        return self.remote(source, target, self.two, (half, s), self.near[1 - half])

    def begin(self):
        for s in range(len(self.parts)):
            if self.parts[s] is not None:
                self.fetch(s).start()

    def start(self, slots=None):
        for s in range(len(self.parts)) if slots is None else slots:
            if self.parts[s] is not None:
                self.fetch(s).wait()
            for b in (1, 0):
                for half in range(2):
                    self.first(half, s, b).start()

    def middle(self, s):
        kept, got = self.kept[s], self.got[s]
        size = got.shape[2]
        for half in range(2):
            block = self.near[1 - half]
            self.first(half, s, 1).wait_recv()

            def group(g, carry):
                part = pl.ds(pl.multiple_of(g * 16, 16), 16)
                rows = pl.ds(pl.multiple_of(half * size + g * 16, 16), 16)
                total = kept[block, rows, :].astype(F32) + got[half, 1, part, :].astype(F32)
                kept[block, rows, :] = total.astype(BF)
                return carry

            lax.fori_loop(0, size // 16, group, 0)
            self.second(half, s).start()

    def end(self):
        for s in range(len(self.parts)):
            kept, got, last, sums = self.kept[s], self.got[s], self.last[s], self.sums[s]
            size = got.shape[2]
            for half in range(2):
                self.first(half, s, 0).wait_recv()
                self.second(half, s).wait_recv()

                def group(g, carry):
                    part = pl.ds(pl.multiple_of(g * 16, 16), 16)
                    rows = pl.ds(pl.multiple_of(half * size + g * 16, 16), 16)
                    total = kept[self.plane, rows, :].astype(F32)
                    total = total + got[half, 0, part, :].astype(F32)
                    total = total + last[half, part, :].astype(F32)
                    sums[rows, :] = total
                    return carry

                lax.fori_loop(0, size // 16, group, 0)
        for s in range(len(self.parts)):
            for half in range(2):
                self.first(half, s, 0).wait_send()
                self.first(half, s, 1).wait_send()
                self.second(half, s).wait_send()

    @staticmethod
    def rows_of(arrays):
        return [array.shape[2] for array in arrays for _ in range(array.shape[0])]

    @staticmethod
    def out_shapes(arrays):
        return [jax.ShapeDtypeStruct((rows, D), F32) for rows in Cargo.rows_of(arrays)]

    @staticmethod
    def scratch(arrays):
        rows = Cargo.rows_of(arrays)
        if not rows:
            return []
        dma = pltpu.SemaphoreType.DMA
        return (
            [pltpu.VMEM((4, r, D), BF) for r in rows]
            + [pltpu.VMEM((2, 2, r // 2, D), BF) for r in rows]
            + [pltpu.VMEM((2, r // 2, D), BF) for r in rows]
            + [dma((len(rows),)), dma((2, 2, len(rows), 2)), dma((2, 2, len(rows)))]
        )


def team_sum_kernel(ctxs, pairs, refs, cargo, more):
    lhs, rhs, out_ref = refs[:pairs], refs[pairs : 2 * pairs], refs[2 * pairs]
    refs = refs[2 * pairs + 1 :]
    lhs_v, rhs_v = refs[:pairs], refs[pairs : 2 * pairs]
    staged, theirs, mine, from_left, from_right, load, side, hops = refs[2 * pairs :]
    plane, core, ctx = lax.axis_index("plane"), lax.axis_index("core"), lax.axis_index("ctx")
    last = ctxs - 1
    away = last - ctx
    own = out_ref.shape[0]
    rows = own // CHUNKS
    other = (plane, 1 - core, ctx)
    loads = [pltpu.make_async_copy(rhs[i], rhs_v[i], load.at[2 * ctxs, i]) for i in range(pairs)]
    for copy in loads:
        copy.start()

    def lhs_load(block, i):
        where = pl.ds(pl.multiple_of(block * own, own), own)
        return pltpu.make_async_copy(lhs[i].at[where], lhs_v[i].at[where], load.at[block, i])

    order = []
    for i in range((ctxs + 1) // 2):
        order += [last - i, i] if last - i != i else [i]
    order = [jnp.where(2 * ctx >= ctxs, last - place, place) for place in order]
    for index in order:
        for side_core in (1 - core, core):
            for i in range(pairs):
                lhs_load(side_core * ctxs + index, i).start()
    if cargo:
        cargo.begin()
    greet_all(
        [other]
        + [(plane, core, lax.rem(ctx + k, ctxs)) for k in range(1, ctxs)]
        + (cargo.peers() if cargo else [])
    )
    pending = list(range(len(cargo.parts))) if cargo else []
    ready = [i for i in pending if cargo.parts[i] is not None]
    if cargo:
        cargo.start(ready)
    for copy in loads:
        copy.wait()
    fills = []
    if more:
        other_in, other_v, made, tiles, sems = more
        other_copy = pltpu.make_async_copy(other_in, other_v, sems.at[2])
        other_copy.start()
        if made:

            def store(i, p):
                slot = (4 * i + p) % 2
                return pltpu.make_async_copy(tiles.at[slot], made[i].at[0, p], sems.at[slot])

            def tile(i, p):
                size = lhs_v[i].shape[1] // 4
                index = 4 * i + p
                if index >= 2:
                    store((index - 2) // 4, (index - 2) % 4).wait()
                part = lhs_v[i][:, p * size : (p + 1) * size]
                tiles[index % 2] = mm(part, other_v[...], 0, 0).astype(BF)
                store(i, p).start()

            fills = [functools.partial(tile, i, p) for i in range(len(made)) for p in range(4)]

    def produce(block, target):
        where = pl.ds(pl.multiple_of(block * own, own), own)
        for i in range(pairs):
            lhs_load(block, i).wait()

        def tile(t, carry):
            cols = pl.ds(pl.multiple_of(t * 512, 512), 512)
            total = mm(lhs_v[0][where, :], rhs_v[0][:, cols], 1, 0)
            for i in range(1, pairs):
                total = total + mm(lhs_v[i][where, :], rhs_v[i][:, cols], 1, 0)
            target[:, cols] = total.astype(BF)
            return carry

        lax.fori_loop(0, D // 512, tile, 0)

    def add(index, chunk, extra, slot):
        def group(g, carry):
            part = pl.ds(pl.multiple_of(chunk * rows + g * 16, 16), 16)
            total = mine[index, part, :].astype(F32) + theirs[index, part, :].astype(F32)
            if extra is not None:
                total = total + extra[slot, part, :].astype(F32)
            mine[index, part, :] = total.astype(BF)
            return carry

        lax.fori_loop(0, rows // 16, group, 0)

    def share(index):
        return pltpu.make_async_remote_copy(
            src_ref=staged.at[index],
            dst_ref=theirs.at[index],
            send_sem=side.at[0, index],
            recv_sem=side.at[1, index],
            device_id=other,
            device_id_type=MESH_ID,
        )

    def hop(way, slot, chunk, index):
        part = pl.ds(chunk * rows, rows)
        inbox = from_left if way == 0 else from_right
        return pltpu.make_async_remote_copy(
            src_ref=mine.at[index, part],
            dst_ref=inbox.at[slot, part],
            send_sem=hops.at[0, way, slot, chunk],
            recv_sem=hops.at[1, way, slot, chunk],
            device_id=(plane, core, lax.rem(ctx + (1 if way == 0 else last), ctxs)),
            device_id_type=MESH_ID,
        )

    places = []
    for i in range((ctxs + 1) // 2):
        places += [last - i, i] if last - i != i else [i]
    for place, index in zip(places, order):
        produce((1 - core) * ctxs + index, staged.at[index])
        share(index).start()
        produce(core * ctxs + index, mine.at[index])

        if place > 0:

            @pl.when(ctx == 0)
            def _():
                share(place).wait_recv()
                for chunk in range(CHUNKS):
                    add(place, chunk, None, 0)
                    hop(0, ctxs - place, chunk, place).start()

            @pl.when(ctx == last)
            def _():
                share(last - place).wait_recv()
                for chunk in range(CHUNKS):
                    add(last - place, chunk, None, 0)
                    hop(1, ctxs - place, chunk, last - place).start()

    if more:
        other_copy.wait()
        if not made:
            fresh = [i for i in pending if cargo.parts[i] is None]
            for i, slot in enumerate(fresh):
                size = lhs_v[i].shape[1]
                product = mm(lhs_v[i][...], other_v[...], 0, 0).astype(BF)
                cargo.kept[slot][...] = product.reshape(4, size // 4, D)
                cargo.start([slot])

    for step in range(1, last):

        @pl.when((ctx > 0) & (step >= ctx))
        def _():
            index = last + ctx - step
            share(index).wait_recv()
            for chunk in range(CHUNKS):
                hop(0, step, chunk, index).wait_recv()
                add(index, chunk, from_left, step)

                @pl.when(ctx < last)
                def _():
                    hop(0, step + 1, chunk, index).start()

        @pl.when((away > 0) & (step >= away))
        def _():
            index = step - away
            share(index).wait_recv()
            for chunk in range(CHUNKS):
                hop(1, step, chunk, index).wait_recv()
                add(index, chunk, from_right, step)

                @pl.when(ctx > 0)
                def _():
                    hop(1, step + 1, chunk, index).start()

        for fill in fills[:3]:
            fill()
        fills = fills[3:]
        if pending:
            cargo.middle(pending.pop(0))
    for fill in fills:
        fill()
    for s in pending:
        cargo.middle(s)

    share(ctx).wait_recv()

    def close(way):
        for chunk in range(CHUNKS):
            hop(way, last, chunk, ctx).wait_recv()

    def finish(inboxes):
        def group(g, carry):
            part = pl.ds(pl.multiple_of(g * 16, 16), 16)
            total = mine[ctx, part, :].astype(F32) + theirs[ctx, part, :].astype(F32)
            for inbox in inboxes:
                total = total + inbox[last, part, :].astype(F32)
            out_ref[part, :] = total
            return carry

        lax.fori_loop(0, own // 16, group, 0)

    @pl.when(ctx == 0)
    def _():
        close(1)
        finish([from_right])

    @pl.when(ctx == last)
    def _():
        close(0)
        finish([from_left])

    @pl.when((ctx > 0) & (ctx < last))
    def _():
        close(0)
        close(1)
        finish([from_left, from_right])

    for index in range(ctxs):
        share(index).wait_send()
    for slot in range(1, ctxs):

        @pl.when((ctx < last) & (slot >= ctx + 1))
        def _():
            for chunk in range(CHUNKS):
                hop(0, slot, chunk, ctxs + ctx - slot).wait_send()

        @pl.when((ctx > 0) & (slot >= away + 1))
        def _():
            for chunk in range(CHUNKS):
                hop(1, slot, chunk, slot - 1 - away).wait_send()

    if more and made:
        store(len(made) - 1, 2).wait()
        store(len(made) - 1, 3).wait()
    if cargo:
        cargo.end()


def team_sum(ctxs, number, pairs, name, freight=(), other=None, outer=False):
    count = pairs[0][0].shape[0]
    own = count // (2 * ctxs)
    lhs, rhs = [a for a, _ in pairs], [b for _, b in pairs]
    dma = pltpu.SemaphoreType.DMA

    inputs = 2 * len(pairs)
    given = Cargo.given(freight)
    outputs = 1 + len(Cargo.rows_of(freight))
    scratch = [pltpu.VMEM(a.shape, BF) for a in lhs + rhs]
    scratch += [pltpu.VMEM((ctxs, own, D), BF)] * 5
    scratch += [dma((2 * ctxs + 1, len(pairs))), dma((2, ctxs)), dma((2, 2, ctxs, CHUNKS))]
    made = [(1, 4, a.shape[1] // 4, D) for a in lhs] if outer else []
    extra = [other] if other is not None else []
    held = [pltpu.VMEM(a.shape, BF) for a in extra]
    held += [pltpu.VMEM((2,) + made[0][2:], BF)] if made else []
    held += [dma((3,))] if extra else []

    def kernel(*refs):
        ins, refs = refs[:inputs], refs[inputs:]
        parts, refs = refs[: len(given)], refs[len(given) :]
        more, refs = refs[: len(extra)], refs[len(extra) :]
        outs, refs = refs[:outputs], refs[outputs:]
        products, refs = refs[: len(made)], refs[len(made) :]
        mine, refs = refs[: len(scratch)], refs[len(scratch) :]
        spare, buffers = refs[: len(refs) - len(held)], refs[len(refs) - len(held) :]
        cargo = Cargo(freight, parts + outs[1:] + spare) if freight else None
        if more:
            tiles = buffers[1] if made else None
            more = (more[0], buffers[0], products, tiles, buffers[-1])
        team_sum_kernel(ctxs, len(pairs), ins + outs[:1] + mine, cargo, more)

    depth = sum(b.shape[0] for b in rhs)
    return pl.pallas_call(
        kernel,
        out_shape=[jax.ShapeDtypeStruct((own, D), F32)]
        + Cargo.out_shapes(freight)
        + [jax.ShapeDtypeStruct(shape, BF) for shape in made],
        in_specs=[pl.BlockSpec(memory_space=pl.ANY)] * (inputs + len(given) + len(extra)),
        out_specs=[pl.BlockSpec(memory_space=pltpu.VMEM)] * outputs
        + [pl.BlockSpec(memory_space=pl.ANY)] * len(made),
        scratch_shapes=scratch + Cargo.scratch(freight) + held,
        compiler_params=pltpu.CompilerParams(
            collective_id=number, has_side_effects=True, vmem_limit_bytes=VMEM_LIMIT
        ),
        cost_estimate=pl.CostEstimate(
            flops=2 * count * depth * D,
            bytes_accessed=2 * (count + D) * depth + 4 * own * D,
            transcendentals=0,
        ),
        name=name,
    )(*lhs, *rhs, *given, *extra)


def middle_kernel(ctxs, refs, freight):
    da, att, proj, out_part = refs[:4]
    refs = refs[4:]
    part, grad, joined, outs = refs[0], refs[1], refs[2], refs[3 : 3 + ctxs]
    first, sums, refs = refs[3 + ctxs], refs[4 + ctxs], refs[5 + ctxs :]
    pv, ov, sent, staged, mine, theirs, others, load, swap, side, shift = refs[:11]
    cargo = Cargo(freight, [part, sums] + list(refs[11:]))
    plane, core, ctx = cargo.plane, cargo.core, cargo.ctx
    me = core * ctxs + ctx
    loads = [
        pltpu.make_async_copy(proj, pv, load.at[0]),
        pltpu.make_async_copy(out_part, ov, load.at[1]),
    ]
    loads[1].start()
    loads[0].start()
    cargo.begin()
    partners = [
        (dc, dz) for dz in range(ctxs - 1, -1, -1) for dc in range(2) if dc + dz > 0
    ]

    def partner(dc, dz):
        return (core if dc == 0 else 1 - core, lax.rem(ctx + dz, ctxs))

    greet_all([(plane,) + partner(*step) for step in partners] + cargo.peers())

    def remote(source, target, sems, index, peer):
        return pltpu.make_async_remote_copy(
            src_ref=source,
            dst_ref=target,
            send_sem=sems.at[(0,) + index],
            recv_sem=sems.at[(1,) + index],
            device_id=(plane,) + peer,
            device_id_type=MESH_ID,
        )

    def piece(i, c, z, home):
        return remote(sent.at[c * ctxs + z], grad.at[home], swap, (i,), (c, z))

    def share(kind, z):
        source = ov.at[(1 - core) * ctxs + z] if kind == 0 else staged.at[z]
        target = others.at[z] if kind == 0 else theirs.at[z]
        return remote(source, target, side, (kind, z), (1 - core, ctx))

    loads[1].wait()
    for k in list(range(1, ctxs)) + [0]:
        share(0, lax.rem(ctx + k, ctxs)).start()
    loads[0].wait()
    for i, step in enumerate(partners):
        c, z = partner(*step)
        sent[c * ctxs + z] = mm(da[...], pv[c * ctxs + z], 1, 1).astype(BF)
        piece(i, c, z, me).start()
    cargo.start()

    def join(k):
        z = lax.rem(ctx + k, ctxs)
        share(0, z).wait_recv()
        target = outs[k - 1]

        def group(g, carry):
            part_ = pl.ds(pl.multiple_of(g * 16, 16), 16)
            total = ov[core * ctxs + z, part_, :].astype(F32) + others[z, part_, :].astype(F32)
            target[part_, :] = total.astype(BF)
            return carry

        lax.fori_loop(0, target.shape[0] // 16, group, 0)

    join(1)
    pass_on = remote(outs[0], first, shift, (0,), (core, lax.rem(ctx + 1, ctxs)))
    pass_on.start()
    grad[me] = mm(da[...], pv[me], 1, 1).astype(BF)
    width = grad.shape[2]

    def heads(t):
        return att[:, pl.ds(pl.multiple_of(t * width, width), width)]

    for z in range(ctxs):
        staged[z] = mm(heads((1 - core) * ctxs + z), da[...], 0, 0).astype(BF)
        share(1, z).start()
    for z in range(ctxs):
        mine[z] = mm(heads(core * ctxs + z), da[...], 0, 0).astype(BF)
    size = pv.shape[1]
    for k in list(range(2, ctxs)) + [0]:
        join(k)
    cargo.middle(0)
    for z in range(ctxs):
        share(1, z).wait_recv()
        for p in range(4):

            def group(g, carry):
                rows = pl.ds(pl.multiple_of(p * (size // 4) + g * 16, 16), 16)
                total = mine[z, rows, :].astype(F32) + theirs[z, rows, :].astype(F32)
                joined[p, z, pl.ds(pl.multiple_of(g * 16, 16), 16), :] = total.astype(BF)
                return carry

            lax.fori_loop(0, size // 64, group, 0)
    for i, (dc, dz) in enumerate(partners):
        c, z = core if dc == 0 else 1 - core, lax.rem(ctx + ctxs - dz, ctxs)
        piece(i, c, z, c * ctxs + z).wait_recv()
    cargo.end()
    pass_on.wait()
    for i, step in enumerate(partners):
        c, z = partner(*step)
        piece(i, c, z, me).wait_send()
    for z in range(ctxs):
        share(0, z).wait_send()
        share(1, z).wait_send()


def middle_call(ctxs, da, att, proj, out_part, part):
    team, own = 2 * ctxs, da.shape[0]
    feats = proj.shape[1]
    freight = (part,)
    dma = pltpu.SemaphoreType.DMA
    hbm, vmem = pl.BlockSpec(memory_space=pl.ANY), pl.BlockSpec(memory_space=pltpu.VMEM)
    block = (ctxs, own, D)

    def kernel(*refs):
        middle_kernel(ctxs, refs, freight)

    return pl.pallas_call(
        kernel,
        out_shape=[
            jax.ShapeDtypeStruct((team, own, feats), BF),
            jax.ShapeDtypeStruct((4, ctxs, feats // 4, D), BF),
        ]
        + [jax.ShapeDtypeStruct((own, D), BF)] * (ctxs + 1)
        + Cargo.out_shapes(freight),
        in_specs=[vmem, vmem, hbm, hbm, hbm],
        out_specs=[vmem] * (4 + ctxs),
        scratch_shapes=[
            pltpu.VMEM(proj.shape, BF),
            pltpu.VMEM(out_part.shape, BF),
            pltpu.VMEM((team, own, feats), BF),
            pltpu.VMEM((ctxs, feats, D), BF),
            pltpu.VMEM((ctxs, feats, D), BF),
            pltpu.VMEM((ctxs, feats, D), BF),
            pltpu.VMEM(block, BF),
            dma((2,)),
            dma((2, team - 1)),
            dma((2, 2, ctxs)),
            dma((2, 1)),
        ]
        + Cargo.scratch(freight),
        compiler_params=pltpu.CompilerParams(
            collective_id=7, has_side_effects=True, vmem_limit_bytes=VMEM_LIMIT
        ),
        cost_estimate=pl.CostEstimate(
            flops=4 * own * D * D, bytes_accessed=60 * own * D, transcendentals=0
        ),
        name="middle",
    )(da, att, proj, out_part, part)


def qkv_kernel(feats, x_ref, gain_ref, w_ref, c_ref, a_ref, b_ref, n_ref, q_ref, k_ref, v_ref):
    values = x_ref[...].astype(F32)
    normed = (values * norm_scale(values) * gain_ref[...]).astype(BF)
    n_ref[...] = normed
    cosine, low_sine, high_sine = [widen(ref[...], feats) for ref in (c_ref, a_ref, b_ref)]
    q = mm(normed, w_ref[0:feats], 1, 1)
    q_ref[...] = rope(q, cosine, low_sine, high_sine).astype(BF)
    k = mm(normed, w_ref[feats : 2 * feats], 1, 1)
    k_ref[...] = rope(k, cosine, low_sine, high_sine).astype(BF)
    v_ref[...] = mm(normed, w_ref[2 * feats :], 1, 1).astype(BF)


def qkv_call(x_all, gain, weights, tables):
    count = x_all.shape[0]
    feats = weights.shape[0] // 3
    turns = tables[0].shape[0] // BLOCK
    rows = pl.BlockSpec((BLOCK, D), lambda i: (i, 0))
    part = pl.BlockSpec((BLOCK, feats), lambda i: (i, 0))
    table = pl.BlockSpec((BLOCK, 128), lambda i: (i % turns, 0))
    out = jax.ShapeDtypeStruct((count, feats), BF)
    return pl.pallas_call(
        functools.partial(qkv_kernel, feats),
        grid=(count // BLOCK,),
        out_shape=(jax.ShapeDtypeStruct((count, D), BF), out, out, out),
        in_specs=[
            rows,
            pl.BlockSpec((1, D), lambda i: (0, 0)),
            pl.BlockSpec((3 * feats, D), lambda i: (0, 0)),
            table,
            table,
            table,
        ],
        out_specs=(rows, part, part, part),
        compiler_params=params(),
        cost_estimate=pl.CostEstimate(
            flops=6 * count * D * feats, bytes_accessed=4 * count * D, transcendentals=0
        ),
        name="qkv",
    )(x_all, gain, weights, *tables)


def allowed_keys(col_ref, row_ref, first, size, keys):
    same = col_ref[first : first + size, :] == row_ref[:, 0:keys]
    query_place = first + lax.broadcasted_iota(jnp.int32, (size, keys), 0)
    key_place = lax.broadcasted_iota(jnp.int32, (size, keys), 1)
    return same & (key_place <= query_place)


def attend_kernel(q_ref, k_ref, v_ref, col_ref, row_ref, o_ref, l_ref):
    length = q_ref.shape[0]
    for first in range(0, length, BLOCK):
        keys = first + BLOCK
        allowed = allowed_keys(col_ref, row_ref, first, BLOCK, keys)
        parts = []
        for head in range(q_ref.shape[1] // HD):
            lanes = slice(head * HD, (head + 1) * HD)
            query = q_ref[first:keys, lanes] * HD ** (-0.5)
            scores = jnp.where(allowed, mm(query, k_ref[0:keys, lanes], 1, 1), MASKED)
            highest = jnp.max(scores, -1, keepdims=True)
            shifted = jnp.exp(scores - highest)
            totals = jnp.sum(shifted, -1, keepdims=True)
            weights = (shifted * (1.0 / totals)).astype(BF)
            parts.append(mm(weights, v_ref[0:keys, lanes], 1, 0))
            l_ref[head, first:keys, :] = highest + jnp.log(totals)
        o_ref[first:keys, :] = jnp.concatenate(parts, 1).astype(BF)


def attend_call(query, key, value, col, row, seq):
    count, feats = query.shape
    pairs = feats // 128
    part = pl.BlockSpec((seq, 128), lambda s, h: (s, h))
    each = 128 // HD
    return pl.pallas_call(
        attend_kernel,
        grid=(2, pairs),
        out_shape=(
            jax.ShapeDtypeStruct((count, feats), BF),
            jax.ShapeDtypeStruct((2 * pairs * each, seq, 1), F32),
        ),
        in_specs=[
            part,
            part,
            part,
            pl.BlockSpec((seq, 1), lambda s, h: (s, 0)),
            pl.BlockSpec((None, 1, seq), lambda s, h: (s, 0, 0)),
        ],
        out_specs=(part, pl.BlockSpec((each, seq, 1), lambda s, h: (s * pairs + h, 0, 0))),
        compiler_params=params(2),
        cost_estimate=pl.CostEstimate(
            flops=4 * count * seq * feats, bytes_accessed=8 * count * feats, transcendentals=0
        ),
        name="attend",
    )(query, key, value, col, row)


def attend_back_kernel(
    q_ref, k_ref, v_ref, g_ref, l_ref, col_ref, row_ref, c_ref, a_ref, b_ref,
    dq_ref, dk_ref, dv_ref, key_total, value_total, query_total,
):
    length = q_ref.shape[0]
    scale = HD ** (-0.5)
    key_total[...] = jnp.zeros_like(key_total)
    value_total[...] = jnp.zeros_like(value_total)
    for first in range(0, length, BLOCK):
        keys = first + BLOCK
        allowed = allowed_keys(col_ref, row_ref, first, BLOCK, keys)
        dq_parts, dk_parts, dv_parts = [], [], []
        for head in range(q_ref.shape[1] // HD):
            lanes = slice(head * HD, (head + 1) * HD)
            query = q_ref[first:keys, lanes] * scale
            key = k_ref[0:keys, lanes]
            grad = g_ref[first:keys, lanes]
            scores = jnp.where(allowed, mm(query, key, 1, 1), MASKED)
            probs = jnp.exp(scores - l_ref[head, first:keys, :])
            grad_probs = mm(grad, v_ref[0:keys, lanes], 1, 1)
            inner = jnp.sum(probs * grad_probs, -1, keepdims=True)
            grad_scores = (probs * (grad_probs - inner)).astype(BF)
            dq_parts.append(mm(grad_scores, key, 1, 0) * scale)
            dk_parts.append(mm(grad_scores, query, 0, 0))
            dv_parts.append(mm(probs.astype(BF), grad, 0, 0))
        query_total[first:keys, :] = jnp.concatenate(dq_parts, 1)
        key_total[0:keys, :] += jnp.concatenate(dk_parts, 1)
        value_total[0:keys, :] += jnp.concatenate(dv_parts, 1)
    cosine, low_sine, high_sine = c_ref[...], a_ref[...], b_ref[...]
    dq_ref[...] = rope_back(query_total[...], cosine, low_sine, high_sine).astype(BF)
    dk_ref[...] = rope_back(key_total[...], cosine, low_sine, high_sine).astype(BF)
    dv_ref[...] = value_total[...].astype(BF)


def attend_back_call(
    query, key, value, grad, log_sums, col, row, tables, seq, freight=(), rider=(), number=None
):
    count, feats = query.shape
    pairs = feats // 128
    part = pl.BlockSpec((seq, 128), lambda s, h: (s, h))
    table = pl.BlockSpec((seq, 128), lambda s, h: (0, 0))
    each = 128 // HD
    out = jax.ShapeDtypeStruct((count, feats), BF)
    outputs = len(Cargo.rows_of(freight))

    def kernel(*refs):
        ins, refs = refs[:10], refs[10:]
        parts, refs = refs[: len(freight)], refs[len(freight) :]
        riders, refs = refs[: len(rider)], refs[len(rider) :]
        outs, refs = refs[:3], refs[3:]
        sums, refs = refs[:outputs], refs[outputs:]
        landed, refs = refs[: len(rider)], refs[len(rider) :]
        mine, spare = refs[:3], refs[3:]
        step = pl.program_id(0) * pairs + pl.program_id(1)
        if rider:
            held, got, sems = spare[-3:]
            spare = spare[:-3]
            plane, core, ctx = [lax.axis_index(name) for name in ALL]
            across = (plane, core, lax.rem(ctx + 2, 4))
            fetch = pltpu.make_async_copy(riders[0], held, sems.at[0])
            ride = pltpu.make_async_remote_copy(
                src_ref=held,
                dst_ref=got,
                send_sem=sems.at[1],
                recv_sem=sems.at[2],
                device_id=across,
                device_id_type=MESH_ID,
            )
        cargo = Cargo(freight, parts + sums + spare) if freight else None
        if freight:

            @pl.when(step == 0)
            def _():
                cargo.begin()
                if rider:
                    fetch.start()
                greet_all(cargo.peers() + ([across] if rider else []))
                if rider:
                    fetch.wait()
                    ride.start()
                cargo.start()

            @pl.when(step == 2 * pairs - 1)
            def _():
                for s in range(outputs):
                    cargo.middle(s)

        attend_back_kernel(*ins, *outs, *mine)
        if freight:

            @pl.when(step == 2 * pairs - 1)
            def _():
                cargo.end()
                if rider:
                    ride.wait()
                    landed[0][...] = got[...]

    more = dict(collective_id=number, has_side_effects=True) if freight else {}
    return pl.pallas_call(
        kernel,
        grid=(2, pairs),
        out_shape=[out, out, out]
        + Cargo.out_shapes(freight)
        + [jax.ShapeDtypeStruct(array.shape, BF) for array in rider],
        in_specs=[
            part,
            part,
            part,
            part,
            pl.BlockSpec((each, seq, 1), lambda s, h: (s * pairs + h, 0, 0)),
            pl.BlockSpec((seq, 1), lambda s, h: (s, 0)),
            pl.BlockSpec((None, 1, seq), lambda s, h: (s, 0, 0)),
            table,
            table,
            table,
        ]
        + [pl.BlockSpec(memory_space=pl.ANY)] * (len(freight) + len(rider)),
        out_specs=[part, part, part]
        + [pl.BlockSpec((rows, D), lambda s, h: (0, 0)) for rows in Cargo.rows_of(freight)]
        + [pl.BlockSpec(array.shape, lambda s, h: (0, 0)) for array in rider],
        scratch_shapes=[pltpu.VMEM((seq, 128), F32)] * 3
        + Cargo.scratch(freight)
        + ([pltpu.VMEM(rider[0].shape, BF)] * 2 + [pltpu.SemaphoreType.DMA((3,))] if rider else []),
        compiler_params=params(2, **more),
        cost_estimate=pl.CostEstimate(
            flops=10 * count * seq * feats, bytes_accessed=14 * count * feats, transcendentals=0
        ),
        name="attend_back",
    )(query, key, value, grad, log_sums, col, row, *tables, *freight, *rider)


def project_kernel(o_ref, w_ref, x_ref, gain_ref, m_ref, n_ref):
    total = x_ref[...].astype(F32)
    for index in range(o_ref.shape[0]):
        total = total + mm(o_ref[index], w_ref[index], 1, 0)
    m_ref[...] = total
    n_ref[...] = (total * norm_scale(total) * gain_ref[...]).astype(BF)


def project_call(attended, weights, x_all, gain):
    team, count, feats = attended.shape
    rows = pl.BlockSpec((BLOCK, D), lambda i: (i, 0))
    return pl.pallas_call(
        project_kernel,
        grid=(count // BLOCK,),
        out_shape=(
            jax.ShapeDtypeStruct((count, D), F32),
            jax.ShapeDtypeStruct((count, D), BF),
        ),
        in_specs=[
            pl.BlockSpec((team, BLOCK, feats), lambda i: (0, i, 0)),
            pl.BlockSpec((team, feats, D), lambda i: (0, 0, 0), pipeline_mode=pl.Buffered(1)),
            rows,
            pl.BlockSpec((1, D), lambda i: (0, 0)),
        ],
        out_specs=(rows, rows),
        compiler_params=params(),
        cost_estimate=pl.CostEstimate(
            flops=2 * count * D * D, bytes_accessed=10 * count * D, transcendentals=0
        ),
        name="project",
    )(attended, weights, x_all, gain)


def shifted(value, axis, size, step):
    return lax.ppermute(value, axis, [(i, (i + step) % size) for i in range(size)])


def plane_reduce(parts, planes):
    home = lax.axis_index("plane")
    rows = parts[0].shape[1]

    def block(index, first, size):
        return jnp.stack(
            [
                lax.dynamic_slice(part, (index, first, 0), (1, size, D))[0].astype(BF)
                for part in parts
            ],
            0,
        )

    if planes != 4:
        total = block(home, 0, rows).astype(F32)
        for k in range(1, planes):
            part = block(lax.rem(home + k, planes), 0, rows)
            total = total + shifted(part, "plane", planes, k).astype(F32)
        return total
    near_x, near_y = home + 1 - 2 * lax.rem(home, 2), lax.rem(home + 2, 4)
    far = 3 - home
    along = ([(0, 1), (1, 0), (2, 3), (3, 2)], [(0, 2), (2, 0), (1, 3), (3, 1)])
    size = rows // 2
    sums = []
    for half in range(2):
        one, two = (near_x, near_y) if half == 0 else (near_y, near_x)
        first = half * size
        sent = jnp.stack([block(one, first, size), block(far, first, size)], 0)
        got = lax.ppermute(sent, "plane", along[half]).astype(F32)
        kept = block(home, first, size).astype(F32) + got[0]
        passed = (block(two, first, size).astype(F32) + got[1]).astype(BF)
        sums.append(kept + lax.ppermute(passed, "plane", along[1 - half]).astype(F32))
    return jnp.concatenate(sums, 1)


def core_join(parts, ctxs):
    core = lax.axis_index("core")
    parts = parts.reshape((2, ctxs) + parts.shape[1:])
    got = shifted(lax.dynamic_index_in_dim(parts, 1 - core, 0, False), "core", 2, 1)
    kept = lax.dynamic_index_in_dim(parts, core, 0, False)
    joined = (kept.astype(F32) + got.astype(F32)).astype(BF)
    return jnp.moveaxis(joined, 1, 0)


def line_reduce(parts, ctxs):
    ctx = lax.axis_index("ctx")
    total = lax.dynamic_index_in_dim(parts, ctx, 0, False)
    for k in range(1, ctxs):
        part = lax.dynamic_index_in_dim(parts, lax.rem(ctx + k, ctxs), 0, False)
        total = total + shifted(part.astype(BF), "ctx", ctxs, k).astype(F32)
    return total


def after(value, *others):
    return lax.optimization_barrier((value,) + others)[0]


def team_join(parts, ctxs):
    core, ctx = lax.axis_index("core"), lax.axis_index("ctx")
    own = parts.shape[0] // (2 * ctxs)
    parts = parts.reshape(2 * ctxs, own, D)

    def block(which, k):
        return lax.dynamic_index_in_dim(parts, which * ctxs + (ctx + k) % ctxs, 0, False)

    joined = []
    for k in list(range(1, ctxs)) + [0]:
        got = shifted(block(1 - core, k), "core", 2, 1)
        both = block(core, k).astype(F32) + got.astype(F32)
        joined.append(both.astype(BF) if k > 0 else both)
    return joined


def team_finish(joined, ctxs):
    total = joined[-1].astype(F32)
    for k in range(1, ctxs):
        total = total + shifted(joined[k - 1], "ctx", ctxs, k).astype(F32)
    return total


def local(
    planes,
    ctxs,
    tokens,
    cotangent,
    segments,
    attn_weight,
    attn_first,
    attn_second,
    mlp_weight,
    mlp_first,
    mlp_second,
    gain_weight,
    gain_first,
    gain_second,
):
    team = 2 * ctxs
    devices = planes * team
    own = tokens.shape[0]
    seq = ctxs * own
    count = 2 * seq
    arows = attn_weight.shape[0]
    frows = mlp_weight.shape[0]
    gcols = gain_weight.shape[1]
    feats = planes * arows
    hidden_count = planes * frows
    whole_heads = arows % HD == 0
    me = lax.axis_index(TEAM)

    lines_seg = own // 128
    square = planes == 4 and ctxs == 4 and whole_heads and gcols == 64
    packed = jnp.zeros((8, 128), F32)
    own_gain = lax.reduce_precision(gain_weight, 8, 7)
    if square:
        side = lax.rem(lax.axis_index("ctx"), 2)
        packed = lax.dynamic_update_slice(packed, own_gain, (0, side * gcols))
    else:
        packed = packed.at[0:2, 0:gcols].set(own_gain)
    packed = packed.at[2 : 2 + lines_seg].set(segments.astype(F32).reshape(lines_seg, 128))
    attn_low = attn_weight.astype(BF)
    qkv_low = jnp.moveaxis(attn_low[:, :3], 1, 0)
    proj_low = attn_low[:, 3]
    gate_low, up_low, down_low = [mlp_weight[:, i].astype(BF) for i in range(3)]
    tables = rope_tables(seq)
    if square:
        mlp_slots = jnp.moveaxis(mlp_weight, 1, 0)
        x_all, normed, query, key, value, qkv, gate_w, small = front_call(
            ctxs, tokens, qkv_low, mlp_slots, packed, tables
        )
        normed = normed.reshape(count, D)
        query, key, value = [part.reshape(count, feats) for part in (query, key, value)]
        qkv = qkv.reshape(3 * feats, D)
        gate_w = gate_w.reshape(hidden_count, D)
        gains = small.reshape(planes, ctxs, 2, 8, 128)[:, :, :, 0:2].sum(2)
        gains = gains.transpose(2, 0, 1, 3).reshape(2, D)
        team_small = lax.dynamic_index_in_dim(small, lax.axis_index("plane"), 0, False)
        seg = team_small[:, 2 : 2 + lines_seg].reshape(count)
        seg_col, seg_row = seg.reshape(count, 1), seg.reshape(2, 1, seq)
        att_all, proj, up_w, log_sums = second_call(
            ctxs, query, key, value, seg_col, seg_row, proj_low, mlp_slots
        )
        proj = proj.reshape(team, feats, D)
        up_w = up_w.reshape(hidden_count, D)
        middle_own, att_own, normed_two, out_part, dgate, dup, down_part = third_call(
            ctxs, att_all, proj, x_all, gains[1:2], gate_w, up_w, mlp_slots, cotangent
        )
        normed_two, out_part = normed_two.reshape(count, D), out_part.reshape(count, D)
        dgate, dup = dgate.reshape(count, hidden_count), dup.reshape(count, hidden_count)
        down_part = down_part.reshape(1, planes, frows, D)
    else:
        inputs = [tokens, packed, gate_low, up_low]
        lines = [(0, 0, 2), (1, 1, 1)]
        shapes = [((team, own, D), BF), ((team, 8, 128), F32)]
        boards = []
        if whole_heads:
            inputs += [proj_low, qkv_low]
            lines.append((4, 2, 1))
            shapes.append(((team, arows, D), BF))
            boards.append(("slots", lambda ins, outs: ins[5], len(shapes)))
            shapes.append(((3, planes, arows, D), BF))
        boards.append(("block", lambda ins, outs: ins[2], len(shapes)))
        shapes.append(((planes, frows, D), BF))
        boards.append(("block", lambda ins, outs: ins[3], len(shapes)))
        shapes.append(((planes, frows, D), BF))
        boards.append(("late", lambda ins, outs: outs[1], len(shapes)))
        shapes.append(((planes, team, 8, 128), F32))
        gathered = gather_call(planes, ctxs, 0, inputs, lines, boards, shapes, "gather_first")
        x_all = gathered[0].reshape(count, D)
        small = gathered[-1]
        gate_w = gathered[-3].reshape(hidden_count, D)
        up_w = gathered[-2].reshape(hidden_count, D)
        gains = small[:, :, 0:2, 0:gcols].transpose(2, 0, 1, 3).reshape(2, D)
        seg = gathered[1][:, 2 : 2 + lines_seg].reshape(count)
        seg_col, seg_row = seg.reshape(count, 1), seg.reshape(2, 1, seq)
        if whole_heads:
            qkv = gathered[3].reshape(3 * feats, D)
        else:
            qkv = lax.all_gather(qkv_low, ALL, axis=1, tiled=True)
            qkv = lax.dynamic_slice_in_dim(qkv, me * feats, feats, 1).reshape(3 * feats, D)
            proj = lax.all_gather(proj_low, ALL, axis=0, tiled=True).reshape(team, feats, D)

        normed, query, key, value = qkv_call(x_all, gains[0:1], qkv, tables)
        attended, log_sums = attend_call(query, key, value, seg_col, seg_row, seq)

        inputs = [attended, down_low]
        lines = [(0, 0, 2)]
        shapes = [((team, count, feats), BF)]
        boards = []
        if whole_heads:
            inputs.append(gathered[2])
            boards.append(("half", lambda ins, outs: ins[2], len(shapes)))
            shapes.append(((team, planes, arows, D), BF))
        boards.append(("block", lambda ins, outs: ins[1], len(shapes)))
        shapes.append(((planes, frows, D), BF))
        gathered = gather_call(planes, ctxs, 2, inputs, lines, boards, shapes, "gather_second")
        att_all = gathered[0]
        down_w = gathered[-1].reshape(hidden_count, D)
        if whole_heads:
            proj = gathered[1].reshape(team, feats, D)
        dy_all = lax.all_gather(after(cotangent, att_all), TEAM, axis=0, tiled=True)
        middle, normed_two = project_call(att_all, proj, x_all, gains[1:2])
        mlp_w = (gate_w, up_w, down_w)

        gate = mm(normed_two, mlp_w[0], 1, 1)
        up = mm(normed_two, mlp_w[1], 1, 1)
        hidden = (jax.nn.silu(gate) * up).astype(BF)
        out_part = mm(hidden, mlp_w[2], 1, 0).astype(BF)
        grad_hidden = mm(after(dy_all, out_part), mlp_w[2], 1, 1)
        sig = jax.nn.sigmoid(gate)
        dgate = (grad_hidden * up * sig * (1.0 + gate * (1.0 - sig))).astype(BF)
        dup = (grad_hidden * gate * sig).astype(BF)
        down_part = mm(hidden, dy_all, 0, 0).astype(BF).reshape(1, planes, frows, D)
        middle_own = lax.dynamic_slice_in_dim(middle, me * own, own, 0)
        att_own = lax.dynamic_slice_in_dim(att_all, me * own, own, 1)
    if square:
        dn2, *down_sum, gate_part, up_part = team_sum(
            ctxs,
            3,
            [(dgate, gate_w), (dup, up_w)],
            "sum_two",
            (down_part,),
            normed_two,
            True,
        )
    else:
        (dn2,) = team_sum(ctxs, 3, [(dgate, gate_w), (dup, up_w)], "sum_two")
        gate_part = mm(dgate, normed_two, 0, 0).astype(BF).reshape(1, planes, frows, D)
        up_part = mm(dup, normed_two, 0, 0).astype(BF).reshape(1, planes, frows, D)

    middle_part, gain_two_grad = norm_back(dn2, middle_own, norm_scale(middle_own), gains[1])
    grad_middle = cotangent.astype(F32) + middle_part
    grad_branch = grad_middle.astype(BF)
    freight, rider = (), ()
    if square:
        grad_att, proj_part, *rest = middle_call(
            ctxs, grad_branch, att_own, proj, out_part.reshape(team, own, D), gate_part
        )
        joined, first_out, gate_sum = rest[:ctxs], rest[ctxs], rest[ctxs + 1]
        rider = (joined[1],)
        freight = (proj_part.reshape(1, planes, ctxs * arows, D),)
    else:
        grad_att = jnp.einsum("td,sfd->stf", grad_branch, proj, preferred_element_type=F32)
        grad_att = lax.all_to_all(
            grad_att.astype(BF), TEAM, split_axis=0, concat_axis=0, tiled=True
        )
        output = (middle_own + team_finish(team_join(out_part, ctxs), ctxs)).astype(BF)
        proj_part = jnp.einsum("tsf,sd->tfd", att_own, grad_branch, preferred_element_type=F32)
        proj_part = proj_part.astype(BF)
        if whole_heads:
            proj_part = core_join(proj_part.reshape(team, planes, arows, D), ctxs)
            proj_part = proj_part.reshape(1, planes, ctxs * arows, D)
        else:
            proj_grad = lax.psum_scatter(
                proj_part.reshape(D, D), ALL, scatter_dimension=0, tiled=True
            ).astype(F32)

    dq, dk, dv, *proj_sum = attend_back_call(
        query,
        key,
        value,
        grad_att.reshape(count, feats),
        log_sums,
        seg_col,
        seg_row,
        tables,
        seq,
        freight,
        rider,
        5,
    )
    pairs = [(dq, qkv[0:feats]), (dk, qkv[feats : 2 * feats]), (dv, qkv[2 * feats :])]
    if square:
        freight = (up_part, jax.ShapeDtypeStruct((3, planes, arows, D), BF))
        dn1, up_sum, *attn_sums = team_sum(ctxs, 4, pairs, "sum_one", freight, normed)
        proj_sum, second_out = proj_sum
        mlp_grad = jnp.stack([gate_sum, up_sum, down_sum[0]], 1)
    else:
        (dn1,) = team_sum(ctxs, 4, pairs, "sum_one")
        dqkv = jnp.concatenate([dq, dk, dv], 1)
        qkv_part = mm(dqkv, normed, 0, 0).astype(BF)
        mlp_grad = [plane_reduce([p[0]], planes)[0] for p in (gate_part, up_part, down_part)]
        mlp_grad = jnp.stack(mlp_grad, 1)
        if whole_heads:
            attn_part = qkv_part.reshape(3, planes, arows, D)
            attn_grad = plane_reduce([attn_part[i] for i in range(3)], planes)
            proj_grad = plane_reduce([proj_part[0]], planes)[0].reshape(ctxs, arows, D)
            proj_grad = line_reduce(proj_grad, ctxs)
        else:
            padded = lax.dynamic_update_slice_in_dim(
                jnp.zeros((3, D, D), BF), qkv_part.reshape(3, feats, D), me * feats, 1
            )
            attn_grad = lax.psum_scatter(padded, ALL, scatter_dimension=1, tiled=True)
            attn_grad = attn_grad.astype(F32)
            proj_grad = lax.psum_scatter(
                proj_part.reshape(D, D), ALL, scatter_dimension=0, tiled=True
            ).astype(F32)
        attn_grad = jnp.moveaxis(jnp.concatenate([attn_grad, proj_grad[None]], 0), 0, 1)

    source = tokens.astype(F32)
    source_part, gain_one_grad = norm_back(dn1, source, norm_scale(source), gains[0])
    grad_input = grad_middle + source_part
    gain_part = jnp.stack([gain_one_grad, gain_two_grad], 0).reshape(2, planes, team, gcols)
    gain_part = gain_part.transpose(1, 2, 0, 3)
    gain_part = jnp.pad(gain_part, ((0, 0), (0, 0), (0, 6), (0, 128 - gcols)))
    gain_grad = small_sum(planes, ctxs, gain_part)
    if square:
        gain_grad, proj_sum = lax.optimization_barrier((gain_grad, proj_sum))
        proj_sum = line_reduce(proj_sum.reshape(ctxs, arows, D), ctxs)
        proj_sum, last_out = lax.optimization_barrier((proj_sum, joined[2]))
        output = middle_own + joined[3].astype(F32) + first_out.astype(F32)
        output = output + second_out.astype(F32) + shifted(last_out, "ctx", 4, 3).astype(F32)
        output = output.astype(BF)
        attn_grad = jnp.stack(attn_sums + [proj_sum], 1)
    gain_grad = gain_grad[0:2, 0:gcols]

    attn_rate = (
        RATE_FACTOR
        * D ** (-0.5)
        * jnp.array([1.0, 1.0, 1.0, OUTPUT_BOOST], jnp.float32).reshape(1, 4, 1)
    )
    mlp_rate = RATE_FACTOR * jnp.array(
        [D ** (-0.5), D ** (-0.5), FF ** (-0.5)], jnp.float32
    ).reshape(1, 3, 1)
    attn_new = adam_update(attn_weight, attn_first, attn_second, attn_grad, attn_rate, WEIGHT_DECAY)
    mlp_new = adam_update(mlp_weight, mlp_first, mlp_second, mlp_grad, mlp_rate, WEIGHT_DECAY)
    gain_new = adam_update(gain_weight, gain_first, gain_second, gain_grad, GAIN_RATE, 0.0)
    return (
        output,
        grad_input,
        attn_new[0],
        attn_new[1][:, :3, :],
        attn_new[1][:, 3, :],
        attn_new[2],
        mlp_new[0],
        mlp_new[1],
        mlp_new[2],
        gain_new[0],
        gain_new[1],
        gain_new[2],
    )


def solution(mesh):
    dp, ctxs = mesh.shape["dp"], mesh.shape["ctx"]
    planes = dp // 2
    inner = Mesh(mesh.devices.reshape(planes, 2, ctxs), ALL)
    rows = P(ALL, None)
    cube = P(ALL, None, None)
    gain = P(None, ALL)

    def step(*args):
        return local(planes, ctxs, *args)

    return jax.shard_map(
        step,
        mesh=inner,
        in_specs=(rows, rows, P(ALL)) + (cube,) * 6 + (gain,) * 3,
        out_specs=(rows, rows, cube, cube, rows) + (cube,) * 4 + (gain,) * 3,
        check_vma=False,
    )
```

```python
import functools

import jax
import jax.numpy as jnp
import numpy as np
from jax import lax
from jax.experimental import pallas as pl
from jax.experimental.pallas import tpu as pltpu
from jax.sharding import Mesh
from jax.sharding import PartitionSpec as P

D = 2048
HEADS = 32
HD = 64
FF = 8192
STEP = 10


NORM_EPS = 1e-05
ROPE_BASE = 130000.0
BETA_ONE = 0.9
BETA_TWO = 0.95
ADAM_EPS = 1e-08
WEIGHT_DECAY = 0.1
RATE_FACTOR = 1.5
GAIN_RATE = 0.6
OUTPUT_BOOST = 12.0
MASKED = -1e30
BF = jnp.bfloat16
F32 = jnp.float32
ALL = ("plane", "core", "ctx")
TEAM = ("core", "ctx")


BLOCK = 256
CHUNKS = 2
VMEM_LIMIT = 60 * 1024 * 1024
MESH_ID = pl.DeviceIdType.MESH


def params(semantics=1, **more):
    return pltpu.CompilerParams(
        dimension_semantics=("arbitrary",) * semantics, vmem_limit_bytes=VMEM_LIMIT, **more
    )


def rope_tables(length):
    halved = HD // 2
    frequency = (ROPE_BASE ** (-(np.arange(halved) * 2.0 / HD))).astype(np.float32)
    angle = np.arange(length, dtype=np.float32)[:, None] * frequency[None, :]
    cosine, sine = np.cos(angle).astype(np.float32), np.sin(angle).astype(np.float32)
    zero = np.zeros_like(sine)
    return (
        jnp.asarray(np.concatenate([cosine] * 4, 1)),
        jnp.asarray(np.concatenate([-sine, zero] * 2, 1)),
        jnp.asarray(np.concatenate([zero, sine] * 2, 1)),
    )


def widen(table, feats):
    return jnp.concatenate([table] * (feats // 128), 1) if feats > 128 else table


def rope(values, cosine, low_sine, high_sine):
    width = values.shape[-1]
    ahead = pltpu.roll(values, width - HD // 2, 1)
    behind = pltpu.roll(values, HD // 2, 1)
    return values * cosine + ahead * low_sine + behind * high_sine


def rope_back(values, cosine, low_sine, high_sine):
    width = values.shape[-1]
    ahead = pltpu.roll(values, width - HD // 2, 1)
    behind = pltpu.roll(values, HD // 2, 1)
    return values * cosine - ahead * low_sine - behind * high_sine


def mm(a, b, ca, cb):
    return lax.dot_general(a, b, (((ca,), (cb,)), ((), ())), preferred_element_type=F32)


def norm_scale(values):
    return lax.rsqrt(jnp.mean(values * values, -1, keepdims=True) + NORM_EPS)


def norm_back(grad_normed, values, scale, gain):
    weighted = grad_normed * gain
    grad_values = scale * (
        weighted - values * scale * scale * jnp.mean(weighted * values, -1, keepdims=True)
    )
    return (grad_values, jnp.sum(grad_normed * values * scale, 0))


def adam_update(master, first, second, grad, rate, decay):
    first_new = BETA_ONE * first + (1.0 - BETA_ONE) * grad
    second_new = BETA_TWO * second + (1.0 - BETA_TWO) * grad * grad
    direction = (
        first_new
        / (1.0 - BETA_ONE**STEP)
        / (jnp.sqrt(second_new / (1.0 - BETA_TWO**STEP)) + ADAM_EPS)
    )
    return (first_new, second_new, master - rate * (direction + decay * master))


def greet_all(peers):
    barrier = pltpu.get_barrier_semaphore()
    for peer in peers:
        pl.semaphore_signal(barrier, inc=1, device_id=peer, device_id_type=MESH_ID)
    pl.semaphore_wait(barrier, len(peers))


def neighbours(planes, ctxs):
    plane, core, ctx = lax.axis_index("plane"), lax.axis_index("core"), lax.axis_index("ctx")
    column = [lax.rem(plane + k, planes) for k in range(1, planes)]
    group = [
        (core if dc == 0 else 1 - core, lax.rem(ctx + dz, ctxs))
        for dc in range(2)
        for dz in range(ctxs)
        if dc + dz > 0
    ]
    return plane, core, ctx, column, group


def gather_kernel(planes, ctxs, lines, boards, inputs, refs):
    ins, outs = refs[:inputs], refs[inputs : inputs + len(lines) + len(boards)]
    line_send, line_recv, side_send, side_recv, board_send, board_recv, pass_send, pass_recv, here = refs[
        inputs + len(lines) + len(boards) :
    ]
    plane, core, ctx = lax.axis_index("plane"), lax.axis_index("core"), lax.axis_index("ctx")
    last = ctxs - 1
    column = [lax.rem(plane + k, planes) for k in range(1, planes)]
    greet_all(
        [(p, core, ctx) for p in column]
        + [(plane, core, lax.rem(ctx + k, ctxs)) for k in range(1, ctxs)]
        + [(plane, 1 - core, ctx)]
    )
    other = (plane, 1 - core, ctx)
    pieces = []
    for source, target, chunks in lines:
        rows = ins[source].shape[0] // chunks
        for chunk in range(chunks):
            pieces.append((ins[source], outs[target], pl.ds(chunk * rows, rows)))

    def remote(source, target, send, recv, peer):
        return pltpu.make_async_remote_copy(
            src_ref=source,
            dst_ref=target,
            send_sem=send,
            recv_sem=recv,
            device_id=peer,
            device_id_type=MESH_ID,
        )

    def line(index, way, hop, block, peer_ctx, own):
        value, out, rows = pieces[index]
        slot = out.at[core * ctxs + block, rows]
        return remote(
            value.at[rows] if own else slot,
            slot,
            line_send.at[index, way, hop],
            line_recv.at[index, way, hop],
            (plane, core, peer_ctx),
        )

    def side(index, order, side_core, block, own):
        value, out, rows = pieces[index]
        slot = out.at[side_core * ctxs + block, rows]
        return remote(
            value.at[rows] if own else slot,
            slot,
            side_send.at[index, order],
            side_recv.at[index, order],
            other,
        )

    square = planes == 4
    near_x = plane + 1 - 2 * lax.rem(plane, 2)
    near_y = lax.rem(plane + 2, 4)
    far = 3 - plane

    def board_refs(index, home, half=None, own=True):
        kind, source, target = boards[index]
        value, out = source(ins, outs), outs[target]
        if kind in ("block", "late"):
            size = value.shape[0]
            part = pl.ds(0, size) if half is None else pl.ds(half * (size // 2), size // 2)
            slot = out.at[home, part]
            return (value.at[part] if own else slot), slot
        if kind == "slots":
            size = value.shape[1]
            part = pl.ds(0, size) if half is None else pl.ds(half * (size // 2), size // 2)
            slot = out.at[:, home, part]
            return (value.at[:, part] if own else slot), slot
        size = ctxs if half is None else ctxs // 2
        part = pl.ds(core * ctxs + (0 if half is None else half * size), size)
        slot = out.at[part, home]
        return (value.at[part] if own else slot), slot

    def board(index, k, home, peer):
        value, slot = board_refs(index, home)
        return remote(
            value, slot, board_send.at[index, k], board_recv.at[index, k], (peer, core, ctx)
        )

    sent = [(plane, 0, near_x), (plane, 1, near_x), (plane, 0, near_y), (plane, 1, near_y)]
    sent += [(near_y, 0, near_x), (near_x, 1, near_y)]
    landed = [near_x, near_x, near_y, near_y, far, far]

    def relay(index, k, arriving=False):
        home, half, peer = sent[k]
        value, slot = board_refs(index, landed[k] if arriving else home, half, k < 4)
        return remote(
            value, slot, board_send.at[index, k], board_recv.at[index, k], (peer, core, ctx)
        )

    def relayed(index):
        return square and boards[index][0] != "late"

    def board_start(index):
        if relayed(index):
            for k in (1, 2, 0, 3):
                relay(index, k).start()
            return
        for k, peer in enumerate(column):
            board(index, k, plane, peer).start()

    def board_pass(index):
        if relayed(index):
            relay(index, 2, True).wait_recv()
            relay(index, 4).start()
            relay(index, 1, True).wait_recv()
            relay(index, 5).start()

    def sources(index):
        if relayed(index):
            return [near_x, near_y, far]
        return [lax.rem(plane + planes - 1 - k, planes) for k in range(planes - 1)]

    def share(index, k, home):
        _, slot = board_refs(index, home)
        return remote(slot, slot, pass_send.at[index, k], pass_recv.at[index, k], other)

    def board_finish(index):
        if relayed(index):
            for k in (0, 3, 4, 5):
                relay(index, k, True).wait_recv()
        for k, home in enumerate(sources(index)):
            if not relayed(index):
                board(index, k, home, home).wait_recv()
            if boards[index][0] == "half":
                share(index, k, home).start()

    def board_close(index):
        if relayed(index):
            for k in range(6):
                relay(index, k).wait_send()
        else:
            for k, peer in enumerate(column):
                board(index, k, plane, peer).wait_send()
        if boards[index][0] == "half":
            out = outs[boards[index][2]]
            for k, home in enumerate(sources(index)):
                share(index, k, home).wait_send()
                slot = out.at[pl.ds((1 - core) * ctxs, ctxs), home]
                remote(
                    slot, slot, pass_send.at[index, k], pass_recv.at[index, k], other
                ).wait_recv()

    count = len(pieces)
    late = [i for i in range(len(boards)) if boards[i][0] == "late"]
    early = [i for i in range(len(boards)) if boards[i][0] != "late"]
    board_start(early[0]) if early else None

    @pl.when(ctx < last)
    def _():
        for i in range(count):
            line(i, 0, 1, ctx, ctx + 1, True).start()

    @pl.when(ctx > 0)
    def _():
        for i in range(count):
            line(i, 1, 1, ctx, ctx - 1, True).start()

    for i in range(count):
        side(i, 0, core, ctx, True).start()
    copies = []
    for i, (value, out, rows) in enumerate(pieces):
        copies.append(
            pltpu.make_async_copy(value.at[rows], out.at[core * ctxs + ctx, rows], here.at[i])
        )
    for i in early:
        kind, source, target = boards[i]
        slot = outs[target].at[plane] if kind == "block" else outs[target].at[:, plane]
        copies.append(pltpu.make_async_copy(source(ins, outs), slot, here.at[count + i]))
    for copy in copies:
        copy.start()

    passed = 0
    board_pass(early[0])
    if len(early) > 1:
        board_start(early[1])
    for hop in range(1, ctxs):

        @pl.when(ctx >= hop)
        def _():
            block = ctx - hop
            for i in range(count):
                line(i, 0, hop, block, ctx - 1, False).wait_recv()

                @pl.when(ctx < last)
                def _():
                    line(i, 0, hop + 1, block, ctx + 1, False).start()

                side(i, hop, core, block, False).start()

        @pl.when(ctx + hop <= last)
        def _():
            block = ctx + hop
            for i in range(count):
                line(i, 1, hop, block, ctx + 1, False).wait_recv()

                @pl.when(ctx > 0)
                def _():
                    line(i, 1, hop + 1, block, ctx - 1, False).start()

                side(i, last + hop, core, block, False).start()

        if passed + 1 < len(early):
            passed += 1
            board_pass(early[passed])
            if passed + 1 < len(early):
                board_start(early[passed + 1])
    for i in early:
        board_finish(i)

    for i in range(count):
        side(i, 0, 1 - core, ctx, False).wait_recv()
    for hop in range(1, ctxs):

        @pl.when(ctx >= hop)
        def _():
            for i in range(count):
                side(i, hop, 1 - core, ctx - hop, False).wait_recv()

        @pl.when(ctx + hop <= last)
        def _():
            for i in range(count):
                side(i, last + hop, 1 - core, ctx + hop, False).wait_recv()

    for copy in copies:
        copy.wait()
    for i in late:
        board_start(i)
        kind, source, target = boards[i]
        copy = pltpu.make_async_copy(source(ins, outs), outs[target].at[plane], here.at[count + i])
        copy.start()
        copy.wait()
    for i in late:
        board_finish(i)

    for i in range(len(boards)):
        board_close(i)
    for i in range(count):
        side(i, 0, core, ctx, True).wait_send()
    for hop in range(1, ctxs):

        @pl.when(ctx >= hop)
        def _():
            for i in range(count):
                side(i, hop, core, ctx - hop, False).wait_send()

        @pl.when(ctx + hop <= last)
        def _():
            for i in range(count):
                side(i, last + hop, core, ctx + hop, False).wait_send()

        @pl.when((ctx < last) & (ctx >= hop - 1))
        def _():
            for i in range(count):
                line(i, 0, hop, ctx - hop + 1, ctx + 1, False).wait_send()

        @pl.when((ctx > 0) & (ctx + hop - 1 <= last))
        def _():
            for i in range(count):
                line(i, 1, hop, ctx + hop - 1, ctx - 1, False).wait_send()


def gather_call(planes, ctxs, number, inputs, lines, boards, shapes, name):
    pieces = sum(chunks for _, _, chunks in lines)
    dma = pltpu.SemaphoreType.DMA

    def kernel(*refs):
        gather_kernel(planes, ctxs, lines, boards, len(inputs), refs)

    return pl.pallas_call(
        kernel,
        out_shape=tuple(jax.ShapeDtypeStruct(shape, dtype) for shape, dtype in shapes),
        in_specs=[pl.BlockSpec(memory_space=pl.ANY)] * len(inputs),
        out_specs=tuple(pl.BlockSpec(memory_space=pl.ANY) for _ in shapes),
        scratch_shapes=[
            dma((pieces, 2, ctxs + 1)),
            dma((pieces, 2, ctxs + 1)),
            dma((pieces, 2 * ctxs)),
            dma((pieces, 2 * ctxs)),
            dma((len(boards), max(planes, 6))),
            dma((len(boards), max(planes, 6))),
            dma((len(boards), planes)),
            dma((len(boards), planes)),
            dma((pieces + len(boards),)),
        ],
        compiler_params=pltpu.CompilerParams(collective_id=number, has_side_effects=True),
        name=name,
    )(*inputs)


def small_sum_kernel(planes, ctxs, value_ref, out_ref, got_one, middle, got_two, sems):
    plane, core, ctx, column, group = neighbours(planes, ctxs)
    greet_all([(p, core, ctx) for p in column] + [(plane, c, z) for c, z in group])

    def hop(index, source, target, peer):
        return pltpu.make_async_remote_copy(
            src_ref=source,
            dst_ref=target,
            send_sem=sems.at[0, index],
            recv_sem=sems.at[1, index],
            device_id=peer,
            device_id_type=MESH_ID,
        )

    first = [
        hop(i, value_ref.at[p], got_one.at[i], (p, core, ctx)) for i, p in enumerate(column)
    ]
    for copy in first:
        copy.start()
    total = value_ref[plane]
    for i, copy in enumerate(first):
        copy.wait_recv()
        total = total + got_one[i]
    middle[...] = total
    base = len(column)
    second = [
        hop(base + i, middle.at[c * ctxs + z], got_two.at[i], (plane, c, z))
        for i, (c, z) in enumerate(group)
    ]
    for copy in second:
        copy.start()
    total = middle[core * ctxs + ctx]
    for i, copy in enumerate(second):
        copy.wait_recv()
        total = total + got_two[i]
    out_ref[...] = total
    for copy in first + second:
        copy.wait_send()


def small_sum(planes, ctxs, value):
    hops = planes + 2 * ctxs - 2
    tile = value.shape[2:]
    return pl.pallas_call(
        functools.partial(small_sum_kernel, planes, ctxs),
        out_shape=jax.ShapeDtypeStruct(tile, F32),
        in_specs=[pl.BlockSpec(memory_space=pltpu.VMEM)],
        out_specs=pl.BlockSpec(memory_space=pltpu.VMEM),
        scratch_shapes=[
            pltpu.VMEM((planes - 1, 2 * ctxs) + tile, F32),
            pltpu.VMEM((2 * ctxs,) + tile, F32),
            pltpu.VMEM((2 * ctxs - 1,) + tile, F32),
            pltpu.SemaphoreType.DMA((2, hops)),
        ],
        compiler_params=pltpu.CompilerParams(collective_id=1, has_side_effects=True),
        name="small_sum",
    )(value)


class Gather:
    def __init__(self, ctxs, pieces, boards, sems):
        self.ctxs, self.pieces, self.boards = ctxs, pieces, boards
        self.line_sem, self.side_sem, self.board_sem, self.pass_sem = sems
        self.plane, self.core, self.ctx = (
            lax.axis_index("plane"),
            lax.axis_index("core"),
            lax.axis_index("ctx"),
        )
        self.last = ctxs - 1
        self.near_x = self.plane + 1 - 2 * lax.rem(self.plane, 2)
        self.near_y = lax.rem(self.plane + 2, 4)
        self.far = 3 - self.plane

    @staticmethod
    def scratch(ctxs, pieces, boards):
        dma = pltpu.SemaphoreType.DMA
        return [
            dma((2, pieces, 2, ctxs + 1)),
            dma((2, pieces, 2 * ctxs)),
            dma((2, boards, 6)),
            dma((2, boards, 3)),
        ]

    def peers(self):
        plane, core, ctx, ctxs = self.plane, self.core, self.ctx, self.ctxs
        return (
            [(plane, core, lax.rem(ctx + k, ctxs)) for k in range(1, ctxs)]
            + [(plane, 1 - core, ctx)]
            + [(near, core, ctx) for near in (self.near_x, self.near_y)]
        )

    def remote(self, slot, sem, index, peer):
        return pltpu.make_async_remote_copy(
            src_ref=slot,
            dst_ref=slot,
            send_sem=sem.at[(0,) + index],
            recv_sem=sem.at[(1,) + index],
            device_id=peer,
            device_id_type=MESH_ID,
        )

    def line(self, i, way, hop, block):
        buffer, rows = self.pieces[i]
        slot = buffer.at[self.core * self.ctxs + block, rows]
        away = 1 if way == 0 else self.ctxs - 1
        peer = (self.plane, self.core, lax.rem(self.ctx + away, self.ctxs))
        return self.remote(slot, self.line_sem, (i, way, hop), peer)

    def side(self, i, order, core, block):
        buffer, rows = self.pieces[i]
        slot = buffer.at[core * self.ctxs + block, rows]
        return self.remote(slot, self.side_sem, (i, order), (self.plane, 1 - self.core, self.ctx))

    def send_own(self, items):
        @pl.when(self.ctx < self.last)
        def _():
            for i in items:
                self.line(i, 0, 1, self.ctx).start()

        @pl.when(self.ctx > 0)
        def _():
            for i in items:
                self.line(i, 1, 1, self.ctx).start()

        for i in items:
            self.side(i, 0, self.core, self.ctx).start()

    def hop(self, k, items):
        ctx, last = self.ctx, self.last

        for i in items:

            @pl.when(ctx >= k)
            def _():
                self.line(i, 0, k, ctx - k).wait_recv()

                @pl.when(ctx < last)
                def _():
                    self.line(i, 0, k + 1, ctx - k).start()

                self.side(i, k, self.core, ctx - k).start()

            @pl.when(ctx + k <= last)
            def _():
                self.line(i, 1, k, ctx + k).wait_recv()

                @pl.when(ctx > 0)
                def _():
                    self.line(i, 1, k + 1, ctx + k).start()

                self.side(i, last + k, self.core, ctx + k).start()

    def side_arrive(self, k, items):
        ctx, last = self.ctx, self.last
        if k == 0:
            for i in items:
                self.side(i, 0, 1 - self.core, ctx).wait_recv()
            return

        @pl.when(ctx >= k)
        def _():
            for i in items:
                self.side(i, k, 1 - self.core, ctx - k).wait_recv()

        @pl.when(ctx + k <= last)
        def _():
            for i in items:
                self.side(i, last + k, 1 - self.core, ctx + k).wait_recv()

    def distant(self, k, action):
        ctx, last = self.ctx, self.last
        behind = (ctx >= k).astype(jnp.int32)
        ahead = (ctx + k <= last).astype(jnp.int32)

        def body(i, carry):
            action(jnp.where((behind == 1) & (i == 0), ctx - k, ctx + k))
            return carry

        lax.fori_loop(0, behind + ahead, body, 0)

    def board_slot(self, index, home, half):
        kind, buffer = self.boards[index]
        if kind == "block":
            size = buffer.shape[1] // 2
            return buffer.at[home, pl.ds(half * size, size)]
        if kind == "slots":
            size = buffer.shape[2] // 2
            return buffer.at[:, home, pl.ds(half * size, size)]
        size = self.ctxs // 2
        return buffer.at[pl.ds(self.core * self.ctxs + half * size, size), home]

    def relay(self, index, k, arriving=False):
        plane, near_x, near_y, far = self.plane, self.near_x, self.near_y, self.far
        sent = [(plane, 0, near_x), (plane, 1, near_x), (plane, 0, near_y), (plane, 1, near_y)]
        home, half, peer = (sent + [(near_y, 0, near_x), (near_x, 1, near_y)])[k]
        if arriving:
            home = [near_x, near_x, near_y, near_y, far, far][k]
        slot = self.board_slot(index, home, half)
        return self.remote(slot, self.board_sem, (index, k), (peer, self.core, self.ctx))

    def board_start(self, index):
        for k in (1, 2, 0, 3):
            self.relay(index, k).start()

    def board_pass(self, index):
        self.relay(index, 2, True).wait_recv()
        self.relay(index, 4).start()
        self.relay(index, 1, True).wait_recv()
        self.relay(index, 5).start()

    def share(self, index, k, core):
        buffer = self.boards[index][1]
        home = [self.near_x, self.near_y, self.far][k]
        slot = buffer.at[pl.ds(core * self.ctxs, self.ctxs), home]
        return self.remote(
            slot, self.pass_sem, (index, k), (self.plane, 1 - self.core, self.ctx)
        )

    def board_finish(self, index):
        for k in (0, 3, 4, 5):
            self.relay(index, k, True).wait_recv()
        if self.boards[index][0] == "half":
            for k in range(3):
                self.share(index, k, self.core).start()

    def board_shared(self, index):
        for k in range(3):
            self.share(index, k, 1 - self.core).wait_recv()

    def close(self):
        ctx, last = self.ctx, self.last
        items = range(len(self.pieces))
        for index in range(len(self.boards)):
            for k in range(6):
                self.relay(index, k).wait_send()
            if self.boards[index][0] == "half":
                for k in range(3):
                    self.share(index, k, self.core).wait_send()
        for i in items:
            self.side(i, 0, self.core, ctx).wait_send()
        for k in range(1, self.ctxs):

            @pl.when(ctx >= k)
            def _():
                for i in items:
                    self.side(i, k, self.core, ctx - k).wait_send()

            @pl.when(ctx + k <= last)
            def _():
                for i in items:
                    self.side(i, last + k, self.core, ctx + k).wait_send()

            @pl.when((ctx < last) & (ctx >= k - 1))
            def _():
                for i in items:
                    self.line(i, 0, k, ctx - k + 1).wait_send()

            @pl.when((ctx > 0) & (ctx + k - 1 <= last))
            def _():
                for i in items:
                    self.line(i, 1, k, ctx + k - 1).wait_send()


def front_kernel(ctxs, refs):
    tokens, qkv, mlp, packed, c_ref, a_ref, b_ref = refs[:7]
    x_out, n_out, q_out, k_out, v_out, w_out, g_out, small = refs[7:15]
    xs, ns, qs, ks, vs, ws, gs, wide, load, store, small_sem = refs[15:26]
    own = tokens.shape[0]
    half = own // 2
    pieces = [(xs, pl.ds(0, half)), (xs, pl.ds(half, half))]
    boards = [("slots", ws), ("block", gs)]
    net = Gather(ctxs, pieces, boards, refs[26:])
    plane, core, ctx = net.plane, net.core, net.ctx
    me = core * ctxs + ctx
    loads = [
        pltpu.make_async_copy(qkv, ws.at[:, plane], load.at[0]),
        pltpu.make_async_copy(tokens, xs.at[me], load.at[1]),
        pltpu.make_async_copy(mlp.at[0], wide, load.at[2]),
    ]
    for copy in loads:
        copy.start()
    others = [
        (core if dc == 0 else 1 - core, lax.rem(ctx + dz, ctxs))
        for dc in range(2)
        for dz in range(ctxs)
        if dc + dz > 0
    ]
    column = [lax.rem(plane + k, 4) for k in range(1, 4)]
    greet_all([(plane, c, z) for c, z in others] + [(p, core, ctx) for p in column])

    def tiny(index, source, target, peer):
        return pltpu.make_async_remote_copy(
            src_ref=source,
            dst_ref=target,
            send_sem=small_sem.at[0, index],
            recv_sem=small_sem.at[1, index],
            device_id=peer,
            device_id_type=MESH_ID,
        )

    small[plane, me] = packed[...]
    one = [
        tiny(i, packed, small.at[plane, me], (plane, c, z)) for i, (c, z) in enumerate(others)
    ]
    for copy in one:
        copy.start()
    for copy in loads[:2]:
        copy.wait()
    net.board_start(0)
    net.send_own([0, 1])
    i = 0
    for dc in range(2):
        for dz in range(ctxs):
            if dc + dz > 0:
                c, z = core if dc == 0 else 1 - core, lax.rem(ctx + ctxs - dz, ctxs)
                tiny(i, packed, small.at[plane, c * ctxs + z], (plane, c, z)).wait_recv()
                i += 1
    two = [
        tiny(i + k, small.at[plane], small.at[plane], (p, core, ctx))
        for k, p in enumerate(column)
    ]
    for copy in two:
        copy.start()
    loads[2].wait()

    def narrow(g, carry):
        part = pl.ds(pl.multiple_of(g * 16, 16), 16)
        gs[plane, part, :] = wide[part, :].astype(BF)
        return carry

    lax.fori_loop(0, wide.shape[0] // 16, narrow, 0)
    net.board_pass(0)
    net.board_start(1)
    for k in range(3):
        home = lax.rem(plane + 3 - k, 4)
        tiny(i + k, small.at[plane], small.at[home], (home, core, ctx)).wait_recv()
    tiles = [
        small[p, 2 * j][0:1] + small[p, 2 * j + 1][0:1] for p in range(4) for j in range(ctxs)
    ]
    gain = jnp.concatenate(tiles, 1)
    feats = q_out.shape[-1]
    stores = []

    blocks = [(xs, x_out), (ns, n_out), (qs, q_out), (ks, k_out), (vs, v_out)]

    def put(source, target, index):
        return pltpu.make_async_copy(source, target, store.at[index])

    def compute(side_core):
        def action(block):
            b = side_core * ctxs + block
            values = xs[b].astype(F32)
            normed = (values * norm_scale(values) * gain).astype(BF)
            ns[b] = normed
            rows = pl.ds(pl.multiple_of(block * own, own), own)
            cosine, low_sine, high_sine = [
                widen(ref[rows, :], feats) for ref in (c_ref, a_ref, b_ref)
            ]
            q = mm(normed, ws[0].reshape(feats, D), 1, 1)
            qs[b] = rope(q, cosine, low_sine, high_sine).astype(BF)
            k = mm(normed, ws[1].reshape(feats, D), 1, 1)
            ks[b] = rope(k, cosine, low_sine, high_sine).astype(BF)
            vs[b] = mm(normed, ws[2].reshape(feats, D), 1, 1).astype(BF)
            for i, (source, target) in enumerate(blocks):
                put(source.at[b], target.at[b], 5 * b + i).start()

        return action

    base = 10 * ctxs
    parts = [0, 1]
    stores = [put(s, t, base + i) for i, (s, t) in enumerate([(ws, w_out), (gs, g_out)])]
    net.hop(1, parts)
    net.board_finish(0)
    stores[0].start()
    compute(core)(ctx)
    net.side_arrive(0, parts)
    compute(1 - core)(ctx)
    net.board_pass(1)
    for k in range(1, ctxs):
        net.distant(k, compute(core))
        if k + 1 < ctxs:
            net.hop(k + 1, parts)
        net.side_arrive(k, parts)
        net.distant(k, compute(1 - core))
        if k == min(2, ctxs - 1):
            net.board_finish(1)
            stores[1].start()
    net.close()
    for copy in one + two:
        copy.wait_send()
    for copy in stores:
        copy.wait()
    for b in range(2 * ctxs):
        for i, (source, target) in enumerate(blocks):
            put(source.at[b], target.at[b], 5 * b + i).wait()


def front_call(ctxs, tokens, qkv, mlp, packed, tables):
    team = 2 * ctxs
    own, arows, frows = tokens.shape[0], qkv.shape[1], mlp.shape[1]
    feats = 4 * arows
    block, part = (team, own, D), (team, own, feats)
    shapes = [block, block, part, part, part, (3, 4, arows, D)]
    shapes += [(4, frows, D)]
    dma = pltpu.SemaphoreType.DMA
    hbm, vmem = pl.BlockSpec(memory_space=pl.ANY), pl.BlockSpec(memory_space=pltpu.VMEM)

    def kernel(*refs):
        front_kernel(ctxs, refs)

    return pl.pallas_call(
        kernel,
        out_shape=[jax.ShapeDtypeStruct(shape, BF) for shape in shapes]
        + [jax.ShapeDtypeStruct((4, team, 8, 128), F32)],
        in_specs=[hbm] * 3 + [vmem] * 4,
        out_specs=[hbm] * len(shapes) + [vmem],
        scratch_shapes=[pltpu.VMEM(shape, BF) for shape in shapes]
        + [pltpu.VMEM((frows, D), F32)]
        + [dma((3,)), dma((5 * team + 2,)), dma((2, team + 2))]
        + Gather.scratch(ctxs, 2, 2),
        compiler_params=pltpu.CompilerParams(
            collective_id=0, has_side_effects=True, vmem_limit_bytes=VMEM_LIMIT
        ),
        cost_estimate=pl.CostEstimate(
            flops=6 * team * own * D * feats, bytes_accessed=40 * own * D, transcendentals=0
        ),
        name="front",
    )(tokens, qkv, mlp, packed, *tables)


def attend_part(q_ref, k_ref, v_ref, col_ref, row_ref, l_ref, put, start, length, pair, unit):
    lanes = pl.ds(pl.multiple_of(pair * 128, 128), 128)
    for first in range(0, length, BLOCK):
        keys = first + BLOCK
        rows = pl.ds(pl.multiple_of(start + first, BLOCK), BLOCK)
        past = pl.ds(pl.multiple_of(start, BLOCK), keys)
        same = col_ref[rows, :] == row_ref[:, 0:keys]
        query_place = first + lax.broadcasted_iota(jnp.int32, (BLOCK, keys), 0)
        key_place = lax.broadcasted_iota(jnp.int32, (BLOCK, keys), 1)
        allowed = same & (key_place <= query_place)
        query, key, value = q_ref[rows, lanes], k_ref[past, lanes], v_ref[past, lanes]
        parts = []
        for head in range(128 // HD):
            cut = slice(head * HD, (head + 1) * HD)
            scores = mm(query[:, cut] * HD ** (-0.5), key[:, cut], 1, 1)
            scores = jnp.where(allowed, scores, MASKED)
            highest = jnp.max(scores, -1, keepdims=True)
            shifted = jnp.exp(scores - highest)
            totals = jnp.sum(shifted, -1, keepdims=True)
            weights = (shifted * (1.0 / totals)).astype(BF)
            parts.append(mm(weights, value[:, cut], 1, 0))
            l_ref[unit + head, first:keys, :] = highest + jnp.log(totals)
        put(rows, lanes, jnp.concatenate(parts, 1).astype(BF))


def second_kernel(ctxs, refs):
    q_ref, k_ref, v_ref, col_ref, row_ref, proj, mlp = refs[:7]
    o_out, p_out, d_out, l_ref = refs[7:11]
    outs, ps, ds_, wide, load, store = refs[11:17]
    count, feats = q_ref.shape
    seq = count // 2
    pairs = feats // 128
    plane = lax.axis_index("plane")
    pieces = [(outs, pl.ds(0, seq)), (outs, pl.ds(seq, seq)), (ps, plane)]
    net = Gather(ctxs, pieces, [("block", ds_), ("half", ps)], refs[17:])
    core, ctx = net.core, net.ctx
    me = core * ctxs + ctx
    loads = [
        pltpu.make_async_copy(proj, ps.at[me, plane], load.at[0]),
        pltpu.make_async_copy(mlp.at[1], wide, load.at[1]),
    ]
    for copy in loads:
        copy.start()
    greet_all(net.peers())
    loads[0].wait()
    net.send_own([2])
    loads[1].wait()

    def narrow(g, carry):
        part = pl.ds(pl.multiple_of(g * 16, 16), 16)
        ds_[plane, part, :] = wide[part, :].astype(BF)
        return carry

    lax.fori_loop(0, wide.shape[0] // 16, narrow, 0)
    net.board_start(0)

    def put(rows, lanes, values):
        outs[me, rows, lanes] = values

    hops = list(range(1, ctxs))
    for s in range(2):
        for pair in range(pairs):
            attend_part(
                q_ref, k_ref, v_ref, col_ref, row_ref.at[s], l_ref, put,
                s * seq, seq, pair, (s * pairs + pair) * (128 // HD),
            )
            if s * pairs + pair == 2 * pairs - 1:
                net.send_own([1])
            if hops:
                net.hop(hops.pop(0), [2])
                if not hops:
                    net.board_start(1)
            if s * pairs + pair == pairs - 1:
                net.send_own([0])
                net.board_pass(0)
    for k in hops:
        net.hop(k, [2])
    if hops:
        net.board_start(1)

    def copy_out(b):
        return pltpu.make_async_copy(outs.at[b], o_out.at[b], store.at[b])

    copy_out(me).start()
    for k in range(1, ctxs):
        net.hop(k, [0])
        if k == 2 or ctxs == 2:
            net.board_pass(1)
        net.hop(k, [1])
        net.distant(k, lambda block: copy_out(core * ctxs + block).start())
        net.side_arrive(k - 1, [0, 1])
        if k == 1:
            copy_out((1 - core) * ctxs + ctx).start()
            net.board_finish(0)
        else:
            net.distant(k - 1, lambda block: copy_out((1 - core) * ctxs + block).start())
    tail = [
        pltpu.make_async_copy(ds_, d_out, store.at[2 * ctxs]),
        pltpu.make_async_copy(ps, p_out, store.at[2 * ctxs + 1]),
    ]
    tail[0].start()
    for k in range(ctxs):
        net.side_arrive(k, [2])
    net.board_finish(1)
    net.board_shared(1)
    tail[1].start()
    net.side_arrive(ctxs - 1, [0, 1])
    net.distant(ctxs - 1, lambda block: copy_out((1 - core) * ctxs + block).start())
    net.close()
    for copy in tail:
        copy.wait()
    for b in range(2 * ctxs):
        copy_out(b).wait()


def second_call(ctxs, query, key, value, col, row, proj, mlp):
    team = 2 * ctxs
    count, feats = query.shape
    seq = count // 2
    arows, frows = proj.shape[0], mlp.shape[1]
    shapes = [(team, count, feats), (team, 4, arows, D), (4, frows, D)]
    dma = pltpu.SemaphoreType.DMA
    hbm, vmem = pl.BlockSpec(memory_space=pl.ANY), pl.BlockSpec(memory_space=pltpu.VMEM)

    def kernel(*refs):
        second_kernel(ctxs, refs)

    return pl.pallas_call(
        kernel,
        out_shape=[jax.ShapeDtypeStruct(shape, BF) for shape in shapes]
        + [jax.ShapeDtypeStruct((2 * feats // HD, seq, 1), F32)],
        in_specs=[vmem] * 5 + [hbm] * 2,
        out_specs=[hbm] * 3 + [vmem],
        scratch_shapes=[pltpu.VMEM(shape, BF) for shape in shapes]
        + [pltpu.VMEM((frows, D), F32)]
        + [dma((2,)), dma((team + 2,))]
        + Gather.scratch(ctxs, 3, 2),
        compiler_params=pltpu.CompilerParams(
            collective_id=2, has_side_effects=True, vmem_limit_bytes=VMEM_LIMIT
        ),
        cost_estimate=pl.CostEstimate(
            flops=4 * count * seq * feats, bytes_accessed=24 * count * feats, transcendentals=0
        ),
        name="second",
    )(query, key, value, col, row, proj, mlp)


def third_kernel(ctxs, refs):
    att, proj, x_all, gain, gate, up, mlp, dy = refs[:8]
    m_out, a_out, n_out, o_out, g_out, u_out, d_out = refs[8:15]
    pv, gv, uv, dv, ys, hs, gs, us, ob, xb, nb, sb, narrowed = refs[15:28]
    load, block_sem, store, late = refs[28:32]
    team, own = ys.shape[0], ys.shape[1]
    wide = gv.shape[0]
    pieces = [(ys, pl.ds(0, own // 2)), (ys, pl.ds(own // 2, own // 2))]
    net = Gather(ctxs, pieces, [("block", dv)], refs[32:])
    plane, core, ctx = net.plane, net.core, net.ctx
    me = core * ctxs + ctx
    loads = [
        pltpu.make_async_copy(dy, ys.at[me], load.at[0]),
        pltpu.make_async_copy(mlp.at[2], narrowed, load.at[1]),
        pltpu.make_async_copy(proj, pv, load.at[2]),
        pltpu.make_async_copy(gate, gv, load.at[3]),
        pltpu.make_async_copy(up, uv, load.at[4]),
    ]

    def fetch(i):
        slot = lax.rem(i, 2)
        rows = pl.ds(pl.multiple_of(i * own, own), own)
        size = att.shape[2]
        copies = [
            pltpu.make_async_copy(
                att.at[t, rows], ob.at[slot, :, pl.ds(t * size, size)], block_sem.at[t, slot]
            )
            for t in range(team)
        ]
        return copies + [pltpu.make_async_copy(x_all.at[i], xb.at[slot], block_sem.at[team, slot])]

    def n_store(i):
        return pltpu.make_async_copy(nb.at[lax.rem(i, 2)], n_out.at[i], store.at[0, lax.rem(i, 2)])

    def s_store(i, out):
        return pltpu.make_async_copy(sb.at[lax.rem(i, 2)], out.at[i], store.at[1, lax.rem(i, 2)])

    for copy in loads:
        copy.start()
    for copy in fetch(0):
        copy.start()
    greet_all(net.peers())
    loads[0].wait()
    net.send_own([0, 1])
    loads[1].wait()

    def narrow(g, carry):
        part = pl.ds(pl.multiple_of(g * 16, 16), 16)
        dv[plane, part, :] = narrowed[part, :].astype(BF)
        return carry

    lax.fori_loop(0, narrowed.shape[0] // 16, narrow, 0)
    net.board_start(0)
    for copy in loads[2:]:
        copy.wait()

    steps = [(hop, chunk) for hop in range(1, ctxs) for chunk in range(2)]
    stages = []
    for i, step in enumerate(steps[: 2 * (ctxs - 2)] if ctxs > 2 else []):
        stages.append((min(2 * i + 1, team - 1), step))

    def forward(i, carry):
        slot = lax.rem(i, 2)
        for copy in fetch(i):
            copy.wait()

        @pl.when(i + 1 < team)
        def _():
            for copy in fetch(i + 1):
                copy.start()

        total = xb[slot].astype(F32)
        total = total + mm(ob[slot], pv[...].reshape(ob.shape[2], D), 1, 0)

        @pl.when(i >= 2)
        def _():
            n_store(i - 2).wait()

        nb[slot] = (total * norm_scale(total) * gain[...]).astype(BF)
        n_store(i).start()

        @pl.when(i == me)
        def _():
            m_out[...] = total
            keep = pltpu.make_async_copy(ob.at[slot], a_out, late.at[0])
            keep.start()
            keep.wait()

        normed = nb[slot]
        for first in range(0, wide, 512):
            part = slice(first, first + 512)
            g = mm(normed, gv[part, :], 1, 1)
            u = mm(normed, uv[part, :], 1, 1)
            sig = 1.0 / (1.0 + jnp.exp(-g))
            lit = g * sig
            hs[i, :, part] = (lit * u).astype(BF)
            gs[i, :, part] = (u * sig * (1.0 + g * (1.0 - sig))).astype(BF)
            us[i, :, part] = lit.astype(BF)
        for at, (hop, chunk) in stages:

            @pl.when(i == at)
            def _():
                net.hop(hop, [chunk])

        @pl.when(i == 1)
        def _():
            net.board_pass(0)

        return carry

    lax.fori_loop(0, team, forward, 0)
    n_store(team - 2).wait()
    n_store(team - 1).wait()
    net.board_finish(0)

    def outward(i, carry):
        @pl.when(i >= 2)
        def _():
            s_store(i - 2, o_out).wait()

        sb[lax.rem(i, 2)] = mm(hs[i], dv[...].reshape(wide, D), 1, 0).astype(BF)
        s_store(i, o_out).start()
        return carry

    def backward(side_core):
        def action(block):
            b = side_core * ctxs + block
            for p in range(4):
                cols = slice(p * (wide // 4), (p + 1) * (wide // 4))
                dh = mm(ys[b], dv[p], 1, 1)
                gs[b, :, cols] = (dh * gs[b, :, cols].astype(F32)).astype(BF)
                us[b, :, cols] = (dh * us[b, :, cols].astype(F32)).astype(BF)
            pltpu.make_async_copy(gs.at[b], g_out.at[b], late.at[1 + b]).start()
            pltpu.make_async_copy(us.at[b], u_out.at[b], late.at[1 + team + b]).start()

        return action

    backward(core)(ctx)
    net.side_arrive(0, [0, 1])
    backward(1 - core)(ctx)
    for k in range(1, ctxs - 1):
        if k == ctxs - 2:
            net.hop(ctxs - 1, [0])
        net.distant(k, backward(core))
        net.side_arrive(k, [0, 1])
        net.distant(k, backward(1 - core))
    lax.fori_loop(0, team, outward, 0)
    s_store(team - 2, o_out).wait()
    s_store(team - 1, o_out).wait()
    net.hop(ctxs - 1, [1])
    net.distant(ctxs - 1, backward(core))
    net.side_arrive(ctxs - 1, [0, 1])
    net.distant(ctxs - 1, backward(1 - core))
    for p in range(4):
        if p >= 2:
            s_store(p - 2, d_out).wait()
        hidden = hs[:, :, p * (wide // 4) : (p + 1) * (wide // 4)].reshape(team * own, wide // 4)
        sb[p % 2] = mm(hidden, ys[...].reshape(team * own, D), 0, 0).astype(BF)
        s_store(p, d_out).start()
    s_store(2, d_out).wait()
    s_store(3, d_out).wait()
    net.close()
    for b in range(team):
        pltpu.make_async_copy(gs.at[b], g_out.at[b], late.at[1 + b]).wait()
        pltpu.make_async_copy(us.at[b], u_out.at[b], late.at[1 + team + b]).wait()


def third_call(ctxs, att, proj, x_all, gain, gate, up, mlp, dy):
    team, own, wide = 2 * ctxs, dy.shape[0], gate.shape[0]
    feats = proj.shape[1]
    block, hidden = (team, own, D), (team, own, wide)
    shapes = [(own, team * feats), block, block, hidden, hidden, (4, wide // 4, D)]
    dma = pltpu.SemaphoreType.DMA
    hbm, vmem = pl.BlockSpec(memory_space=pl.ANY), pl.BlockSpec(memory_space=pltpu.VMEM)
    held = [proj.shape, gate.shape, up.shape, (4, wide // 4, D), block, hidden, hidden, hidden]
    held += [(2, own, team * feats), (2, own, D), (2, own, D), (2, own, D)]

    def kernel(*refs):
        third_kernel(ctxs, refs)

    return pl.pallas_call(
        kernel,
        out_shape=[jax.ShapeDtypeStruct((own, D), F32)]
        + [jax.ShapeDtypeStruct(shape, BF) for shape in shapes],
        in_specs=[hbm] * 3 + [vmem] + [hbm] * 4,
        out_specs=[vmem] + [hbm] * len(shapes),
        scratch_shapes=[pltpu.VMEM(shape, BF) for shape in held]
        + [pltpu.VMEM((wide // 4, D), F32)]
        + [dma((5,)), dma((team + 1, 2)), dma((2, 2)), dma((2 * team + 1,))]
        + Gather.scratch(ctxs, 2, 1),
        compiler_params=pltpu.CompilerParams(
            collective_id=6, has_side_effects=True, vmem_limit_bytes=VMEM_LIMIT
        ),
        cost_estimate=pl.CostEstimate(
            flops=2 * team * own * D * (D + 5 * wide),
            bytes_accessed=30 * own * D,
            transcendentals=0,
        ),
        name="third",
    )(att, proj, x_all, gain, gate, up, mlp, dy)


class Cargo:
    def __init__(self, arrays, refs):
        refs = list(refs)
        self.parts = []
        for array in arrays:
            ref = None if Cargo.made(array) else refs.pop(0)
            self.parts += [None if ref is None else ref.at[i] for i in range(array.shape[0])]
        count = len(self.parts)
        self.sums, refs = refs[:count], refs[count:]
        self.kept, refs = refs[:count], refs[count:]
        self.got, refs = refs[:count], refs[count:]
        self.last, refs = refs[:count], refs[count:]
        self.load, self.one, self.two = refs
        self.plane, self.core, self.ctx = (
            lax.axis_index("plane"),
            lax.axis_index("core"),
            lax.axis_index("ctx"),
        )
        self.near = (
            self.plane + 1 - 2 * lax.rem(self.plane, 2),
            lax.rem(self.plane + 2, 4),
        )

    @staticmethod
    def made(array):
        return isinstance(array, jax.ShapeDtypeStruct)

    @staticmethod
    def given(arrays):
        return [array for array in arrays if not Cargo.made(array)]

    def peers(self):
        return [(near, self.core, self.ctx) for near in self.near]

    def rows(self, s, half):
        size = self.kept[s].shape[1] // 2
        return pl.ds(half * size, size)

    def remote(self, source, target, sems, index, near):
        return pltpu.make_async_remote_copy(
            src_ref=source,
            dst_ref=target,
            send_sem=sems.at[(0,) + index],
            recv_sem=sems.at[(1,) + index],
            device_id=(near, self.core, self.ctx),
            device_id_type=MESH_ID,
        )

    def first(self, half, s, b):
        block = self.near[half] if b == 0 else 3 - self.plane
        source = self.kept[s].at[block, self.rows(s, half)]
        target = self.got[s].at[half, b]
        return self.remote(source, target, self.one, (half, s, b), self.near[half])

    def fetch(self, s):
        return pltpu.make_async_copy(self.parts[s], self.kept[s], self.load.at[s])

    def second(self, half, s):
        source = self.kept[s].at[self.near[1 - half], self.rows(s, half)]
        target = self.last[s].at[half]
        return self.remote(source, target, self.two, (half, s), self.near[1 - half])

    def begin(self):
        for s in range(len(self.parts)):
            if self.parts[s] is not None:
                self.fetch(s).start()

    def start(self, slots=None):
        for s in range(len(self.parts)) if slots is None else slots:
            if self.parts[s] is not None:
                self.fetch(s).wait()
            for b in (1, 0):
                for half in range(2):
                    self.first(half, s, b).start()

    def middle(self, s):
        kept, got = self.kept[s], self.got[s]
        size = got.shape[2]
        for half in range(2):
            block = self.near[1 - half]
            self.first(half, s, 1).wait_recv()

            def group(g, carry):
                part = pl.ds(pl.multiple_of(g * 16, 16), 16)
                rows = pl.ds(pl.multiple_of(half * size + g * 16, 16), 16)
                total = kept[block, rows, :].astype(F32) + got[half, 1, part, :].astype(F32)
                kept[block, rows, :] = total.astype(BF)
                return carry

            lax.fori_loop(0, size // 16, group, 0)
            self.second(half, s).start()

    def end(self):
        for s in range(len(self.parts)):
            kept, got, last, sums = self.kept[s], self.got[s], self.last[s], self.sums[s]
            size = got.shape[2]
            for half in range(2):
                self.first(half, s, 0).wait_recv()
                self.second(half, s).wait_recv()

                def group(g, carry):
                    part = pl.ds(pl.multiple_of(g * 16, 16), 16)
                    rows = pl.ds(pl.multiple_of(half * size + g * 16, 16), 16)
                    total = kept[self.plane, rows, :].astype(F32)
                    total = total + got[half, 0, part, :].astype(F32)
                    total = total + last[half, part, :].astype(F32)
                    sums[rows, :] = total
                    return carry

                lax.fori_loop(0, size // 16, group, 0)
        for s in range(len(self.parts)):
            for half in range(2):
                self.first(half, s, 0).wait_send()
                self.first(half, s, 1).wait_send()
                self.second(half, s).wait_send()

    @staticmethod
    def rows_of(arrays):
        return [array.shape[2] for array in arrays for _ in range(array.shape[0])]

    @staticmethod
    def out_shapes(arrays):
        return [jax.ShapeDtypeStruct((rows, D), F32) for rows in Cargo.rows_of(arrays)]

    @staticmethod
    def scratch(arrays):
        rows = Cargo.rows_of(arrays)
        if not rows:
            return []
        dma = pltpu.SemaphoreType.DMA
        return (
            [pltpu.VMEM((4, r, D), BF) for r in rows]
            + [pltpu.VMEM((2, 2, r // 2, D), BF) for r in rows]
            + [pltpu.VMEM((2, r // 2, D), BF) for r in rows]
            + [dma((len(rows),)), dma((2, 2, len(rows), 2)), dma((2, 2, len(rows)))]
        )


def team_sum_kernel(ctxs, pairs, refs, cargo, more):
    lhs, rhs, out_ref = refs[:pairs], refs[pairs : 2 * pairs], refs[2 * pairs]
    refs = refs[2 * pairs + 1 :]
    lhs_v, rhs_v = refs[:pairs], refs[pairs : 2 * pairs]
    staged, theirs, mine, from_left, from_right, load, side, hops = refs[2 * pairs :]
    plane, core, ctx = lax.axis_index("plane"), lax.axis_index("core"), lax.axis_index("ctx")
    last = ctxs - 1
    away = last - ctx
    own = out_ref.shape[0]
    rows = own // CHUNKS
    other = (plane, 1 - core, ctx)
    loads = [pltpu.make_async_copy(rhs[i], rhs_v[i], load.at[2 * ctxs, i]) for i in range(pairs)]
    for copy in loads:
        copy.start()

    def lhs_load(block, i):
        where = pl.ds(pl.multiple_of(block * own, own), own)
        return pltpu.make_async_copy(lhs[i].at[where], lhs_v[i].at[where], load.at[block, i])

    order = []
    for i in range((ctxs + 1) // 2):
        order += [last - i, i] if last - i != i else [i]
    order = [jnp.where(2 * ctx >= ctxs, last - place, place) for place in order]
    for index in order:
        for side_core in (1 - core, core):
            for i in range(pairs):
                lhs_load(side_core * ctxs + index, i).start()
    if cargo:
        cargo.begin()
    greet_all(
        [other]
        + [(plane, core, lax.rem(ctx + k, ctxs)) for k in range(1, ctxs)]
        + (cargo.peers() if cargo else [])
    )
    pending = list(range(len(cargo.parts))) if cargo else []
    ready = [i for i in pending if cargo.parts[i] is not None]
    if cargo:
        cargo.start(ready)
    for copy in loads:
        copy.wait()
    fills = []
    if more:
        other_in, other_v, made, tiles, sems = more
        other_copy = pltpu.make_async_copy(other_in, other_v, sems.at[2])
        other_copy.start()
        if made:

            def store(i, p):
                slot = (4 * i + p) % 2
                return pltpu.make_async_copy(tiles.at[slot], made[i].at[0, p], sems.at[slot])

            def tile(i, p):
                size = lhs_v[i].shape[1] // 4
                index = 4 * i + p
                if index >= 2:
                    store((index - 2) // 4, (index - 2) % 4).wait()
                part = lhs_v[i][:, p * size : (p + 1) * size]
                tiles[index % 2] = mm(part, other_v[...], 0, 0).astype(BF)
                store(i, p).start()

            fills = [functools.partial(tile, i, p) for i in range(len(made)) for p in range(4)]

    def produce(block, target):
        where = pl.ds(pl.multiple_of(block * own, own), own)
        for i in range(pairs):
            lhs_load(block, i).wait()

        def tile(t, carry):
            cols = pl.ds(pl.multiple_of(t * 512, 512), 512)
            total = mm(lhs_v[0][where, :], rhs_v[0][:, cols], 1, 0)
            for i in range(1, pairs):
                total = total + mm(lhs_v[i][where, :], rhs_v[i][:, cols], 1, 0)
            target[:, cols] = total.astype(BF)
            return carry

        lax.fori_loop(0, D // 512, tile, 0)

    def add(index, chunk, extra, slot):
        def group(g, carry):
            part = pl.ds(pl.multiple_of(chunk * rows + g * 16, 16), 16)
            total = mine[index, part, :].astype(F32) + theirs[index, part, :].astype(F32)
            if extra is not None:
                total = total + extra[slot, part, :].astype(F32)
            mine[index, part, :] = total.astype(BF)
            return carry

        lax.fori_loop(0, rows // 16, group, 0)

    def share(index):
        return pltpu.make_async_remote_copy(
            src_ref=staged.at[index],
            dst_ref=theirs.at[index],
            send_sem=side.at[0, index],
            recv_sem=side.at[1, index],
            device_id=other,
            device_id_type=MESH_ID,
        )

    def hop(way, slot, chunk, index):
        part = pl.ds(chunk * rows, rows)
        inbox = from_left if way == 0 else from_right
        return pltpu.make_async_remote_copy(
            src_ref=mine.at[index, part],
            dst_ref=inbox.at[slot, part],
            send_sem=hops.at[0, way, slot, chunk],
            recv_sem=hops.at[1, way, slot, chunk],
            device_id=(plane, core, lax.rem(ctx + (1 if way == 0 else last), ctxs)),
            device_id_type=MESH_ID,
        )

    places = []
    for i in range((ctxs + 1) // 2):
        places += [last - i, i] if last - i != i else [i]
    for place, index in zip(places, order):
        produce((1 - core) * ctxs + index, staged.at[index])
        share(index).start()
        produce(core * ctxs + index, mine.at[index])

        if place > 0:

            @pl.when(ctx == 0)
            def _():
                share(place).wait_recv()
                for chunk in range(CHUNKS):
                    add(place, chunk, None, 0)
                    hop(0, ctxs - place, chunk, place).start()

            @pl.when(ctx == last)
            def _():
                share(last - place).wait_recv()
                for chunk in range(CHUNKS):
                    add(last - place, chunk, None, 0)
                    hop(1, ctxs - place, chunk, last - place).start()

    if more:
        other_copy.wait()
        if not made:
            fresh = [i for i in pending if cargo.parts[i] is None]
            for i, slot in enumerate(fresh):
                size = lhs_v[i].shape[1]
                product = mm(lhs_v[i][...], other_v[...], 0, 0).astype(BF)
                cargo.kept[slot][...] = product.reshape(4, size // 4, D)
                cargo.start([slot])

    for step in range(1, last):

        @pl.when((ctx > 0) & (step >= ctx))
        def _():
            index = last + ctx - step
            share(index).wait_recv()
            for chunk in range(CHUNKS):
                hop(0, step, chunk, index).wait_recv()
                add(index, chunk, from_left, step)

                @pl.when(ctx < last)
                def _():
                    hop(0, step + 1, chunk, index).start()

        @pl.when((away > 0) & (step >= away))
        def _():
            index = step - away
            share(index).wait_recv()
            for chunk in range(CHUNKS):
                hop(1, step, chunk, index).wait_recv()
                add(index, chunk, from_right, step)

                @pl.when(ctx > 0)
                def _():
                    hop(1, step + 1, chunk, index).start()

        for fill in fills[:3]:
            fill()
        fills = fills[3:]
        if pending:
            cargo.middle(pending.pop(0))
    for fill in fills:
        fill()
    for s in pending:
        cargo.middle(s)

    share(ctx).wait_recv()

    def close(way):
        for chunk in range(CHUNKS):
            hop(way, last, chunk, ctx).wait_recv()

    def finish(inboxes):
        def group(g, carry):
            part = pl.ds(pl.multiple_of(g * 16, 16), 16)
            total = mine[ctx, part, :].astype(F32) + theirs[ctx, part, :].astype(F32)
            for inbox in inboxes:
                total = total + inbox[last, part, :].astype(F32)
            out_ref[part, :] = total
            return carry

        lax.fori_loop(0, own // 16, group, 0)

    @pl.when(ctx == 0)
    def _():
        close(1)
        finish([from_right])

    @pl.when(ctx == last)
    def _():
        close(0)
        finish([from_left])

    @pl.when((ctx > 0) & (ctx < last))
    def _():
        close(0)
        close(1)
        finish([from_left, from_right])

    for index in range(ctxs):
        share(index).wait_send()
    for slot in range(1, ctxs):

        @pl.when((ctx < last) & (slot >= ctx + 1))
        def _():
            for chunk in range(CHUNKS):
                hop(0, slot, chunk, ctxs + ctx - slot).wait_send()

        @pl.when((ctx > 0) & (slot >= away + 1))
        def _():
            for chunk in range(CHUNKS):
                hop(1, slot, chunk, slot - 1 - away).wait_send()

    if more and made:
        store(len(made) - 1, 2).wait()
        store(len(made) - 1, 3).wait()
    if cargo:
        cargo.end()


def team_sum(ctxs, number, pairs, name, freight=(), other=None, outer=False):
    count = pairs[0][0].shape[0]
    own = count // (2 * ctxs)
    lhs, rhs = [a for a, _ in pairs], [b for _, b in pairs]
    dma = pltpu.SemaphoreType.DMA

    inputs = 2 * len(pairs)
    given = Cargo.given(freight)
    outputs = 1 + len(Cargo.rows_of(freight))
    scratch = [pltpu.VMEM(a.shape, BF) for a in lhs + rhs]
    scratch += [pltpu.VMEM((ctxs, own, D), BF)] * 5
    scratch += [dma((2 * ctxs + 1, len(pairs))), dma((2, ctxs)), dma((2, 2, ctxs, CHUNKS))]
    made = [(1, 4, a.shape[1] // 4, D) for a in lhs] if outer else []
    extra = [other] if other is not None else []
    held = [pltpu.VMEM(a.shape, BF) for a in extra]
    held += [pltpu.VMEM((2,) + made[0][2:], BF)] if made else []
    held += [dma((3,))] if extra else []

    def kernel(*refs):
        ins, refs = refs[:inputs], refs[inputs:]
        parts, refs = refs[: len(given)], refs[len(given) :]
        more, refs = refs[: len(extra)], refs[len(extra) :]
        outs, refs = refs[:outputs], refs[outputs:]
        products, refs = refs[: len(made)], refs[len(made) :]
        mine, refs = refs[: len(scratch)], refs[len(scratch) :]
        spare, buffers = refs[: len(refs) - len(held)], refs[len(refs) - len(held) :]
        cargo = Cargo(freight, parts + outs[1:] + spare) if freight else None
        if more:
            tiles = buffers[1] if made else None
            more = (more[0], buffers[0], products, tiles, buffers[-1])
        team_sum_kernel(ctxs, len(pairs), ins + outs[:1] + mine, cargo, more)

    depth = sum(b.shape[0] for b in rhs)
    return pl.pallas_call(
        kernel,
        out_shape=[jax.ShapeDtypeStruct((own, D), F32)]
        + Cargo.out_shapes(freight)
        + [jax.ShapeDtypeStruct(shape, BF) for shape in made],
        in_specs=[pl.BlockSpec(memory_space=pl.ANY)] * (inputs + len(given) + len(extra)),
        out_specs=[pl.BlockSpec(memory_space=pltpu.VMEM)] * outputs
        + [pl.BlockSpec(memory_space=pl.ANY)] * len(made),
        scratch_shapes=scratch + Cargo.scratch(freight) + held,
        compiler_params=pltpu.CompilerParams(
            collective_id=number, has_side_effects=True, vmem_limit_bytes=VMEM_LIMIT
        ),
        cost_estimate=pl.CostEstimate(
            flops=2 * count * depth * D,
            bytes_accessed=2 * (count + D) * depth + 4 * own * D,
            transcendentals=0,
        ),
        name=name,
    )(*lhs, *rhs, *given, *extra)


def middle_kernel(ctxs, refs, freight):
    da, att, proj, out_part = refs[:4]
    refs = refs[4:]
    part, grad, joined, outs = refs[0], refs[1], refs[2], refs[3 : 3 + ctxs]
    first, sums, refs = refs[3 + ctxs], refs[4 + ctxs], refs[5 + ctxs :]
    pv, ov, sent, staged, mine, theirs, others, load, swap, side, shift = refs[:11]
    cargo = Cargo(freight, [part, sums] + list(refs[11:]))
    plane, core, ctx = cargo.plane, cargo.core, cargo.ctx
    me = core * ctxs + ctx
    loads = [
        pltpu.make_async_copy(proj, pv, load.at[0]),
        pltpu.make_async_copy(out_part, ov, load.at[1]),
    ]
    loads[1].start()
    loads[0].start()
    cargo.begin()
    partners = [
        (dc, dz) for dz in range(ctxs - 1, -1, -1) for dc in range(2) if dc + dz > 0
    ]

    def partner(dc, dz):
        return (core if dc == 0 else 1 - core, lax.rem(ctx + dz, ctxs))

    greet_all([(plane,) + partner(*step) for step in partners] + cargo.peers())

    def remote(source, target, sems, index, peer):
        return pltpu.make_async_remote_copy(
            src_ref=source,
            dst_ref=target,
            send_sem=sems.at[(0,) + index],
            recv_sem=sems.at[(1,) + index],
            device_id=(plane,) + peer,
            device_id_type=MESH_ID,
        )

    def piece(i, c, z, home):
        return remote(sent.at[c * ctxs + z], grad.at[home], swap, (i,), (c, z))

    def share(kind, z):
        source = ov.at[(1 - core) * ctxs + z] if kind == 0 else staged.at[z]
        target = others.at[z] if kind == 0 else theirs.at[z]
        return remote(source, target, side, (kind, z), (1 - core, ctx))

    loads[1].wait()
    for k in list(range(1, ctxs)) + [0]:
        share(0, lax.rem(ctx + k, ctxs)).start()
    loads[0].wait()
    for i, step in enumerate(partners):
        c, z = partner(*step)
        sent[c * ctxs + z] = mm(da[...], pv[c * ctxs + z], 1, 1).astype(BF)
        piece(i, c, z, me).start()
    cargo.start()

    def join(k):
        z = lax.rem(ctx + k, ctxs)
        share(0, z).wait_recv()
        target = outs[k - 1]

        def group(g, carry):
            part_ = pl.ds(pl.multiple_of(g * 16, 16), 16)
            total = ov[core * ctxs + z, part_, :].astype(F32) + others[z, part_, :].astype(F32)
            target[part_, :] = total.astype(BF)
            return carry

        lax.fori_loop(0, target.shape[0] // 16, group, 0)

    join(1)
    pass_on = remote(outs[0], first, shift, (0,), (core, lax.rem(ctx + 1, ctxs)))
    pass_on.start()
    grad[me] = mm(da[...], pv[me], 1, 1).astype(BF)
    width = grad.shape[2]

    def heads(t):
        return att[:, pl.ds(pl.multiple_of(t * width, width), width)]

    for z in range(ctxs):
        staged[z] = mm(heads((1 - core) * ctxs + z), da[...], 0, 0).astype(BF)
        share(1, z).start()
    for z in range(ctxs):
        mine[z] = mm(heads(core * ctxs + z), da[...], 0, 0).astype(BF)
    size = pv.shape[1]
    for k in list(range(2, ctxs)) + [0]:
        join(k)
    cargo.middle(0)
    for z in range(ctxs):
        share(1, z).wait_recv()
        for p in range(4):

            def group(g, carry):
                rows = pl.ds(pl.multiple_of(p * (size // 4) + g * 16, 16), 16)
                total = mine[z, rows, :].astype(F32) + theirs[z, rows, :].astype(F32)
                joined[p, z, pl.ds(pl.multiple_of(g * 16, 16), 16), :] = total.astype(BF)
                return carry

            lax.fori_loop(0, size // 64, group, 0)
    for i, (dc, dz) in enumerate(partners):
        c, z = core if dc == 0 else 1 - core, lax.rem(ctx + ctxs - dz, ctxs)
        piece(i, c, z, c * ctxs + z).wait_recv()
    cargo.end()
    pass_on.wait()
    for i, step in enumerate(partners):
        c, z = partner(*step)
        piece(i, c, z, me).wait_send()
    for z in range(ctxs):
        share(0, z).wait_send()
        share(1, z).wait_send()


def middle_call(ctxs, da, att, proj, out_part, part):
    team, own = 2 * ctxs, da.shape[0]
    feats = proj.shape[1]
    freight = (part,)
    dma = pltpu.SemaphoreType.DMA
    hbm, vmem = pl.BlockSpec(memory_space=pl.ANY), pl.BlockSpec(memory_space=pltpu.VMEM)
    block = (ctxs, own, D)

    def kernel(*refs):
        middle_kernel(ctxs, refs, freight)

    return pl.pallas_call(
        kernel,
        out_shape=[
            jax.ShapeDtypeStruct((team, own, feats), BF),
            jax.ShapeDtypeStruct((4, ctxs, feats // 4, D), BF),
        ]
        + [jax.ShapeDtypeStruct((own, D), BF)] * (ctxs + 1)
        + Cargo.out_shapes(freight),
        in_specs=[vmem, vmem, hbm, hbm, hbm],
        out_specs=[vmem] * (4 + ctxs),
        scratch_shapes=[
            pltpu.VMEM(proj.shape, BF),
            pltpu.VMEM(out_part.shape, BF),
            pltpu.VMEM((team, own, feats), BF),
            pltpu.VMEM((ctxs, feats, D), BF),
            pltpu.VMEM((ctxs, feats, D), BF),
            pltpu.VMEM((ctxs, feats, D), BF),
            pltpu.VMEM(block, BF),
            dma((2,)),
            dma((2, team - 1)),
            dma((2, 2, ctxs)),
            dma((2, 1)),
        ]
        + Cargo.scratch(freight),
        compiler_params=pltpu.CompilerParams(
            collective_id=7, has_side_effects=True, vmem_limit_bytes=VMEM_LIMIT
        ),
        cost_estimate=pl.CostEstimate(
            flops=4 * own * D * D, bytes_accessed=60 * own * D, transcendentals=0
        ),
        name="middle",
    )(da, att, proj, out_part, part)


def qkv_kernel(feats, x_ref, gain_ref, w_ref, c_ref, a_ref, b_ref, n_ref, q_ref, k_ref, v_ref):
    values = x_ref[...].astype(F32)
    normed = (values * norm_scale(values) * gain_ref[...]).astype(BF)
    n_ref[...] = normed
    cosine, low_sine, high_sine = [widen(ref[...], feats) for ref in (c_ref, a_ref, b_ref)]
    q = mm(normed, w_ref[0:feats], 1, 1)
    q_ref[...] = rope(q, cosine, low_sine, high_sine).astype(BF)
    k = mm(normed, w_ref[feats : 2 * feats], 1, 1)
    k_ref[...] = rope(k, cosine, low_sine, high_sine).astype(BF)
    v_ref[...] = mm(normed, w_ref[2 * feats :], 1, 1).astype(BF)


def qkv_call(x_all, gain, weights, tables):
    count = x_all.shape[0]
    feats = weights.shape[0] // 3
    turns = tables[0].shape[0] // BLOCK
    rows = pl.BlockSpec((BLOCK, D), lambda i: (i, 0))
    part = pl.BlockSpec((BLOCK, feats), lambda i: (i, 0))
    table = pl.BlockSpec((BLOCK, 128), lambda i: (i % turns, 0))
    out = jax.ShapeDtypeStruct((count, feats), BF)
    return pl.pallas_call(
        functools.partial(qkv_kernel, feats),
        grid=(count // BLOCK,),
        out_shape=(jax.ShapeDtypeStruct((count, D), BF), out, out, out),
        in_specs=[
            rows,
            pl.BlockSpec((1, D), lambda i: (0, 0)),
            pl.BlockSpec((3 * feats, D), lambda i: (0, 0)),
            table,
            table,
            table,
        ],
        out_specs=(rows, part, part, part),
        compiler_params=params(),
        cost_estimate=pl.CostEstimate(
            flops=6 * count * D * feats, bytes_accessed=4 * count * D, transcendentals=0
        ),
        name="qkv",
    )(x_all, gain, weights, *tables)


def allowed_keys(col_ref, row_ref, first, size, keys):
    same = col_ref[first : first + size, :] == row_ref[:, 0:keys]
    query_place = first + lax.broadcasted_iota(jnp.int32, (size, keys), 0)
    key_place = lax.broadcasted_iota(jnp.int32, (size, keys), 1)
    return same & (key_place <= query_place)


def attend_kernel(q_ref, k_ref, v_ref, col_ref, row_ref, o_ref, l_ref):
    length = q_ref.shape[0]
    for first in range(0, length, BLOCK):
        keys = first + BLOCK
        allowed = allowed_keys(col_ref, row_ref, first, BLOCK, keys)
        parts = []
        for head in range(q_ref.shape[1] // HD):
            lanes = slice(head * HD, (head + 1) * HD)
            query = q_ref[first:keys, lanes] * HD ** (-0.5)
            scores = jnp.where(allowed, mm(query, k_ref[0:keys, lanes], 1, 1), MASKED)
            highest = jnp.max(scores, -1, keepdims=True)
            shifted = jnp.exp(scores - highest)
            totals = jnp.sum(shifted, -1, keepdims=True)
            weights = (shifted * (1.0 / totals)).astype(BF)
            parts.append(mm(weights, v_ref[0:keys, lanes], 1, 0))
            l_ref[head, first:keys, :] = highest + jnp.log(totals)
        o_ref[first:keys, :] = jnp.concatenate(parts, 1).astype(BF)


def attend_call(query, key, value, col, row, seq):
    count, feats = query.shape
    pairs = feats // 128
    part = pl.BlockSpec((seq, 128), lambda s, h: (s, h))
    each = 128 // HD
    return pl.pallas_call(
        attend_kernel,
        grid=(2, pairs),
        out_shape=(
            jax.ShapeDtypeStruct((count, feats), BF),
            jax.ShapeDtypeStruct((2 * pairs * each, seq, 1), F32),
        ),
        in_specs=[
            part,
            part,
            part,
            pl.BlockSpec((seq, 1), lambda s, h: (s, 0)),
            pl.BlockSpec((None, 1, seq), lambda s, h: (s, 0, 0)),
        ],
        out_specs=(part, pl.BlockSpec((each, seq, 1), lambda s, h: (s * pairs + h, 0, 0))),
        compiler_params=params(2),
        cost_estimate=pl.CostEstimate(
            flops=4 * count * seq * feats, bytes_accessed=8 * count * feats, transcendentals=0
        ),
        name="attend",
    )(query, key, value, col, row)


def attend_back_kernel(
    q_ref, k_ref, v_ref, g_ref, l_ref, col_ref, row_ref, c_ref, a_ref, b_ref,
    dq_ref, dk_ref, dv_ref, key_total, value_total, query_total,
):
    length = q_ref.shape[0]
    scale = HD ** (-0.5)
    key_total[...] = jnp.zeros_like(key_total)
    value_total[...] = jnp.zeros_like(value_total)
    for first in range(0, length, BLOCK):
        keys = first + BLOCK
        allowed = allowed_keys(col_ref, row_ref, first, BLOCK, keys)
        dq_parts, dk_parts, dv_parts = [], [], []
        for head in range(q_ref.shape[1] // HD):
            lanes = slice(head * HD, (head + 1) * HD)
            query = q_ref[first:keys, lanes] * scale
            key = k_ref[0:keys, lanes]
            grad = g_ref[first:keys, lanes]
            scores = jnp.where(allowed, mm(query, key, 1, 1), MASKED)
            probs = jnp.exp(scores - l_ref[head, first:keys, :])
            grad_probs = mm(grad, v_ref[0:keys, lanes], 1, 1)
            inner = jnp.sum(probs * grad_probs, -1, keepdims=True)
            grad_scores = (probs * (grad_probs - inner)).astype(BF)
            dq_parts.append(mm(grad_scores, key, 1, 0) * scale)
            dk_parts.append(mm(grad_scores, query, 0, 0))
            dv_parts.append(mm(probs.astype(BF), grad, 0, 0))
        query_total[first:keys, :] = jnp.concatenate(dq_parts, 1)
        key_total[0:keys, :] += jnp.concatenate(dk_parts, 1)
        value_total[0:keys, :] += jnp.concatenate(dv_parts, 1)
    cosine, low_sine, high_sine = c_ref[...], a_ref[...], b_ref[...]
    dq_ref[...] = rope_back(query_total[...], cosine, low_sine, high_sine).astype(BF)
    dk_ref[...] = rope_back(key_total[...], cosine, low_sine, high_sine).astype(BF)
    dv_ref[...] = value_total[...].astype(BF)


def attend_back_call(
    query, key, value, grad, log_sums, col, row, tables, seq, freight=(), rider=(), number=None
):
    count, feats = query.shape
    pairs = feats // 128
    part = pl.BlockSpec((seq, 128), lambda s, h: (s, h))
    table = pl.BlockSpec((seq, 128), lambda s, h: (0, 0))
    each = 128 // HD
    out = jax.ShapeDtypeStruct((count, feats), BF)
    outputs = len(Cargo.rows_of(freight))

    def kernel(*refs):
        ins, refs = refs[:10], refs[10:]
        parts, refs = refs[: len(freight)], refs[len(freight) :]
        riders, refs = refs[: len(rider)], refs[len(rider) :]
        outs, refs = refs[:3], refs[3:]
        sums, refs = refs[:outputs], refs[outputs:]
        landed, refs = refs[: len(rider)], refs[len(rider) :]
        mine, spare = refs[:3], refs[3:]
        step = pl.program_id(0) * pairs + pl.program_id(1)
        if rider:
            held, got, sems = spare[-3:]
            spare = spare[:-3]
            plane, core, ctx = [lax.axis_index(name) for name in ALL]
            across = (plane, core, lax.rem(ctx + 2, 4))
            fetch = pltpu.make_async_copy(riders[0], held, sems.at[0])
            ride = pltpu.make_async_remote_copy(
                src_ref=held,
                dst_ref=got,
                send_sem=sems.at[1],
                recv_sem=sems.at[2],
                device_id=across,
                device_id_type=MESH_ID,
            )
        cargo = Cargo(freight, parts + sums + spare) if freight else None
        if freight:

            @pl.when(step == 0)
            def _():
                cargo.begin()
                if rider:
                    fetch.start()
                greet_all(cargo.peers() + ([across] if rider else []))
                if rider:
                    fetch.wait()
                    ride.start()
                cargo.start()

            @pl.when(step == 2 * pairs - 1)
            def _():
                for s in range(outputs):
                    cargo.middle(s)

        attend_back_kernel(*ins, *outs, *mine)
        if freight:

            @pl.when(step == 2 * pairs - 1)
            def _():
                cargo.end()
                if rider:
                    ride.wait()
                    landed[0][...] = got[...]

    more = dict(collective_id=number, has_side_effects=True) if freight else {}
    return pl.pallas_call(
        kernel,
        grid=(2, pairs),
        out_shape=[out, out, out]
        + Cargo.out_shapes(freight)
        + [jax.ShapeDtypeStruct(array.shape, BF) for array in rider],
        in_specs=[
            part,
            part,
            part,
            part,
            pl.BlockSpec((each, seq, 1), lambda s, h: (s * pairs + h, 0, 0)),
            pl.BlockSpec((seq, 1), lambda s, h: (s, 0)),
            pl.BlockSpec((None, 1, seq), lambda s, h: (s, 0, 0)),
            table,
            table,
            table,
        ]
        + [pl.BlockSpec(memory_space=pl.ANY)] * (len(freight) + len(rider)),
        out_specs=[part, part, part]
        + [pl.BlockSpec((rows, D), lambda s, h: (0, 0)) for rows in Cargo.rows_of(freight)]
        + [pl.BlockSpec(array.shape, lambda s, h: (0, 0)) for array in rider],
        scratch_shapes=[pltpu.VMEM((seq, 128), F32)] * 3
        + Cargo.scratch(freight)
        + ([pltpu.VMEM(rider[0].shape, BF)] * 2 + [pltpu.SemaphoreType.DMA((3,))] if rider else []),
        compiler_params=params(2, **more),
        cost_estimate=pl.CostEstimate(
            flops=10 * count * seq * feats, bytes_accessed=14 * count * feats, transcendentals=0
        ),
        name="attend_back",
    )(query, key, value, grad, log_sums, col, row, *tables, *freight, *rider)


def project_kernel(o_ref, w_ref, x_ref, gain_ref, m_ref, n_ref):
    total = x_ref[...].astype(F32)
    for index in range(o_ref.shape[0]):
        total = total + mm(o_ref[index], w_ref[index], 1, 0)
    m_ref[...] = total
    n_ref[...] = (total * norm_scale(total) * gain_ref[...]).astype(BF)


def project_call(attended, weights, x_all, gain):
    team, count, feats = attended.shape
    rows = pl.BlockSpec((BLOCK, D), lambda i: (i, 0))
    return pl.pallas_call(
        project_kernel,
        grid=(count // BLOCK,),
        out_shape=(
            jax.ShapeDtypeStruct((count, D), F32),
            jax.ShapeDtypeStruct((count, D), BF),
        ),
        in_specs=[
            pl.BlockSpec((team, BLOCK, feats), lambda i: (0, i, 0)),
            pl.BlockSpec((team, feats, D), lambda i: (0, 0, 0), pipeline_mode=pl.Buffered(1)),
            rows,
            pl.BlockSpec((1, D), lambda i: (0, 0)),
        ],
        out_specs=(rows, rows),
        compiler_params=params(),
        cost_estimate=pl.CostEstimate(
            flops=2 * count * D * D, bytes_accessed=10 * count * D, transcendentals=0
        ),
        name="project",
    )(attended, weights, x_all, gain)


def shifted(value, axis, size, step):
    return lax.ppermute(value, axis, [(i, (i + step) % size) for i in range(size)])


def plane_reduce(parts, planes):
    home = lax.axis_index("plane")
    rows = parts[0].shape[1]

    def block(index, first, size):
        return jnp.stack(
            [
                lax.dynamic_slice(part, (index, first, 0), (1, size, D))[0].astype(BF)
                for part in parts
            ],
            0,
        )

    if planes != 4:
        total = block(home, 0, rows).astype(F32)
        for k in range(1, planes):
            part = block(lax.rem(home + k, planes), 0, rows)
            total = total + shifted(part, "plane", planes, k).astype(F32)
        return total
    near_x, near_y = home + 1 - 2 * lax.rem(home, 2), lax.rem(home + 2, 4)
    far = 3 - home
    along = ([(0, 1), (1, 0), (2, 3), (3, 2)], [(0, 2), (2, 0), (1, 3), (3, 1)])
    size = rows // 2
    sums = []
    for half in range(2):
        one, two = (near_x, near_y) if half == 0 else (near_y, near_x)
        first = half * size
        sent = jnp.stack([block(one, first, size), block(far, first, size)], 0)
        got = lax.ppermute(sent, "plane", along[half]).astype(F32)
        kept = block(home, first, size).astype(F32) + got[0]
        passed = (block(two, first, size).astype(F32) + got[1]).astype(BF)
        sums.append(kept + lax.ppermute(passed, "plane", along[1 - half]).astype(F32))
    return jnp.concatenate(sums, 1)


def core_join(parts, ctxs):
    core = lax.axis_index("core")
    parts = parts.reshape((2, ctxs) + parts.shape[1:])
    got = shifted(lax.dynamic_index_in_dim(parts, 1 - core, 0, False), "core", 2, 1)
    kept = lax.dynamic_index_in_dim(parts, core, 0, False)
    joined = (kept.astype(F32) + got.astype(F32)).astype(BF)
    return jnp.moveaxis(joined, 1, 0)


def line_reduce(parts, ctxs):
    ctx = lax.axis_index("ctx")
    total = lax.dynamic_index_in_dim(parts, ctx, 0, False)
    for k in range(1, ctxs):
        part = lax.dynamic_index_in_dim(parts, lax.rem(ctx + k, ctxs), 0, False)
        total = total + shifted(part.astype(BF), "ctx", ctxs, k).astype(F32)
    return total


def after(value, *others):
    return lax.optimization_barrier((value,) + others)[0]


def team_join(parts, ctxs):
    core, ctx = lax.axis_index("core"), lax.axis_index("ctx")
    own = parts.shape[0] // (2 * ctxs)
    parts = parts.reshape(2 * ctxs, own, D)

    def block(which, k):
        return lax.dynamic_index_in_dim(parts, which * ctxs + (ctx + k) % ctxs, 0, False)

    joined = []
    for k in list(range(1, ctxs)) + [0]:
        got = shifted(block(1 - core, k), "core", 2, 1)
        both = block(core, k).astype(F32) + got.astype(F32)
        joined.append(both.astype(BF) if k > 0 else both)
    return joined


def team_finish(joined, ctxs):
    total = joined[-1].astype(F32)
    for k in range(1, ctxs):
        total = total + shifted(joined[k - 1], "ctx", ctxs, k).astype(F32)
    return total


def local(
    planes,
    ctxs,
    tokens,
    cotangent,
    segments,
    attn_weight,
    attn_first,
    attn_second,
    mlp_weight,
    mlp_first,
    mlp_second,
    gain_weight,
    gain_first,
    gain_second,
):
    team = 2 * ctxs
    devices = planes * team
    own = tokens.shape[0]
    seq = ctxs * own
    count = 2 * seq
    arows = attn_weight.shape[0]
    frows = mlp_weight.shape[0]
    gcols = gain_weight.shape[1]
    feats = planes * arows
    hidden_count = planes * frows
    whole_heads = arows % HD == 0
    me = lax.axis_index(TEAM)

    lines_seg = own // 128
    square = planes == 4 and ctxs == 4 and whole_heads and gcols == 64
    packed = jnp.zeros((8, 128), F32)
    own_gain = lax.reduce_precision(gain_weight, 8, 7)
    if square:
        side = lax.rem(lax.axis_index("ctx"), 2)
        packed = lax.dynamic_update_slice(packed, own_gain, (0, side * gcols))
    else:
        packed = packed.at[0:2, 0:gcols].set(own_gain)
    packed = packed.at[2 : 2 + lines_seg].set(segments.astype(F32).reshape(lines_seg, 128))
    attn_low = attn_weight.astype(BF)
    qkv_low = jnp.moveaxis(attn_low[:, :3], 1, 0)
    proj_low = attn_low[:, 3]
    gate_low, up_low, down_low = [mlp_weight[:, i].astype(BF) for i in range(3)]
    tables = rope_tables(seq)
    if square:
        mlp_slots = jnp.moveaxis(mlp_weight, 1, 0)
        x_all, normed, query, key, value, qkv, gate_w, small = front_call(
            ctxs, tokens, qkv_low, mlp_slots, packed, tables
        )
        normed = normed.reshape(count, D)
        query, key, value = [part.reshape(count, feats) for part in (query, key, value)]
        qkv = qkv.reshape(3 * feats, D)
        gate_w = gate_w.reshape(hidden_count, D)
        gains = small.reshape(planes, ctxs, 2, 8, 128)[:, :, :, 0:2].sum(2)
        gains = gains.transpose(2, 0, 1, 3).reshape(2, D)
        team_small = lax.dynamic_index_in_dim(small, lax.axis_index("plane"), 0, False)
        seg = team_small[:, 2 : 2 + lines_seg].reshape(count)
        seg_col, seg_row = seg.reshape(count, 1), seg.reshape(2, 1, seq)
        att_all, proj, up_w, log_sums = second_call(
            ctxs, query, key, value, seg_col, seg_row, proj_low, mlp_slots
        )
        proj = proj.reshape(team, feats, D)
        up_w = up_w.reshape(hidden_count, D)
        middle_own, att_own, normed_two, out_part, dgate, dup, down_part = third_call(
            ctxs, att_all, proj, x_all, gains[1:2], gate_w, up_w, mlp_slots, cotangent
        )
        normed_two, out_part = normed_two.reshape(count, D), out_part.reshape(count, D)
        dgate, dup = dgate.reshape(count, hidden_count), dup.reshape(count, hidden_count)
        down_part = down_part.reshape(1, planes, frows, D)
    else:
        inputs = [tokens, packed, gate_low, up_low]
        lines = [(0, 0, 2), (1, 1, 1)]
        shapes = [((team, own, D), BF), ((team, 8, 128), F32)]
        boards = []
        if whole_heads:
            inputs += [proj_low, qkv_low]
            lines.append((4, 2, 1))
            shapes.append(((team, arows, D), BF))
            boards.append(("slots", lambda ins, outs: ins[5], len(shapes)))
            shapes.append(((3, planes, arows, D), BF))
        boards.append(("block", lambda ins, outs: ins[2], len(shapes)))
        shapes.append(((planes, frows, D), BF))
        boards.append(("block", lambda ins, outs: ins[3], len(shapes)))
        shapes.append(((planes, frows, D), BF))
        boards.append(("late", lambda ins, outs: outs[1], len(shapes)))
        shapes.append(((planes, team, 8, 128), F32))
        gathered = gather_call(planes, ctxs, 0, inputs, lines, boards, shapes, "gather_first")
        x_all = gathered[0].reshape(count, D)
        small = gathered[-1]
        gate_w = gathered[-3].reshape(hidden_count, D)
        up_w = gathered[-2].reshape(hidden_count, D)
        gains = small[:, :, 0:2, 0:gcols].transpose(2, 0, 1, 3).reshape(2, D)
        seg = gathered[1][:, 2 : 2 + lines_seg].reshape(count)
        seg_col, seg_row = seg.reshape(count, 1), seg.reshape(2, 1, seq)
        if whole_heads:
            qkv = gathered[3].reshape(3 * feats, D)
        else:
            qkv = lax.all_gather(qkv_low, ALL, axis=1, tiled=True)
            qkv = lax.dynamic_slice_in_dim(qkv, me * feats, feats, 1).reshape(3 * feats, D)
            proj = lax.all_gather(proj_low, ALL, axis=0, tiled=True).reshape(team, feats, D)

        normed, query, key, value = qkv_call(x_all, gains[0:1], qkv, tables)
        attended, log_sums = attend_call(query, key, value, seg_col, seg_row, seq)

        inputs = [attended, down_low]
        lines = [(0, 0, 2)]
        shapes = [((team, count, feats), BF)]
        boards = []
        if whole_heads:
            inputs.append(gathered[2])
            boards.append(("half", lambda ins, outs: ins[2], len(shapes)))
            shapes.append(((team, planes, arows, D), BF))
        boards.append(("block", lambda ins, outs: ins[1], len(shapes)))
        shapes.append(((planes, frows, D), BF))
        gathered = gather_call(planes, ctxs, 2, inputs, lines, boards, shapes, "gather_second")
        att_all = gathered[0]
        down_w = gathered[-1].reshape(hidden_count, D)
        if whole_heads:
            proj = gathered[1].reshape(team, feats, D)
        dy_all = lax.all_gather(after(cotangent, att_all), TEAM, axis=0, tiled=True)
        middle, normed_two = project_call(att_all, proj, x_all, gains[1:2])
        mlp_w = (gate_w, up_w, down_w)

        gate = mm(normed_two, mlp_w[0], 1, 1)
        up = mm(normed_two, mlp_w[1], 1, 1)
        hidden = (jax.nn.silu(gate) * up).astype(BF)
        out_part = mm(hidden, mlp_w[2], 1, 0).astype(BF)
        grad_hidden = mm(after(dy_all, out_part), mlp_w[2], 1, 1)
        sig = jax.nn.sigmoid(gate)
        dgate = (grad_hidden * up * sig * (1.0 + gate * (1.0 - sig))).astype(BF)
        dup = (grad_hidden * gate * sig).astype(BF)
        down_part = mm(hidden, dy_all, 0, 0).astype(BF).reshape(1, planes, frows, D)
        middle_own = lax.dynamic_slice_in_dim(middle, me * own, own, 0)
        att_own = lax.dynamic_slice_in_dim(att_all, me * own, own, 1)
    if square:
        dn2, *down_sum, gate_part, up_part = team_sum(
            ctxs,
            3,
            [(dgate, gate_w), (dup, up_w)],
            "sum_two",
            (down_part,),
            normed_two,
            True,
        )
    else:
        (dn2,) = team_sum(ctxs, 3, [(dgate, gate_w), (dup, up_w)], "sum_two")
        gate_part = mm(dgate, normed_two, 0, 0).astype(BF).reshape(1, planes, frows, D)
        up_part = mm(dup, normed_two, 0, 0).astype(BF).reshape(1, planes, frows, D)

    middle_part, gain_two_grad = norm_back(dn2, middle_own, norm_scale(middle_own), gains[1])
    grad_middle = cotangent.astype(F32) + middle_part
    grad_branch = grad_middle.astype(BF)
    freight, rider = (), ()
    if square:
        grad_att, proj_part, *rest = middle_call(
            ctxs, grad_branch, att_own, proj, out_part.reshape(team, own, D), gate_part
        )
        joined, first_out, gate_sum = rest[:ctxs], rest[ctxs], rest[ctxs + 1]
        rider = (joined[1],)
        freight = (proj_part.reshape(1, planes, ctxs * arows, D),)
    else:
        grad_att = jnp.einsum("td,sfd->stf", grad_branch, proj, preferred_element_type=F32)
        grad_att = lax.all_to_all(
            grad_att.astype(BF), TEAM, split_axis=0, concat_axis=0, tiled=True
        )
        output = (middle_own + team_finish(team_join(out_part, ctxs), ctxs)).astype(BF)
        proj_part = jnp.einsum("tsf,sd->tfd", att_own, grad_branch, preferred_element_type=F32)
        proj_part = proj_part.astype(BF)
        if whole_heads:
            proj_part = core_join(proj_part.reshape(team, planes, arows, D), ctxs)
            proj_part = proj_part.reshape(1, planes, ctxs * arows, D)
        else:
            proj_grad = lax.psum_scatter(
                proj_part.reshape(D, D), ALL, scatter_dimension=0, tiled=True
            ).astype(F32)

    dq, dk, dv, *proj_sum = attend_back_call(
        query,
        key,
        value,
        grad_att.reshape(count, feats),
        log_sums,
        seg_col,
        seg_row,
        tables,
        seq,
        freight,
        rider,
        5,
    )
    pairs = [(dq, qkv[0:feats]), (dk, qkv[feats : 2 * feats]), (dv, qkv[2 * feats :])]
    if square:
        freight = (up_part, jax.ShapeDtypeStruct((3, planes, arows, D), BF))
        dn1, up_sum, *attn_sums = team_sum(ctxs, 4, pairs, "sum_one", freight, normed)
        proj_sum, second_out = proj_sum
        dn1, last_out, proj_sum = lax.optimization_barrier((dn1, joined[2], proj_sum))
        output = middle_own + joined[3].astype(F32) + first_out.astype(F32)
        output = output + second_out.astype(F32) + shifted(last_out, "ctx", 4, 3).astype(F32)
        output = output.astype(BF)
        proj_sum = line_reduce(proj_sum.reshape(ctxs, arows, D), ctxs)
        attn_grad = jnp.stack(attn_sums + [proj_sum], 1)
        mlp_grad = jnp.stack([gate_sum, up_sum, down_sum[0]], 1)
    else:
        (dn1,) = team_sum(ctxs, 4, pairs, "sum_one")
        dqkv = jnp.concatenate([dq, dk, dv], 1)
        qkv_part = mm(dqkv, normed, 0, 0).astype(BF)
        mlp_grad = [plane_reduce([p[0]], planes)[0] for p in (gate_part, up_part, down_part)]
        mlp_grad = jnp.stack(mlp_grad, 1)
        if whole_heads:
            attn_part = qkv_part.reshape(3, planes, arows, D)
            attn_grad = plane_reduce([attn_part[i] for i in range(3)], planes)
            proj_grad = plane_reduce([proj_part[0]], planes)[0].reshape(ctxs, arows, D)
            proj_grad = line_reduce(proj_grad, ctxs)
        else:
            padded = lax.dynamic_update_slice_in_dim(
                jnp.zeros((3, D, D), BF), qkv_part.reshape(3, feats, D), me * feats, 1
            )
            attn_grad = lax.psum_scatter(padded, ALL, scatter_dimension=1, tiled=True)
            attn_grad = attn_grad.astype(F32)
            proj_grad = lax.psum_scatter(
                proj_part.reshape(D, D), ALL, scatter_dimension=0, tiled=True
            ).astype(F32)
        attn_grad = jnp.moveaxis(jnp.concatenate([attn_grad, proj_grad[None]], 0), 0, 1)

    source = tokens.astype(F32)
    source_part, gain_one_grad = norm_back(dn1, source, norm_scale(source), gains[0])
    grad_input = grad_middle + source_part
    gain_part = jnp.stack([gain_one_grad, gain_two_grad], 0).reshape(2, planes, team, gcols)
    gain_part = gain_part.transpose(1, 2, 0, 3)
    gain_part = jnp.pad(gain_part, ((0, 0), (0, 0), (0, 6), (0, 128 - gcols)))
    attn_rate = (
        RATE_FACTOR
        * D ** (-0.5)
        * jnp.array([1.0, 1.0, 1.0, OUTPUT_BOOST], jnp.float32).reshape(1, 4, 1)
    )
    mlp_rate = RATE_FACTOR * jnp.array(
        [D ** (-0.5), D ** (-0.5), FF ** (-0.5)], jnp.float32
    ).reshape(1, 3, 1)
    attn_new = adam_update(attn_weight, attn_first, attn_second, attn_grad, attn_rate, WEIGHT_DECAY)
    mlp_new = adam_update(mlp_weight, mlp_first, mlp_second, mlp_grad, mlp_rate, WEIGHT_DECAY)
    if square:
        gain_part, output, attn_last = lax.optimization_barrier((gain_part, output, attn_new[2]))
        attn_new = (attn_new[0], attn_new[1], attn_last)
    gain_grad = small_sum(planes, ctxs, gain_part)[0:2, 0:gcols]
    gain_new = adam_update(gain_weight, gain_first, gain_second, gain_grad, GAIN_RATE, 0.0)
    return (
        output,
        grad_input,
        attn_new[0],
        attn_new[1][:, :3, :],
        attn_new[1][:, 3, :],
        attn_new[2],
        mlp_new[0],
        mlp_new[1],
        mlp_new[2],
        gain_new[0],
        gain_new[1],
        gain_new[2],
    )


def solution(mesh):
    dp, ctxs = mesh.shape["dp"], mesh.shape["ctx"]
    planes = dp // 2
    inner = Mesh(mesh.devices.reshape(planes, 2, ctxs), ALL)
    rows = P(ALL, None)
    cube = P(ALL, None, None)
    gain = P(None, ALL)

    def step(*args):
        return local(planes, ctxs, *args)

    return jax.shard_map(
        step,
        mesh=inner,
        in_specs=(rows, rows, P(ALL)) + (cube,) * 6 + (gain,) * 3,
        out_specs=(rows, rows, cube, cube, rows) + (cube,) * 4 + (gain,) * 3,
        check_vma=False,
    )
```

```python
import functools

import jax
import jax.numpy as jnp
import numpy as np
from jax import lax
from jax.experimental import pallas as pl
from jax.experimental.pallas import tpu as pltpu
from jax.sharding import Mesh
from jax.sharding import PartitionSpec as P

D = 2048
HEADS = 32
HD = 64
FF = 8192
STEP = 10


NORM_EPS = 1e-05
ROPE_BASE = 130000.0
BETA_ONE = 0.9
BETA_TWO = 0.95
ADAM_EPS = 1e-08
WEIGHT_DECAY = 0.1
RATE_FACTOR = 1.5
GAIN_RATE = 0.6
OUTPUT_BOOST = 12.0
MASKED = -1e30
BF = jnp.bfloat16
F32 = jnp.float32
ALL = ("plane", "core", "ctx")
TEAM = ("core", "ctx")


BLOCK = 256
CHUNKS = 2
VMEM_LIMIT = 60 * 1024 * 1024
MESH_ID = pl.DeviceIdType.MESH


def params(semantics=1, **more):
    return pltpu.CompilerParams(
        dimension_semantics=("arbitrary",) * semantics, vmem_limit_bytes=VMEM_LIMIT, **more
    )


def rope_tables(length):
    halved = HD // 2
    frequency = (ROPE_BASE ** (-(np.arange(halved) * 2.0 / HD))).astype(np.float32)
    angle = np.arange(length, dtype=np.float32)[:, None] * frequency[None, :]
    cosine, sine = np.cos(angle).astype(np.float32), np.sin(angle).astype(np.float32)
    zero = np.zeros_like(sine)
    return (
        jnp.asarray(np.concatenate([cosine] * 4, 1)),
        jnp.asarray(np.concatenate([-sine, zero] * 2, 1)),
        jnp.asarray(np.concatenate([zero, sine] * 2, 1)),
    )


def widen(table, feats):
    return jnp.concatenate([table] * (feats // 128), 1) if feats > 128 else table


def rope(values, cosine, low_sine, high_sine):
    width = values.shape[-1]
    ahead = pltpu.roll(values, width - HD // 2, 1)
    behind = pltpu.roll(values, HD // 2, 1)
    return values * cosine + ahead * low_sine + behind * high_sine


def rope_back(values, cosine, low_sine, high_sine):
    width = values.shape[-1]
    ahead = pltpu.roll(values, width - HD // 2, 1)
    behind = pltpu.roll(values, HD // 2, 1)
    return values * cosine - ahead * low_sine - behind * high_sine


def mm(a, b, ca, cb):
    return lax.dot_general(a, b, (((ca,), (cb,)), ((), ())), preferred_element_type=F32)


def norm_scale(values):
    return lax.rsqrt(jnp.mean(values * values, -1, keepdims=True) + NORM_EPS)


def norm_back(grad_normed, values, scale, gain):
    weighted = grad_normed * gain
    grad_values = scale * (
        weighted - values * scale * scale * jnp.mean(weighted * values, -1, keepdims=True)
    )
    return (grad_values, jnp.sum(grad_normed * values * scale, 0))


def adam_update(master, first, second, grad, rate, decay):
    first_new = BETA_ONE * first + (1.0 - BETA_ONE) * grad
    second_new = BETA_TWO * second + (1.0 - BETA_TWO) * grad * grad
    direction = (
        first_new
        / (1.0 - BETA_ONE**STEP)
        / (jnp.sqrt(second_new / (1.0 - BETA_TWO**STEP)) + ADAM_EPS)
    )
    return (first_new, second_new, master - rate * (direction + decay * master))


def greet_all(peers):
    barrier = pltpu.get_barrier_semaphore()
    for peer in peers:
        pl.semaphore_signal(barrier, inc=1, device_id=peer, device_id_type=MESH_ID)
    pl.semaphore_wait(barrier, len(peers))


def neighbours(planes, ctxs):
    plane, core, ctx = lax.axis_index("plane"), lax.axis_index("core"), lax.axis_index("ctx")
    column = [lax.rem(plane + k, planes) for k in range(1, planes)]
    group = [
        (core if dc == 0 else 1 - core, lax.rem(ctx + dz, ctxs))
        for dc in range(2)
        for dz in range(ctxs)
        if dc + dz > 0
    ]
    return plane, core, ctx, column, group


def gather_kernel(planes, ctxs, lines, boards, inputs, refs):
    ins, outs = refs[:inputs], refs[inputs : inputs + len(lines) + len(boards)]
    line_send, line_recv, side_send, side_recv, board_send, board_recv, pass_send, pass_recv, here = refs[
        inputs + len(lines) + len(boards) :
    ]
    plane, core, ctx = lax.axis_index("plane"), lax.axis_index("core"), lax.axis_index("ctx")
    last = ctxs - 1
    column = [lax.rem(plane + k, planes) for k in range(1, planes)]
    greet_all(
        [(p, core, ctx) for p in column]
        + [(plane, core, lax.rem(ctx + k, ctxs)) for k in range(1, ctxs)]
        + [(plane, 1 - core, ctx)]
    )
    other = (plane, 1 - core, ctx)
    pieces = []
    for source, target, chunks in lines:
        rows = ins[source].shape[0] // chunks
        for chunk in range(chunks):
            pieces.append((ins[source], outs[target], pl.ds(chunk * rows, rows)))

    def remote(source, target, send, recv, peer):
        return pltpu.make_async_remote_copy(
            src_ref=source,
            dst_ref=target,
            send_sem=send,
            recv_sem=recv,
            device_id=peer,
            device_id_type=MESH_ID,
        )

    def line(index, way, hop, block, peer_ctx, own):
        value, out, rows = pieces[index]
        slot = out.at[core * ctxs + block, rows]
        return remote(
            value.at[rows] if own else slot,
            slot,
            line_send.at[index, way, hop],
            line_recv.at[index, way, hop],
            (plane, core, peer_ctx),
        )

    def side(index, order, side_core, block, own):
        value, out, rows = pieces[index]
        slot = out.at[side_core * ctxs + block, rows]
        return remote(
            value.at[rows] if own else slot,
            slot,
            side_send.at[index, order],
            side_recv.at[index, order],
            other,
        )

    square = planes == 4
    near_x = plane + 1 - 2 * lax.rem(plane, 2)
    near_y = lax.rem(plane + 2, 4)
    far = 3 - plane

    def board_refs(index, home, half=None, own=True):
        kind, source, target = boards[index]
        value, out = source(ins, outs), outs[target]
        if kind in ("block", "late"):
            size = value.shape[0]
            part = pl.ds(0, size) if half is None else pl.ds(half * (size // 2), size // 2)
            slot = out.at[home, part]
            return (value.at[part] if own else slot), slot
        if kind == "slots":
            size = value.shape[1]
            part = pl.ds(0, size) if half is None else pl.ds(half * (size // 2), size // 2)
            slot = out.at[:, home, part]
            return (value.at[:, part] if own else slot), slot
        size = ctxs if half is None else ctxs // 2
        part = pl.ds(core * ctxs + (0 if half is None else half * size), size)
        slot = out.at[part, home]
        return (value.at[part] if own else slot), slot

    def board(index, k, home, peer):
        value, slot = board_refs(index, home)
        return remote(
            value, slot, board_send.at[index, k], board_recv.at[index, k], (peer, core, ctx)
        )

    sent = [(plane, 0, near_x), (plane, 1, near_x), (plane, 0, near_y), (plane, 1, near_y)]
    sent += [(near_y, 0, near_x), (near_x, 1, near_y)]
    landed = [near_x, near_x, near_y, near_y, far, far]

    def relay(index, k, arriving=False):
        home, half, peer = sent[k]
        value, slot = board_refs(index, landed[k] if arriving else home, half, k < 4)
        return remote(
            value, slot, board_send.at[index, k], board_recv.at[index, k], (peer, core, ctx)
        )

    def relayed(index):
        return square and boards[index][0] != "late"

    def board_start(index):
        if relayed(index):
            for k in (1, 2, 0, 3):
                relay(index, k).start()
            return
        for k, peer in enumerate(column):
            board(index, k, plane, peer).start()

    def board_pass(index):
        if relayed(index):
            relay(index, 2, True).wait_recv()
            relay(index, 4).start()
            relay(index, 1, True).wait_recv()
            relay(index, 5).start()

    def sources(index):
        if relayed(index):
            return [near_x, near_y, far]
        return [lax.rem(plane + planes - 1 - k, planes) for k in range(planes - 1)]

    def share(index, k, home):
        _, slot = board_refs(index, home)
        return remote(slot, slot, pass_send.at[index, k], pass_recv.at[index, k], other)

    def board_finish(index):
        if relayed(index):
            for k in (0, 3, 4, 5):
                relay(index, k, True).wait_recv()
        for k, home in enumerate(sources(index)):
            if not relayed(index):
                board(index, k, home, home).wait_recv()
            if boards[index][0] == "half":
                share(index, k, home).start()

    def board_close(index):
        if relayed(index):
            for k in range(6):
                relay(index, k).wait_send()
        else:
            for k, peer in enumerate(column):
                board(index, k, plane, peer).wait_send()
        if boards[index][0] == "half":
            out = outs[boards[index][2]]
            for k, home in enumerate(sources(index)):
                share(index, k, home).wait_send()
                slot = out.at[pl.ds((1 - core) * ctxs, ctxs), home]
                remote(
                    slot, slot, pass_send.at[index, k], pass_recv.at[index, k], other
                ).wait_recv()

    count = len(pieces)
    late = [i for i in range(len(boards)) if boards[i][0] == "late"]
    early = [i for i in range(len(boards)) if boards[i][0] != "late"]
    board_start(early[0]) if early else None

    @pl.when(ctx < last)
    def _():
        for i in range(count):
            line(i, 0, 1, ctx, ctx + 1, True).start()

    @pl.when(ctx > 0)
    def _():
        for i in range(count):
            line(i, 1, 1, ctx, ctx - 1, True).start()

    for i in range(count):
        side(i, 0, core, ctx, True).start()
    copies = []
    for i, (value, out, rows) in enumerate(pieces):
        copies.append(
            pltpu.make_async_copy(value.at[rows], out.at[core * ctxs + ctx, rows], here.at[i])
        )
    for i in early:
        kind, source, target = boards[i]
        slot = outs[target].at[plane] if kind == "block" else outs[target].at[:, plane]
        copies.append(pltpu.make_async_copy(source(ins, outs), slot, here.at[count + i]))
    for copy in copies:
        copy.start()

    passed = 0
    board_pass(early[0])
    if len(early) > 1:
        board_start(early[1])
    for hop in range(1, ctxs):

        @pl.when(ctx >= hop)
        def _():
            block = ctx - hop
            for i in range(count):
                line(i, 0, hop, block, ctx - 1, False).wait_recv()

                @pl.when(ctx < last)
                def _():
                    line(i, 0, hop + 1, block, ctx + 1, False).start()

                side(i, hop, core, block, False).start()

        @pl.when(ctx + hop <= last)
        def _():
            block = ctx + hop
            for i in range(count):
                line(i, 1, hop, block, ctx + 1, False).wait_recv()

                @pl.when(ctx > 0)
                def _():
                    line(i, 1, hop + 1, block, ctx - 1, False).start()

                side(i, last + hop, core, block, False).start()

        if passed + 1 < len(early):
            passed += 1
            board_pass(early[passed])
            if passed + 1 < len(early):
                board_start(early[passed + 1])
    for i in early:
        board_finish(i)

    for i in range(count):
        side(i, 0, 1 - core, ctx, False).wait_recv()
    for hop in range(1, ctxs):

        @pl.when(ctx >= hop)
        def _():
            for i in range(count):
                side(i, hop, 1 - core, ctx - hop, False).wait_recv()

        @pl.when(ctx + hop <= last)
        def _():
            for i in range(count):
                side(i, last + hop, 1 - core, ctx + hop, False).wait_recv()

    for copy in copies:
        copy.wait()
    for i in late:
        board_start(i)
        kind, source, target = boards[i]
        copy = pltpu.make_async_copy(source(ins, outs), outs[target].at[plane], here.at[count + i])
        copy.start()
        copy.wait()
    for i in late:
        board_finish(i)

    for i in range(len(boards)):
        board_close(i)
    for i in range(count):
        side(i, 0, core, ctx, True).wait_send()
    for hop in range(1, ctxs):

        @pl.when(ctx >= hop)
        def _():
            for i in range(count):
                side(i, hop, core, ctx - hop, False).wait_send()

        @pl.when(ctx + hop <= last)
        def _():
            for i in range(count):
                side(i, last + hop, core, ctx + hop, False).wait_send()

        @pl.when((ctx < last) & (ctx >= hop - 1))
        def _():
            for i in range(count):
                line(i, 0, hop, ctx - hop + 1, ctx + 1, False).wait_send()

        @pl.when((ctx > 0) & (ctx + hop - 1 <= last))
        def _():
            for i in range(count):
                line(i, 1, hop, ctx + hop - 1, ctx - 1, False).wait_send()


def gather_call(planes, ctxs, number, inputs, lines, boards, shapes, name):
    pieces = sum(chunks for _, _, chunks in lines)
    dma = pltpu.SemaphoreType.DMA

    def kernel(*refs):
        gather_kernel(planes, ctxs, lines, boards, len(inputs), refs)

    return pl.pallas_call(
        kernel,
        out_shape=tuple(jax.ShapeDtypeStruct(shape, dtype) for shape, dtype in shapes),
        in_specs=[pl.BlockSpec(memory_space=pl.ANY)] * len(inputs),
        out_specs=tuple(pl.BlockSpec(memory_space=pl.ANY) for _ in shapes),
        scratch_shapes=[
            dma((pieces, 2, ctxs + 1)),
            dma((pieces, 2, ctxs + 1)),
            dma((pieces, 2 * ctxs)),
            dma((pieces, 2 * ctxs)),
            dma((len(boards), max(planes, 6))),
            dma((len(boards), max(planes, 6))),
            dma((len(boards), planes)),
            dma((len(boards), planes)),
            dma((pieces + len(boards),)),
        ],
        compiler_params=pltpu.CompilerParams(collective_id=number, has_side_effects=True),
        name=name,
    )(*inputs)


def small_sum_kernel(planes, ctxs, value_ref, out_ref, got_one, middle, got_two, sems):
    plane, core, ctx, column, group = neighbours(planes, ctxs)
    greet_all([(p, core, ctx) for p in column] + [(plane, c, z) for c, z in group])

    def hop(index, source, target, peer):
        return pltpu.make_async_remote_copy(
            src_ref=source,
            dst_ref=target,
            send_sem=sems.at[0, index],
            recv_sem=sems.at[1, index],
            device_id=peer,
            device_id_type=MESH_ID,
        )

    first = [
        hop(i, value_ref.at[p], got_one.at[i], (p, core, ctx)) for i, p in enumerate(column)
    ]
    for copy in first:
        copy.start()
    total = value_ref[plane]
    for i, copy in enumerate(first):
        copy.wait_recv()
        total = total + got_one[i]
    middle[...] = total
    base = len(column)
    second = [
        hop(base + i, middle.at[c * ctxs + z], got_two.at[i], (plane, c, z))
        for i, (c, z) in enumerate(group)
    ]
    for copy in second:
        copy.start()
    total = middle[core * ctxs + ctx]
    for i, copy in enumerate(second):
        copy.wait_recv()
        total = total + got_two[i]
    out_ref[...] = total
    for copy in first + second:
        copy.wait_send()


def small_sum(planes, ctxs, value):
    hops = planes + 2 * ctxs - 2
    tile = value.shape[2:]
    return pl.pallas_call(
        functools.partial(small_sum_kernel, planes, ctxs),
        out_shape=jax.ShapeDtypeStruct(tile, F32),
        in_specs=[pl.BlockSpec(memory_space=pltpu.VMEM)],
        out_specs=pl.BlockSpec(memory_space=pltpu.VMEM),
        scratch_shapes=[
            pltpu.VMEM((planes - 1, 2 * ctxs) + tile, F32),
            pltpu.VMEM((2 * ctxs,) + tile, F32),
            pltpu.VMEM((2 * ctxs - 1,) + tile, F32),
            pltpu.SemaphoreType.DMA((2, hops)),
        ],
        compiler_params=pltpu.CompilerParams(collective_id=1, has_side_effects=True),
        name="small_sum",
    )(value)


class Gather:
    def __init__(self, ctxs, pieces, boards, sems):
        self.ctxs, self.pieces, self.boards = ctxs, pieces, boards
        self.line_sem, self.side_sem, self.board_sem, self.pass_sem = sems
        self.plane, self.core, self.ctx = (
            lax.axis_index("plane"),
            lax.axis_index("core"),
            lax.axis_index("ctx"),
        )
        self.last = ctxs - 1
        self.near_x = self.plane + 1 - 2 * lax.rem(self.plane, 2)
        self.near_y = lax.rem(self.plane + 2, 4)
        self.far = 3 - self.plane

    @staticmethod
    def scratch(ctxs, pieces, boards):
        dma = pltpu.SemaphoreType.DMA
        return [
            dma((2, pieces, 2, ctxs + 1)),
            dma((2, pieces, 2 * ctxs)),
            dma((2, boards, 6)),
            dma((2, boards, 3)),
        ]

    def peers(self):
        plane, core, ctx, ctxs = self.plane, self.core, self.ctx, self.ctxs
        return (
            [(plane, core, lax.rem(ctx + k, ctxs)) for k in range(1, ctxs)]
            + [(plane, 1 - core, ctx)]
            + [(near, core, ctx) for near in (self.near_x, self.near_y)]
        )

    def remote(self, slot, sem, index, peer):
        return pltpu.make_async_remote_copy(
            src_ref=slot,
            dst_ref=slot,
            send_sem=sem.at[(0,) + index],
            recv_sem=sem.at[(1,) + index],
            device_id=peer,
            device_id_type=MESH_ID,
        )

    def line(self, i, way, hop, block):
        buffer, rows = self.pieces[i]
        slot = buffer.at[self.core * self.ctxs + block, rows]
        away = 1 if way == 0 else self.ctxs - 1
        peer = (self.plane, self.core, lax.rem(self.ctx + away, self.ctxs))
        return self.remote(slot, self.line_sem, (i, way, hop), peer)

    def side(self, i, order, core, block):
        buffer, rows = self.pieces[i]
        slot = buffer.at[core * self.ctxs + block, rows]
        return self.remote(slot, self.side_sem, (i, order), (self.plane, 1 - self.core, self.ctx))

    def send_own(self, items):
        @pl.when(self.ctx < self.last)
        def _():
            for i in items:
                self.line(i, 0, 1, self.ctx).start()

        @pl.when(self.ctx > 0)
        def _():
            for i in items:
                self.line(i, 1, 1, self.ctx).start()

        for i in items:
            self.side(i, 0, self.core, self.ctx).start()

    def hop(self, k, items):
        ctx, last = self.ctx, self.last

        for i in items:

            @pl.when(ctx >= k)
            def _():
                self.line(i, 0, k, ctx - k).wait_recv()

                @pl.when(ctx < last)
                def _():
                    self.line(i, 0, k + 1, ctx - k).start()

                self.side(i, k, self.core, ctx - k).start()

            @pl.when(ctx + k <= last)
            def _():
                self.line(i, 1, k, ctx + k).wait_recv()

                @pl.when(ctx > 0)
                def _():
                    self.line(i, 1, k + 1, ctx + k).start()

                self.side(i, last + k, self.core, ctx + k).start()

    def side_arrive(self, k, items):
        ctx, last = self.ctx, self.last
        if k == 0:
            for i in items:
                self.side(i, 0, 1 - self.core, ctx).wait_recv()
            return

        @pl.when(ctx >= k)
        def _():
            for i in items:
                self.side(i, k, 1 - self.core, ctx - k).wait_recv()

        @pl.when(ctx + k <= last)
        def _():
            for i in items:
                self.side(i, last + k, 1 - self.core, ctx + k).wait_recv()

    def distant(self, k, action):
        ctx, last = self.ctx, self.last
        behind = (ctx >= k).astype(jnp.int32)
        ahead = (ctx + k <= last).astype(jnp.int32)

        def body(i, carry):
            action(jnp.where((behind == 1) & (i == 0), ctx - k, ctx + k))
            return carry

        lax.fori_loop(0, behind + ahead, body, 0)

    def board_slot(self, index, home, half):
        kind, buffer = self.boards[index]
        if kind == "block":
            size = buffer.shape[1] // 2
            return buffer.at[home, pl.ds(half * size, size)]
        if kind == "slots":
            size = buffer.shape[2] // 2
            return buffer.at[:, home, pl.ds(half * size, size)]
        size = self.ctxs // 2
        return buffer.at[pl.ds(self.core * self.ctxs + half * size, size), home]

    def relay(self, index, k, arriving=False):
        plane, near_x, near_y, far = self.plane, self.near_x, self.near_y, self.far
        sent = [(plane, 0, near_x), (plane, 1, near_x), (plane, 0, near_y), (plane, 1, near_y)]
        home, half, peer = (sent + [(near_y, 0, near_x), (near_x, 1, near_y)])[k]
        if arriving:
            home = [near_x, near_x, near_y, near_y, far, far][k]
        slot = self.board_slot(index, home, half)
        return self.remote(slot, self.board_sem, (index, k), (peer, self.core, self.ctx))

    def board_start(self, index):
        for k in (1, 2, 0, 3):
            self.relay(index, k).start()

    def board_pass(self, index):
        self.relay(index, 2, True).wait_recv()
        self.relay(index, 4).start()
        self.relay(index, 1, True).wait_recv()
        self.relay(index, 5).start()

    def share(self, index, k, core):
        buffer = self.boards[index][1]
        home = [self.near_x, self.near_y, self.far][k]
        slot = buffer.at[pl.ds(core * self.ctxs, self.ctxs), home]
        return self.remote(
            slot, self.pass_sem, (index, k), (self.plane, 1 - self.core, self.ctx)
        )

    def board_finish(self, index):
        for k in (0, 3, 4, 5):
            self.relay(index, k, True).wait_recv()
        if self.boards[index][0] == "half":
            for k in range(3):
                self.share(index, k, self.core).start()

    def board_shared(self, index):
        for k in range(3):
            self.share(index, k, 1 - self.core).wait_recv()

    def close(self):
        ctx, last = self.ctx, self.last
        items = range(len(self.pieces))
        for index in range(len(self.boards)):
            for k in range(6):
                self.relay(index, k).wait_send()
            if self.boards[index][0] == "half":
                for k in range(3):
                    self.share(index, k, self.core).wait_send()
        for i in items:
            self.side(i, 0, self.core, ctx).wait_send()
        for k in range(1, self.ctxs):

            @pl.when(ctx >= k)
            def _():
                for i in items:
                    self.side(i, k, self.core, ctx - k).wait_send()

            @pl.when(ctx + k <= last)
            def _():
                for i in items:
                    self.side(i, last + k, self.core, ctx + k).wait_send()

            @pl.when((ctx < last) & (ctx >= k - 1))
            def _():
                for i in items:
                    self.line(i, 0, k, ctx - k + 1).wait_send()

            @pl.when((ctx > 0) & (ctx + k - 1 <= last))
            def _():
                for i in items:
                    self.line(i, 1, k, ctx + k - 1).wait_send()


def front_kernel(ctxs, refs):
    tokens, qkv, mlp, packed, c_ref, a_ref, b_ref = refs[:7]
    x_out, n_out, q_out, k_out, v_out, w_out, g_out, small = refs[7:15]
    xs, ns, qs, ks, vs, ws, gs, wide, load, store, small_sem = refs[15:26]
    own = tokens.shape[0]
    half = own // 2
    pieces = [(xs, pl.ds(0, half)), (xs, pl.ds(half, half))]
    boards = [("slots", ws), ("block", gs)]
    net = Gather(ctxs, pieces, boards, refs[26:])
    plane, core, ctx = net.plane, net.core, net.ctx
    me = core * ctxs + ctx
    loads = [
        pltpu.make_async_copy(qkv, ws.at[:, plane], load.at[0]),
        pltpu.make_async_copy(tokens, xs.at[me], load.at[1]),
        pltpu.make_async_copy(mlp.at[0], wide, load.at[2]),
    ]
    for copy in loads:
        copy.start()
    others = [
        (core if dc == 0 else 1 - core, lax.rem(ctx + dz, ctxs))
        for dc in range(2)
        for dz in range(ctxs)
        if dc + dz > 0
    ]
    column = [lax.rem(plane + k, 4) for k in range(1, 4)]
    greet_all([(plane, c, z) for c, z in others] + [(p, core, ctx) for p in column])

    def tiny(index, source, target, peer):
        return pltpu.make_async_remote_copy(
            src_ref=source,
            dst_ref=target,
            send_sem=small_sem.at[0, index],
            recv_sem=small_sem.at[1, index],
            device_id=peer,
            device_id_type=MESH_ID,
        )

    small[plane, me] = packed[...]
    one = [
        tiny(i, packed, small.at[plane, me], (plane, c, z)) for i, (c, z) in enumerate(others)
    ]
    for copy in one:
        copy.start()
    for copy in loads[:2]:
        copy.wait()
    net.board_start(0)
    net.send_own([0, 1])
    i = 0
    for dc in range(2):
        for dz in range(ctxs):
            if dc + dz > 0:
                c, z = core if dc == 0 else 1 - core, lax.rem(ctx + ctxs - dz, ctxs)
                tiny(i, packed, small.at[plane, c * ctxs + z], (plane, c, z)).wait_recv()
                i += 1
    two = [
        tiny(i + k, small.at[plane], small.at[plane], (p, core, ctx))
        for k, p in enumerate(column)
    ]
    for copy in two:
        copy.start()
    loads[2].wait()

    def narrow(g, carry):
        part = pl.ds(pl.multiple_of(g * 16, 16), 16)
        gs[plane, part, :] = wide[part, :].astype(BF)
        return carry

    lax.fori_loop(0, wide.shape[0] // 16, narrow, 0)
    net.board_pass(0)
    net.board_start(1)
    for k in range(3):
        home = lax.rem(plane + 3 - k, 4)
        tiny(i + k, small.at[plane], small.at[home], (home, core, ctx)).wait_recv()
    tiles = [
        small[p, 2 * j][0:1] + small[p, 2 * j + 1][0:1] for p in range(4) for j in range(ctxs)
    ]
    gain = jnp.concatenate(tiles, 1)
    feats = q_out.shape[-1]
    stores = []

    blocks = [(xs, x_out), (ns, n_out), (qs, q_out), (ks, k_out), (vs, v_out)]

    def put(source, target, index):
        return pltpu.make_async_copy(source, target, store.at[index])

    def compute(side_core):
        def action(block):
            b = side_core * ctxs + block
            values = xs[b].astype(F32)
            normed = (values * norm_scale(values) * gain).astype(BF)
            ns[b] = normed
            rows = pl.ds(pl.multiple_of(block * own, own), own)
            cosine, low_sine, high_sine = [
                widen(ref[rows, :], feats) for ref in (c_ref, a_ref, b_ref)
            ]
            q = mm(normed, ws[0].reshape(feats, D), 1, 1)
            qs[b] = rope(q, cosine, low_sine, high_sine).astype(BF)
            k = mm(normed, ws[1].reshape(feats, D), 1, 1)
            ks[b] = rope(k, cosine, low_sine, high_sine).astype(BF)
            vs[b] = mm(normed, ws[2].reshape(feats, D), 1, 1).astype(BF)
            for i, (source, target) in enumerate(blocks):
                put(source.at[b], target.at[b], 5 * b + i).start()

        return action

    base = 10 * ctxs
    parts = [0, 1]
    stores = [put(s, t, base + i) for i, (s, t) in enumerate([(ws, w_out), (gs, g_out)])]
    net.hop(1, parts)
    net.board_finish(0)
    stores[0].start()
    compute(core)(ctx)
    net.side_arrive(0, parts)
    compute(1 - core)(ctx)
    net.board_pass(1)
    for k in range(1, ctxs):
        net.distant(k, compute(core))
        if k + 1 < ctxs:
            net.hop(k + 1, parts)
        net.side_arrive(k, parts)
        net.distant(k, compute(1 - core))
        if k == min(2, ctxs - 1):
            net.board_finish(1)
            stores[1].start()
    net.close()
    for copy in one + two:
        copy.wait_send()
    for copy in stores:
        copy.wait()
    for b in range(2 * ctxs):
        for i, (source, target) in enumerate(blocks):
            put(source.at[b], target.at[b], 5 * b + i).wait()


def front_call(ctxs, tokens, qkv, mlp, packed, tables):
    team = 2 * ctxs
    own, arows, frows = tokens.shape[0], qkv.shape[1], mlp.shape[1]
    feats = 4 * arows
    block, part = (team, own, D), (team, own, feats)
    shapes = [block, block, part, part, part, (3, 4, arows, D)]
    shapes += [(4, frows, D)]
    dma = pltpu.SemaphoreType.DMA
    hbm, vmem = pl.BlockSpec(memory_space=pl.ANY), pl.BlockSpec(memory_space=pltpu.VMEM)

    def kernel(*refs):
        front_kernel(ctxs, refs)

    return pl.pallas_call(
        kernel,
        out_shape=[jax.ShapeDtypeStruct(shape, BF) for shape in shapes]
        + [jax.ShapeDtypeStruct((4, team, 8, 128), F32)],
        in_specs=[hbm] * 3 + [vmem] * 4,
        out_specs=[hbm] * len(shapes) + [vmem],
        scratch_shapes=[pltpu.VMEM(shape, BF) for shape in shapes]
        + [pltpu.VMEM((frows, D), F32)]
        + [dma((3,)), dma((5 * team + 2,)), dma((2, team + 2))]
        + Gather.scratch(ctxs, 2, 2),
        compiler_params=pltpu.CompilerParams(
            collective_id=0, has_side_effects=True, vmem_limit_bytes=VMEM_LIMIT
        ),
        cost_estimate=pl.CostEstimate(
            flops=6 * team * own * D * feats, bytes_accessed=40 * own * D, transcendentals=0
        ),
        name="front",
    )(tokens, qkv, mlp, packed, *tables)


def attend_part(
    q_ref, k_ref, v_ref, col_ref, row_ref, l_ref, put, start, begin, end, pair, unit
):
    lanes = pl.ds(pl.multiple_of(pair * 128, 128), 128)
    for first in range(begin, end, BLOCK):
        keys = first + BLOCK
        rows = pl.ds(pl.multiple_of(start + first, BLOCK), BLOCK)
        past = pl.ds(pl.multiple_of(start, BLOCK), keys)
        same = col_ref[rows, :] == row_ref[:, 0:keys]
        query_place = first + lax.broadcasted_iota(jnp.int32, (BLOCK, keys), 0)
        key_place = lax.broadcasted_iota(jnp.int32, (BLOCK, keys), 1)
        allowed = same & (key_place <= query_place)
        query, key, value = q_ref[rows, lanes], k_ref[past, lanes], v_ref[past, lanes]
        parts = []
        for head in range(128 // HD):
            cut = slice(head * HD, (head + 1) * HD)
            scores = mm(query[:, cut] * HD ** (-0.5), key[:, cut], 1, 1)
            scores = jnp.where(allowed, scores, MASKED)
            highest = jnp.max(scores, -1, keepdims=True)
            shifted = jnp.exp(scores - highest)
            totals = jnp.sum(shifted, -1, keepdims=True)
            weights = (shifted * (1.0 / totals)).astype(BF)
            parts.append(mm(weights, value[:, cut], 1, 0))
            l_ref[unit + head, first:keys, :] = highest + jnp.log(totals)
        put(rows, lanes, jnp.concatenate(parts, 1).astype(BF))


def second_kernel(ctxs, refs):
    q_ref, k_ref, v_ref, col_ref, row_ref, proj, mlp = refs[:7]
    o_out, p_out, d_out, l_ref = refs[7:11]
    outs, ps, ds_, wide, load, store = refs[11:17]
    count, feats = q_ref.shape
    seq = count // 2
    pairs = feats // 128
    plane = lax.axis_index("plane")
    half = seq // 2
    pieces = [(outs, pl.ds(i * half, half)) for i in range(4)] + [(ps, plane)]
    parts, rows_piece = [0, 1, 2, 3], [4]
    net = Gather(ctxs, pieces, [("block", ds_), ("half", ps)], refs[17:])
    core, ctx = net.core, net.ctx
    me = core * ctxs + ctx
    loads = [
        pltpu.make_async_copy(proj, ps.at[me, plane], load.at[0]),
        pltpu.make_async_copy(mlp.at[1], wide, load.at[1]),
    ]
    for copy in loads:
        copy.start()
    greet_all(net.peers())
    loads[0].wait()
    net.send_own(rows_piece)
    loads[1].wait()

    def narrow(g, carry):
        part = pl.ds(pl.multiple_of(g * 16, 16), 16)
        ds_[plane, part, :] = wide[part, :].astype(BF)
        return carry

    lax.fori_loop(0, wide.shape[0] // 16, narrow, 0)
    net.board_start(0)

    def put(rows, lanes, values):
        outs[me, rows, lanes] = values

    hops = list(range(1, ctxs))
    for part in parts:
        s, begin = part // 2, (part % 2) * half
        for pair in range(pairs):
            attend_part(
                q_ref, k_ref, v_ref, col_ref, row_ref.at[s], l_ref, put,
                s * seq, begin, begin + half, pair, (s * pairs + pair) * (128 // HD),
            )
        net.send_own([part])
        if hops:
            net.hop(hops.pop(0), rows_piece)
            if not hops:
                net.board_start(1)
        if part == 1:
            net.board_pass(0)
    for k in hops:
        net.hop(k, rows_piece)
    if hops:
        net.board_start(1)

    def copy_out(b):
        return pltpu.make_async_copy(outs.at[b], o_out.at[b], store.at[b])

    copy_out(me).start()
    for k in range(1, ctxs):
        net.hop(k, parts[:2])
        if k == 2 or ctxs == 2:
            net.board_pass(1)
        net.hop(k, parts[2:])
        net.distant(k, lambda block: copy_out(core * ctxs + block).start())
        net.side_arrive(k - 1, parts)
        if k == 1:
            copy_out((1 - core) * ctxs + ctx).start()
            net.board_finish(0)
        else:
            net.distant(k - 1, lambda block: copy_out((1 - core) * ctxs + block).start())
    tail = [
        pltpu.make_async_copy(ds_, d_out, store.at[2 * ctxs]),
        pltpu.make_async_copy(ps, p_out, store.at[2 * ctxs + 1]),
    ]
    tail[0].start()
    for k in range(ctxs):
        net.side_arrive(k, rows_piece)
    net.board_finish(1)
    net.board_shared(1)
    tail[1].start()
    net.side_arrive(ctxs - 1, parts)
    net.distant(ctxs - 1, lambda block: copy_out((1 - core) * ctxs + block).start())
    net.close()
    for copy in tail:
        copy.wait()
    for b in range(2 * ctxs):
        copy_out(b).wait()


def second_call(ctxs, query, key, value, col, row, proj, mlp):
    team = 2 * ctxs
    count, feats = query.shape
    seq = count // 2
    arows, frows = proj.shape[0], mlp.shape[1]
    shapes = [(team, count, feats), (team, 4, arows, D), (4, frows, D)]
    dma = pltpu.SemaphoreType.DMA
    hbm, vmem = pl.BlockSpec(memory_space=pl.ANY), pl.BlockSpec(memory_space=pltpu.VMEM)

    def kernel(*refs):
        second_kernel(ctxs, refs)

    return pl.pallas_call(
        kernel,
        out_shape=[jax.ShapeDtypeStruct(shape, BF) for shape in shapes]
        + [jax.ShapeDtypeStruct((2 * feats // HD, seq, 1), F32)],
        in_specs=[vmem] * 5 + [hbm] * 2,
        out_specs=[hbm] * 3 + [vmem],
        scratch_shapes=[pltpu.VMEM(shape, BF) for shape in shapes]
        + [pltpu.VMEM((frows, D), F32)]
        + [dma((2,)), dma((team + 2,))]
        + Gather.scratch(ctxs, 5, 2),
        compiler_params=pltpu.CompilerParams(
            collective_id=2, has_side_effects=True, vmem_limit_bytes=VMEM_LIMIT
        ),
        cost_estimate=pl.CostEstimate(
            flops=4 * count * seq * feats, bytes_accessed=24 * count * feats, transcendentals=0
        ),
        name="second",
    )(query, key, value, col, row, proj, mlp)


def third_kernel(ctxs, refs):
    att, proj, x_all, gain, gate, up, mlp, dy = refs[:8]
    m_out, a_out, n_out, o_out, g_out, u_out, d_out = refs[8:15]
    pv, gv, uv, dv, ys, hs, gs, us, ob, xb, nb, sb, narrowed = refs[15:28]
    load, block_sem, store, late = refs[28:32]
    team, own = ys.shape[0], ys.shape[1]
    wide = gv.shape[0]
    pieces = [(ys, pl.ds(0, own // 2)), (ys, pl.ds(own // 2, own // 2))]
    net = Gather(ctxs, pieces, [("block", dv)], refs[32:])
    plane, core, ctx = net.plane, net.core, net.ctx
    me = core * ctxs + ctx
    loads = [
        pltpu.make_async_copy(dy, ys.at[me], load.at[0]),
        pltpu.make_async_copy(mlp.at[2], narrowed, load.at[1]),
        pltpu.make_async_copy(proj, pv, load.at[2]),
        pltpu.make_async_copy(gate, gv, load.at[3]),
        pltpu.make_async_copy(up, uv, load.at[4]),
    ]

    def fetch(i):
        slot = lax.rem(i, 2)
        rows = pl.ds(pl.multiple_of(i * own, own), own)
        size = att.shape[2]
        copies = [
            pltpu.make_async_copy(
                att.at[t, rows], ob.at[slot, :, pl.ds(t * size, size)], block_sem.at[t, slot]
            )
            for t in range(team)
        ]
        return copies + [pltpu.make_async_copy(x_all.at[i], xb.at[slot], block_sem.at[team, slot])]

    def n_store(i):
        return pltpu.make_async_copy(nb.at[lax.rem(i, 2)], n_out.at[i], store.at[0, lax.rem(i, 2)])

    def s_store(i, out):
        return pltpu.make_async_copy(sb.at[lax.rem(i, 2)], out.at[i], store.at[1, lax.rem(i, 2)])

    for copy in loads:
        copy.start()
    for copy in fetch(0):
        copy.start()
    greet_all(net.peers())
    loads[0].wait()
    net.send_own([0, 1])
    loads[1].wait()

    def narrow(g, carry):
        part = pl.ds(pl.multiple_of(g * 16, 16), 16)
        dv[plane, part, :] = narrowed[part, :].astype(BF)
        return carry

    lax.fori_loop(0, narrowed.shape[0] // 16, narrow, 0)
    net.board_start(0)
    for copy in loads[2:]:
        copy.wait()

    steps = [(hop, chunk) for hop in range(1, ctxs) for chunk in range(2)]
    stages = []
    for i, step in enumerate(steps[: 2 * (ctxs - 2)] if ctxs > 2 else []):
        stages.append((min(2 * i + 1, team - 1), step))

    def forward(i, carry):
        slot = lax.rem(i, 2)
        for copy in fetch(i):
            copy.wait()

        @pl.when(i + 1 < team)
        def _():
            for copy in fetch(i + 1):
                copy.start()

        total = xb[slot].astype(F32)
        total = total + mm(ob[slot], pv[...].reshape(ob.shape[2], D), 1, 0)

        @pl.when(i >= 2)
        def _():
            n_store(i - 2).wait()

        nb[slot] = (total * norm_scale(total) * gain[...]).astype(BF)
        n_store(i).start()

        @pl.when(i == me)
        def _():
            m_out[...] = total
            keep = pltpu.make_async_copy(ob.at[slot], a_out, late.at[0])
            keep.start()
            keep.wait()

        normed = nb[slot]
        for first in range(0, wide, 512):
            part = slice(first, first + 512)
            g = mm(normed, gv[part, :], 1, 1)
            u = mm(normed, uv[part, :], 1, 1)
            sig = 1.0 / (1.0 + jnp.exp(-g))
            lit = g * sig
            hs[i, :, part] = (lit * u).astype(BF)
            gs[i, :, part] = (u * sig * (1.0 + g * (1.0 - sig))).astype(BF)
            us[i, :, part] = lit.astype(BF)
        for at, (hop, chunk) in stages:

            @pl.when(i == at)
            def _():
                net.hop(hop, [chunk])

        @pl.when(i == 1)
        def _():
            net.board_pass(0)

        return carry

    lax.fori_loop(0, team, forward, 0)
    n_store(team - 2).wait()
    n_store(team - 1).wait()
    net.board_finish(0)

    def pair_store(i, out):
        return pltpu.make_async_copy(sb, out.at[pl.ds(2 * i, 2)], store.at[1, 0])

    def outward(i, carry):
        both = hs[pl.ds(2 * i, 2)].reshape(2 * own, wide)
        result = mm(both, dv[...].reshape(wide, D), 1, 0).astype(BF)

        @pl.when(i >= 1)
        def _():
            pair_store(i - 1, o_out).wait()

        sb[...] = result.reshape(2, own, D)
        pair_store(i, o_out).start()
        return carry

    def backward(side_core):
        def action(block):
            b = side_core * ctxs + block
            for p in range(4):
                cols = slice(p * (wide // 4), (p + 1) * (wide // 4))
                dh = mm(ys[b], dv[p], 1, 1)
                gs[b, :, cols] = (dh * gs[b, :, cols].astype(F32)).astype(BF)
                us[b, :, cols] = (dh * us[b, :, cols].astype(F32)).astype(BF)
            pltpu.make_async_copy(gs.at[b], g_out.at[b], late.at[1 + b]).start()
            pltpu.make_async_copy(us.at[b], u_out.at[b], late.at[1 + team + b]).start()

        return action

    backward(core)(ctx)
    net.side_arrive(0, [0, 1])
    backward(1 - core)(ctx)
    for k in range(1, ctxs - 1):
        if k == ctxs - 2:
            net.hop(ctxs - 1, [0])
        net.distant(k, backward(core))
        net.side_arrive(k, [0, 1])
        net.distant(k, backward(1 - core))
    lax.fori_loop(0, team // 2, outward, 0)
    pair_store(team // 2 - 1, o_out).wait()
    net.hop(ctxs - 1, [1])
    net.distant(ctxs - 1, backward(core))
    net.side_arrive(ctxs - 1, [0, 1])
    net.distant(ctxs - 1, backward(1 - core))
    for p in range(4):
        if p >= 2:
            s_store(p - 2, d_out).wait()
        hidden = hs[:, :, p * (wide // 4) : (p + 1) * (wide // 4)].reshape(team * own, wide // 4)
        sb[p % 2] = mm(hidden, ys[...].reshape(team * own, D), 0, 0).astype(BF)
        s_store(p, d_out).start()
    s_store(2, d_out).wait()
    s_store(3, d_out).wait()
    net.close()
    for b in range(team):
        pltpu.make_async_copy(gs.at[b], g_out.at[b], late.at[1 + b]).wait()
        pltpu.make_async_copy(us.at[b], u_out.at[b], late.at[1 + team + b]).wait()


def third_call(ctxs, att, proj, x_all, gain, gate, up, mlp, dy):
    team, own, wide = 2 * ctxs, dy.shape[0], gate.shape[0]
    feats = proj.shape[1]
    block, hidden = (team, own, D), (team, own, wide)
    shapes = [(own, team * feats), block, block, hidden, hidden, (4, wide // 4, D)]
    dma = pltpu.SemaphoreType.DMA
    hbm, vmem = pl.BlockSpec(memory_space=pl.ANY), pl.BlockSpec(memory_space=pltpu.VMEM)
    held = [proj.shape, gate.shape, up.shape, (4, wide // 4, D), block, hidden, hidden, hidden]
    held += [(2, own, team * feats), (2, own, D), (2, own, D), (2, own, D)]

    def kernel(*refs):
        third_kernel(ctxs, refs)

    return pl.pallas_call(
        kernel,
        out_shape=[jax.ShapeDtypeStruct((own, D), F32)]
        + [jax.ShapeDtypeStruct(shape, BF) for shape in shapes],
        in_specs=[hbm] * 3 + [vmem] + [hbm] * 4,
        out_specs=[vmem] + [hbm] * len(shapes),
        scratch_shapes=[pltpu.VMEM(shape, BF) for shape in held]
        + [pltpu.VMEM((wide // 4, D), F32)]
        + [dma((5,)), dma((team + 1, 2)), dma((2, 2)), dma((2 * team + 1,))]
        + Gather.scratch(ctxs, 2, 1),
        compiler_params=pltpu.CompilerParams(
            collective_id=6, has_side_effects=True, vmem_limit_bytes=VMEM_LIMIT
        ),
        cost_estimate=pl.CostEstimate(
            flops=2 * team * own * D * (D + 5 * wide),
            bytes_accessed=30 * own * D,
            transcendentals=0,
        ),
        name="third",
    )(att, proj, x_all, gain, gate, up, mlp, dy)


class Cargo:
    def __init__(self, arrays, refs):
        refs = list(refs)
        self.parts = []
        for array in arrays:
            ref = None if Cargo.made(array) else refs.pop(0)
            self.parts += [None if ref is None else ref.at[i] for i in range(array.shape[0])]
        count = len(self.parts)
        self.sums, refs = refs[:count], refs[count:]
        self.kept, refs = refs[:count], refs[count:]
        self.got, refs = refs[:count], refs[count:]
        self.last, refs = refs[:count], refs[count:]
        self.load, self.one, self.two = refs
        self.plane, self.core, self.ctx = (
            lax.axis_index("plane"),
            lax.axis_index("core"),
            lax.axis_index("ctx"),
        )
        self.near = (
            self.plane + 1 - 2 * lax.rem(self.plane, 2),
            lax.rem(self.plane + 2, 4),
        )

    @staticmethod
    def made(array):
        return isinstance(array, jax.ShapeDtypeStruct)

    @staticmethod
    def given(arrays):
        return [array for array in arrays if not Cargo.made(array)]

    def peers(self):
        return [(near, self.core, self.ctx) for near in self.near]

    def rows(self, s, half):
        size = self.kept[s].shape[1] // 2
        return pl.ds(half * size, size)

    def remote(self, source, target, sems, index, near):
        return pltpu.make_async_remote_copy(
            src_ref=source,
            dst_ref=target,
            send_sem=sems.at[(0,) + index],
            recv_sem=sems.at[(1,) + index],
            device_id=(near, self.core, self.ctx),
            device_id_type=MESH_ID,
        )

    def first(self, half, s, b):
        block = self.near[half] if b == 0 else 3 - self.plane
        source = self.kept[s].at[block, self.rows(s, half)]
        target = self.got[s].at[half, b]
        return self.remote(source, target, self.one, (half, s, b), self.near[half])

    def fetch(self, s):
        return pltpu.make_async_copy(self.parts[s], self.kept[s], self.load.at[s])

    def second(self, half, s):
        source = self.kept[s].at[self.near[1 - half], self.rows(s, half)]
        target = self.last[s].at[half]
        return self.remote(source, target, self.two, (half, s), self.near[1 - half])

    def begin(self):
        for s in range(len(self.parts)):
            if self.parts[s] is not None:
                self.fetch(s).start()

    def start(self, slots=None):
        for s in range(len(self.parts)) if slots is None else slots:
            if self.parts[s] is not None:
                self.fetch(s).wait()
            for b in (1, 0):
                for half in range(2):
                    self.first(half, s, b).start()

    def middle(self, s):
        kept, got = self.kept[s], self.got[s]
        size = got.shape[2]
        for half in range(2):
            block = self.near[1 - half]
            self.first(half, s, 1).wait_recv()

            def group(g, carry):
                part = pl.ds(pl.multiple_of(g * 16, 16), 16)
                rows = pl.ds(pl.multiple_of(half * size + g * 16, 16), 16)
                total = kept[block, rows, :].astype(F32) + got[half, 1, part, :].astype(F32)
                kept[block, rows, :] = total.astype(BF)
                return carry

            lax.fori_loop(0, size // 16, group, 0)
            self.second(half, s).start()

    def end(self):
        for s in range(len(self.parts)):
            kept, got, last, sums = self.kept[s], self.got[s], self.last[s], self.sums[s]
            size = got.shape[2]
            for half in range(2):
                self.first(half, s, 0).wait_recv()
                self.second(half, s).wait_recv()

                def group(g, carry):
                    part = pl.ds(pl.multiple_of(g * 16, 16), 16)
                    rows = pl.ds(pl.multiple_of(half * size + g * 16, 16), 16)
                    total = kept[self.plane, rows, :].astype(F32)
                    total = total + got[half, 0, part, :].astype(F32)
                    total = total + last[half, part, :].astype(F32)
                    sums[rows, :] = total
                    return carry

                lax.fori_loop(0, size // 16, group, 0)
        for s in range(len(self.parts)):
            for half in range(2):
                self.first(half, s, 0).wait_send()
                self.first(half, s, 1).wait_send()
                self.second(half, s).wait_send()

    @staticmethod
    def rows_of(arrays):
        return [array.shape[2] for array in arrays for _ in range(array.shape[0])]

    @staticmethod
    def out_shapes(arrays):
        return [jax.ShapeDtypeStruct((rows, D), F32) for rows in Cargo.rows_of(arrays)]

    @staticmethod
    def scratch(arrays):
        rows = Cargo.rows_of(arrays)
        if not rows:
            return []
        dma = pltpu.SemaphoreType.DMA
        return (
            [pltpu.VMEM((4, r, D), BF) for r in rows]
            + [pltpu.VMEM((2, 2, r // 2, D), BF) for r in rows]
            + [pltpu.VMEM((2, r // 2, D), BF) for r in rows]
            + [dma((len(rows),)), dma((2, 2, len(rows), 2)), dma((2, 2, len(rows)))]
        )


def team_sum_kernel(ctxs, pairs, refs, cargo, more):
    lhs, rhs, out_ref = refs[:pairs], refs[pairs : 2 * pairs], refs[2 * pairs]
    refs = refs[2 * pairs + 1 :]
    lhs_v, rhs_v = refs[:pairs], refs[pairs : 2 * pairs]
    staged, theirs, mine, from_left, from_right, load, side, hops = refs[2 * pairs :]
    plane, core, ctx = lax.axis_index("plane"), lax.axis_index("core"), lax.axis_index("ctx")
    last = ctxs - 1
    away = last - ctx
    own = out_ref.shape[0]
    rows = own // CHUNKS
    other = (plane, 1 - core, ctx)
    loads = [pltpu.make_async_copy(rhs[i], rhs_v[i], load.at[2 * ctxs, i]) for i in range(pairs)]
    for copy in loads:
        copy.start()

    def lhs_load(block, i):
        where = pl.ds(pl.multiple_of(block * own, own), own)
        return pltpu.make_async_copy(lhs[i].at[where], lhs_v[i].at[where], load.at[block, i])

    order = []
    for i in range((ctxs + 1) // 2):
        order += [last - i, i] if last - i != i else [i]
    order = [jnp.where(2 * ctx >= ctxs, last - place, place) for place in order]
    for index in order:
        for side_core in (1 - core, core):
            for i in range(pairs):
                lhs_load(side_core * ctxs + index, i).start()
    if cargo:
        cargo.begin()
    greet_all(
        [other]
        + [(plane, core, lax.rem(ctx + k, ctxs)) for k in range(1, ctxs)]
        + (cargo.peers() if cargo else [])
    )
    pending = list(range(len(cargo.parts))) if cargo else []
    ready = [i for i in pending if cargo.parts[i] is not None]
    if cargo:
        cargo.start(ready)
    for copy in loads:
        copy.wait()
    fills = []
    if more:
        other_in, other_v, made, tiles, sems = more
        other_copy = pltpu.make_async_copy(other_in, other_v, sems.at[2])
        other_copy.start()
        if made:

            def store(i, p):
                slot = (4 * i + p) % 2
                return pltpu.make_async_copy(tiles.at[slot], made[i].at[0, p], sems.at[slot])

            def tile(i, p):
                size = lhs_v[i].shape[1] // 4
                index = 4 * i + p
                if index >= 2:
                    store((index - 2) // 4, (index - 2) % 4).wait()
                part = lhs_v[i][:, p * size : (p + 1) * size]
                tiles[index % 2] = mm(part, other_v[...], 0, 0).astype(BF)
                store(i, p).start()

            fills = [functools.partial(tile, i, p) for i in range(len(made)) for p in range(4)]

    def produce(block, target):
        where = pl.ds(pl.multiple_of(block * own, own), own)
        for i in range(pairs):
            lhs_load(block, i).wait()

        def tile(t, carry):
            cols = pl.ds(pl.multiple_of(t * 512, 512), 512)
            total = mm(lhs_v[0][where, :], rhs_v[0][:, cols], 1, 0)
            for i in range(1, pairs):
                total = total + mm(lhs_v[i][where, :], rhs_v[i][:, cols], 1, 0)
            target[:, cols] = total.astype(BF)
            return carry

        lax.fori_loop(0, D // 512, tile, 0)

    def add(index, chunk, extra, slot):
        def group(g, carry):
            part = pl.ds(pl.multiple_of(chunk * rows + g * 16, 16), 16)
            total = mine[index, part, :].astype(F32) + theirs[index, part, :].astype(F32)
            if extra is not None:
                total = total + extra[slot, part, :].astype(F32)
            mine[index, part, :] = total.astype(BF)
            return carry

        lax.fori_loop(0, rows // 16, group, 0)

    def share(index):
        return pltpu.make_async_remote_copy(
            src_ref=staged.at[index],
            dst_ref=theirs.at[index],
            send_sem=side.at[0, index],
            recv_sem=side.at[1, index],
            device_id=other,
            device_id_type=MESH_ID,
        )

    def hop(way, slot, chunk, index):
        part = pl.ds(chunk * rows, rows)
        inbox = from_left if way == 0 else from_right
        return pltpu.make_async_remote_copy(
            src_ref=mine.at[index, part],
            dst_ref=inbox.at[slot, part],
            send_sem=hops.at[0, way, slot, chunk],
            recv_sem=hops.at[1, way, slot, chunk],
            device_id=(plane, core, lax.rem(ctx + (1 if way == 0 else last), ctxs)),
            device_id_type=MESH_ID,
        )

    places = []
    for i in range((ctxs + 1) // 2):
        places += [last - i, i] if last - i != i else [i]
    for place, index in zip(places, order):
        produce((1 - core) * ctxs + index, staged.at[index])
        share(index).start()
        produce(core * ctxs + index, mine.at[index])

        if place > 0:

            @pl.when(ctx == 0)
            def _():
                share(place).wait_recv()
                for chunk in range(CHUNKS):
                    add(place, chunk, None, 0)
                    hop(0, ctxs - place, chunk, place).start()

            @pl.when(ctx == last)
            def _():
                share(last - place).wait_recv()
                for chunk in range(CHUNKS):
                    add(last - place, chunk, None, 0)
                    hop(1, ctxs - place, chunk, last - place).start()

    if more:
        other_copy.wait()
        if not made:
            fresh = [i for i in pending if cargo.parts[i] is None]
            for i, slot in enumerate(fresh):
                size = lhs_v[i].shape[1]
                product = mm(lhs_v[i][...], other_v[...], 0, 0).astype(BF)
                cargo.kept[slot][...] = product.reshape(4, size // 4, D)
                cargo.start([slot])

    for step in range(1, last):

        @pl.when((ctx > 0) & (step >= ctx))
        def _():
            index = last + ctx - step
            share(index).wait_recv()
            for chunk in range(CHUNKS):
                hop(0, step, chunk, index).wait_recv()
                add(index, chunk, from_left, step)

                @pl.when(ctx < last)
                def _():
                    hop(0, step + 1, chunk, index).start()

        @pl.when((away > 0) & (step >= away))
        def _():
            index = step - away
            share(index).wait_recv()
            for chunk in range(CHUNKS):
                hop(1, step, chunk, index).wait_recv()
                add(index, chunk, from_right, step)

                @pl.when(ctx > 0)
                def _():
                    hop(1, step + 1, chunk, index).start()

        for fill in fills[:3]:
            fill()
        fills = fills[3:]
        if pending:
            cargo.middle(pending.pop(0))
    for fill in fills:
        fill()
    for s in pending:
        cargo.middle(s)

    share(ctx).wait_recv()

    def close(way):
        for chunk in range(CHUNKS):
            hop(way, last, chunk, ctx).wait_recv()

    def finish(inboxes):
        def group(g, carry):
            part = pl.ds(pl.multiple_of(g * 16, 16), 16)
            total = mine[ctx, part, :].astype(F32) + theirs[ctx, part, :].astype(F32)
            for inbox in inboxes:
                total = total + inbox[last, part, :].astype(F32)
            out_ref[part, :] = total
            return carry

        lax.fori_loop(0, own // 16, group, 0)

    @pl.when(ctx == 0)
    def _():
        close(1)
        finish([from_right])

    @pl.when(ctx == last)
    def _():
        close(0)
        finish([from_left])

    @pl.when((ctx > 0) & (ctx < last))
    def _():
        close(0)
        close(1)
        finish([from_left, from_right])

    for index in range(ctxs):
        share(index).wait_send()
    for slot in range(1, ctxs):

        @pl.when((ctx < last) & (slot >= ctx + 1))
        def _():
            for chunk in range(CHUNKS):
                hop(0, slot, chunk, ctxs + ctx - slot).wait_send()

        @pl.when((ctx > 0) & (slot >= away + 1))
        def _():
            for chunk in range(CHUNKS):
                hop(1, slot, chunk, slot - 1 - away).wait_send()

    if more and made:
        store(len(made) - 1, 2).wait()
        store(len(made) - 1, 3).wait()
    if cargo:
        cargo.end()


def team_sum(ctxs, number, pairs, name, freight=(), other=None, outer=False):
    count = pairs[0][0].shape[0]
    own = count // (2 * ctxs)
    lhs, rhs = [a for a, _ in pairs], [b for _, b in pairs]
    dma = pltpu.SemaphoreType.DMA

    inputs = 2 * len(pairs)
    given = Cargo.given(freight)
    outputs = 1 + len(Cargo.rows_of(freight))
    scratch = [pltpu.VMEM(a.shape, BF) for a in lhs + rhs]
    scratch += [pltpu.VMEM((ctxs, own, D), BF)] * 5
    scratch += [dma((2 * ctxs + 1, len(pairs))), dma((2, ctxs)), dma((2, 2, ctxs, CHUNKS))]
    made = [(1, 4, a.shape[1] // 4, D) for a in lhs] if outer else []
    extra = [other] if other is not None else []
    held = [pltpu.VMEM(a.shape, BF) for a in extra]
    held += [pltpu.VMEM((2,) + made[0][2:], BF)] if made else []
    held += [dma((3,))] if extra else []

    def kernel(*refs):
        ins, refs = refs[:inputs], refs[inputs:]
        parts, refs = refs[: len(given)], refs[len(given) :]
        more, refs = refs[: len(extra)], refs[len(extra) :]
        outs, refs = refs[:outputs], refs[outputs:]
        products, refs = refs[: len(made)], refs[len(made) :]
        mine, refs = refs[: len(scratch)], refs[len(scratch) :]
        spare, buffers = refs[: len(refs) - len(held)], refs[len(refs) - len(held) :]
        cargo = Cargo(freight, parts + outs[1:] + spare) if freight else None
        if more:
            tiles = buffers[1] if made else None
            more = (more[0], buffers[0], products, tiles, buffers[-1])
        team_sum_kernel(ctxs, len(pairs), ins + outs[:1] + mine, cargo, more)

    depth = sum(b.shape[0] for b in rhs)
    return pl.pallas_call(
        kernel,
        out_shape=[jax.ShapeDtypeStruct((own, D), F32)]
        + Cargo.out_shapes(freight)
        + [jax.ShapeDtypeStruct(shape, BF) for shape in made],
        in_specs=[pl.BlockSpec(memory_space=pl.ANY)] * (inputs + len(given) + len(extra)),
        out_specs=[pl.BlockSpec(memory_space=pltpu.VMEM)] * outputs
        + [pl.BlockSpec(memory_space=pl.ANY)] * len(made),
        scratch_shapes=scratch + Cargo.scratch(freight) + held,
        compiler_params=pltpu.CompilerParams(
            collective_id=number, has_side_effects=True, vmem_limit_bytes=VMEM_LIMIT
        ),
        cost_estimate=pl.CostEstimate(
            flops=2 * count * depth * D,
            bytes_accessed=2 * (count + D) * depth + 4 * own * D,
            transcendentals=0,
        ),
        name=name,
    )(*lhs, *rhs, *given, *extra)


def middle_kernel(ctxs, refs, freight):
    da, att, proj, out_part = refs[:4]
    refs = refs[4:]
    part, grad, joined, outs = refs[0], refs[1], refs[2], refs[3 : 3 + ctxs]
    first, sums, refs = refs[3 + ctxs], refs[4 + ctxs], refs[5 + ctxs :]
    pv, ov, sent, staged, mine, theirs, others, load, swap, side, shift = refs[:11]
    cargo = Cargo(freight, [part, sums] + list(refs[11:]))
    plane, core, ctx = cargo.plane, cargo.core, cargo.ctx
    me = core * ctxs + ctx
    loads = [
        pltpu.make_async_copy(proj, pv, load.at[0]),
        pltpu.make_async_copy(out_part, ov, load.at[1]),
    ]
    loads[1].start()
    loads[0].start()
    cargo.begin()
    partners = [
        (dc, dz) for dz in range(ctxs - 1, -1, -1) for dc in range(2) if dc + dz > 0
    ]

    def partner(dc, dz):
        return (core if dc == 0 else 1 - core, lax.rem(ctx + dz, ctxs))

    greet_all([(plane,) + partner(*step) for step in partners] + cargo.peers())

    def remote(source, target, sems, index, peer):
        return pltpu.make_async_remote_copy(
            src_ref=source,
            dst_ref=target,
            send_sem=sems.at[(0,) + index],
            recv_sem=sems.at[(1,) + index],
            device_id=(plane,) + peer,
            device_id_type=MESH_ID,
        )

    def piece(i, c, z, home):
        return remote(sent.at[c * ctxs + z], grad.at[home], swap, (i,), (c, z))

    def share(kind, z):
        source = ov.at[(1 - core) * ctxs + z] if kind == 0 else staged.at[z]
        target = others.at[z] if kind == 0 else theirs.at[z]
        return remote(source, target, side, (kind, z), (1 - core, ctx))

    loads[1].wait()
    for k in list(range(1, ctxs)) + [0]:
        share(0, lax.rem(ctx + k, ctxs)).start()
    loads[0].wait()
    for i, step in enumerate(partners):
        c, z = partner(*step)
        sent[c * ctxs + z] = mm(da[...], pv[c * ctxs + z], 1, 1).astype(BF)
        piece(i, c, z, me).start()
    cargo.start()

    def join(k):
        z = lax.rem(ctx + k, ctxs)
        share(0, z).wait_recv()
        target = outs[k - 1]

        def group(g, carry):
            part_ = pl.ds(pl.multiple_of(g * 16, 16), 16)
            total = ov[core * ctxs + z, part_, :].astype(F32) + others[z, part_, :].astype(F32)
            target[part_, :] = total.astype(BF)
            return carry

        lax.fori_loop(0, target.shape[0] // 16, group, 0)

    join(1)
    pass_on = remote(outs[0], first, shift, (0,), (core, lax.rem(ctx + 1, ctxs)))
    pass_on.start()
    grad[me] = mm(da[...], pv[me], 1, 1).astype(BF)
    width = grad.shape[2]

    def heads(t):
        return att[:, pl.ds(pl.multiple_of(t * width, width), width)]

    for z in range(ctxs):
        staged[z] = mm(heads((1 - core) * ctxs + z), da[...], 0, 0).astype(BF)
        share(1, z).start()
    for z in range(ctxs):
        mine[z] = mm(heads(core * ctxs + z), da[...], 0, 0).astype(BF)
    size = pv.shape[1]
    for k in list(range(2, ctxs)) + [0]:
        join(k)
    cargo.middle(0)
    for z in range(ctxs):
        share(1, z).wait_recv()
        for p in range(4):

            def group(g, carry):
                rows = pl.ds(pl.multiple_of(p * (size // 4) + g * 16, 16), 16)
                total = mine[z, rows, :].astype(F32) + theirs[z, rows, :].astype(F32)
                joined[p, z, pl.ds(pl.multiple_of(g * 16, 16), 16), :] = total.astype(BF)
                return carry

            lax.fori_loop(0, size // 64, group, 0)
    for i, (dc, dz) in enumerate(partners):
        c, z = core if dc == 0 else 1 - core, lax.rem(ctx + ctxs - dz, ctxs)
        piece(i, c, z, c * ctxs + z).wait_recv()
    cargo.end()
    pass_on.wait()
    for i, step in enumerate(partners):
        c, z = partner(*step)
        piece(i, c, z, me).wait_send()
    for z in range(ctxs):
        share(0, z).wait_send()
        share(1, z).wait_send()


def middle_call(ctxs, da, att, proj, out_part, part):
    team, own = 2 * ctxs, da.shape[0]
    feats = proj.shape[1]
    freight = (part,)
    dma = pltpu.SemaphoreType.DMA
    hbm, vmem = pl.BlockSpec(memory_space=pl.ANY), pl.BlockSpec(memory_space=pltpu.VMEM)
    block = (ctxs, own, D)

    def kernel(*refs):
        middle_kernel(ctxs, refs, freight)

    return pl.pallas_call(
        kernel,
        out_shape=[
            jax.ShapeDtypeStruct((team, own, feats), BF),
            jax.ShapeDtypeStruct((4, ctxs, feats // 4, D), BF),
        ]
        + [jax.ShapeDtypeStruct((own, D), BF)] * (ctxs + 1)
        + Cargo.out_shapes(freight),
        in_specs=[vmem, vmem, hbm, hbm, hbm],
        out_specs=[vmem] * (4 + ctxs),
        scratch_shapes=[
            pltpu.VMEM(proj.shape, BF),
            pltpu.VMEM(out_part.shape, BF),
            pltpu.VMEM((team, own, feats), BF),
            pltpu.VMEM((ctxs, feats, D), BF),
            pltpu.VMEM((ctxs, feats, D), BF),
            pltpu.VMEM((ctxs, feats, D), BF),
            pltpu.VMEM(block, BF),
            dma((2,)),
            dma((2, team - 1)),
            dma((2, 2, ctxs)),
            dma((2, 1)),
        ]
        + Cargo.scratch(freight),
        compiler_params=pltpu.CompilerParams(
            collective_id=7, has_side_effects=True, vmem_limit_bytes=VMEM_LIMIT
        ),
        cost_estimate=pl.CostEstimate(
            flops=4 * own * D * D, bytes_accessed=60 * own * D, transcendentals=0
        ),
        name="middle",
    )(da, att, proj, out_part, part)


def qkv_kernel(feats, x_ref, gain_ref, w_ref, c_ref, a_ref, b_ref, n_ref, q_ref, k_ref, v_ref):
    values = x_ref[...].astype(F32)
    normed = (values * norm_scale(values) * gain_ref[...]).astype(BF)
    n_ref[...] = normed
    cosine, low_sine, high_sine = [widen(ref[...], feats) for ref in (c_ref, a_ref, b_ref)]
    q = mm(normed, w_ref[0:feats], 1, 1)
    q_ref[...] = rope(q, cosine, low_sine, high_sine).astype(BF)
    k = mm(normed, w_ref[feats : 2 * feats], 1, 1)
    k_ref[...] = rope(k, cosine, low_sine, high_sine).astype(BF)
    v_ref[...] = mm(normed, w_ref[2 * feats :], 1, 1).astype(BF)


def qkv_call(x_all, gain, weights, tables):
    count = x_all.shape[0]
    feats = weights.shape[0] // 3
    turns = tables[0].shape[0] // BLOCK
    rows = pl.BlockSpec((BLOCK, D), lambda i: (i, 0))
    part = pl.BlockSpec((BLOCK, feats), lambda i: (i, 0))
    table = pl.BlockSpec((BLOCK, 128), lambda i: (i % turns, 0))
    out = jax.ShapeDtypeStruct((count, feats), BF)
    return pl.pallas_call(
        functools.partial(qkv_kernel, feats),
        grid=(count // BLOCK,),
        out_shape=(jax.ShapeDtypeStruct((count, D), BF), out, out, out),
        in_specs=[
            rows,
            pl.BlockSpec((1, D), lambda i: (0, 0)),
            pl.BlockSpec((3 * feats, D), lambda i: (0, 0)),
            table,
            table,
            table,
        ],
        out_specs=(rows, part, part, part),
        compiler_params=params(),
        cost_estimate=pl.CostEstimate(
            flops=6 * count * D * feats, bytes_accessed=4 * count * D, transcendentals=0
        ),
        name="qkv",
    )(x_all, gain, weights, *tables)


def allowed_keys(col_ref, row_ref, first, size, keys):
    same = col_ref[first : first + size, :] == row_ref[:, 0:keys]
    query_place = first + lax.broadcasted_iota(jnp.int32, (size, keys), 0)
    key_place = lax.broadcasted_iota(jnp.int32, (size, keys), 1)
    return same & (key_place <= query_place)


def attend_kernel(q_ref, k_ref, v_ref, col_ref, row_ref, o_ref, l_ref):
    length = q_ref.shape[0]
    for first in range(0, length, BLOCK):
        keys = first + BLOCK
        allowed = allowed_keys(col_ref, row_ref, first, BLOCK, keys)
        parts = []
        for head in range(q_ref.shape[1] // HD):
            lanes = slice(head * HD, (head + 1) * HD)
            query = q_ref[first:keys, lanes] * HD ** (-0.5)
            scores = jnp.where(allowed, mm(query, k_ref[0:keys, lanes], 1, 1), MASKED)
            highest = jnp.max(scores, -1, keepdims=True)
            shifted = jnp.exp(scores - highest)
            totals = jnp.sum(shifted, -1, keepdims=True)
            weights = (shifted * (1.0 / totals)).astype(BF)
            parts.append(mm(weights, v_ref[0:keys, lanes], 1, 0))
            l_ref[head, first:keys, :] = highest + jnp.log(totals)
        o_ref[first:keys, :] = jnp.concatenate(parts, 1).astype(BF)


def attend_call(query, key, value, col, row, seq):
    count, feats = query.shape
    pairs = feats // 128
    part = pl.BlockSpec((seq, 128), lambda s, h: (s, h))
    each = 128 // HD
    return pl.pallas_call(
        attend_kernel,
        grid=(2, pairs),
        out_shape=(
            jax.ShapeDtypeStruct((count, feats), BF),
            jax.ShapeDtypeStruct((2 * pairs * each, seq, 1), F32),
        ),
        in_specs=[
            part,
            part,
            part,
            pl.BlockSpec((seq, 1), lambda s, h: (s, 0)),
            pl.BlockSpec((None, 1, seq), lambda s, h: (s, 0, 0)),
        ],
        out_specs=(part, pl.BlockSpec((each, seq, 1), lambda s, h: (s * pairs + h, 0, 0))),
        compiler_params=params(2),
        cost_estimate=pl.CostEstimate(
            flops=4 * count * seq * feats, bytes_accessed=8 * count * feats, transcendentals=0
        ),
        name="attend",
    )(query, key, value, col, row)


def attend_back_kernel(
    q_ref, k_ref, v_ref, g_ref, l_ref, col_ref, row_ref, c_ref, a_ref, b_ref,
    dq_ref, dk_ref, dv_ref, key_total, value_total, query_total,
):
    length = q_ref.shape[0]
    scale = HD ** (-0.5)
    key_total[...] = jnp.zeros_like(key_total)
    value_total[...] = jnp.zeros_like(value_total)
    for first in range(0, length, BLOCK):
        keys = first + BLOCK
        allowed = allowed_keys(col_ref, row_ref, first, BLOCK, keys)
        dq_parts, dk_parts, dv_parts = [], [], []
        for head in range(q_ref.shape[1] // HD):
            lanes = slice(head * HD, (head + 1) * HD)
            query = q_ref[first:keys, lanes] * scale
            key = k_ref[0:keys, lanes]
            grad = g_ref[first:keys, lanes]
            scores = jnp.where(allowed, mm(query, key, 1, 1), MASKED)
            probs = jnp.exp(scores - l_ref[head, first:keys, :])
            grad_probs = mm(grad, v_ref[0:keys, lanes], 1, 1)
            inner = jnp.sum(probs * grad_probs, -1, keepdims=True)
            grad_scores = (probs * (grad_probs - inner)).astype(BF)
            dq_parts.append(mm(grad_scores, key, 1, 0) * scale)
            dk_parts.append(mm(grad_scores, query, 0, 0))
            dv_parts.append(mm(probs.astype(BF), grad, 0, 0))
        query_total[first:keys, :] = jnp.concatenate(dq_parts, 1)
        key_total[0:keys, :] += jnp.concatenate(dk_parts, 1)
        value_total[0:keys, :] += jnp.concatenate(dv_parts, 1)
    cosine, low_sine, high_sine = c_ref[...], a_ref[...], b_ref[...]
    dq_ref[...] = rope_back(query_total[...], cosine, low_sine, high_sine).astype(BF)
    dk_ref[...] = rope_back(key_total[...], cosine, low_sine, high_sine).astype(BF)
    dv_ref[...] = value_total[...].astype(BF)


def attend_back_call(
    query, key, value, grad, log_sums, col, row, tables, seq, freight=(), rider=(), number=None
):
    count, feats = query.shape
    pairs = feats // 128
    part = pl.BlockSpec((seq, 128), lambda s, h: (s, h))
    table = pl.BlockSpec((seq, 128), lambda s, h: (0, 0))
    each = 128 // HD
    out = jax.ShapeDtypeStruct((count, feats), BF)
    outputs = len(Cargo.rows_of(freight))

    def kernel(*refs):
        ins, refs = refs[:10], refs[10:]
        parts, refs = refs[: len(freight)], refs[len(freight) :]
        riders, refs = refs[: len(rider)], refs[len(rider) :]
        outs, refs = refs[:3], refs[3:]
        sums, refs = refs[:outputs], refs[outputs:]
        landed, refs = refs[: len(rider)], refs[len(rider) :]
        mine, spare = refs[:3], refs[3:]
        step = pl.program_id(0) * pairs + pl.program_id(1)
        if rider:
            held, got, sems = spare[-3:]
            spare = spare[:-3]
            plane, core, ctx = [lax.axis_index(name) for name in ALL]
            across = (plane, core, lax.rem(ctx + 2, 4))
            fetch = pltpu.make_async_copy(riders[0], held, sems.at[0])
            ride = pltpu.make_async_remote_copy(
                src_ref=held,
                dst_ref=got,
                send_sem=sems.at[1],
                recv_sem=sems.at[2],
                device_id=across,
                device_id_type=MESH_ID,
            )
        cargo = Cargo(freight, parts + sums + spare) if freight else None
        if freight:

            @pl.when(step == 0)
            def _():
                cargo.begin()
                if rider:
                    fetch.start()
                greet_all(cargo.peers() + ([across] if rider else []))
                if rider:
                    fetch.wait()
                    ride.start()
                cargo.start()

            @pl.when(step == 2 * pairs - 1)
            def _():
                for s in range(outputs):
                    cargo.middle(s)

        attend_back_kernel(*ins, *outs, *mine)
        if freight:

            @pl.when(step == 2 * pairs - 1)
            def _():
                cargo.end()
                if rider:
                    ride.wait()
                    landed[0][...] = got[...]

    more = dict(collective_id=number, has_side_effects=True) if freight else {}
    return pl.pallas_call(
        kernel,
        grid=(2, pairs),
        out_shape=[out, out, out]
        + Cargo.out_shapes(freight)
        + [jax.ShapeDtypeStruct(array.shape, BF) for array in rider],
        in_specs=[
            part,
            part,
            part,
            part,
            pl.BlockSpec((each, seq, 1), lambda s, h: (s * pairs + h, 0, 0)),
            pl.BlockSpec((seq, 1), lambda s, h: (s, 0)),
            pl.BlockSpec((None, 1, seq), lambda s, h: (s, 0, 0)),
            table,
            table,
            table,
        ]
        + [pl.BlockSpec(memory_space=pl.ANY)] * (len(freight) + len(rider)),
        out_specs=[part, part, part]
        + [pl.BlockSpec((rows, D), lambda s, h: (0, 0)) for rows in Cargo.rows_of(freight)]
        + [pl.BlockSpec(array.shape, lambda s, h: (0, 0)) for array in rider],
        scratch_shapes=[pltpu.VMEM((seq, 128), F32)] * 3
        + Cargo.scratch(freight)
        + ([pltpu.VMEM(rider[0].shape, BF)] * 2 + [pltpu.SemaphoreType.DMA((3,))] if rider else []),
        compiler_params=params(2, **more),
        cost_estimate=pl.CostEstimate(
            flops=10 * count * seq * feats, bytes_accessed=14 * count * feats, transcendentals=0
        ),
        name="attend_back",
    )(query, key, value, grad, log_sums, col, row, *tables, *freight, *rider)


def project_kernel(o_ref, w_ref, x_ref, gain_ref, m_ref, n_ref):
    total = x_ref[...].astype(F32)
    for index in range(o_ref.shape[0]):
        total = total + mm(o_ref[index], w_ref[index], 1, 0)
    m_ref[...] = total
    n_ref[...] = (total * norm_scale(total) * gain_ref[...]).astype(BF)


def project_call(attended, weights, x_all, gain):
    team, count, feats = attended.shape
    rows = pl.BlockSpec((BLOCK, D), lambda i: (i, 0))
    return pl.pallas_call(
        project_kernel,
        grid=(count // BLOCK,),
        out_shape=(
            jax.ShapeDtypeStruct((count, D), F32),
            jax.ShapeDtypeStruct((count, D), BF),
        ),
        in_specs=[
            pl.BlockSpec((team, BLOCK, feats), lambda i: (0, i, 0)),
            pl.BlockSpec((team, feats, D), lambda i: (0, 0, 0), pipeline_mode=pl.Buffered(1)),
            rows,
            pl.BlockSpec((1, D), lambda i: (0, 0)),
        ],
        out_specs=(rows, rows),
        compiler_params=params(),
        cost_estimate=pl.CostEstimate(
            flops=2 * count * D * D, bytes_accessed=10 * count * D, transcendentals=0
        ),
        name="project",
    )(attended, weights, x_all, gain)


def shifted(value, axis, size, step):
    return lax.ppermute(value, axis, [(i, (i + step) % size) for i in range(size)])


def plane_reduce(parts, planes):
    home = lax.axis_index("plane")
    rows = parts[0].shape[1]

    def block(index, first, size):
        return jnp.stack(
            [
                lax.dynamic_slice(part, (index, first, 0), (1, size, D))[0].astype(BF)
                for part in parts
            ],
            0,
        )

    if planes != 4:
        total = block(home, 0, rows).astype(F32)
        for k in range(1, planes):
            part = block(lax.rem(home + k, planes), 0, rows)
            total = total + shifted(part, "plane", planes, k).astype(F32)
        return total
    near_x, near_y = home + 1 - 2 * lax.rem(home, 2), lax.rem(home + 2, 4)
    far = 3 - home
    along = ([(0, 1), (1, 0), (2, 3), (3, 2)], [(0, 2), (2, 0), (1, 3), (3, 1)])
    size = rows // 2
    sums = []
    for half in range(2):
        one, two = (near_x, near_y) if half == 0 else (near_y, near_x)
        first = half * size
        sent = jnp.stack([block(one, first, size), block(far, first, size)], 0)
        got = lax.ppermute(sent, "plane", along[half]).astype(F32)
        kept = block(home, first, size).astype(F32) + got[0]
        passed = (block(two, first, size).astype(F32) + got[1]).astype(BF)
        sums.append(kept + lax.ppermute(passed, "plane", along[1 - half]).astype(F32))
    return jnp.concatenate(sums, 1)


def core_join(parts, ctxs):
    core = lax.axis_index("core")
    parts = parts.reshape((2, ctxs) + parts.shape[1:])
    got = shifted(lax.dynamic_index_in_dim(parts, 1 - core, 0, False), "core", 2, 1)
    kept = lax.dynamic_index_in_dim(parts, core, 0, False)
    joined = (kept.astype(F32) + got.astype(F32)).astype(BF)
    return jnp.moveaxis(joined, 1, 0)


def line_reduce(parts, ctxs):
    ctx = lax.axis_index("ctx")
    total = lax.dynamic_index_in_dim(parts, ctx, 0, False)
    for k in range(1, ctxs):
        part = lax.dynamic_index_in_dim(parts, lax.rem(ctx + k, ctxs), 0, False)
        total = total + shifted(part.astype(BF), "ctx", ctxs, k).astype(F32)
    return total


def after(value, *others):
    return lax.optimization_barrier((value,) + others)[0]


def team_join(parts, ctxs):
    core, ctx = lax.axis_index("core"), lax.axis_index("ctx")
    own = parts.shape[0] // (2 * ctxs)
    parts = parts.reshape(2 * ctxs, own, D)

    def block(which, k):
        return lax.dynamic_index_in_dim(parts, which * ctxs + (ctx + k) % ctxs, 0, False)

    joined = []
    for k in list(range(1, ctxs)) + [0]:
        got = shifted(block(1 - core, k), "core", 2, 1)
        both = block(core, k).astype(F32) + got.astype(F32)
        joined.append(both.astype(BF) if k > 0 else both)
    return joined


def team_finish(joined, ctxs):
    total = joined[-1].astype(F32)
    for k in range(1, ctxs):
        total = total + shifted(joined[k - 1], "ctx", ctxs, k).astype(F32)
    return total


def local(
    planes,
    ctxs,
    tokens,
    cotangent,
    segments,
    attn_weight,
    attn_first,
    attn_second,
    mlp_weight,
    mlp_first,
    mlp_second,
    gain_weight,
    gain_first,
    gain_second,
):
    team = 2 * ctxs
    devices = planes * team
    own = tokens.shape[0]
    seq = ctxs * own
    count = 2 * seq
    arows = attn_weight.shape[0]
    frows = mlp_weight.shape[0]
    gcols = gain_weight.shape[1]
    feats = planes * arows
    hidden_count = planes * frows
    whole_heads = arows % HD == 0
    me = lax.axis_index(TEAM)

    lines_seg = own // 128
    square = planes == 4 and ctxs == 4 and whole_heads and gcols == 64
    packed = jnp.zeros((8, 128), F32)
    own_gain = lax.reduce_precision(gain_weight, 8, 7)
    if square:
        side = lax.rem(lax.axis_index("ctx"), 2)
        packed = lax.dynamic_update_slice(packed, own_gain, (0, side * gcols))
    else:
        packed = packed.at[0:2, 0:gcols].set(own_gain)
    packed = packed.at[2 : 2 + lines_seg].set(segments.astype(F32).reshape(lines_seg, 128))
    attn_low = attn_weight.astype(BF)
    qkv_low = jnp.moveaxis(attn_low[:, :3], 1, 0)
    proj_low = attn_low[:, 3]
    gate_low, up_low, down_low = [mlp_weight[:, i].astype(BF) for i in range(3)]
    tables = rope_tables(seq)
    if square:
        mlp_slots = jnp.moveaxis(mlp_weight, 1, 0)
        x_all, normed, query, key, value, qkv, gate_w, small = front_call(
            ctxs, tokens, qkv_low, mlp_slots, packed, tables
        )
        normed = normed.reshape(count, D)
        query, key, value = [part.reshape(count, feats) for part in (query, key, value)]
        qkv = qkv.reshape(3 * feats, D)
        gate_w = gate_w.reshape(hidden_count, D)
        gains = small.reshape(planes, ctxs, 2, 8, 128)[:, :, :, 0:2].sum(2)
        gains = gains.transpose(2, 0, 1, 3).reshape(2, D)
        team_small = lax.dynamic_index_in_dim(small, lax.axis_index("plane"), 0, False)
        seg = team_small[:, 2 : 2 + lines_seg].reshape(count)
        seg_col, seg_row = seg.reshape(count, 1), seg.reshape(2, 1, seq)
        att_all, proj, up_w, log_sums = second_call(
            ctxs, query, key, value, seg_col, seg_row, proj_low, mlp_slots
        )
        proj = proj.reshape(team, feats, D)
        up_w = up_w.reshape(hidden_count, D)
        middle_own, att_own, normed_two, out_part, dgate, dup, down_part = third_call(
            ctxs, att_all, proj, x_all, gains[1:2], gate_w, up_w, mlp_slots, cotangent
        )
        normed_two, out_part = normed_two.reshape(count, D), out_part.reshape(count, D)
        dgate, dup = dgate.reshape(count, hidden_count), dup.reshape(count, hidden_count)
        down_part = down_part.reshape(1, planes, frows, D)
    else:
        inputs = [tokens, packed, gate_low, up_low]
        lines = [(0, 0, 2), (1, 1, 1)]
        shapes = [((team, own, D), BF), ((team, 8, 128), F32)]
        boards = []
        if whole_heads:
            inputs += [proj_low, qkv_low]
            lines.append((4, 2, 1))
            shapes.append(((team, arows, D), BF))
            boards.append(("slots", lambda ins, outs: ins[5], len(shapes)))
            shapes.append(((3, planes, arows, D), BF))
        boards.append(("block", lambda ins, outs: ins[2], len(shapes)))
        shapes.append(((planes, frows, D), BF))
        boards.append(("block", lambda ins, outs: ins[3], len(shapes)))
        shapes.append(((planes, frows, D), BF))
        boards.append(("late", lambda ins, outs: outs[1], len(shapes)))
        shapes.append(((planes, team, 8, 128), F32))
        gathered = gather_call(planes, ctxs, 0, inputs, lines, boards, shapes, "gather_first")
        x_all = gathered[0].reshape(count, D)
        small = gathered[-1]
        gate_w = gathered[-3].reshape(hidden_count, D)
        up_w = gathered[-2].reshape(hidden_count, D)
        gains = small[:, :, 0:2, 0:gcols].transpose(2, 0, 1, 3).reshape(2, D)
        seg = gathered[1][:, 2 : 2 + lines_seg].reshape(count)
        seg_col, seg_row = seg.reshape(count, 1), seg.reshape(2, 1, seq)
        if whole_heads:
            qkv = gathered[3].reshape(3 * feats, D)
        else:
            qkv = lax.all_gather(qkv_low, ALL, axis=1, tiled=True)
            qkv = lax.dynamic_slice_in_dim(qkv, me * feats, feats, 1).reshape(3 * feats, D)
            proj = lax.all_gather(proj_low, ALL, axis=0, tiled=True).reshape(team, feats, D)

        normed, query, key, value = qkv_call(x_all, gains[0:1], qkv, tables)
        attended, log_sums = attend_call(query, key, value, seg_col, seg_row, seq)

        inputs = [attended, down_low]
        lines = [(0, 0, 2)]
        shapes = [((team, count, feats), BF)]
        boards = []
        if whole_heads:
            inputs.append(gathered[2])
            boards.append(("half", lambda ins, outs: ins[2], len(shapes)))
            shapes.append(((team, planes, arows, D), BF))
        boards.append(("block", lambda ins, outs: ins[1], len(shapes)))
        shapes.append(((planes, frows, D), BF))
        gathered = gather_call(planes, ctxs, 2, inputs, lines, boards, shapes, "gather_second")
        att_all = gathered[0]
        down_w = gathered[-1].reshape(hidden_count, D)
        if whole_heads:
            proj = gathered[1].reshape(team, feats, D)
        dy_all = lax.all_gather(after(cotangent, att_all), TEAM, axis=0, tiled=True)
        middle, normed_two = project_call(att_all, proj, x_all, gains[1:2])
        mlp_w = (gate_w, up_w, down_w)

        gate = mm(normed_two, mlp_w[0], 1, 1)
        up = mm(normed_two, mlp_w[1], 1, 1)
        hidden = (jax.nn.silu(gate) * up).astype(BF)
        out_part = mm(hidden, mlp_w[2], 1, 0).astype(BF)
        grad_hidden = mm(after(dy_all, out_part), mlp_w[2], 1, 1)
        sig = jax.nn.sigmoid(gate)
        dgate = (grad_hidden * up * sig * (1.0 + gate * (1.0 - sig))).astype(BF)
        dup = (grad_hidden * gate * sig).astype(BF)
        down_part = mm(hidden, dy_all, 0, 0).astype(BF).reshape(1, planes, frows, D)
        middle_own = lax.dynamic_slice_in_dim(middle, me * own, own, 0)
        att_own = lax.dynamic_slice_in_dim(att_all, me * own, own, 1)
    if square:
        dn2, *down_sum, gate_part, up_part = team_sum(
            ctxs,
            3,
            [(dgate, gate_w), (dup, up_w)],
            "sum_two",
            (down_part,),
            normed_two,
            True,
        )
    else:
        (dn2,) = team_sum(ctxs, 3, [(dgate, gate_w), (dup, up_w)], "sum_two")
        gate_part = mm(dgate, normed_two, 0, 0).astype(BF).reshape(1, planes, frows, D)
        up_part = mm(dup, normed_two, 0, 0).astype(BF).reshape(1, planes, frows, D)

    middle_part, gain_two_grad = norm_back(dn2, middle_own, norm_scale(middle_own), gains[1])
    grad_middle = cotangent.astype(F32) + middle_part
    grad_branch = grad_middle.astype(BF)
    freight, rider = (), ()
    if square:
        grad_att, proj_part, *rest = middle_call(
            ctxs, grad_branch, att_own, proj, out_part.reshape(team, own, D), gate_part
        )
        joined, first_out, gate_sum = rest[:ctxs], rest[ctxs], rest[ctxs + 1]
        rider = (joined[1],)
        freight = (proj_part.reshape(1, planes, ctxs * arows, D),)
    else:
        grad_att = jnp.einsum("td,sfd->stf", grad_branch, proj, preferred_element_type=F32)
        grad_att = lax.all_to_all(
            grad_att.astype(BF), TEAM, split_axis=0, concat_axis=0, tiled=True
        )
        output = (middle_own + team_finish(team_join(out_part, ctxs), ctxs)).astype(BF)
        proj_part = jnp.einsum("tsf,sd->tfd", att_own, grad_branch, preferred_element_type=F32)
        proj_part = proj_part.astype(BF)
        if whole_heads:
            proj_part = core_join(proj_part.reshape(team, planes, arows, D), ctxs)
            proj_part = proj_part.reshape(1, planes, ctxs * arows, D)
        else:
            proj_grad = lax.psum_scatter(
                proj_part.reshape(D, D), ALL, scatter_dimension=0, tiled=True
            ).astype(F32)

    dq, dk, dv, *proj_sum = attend_back_call(
        query,
        key,
        value,
        grad_att.reshape(count, feats),
        log_sums,
        seg_col,
        seg_row,
        tables,
        seq,
        freight,
        rider,
        5,
    )
    pairs = [(dq, qkv[0:feats]), (dk, qkv[feats : 2 * feats]), (dv, qkv[2 * feats :])]
    if square:
        freight = (up_part, jax.ShapeDtypeStruct((3, planes, arows, D), BF))
        dn1, up_sum, *attn_sums = team_sum(ctxs, 4, pairs, "sum_one", freight, normed)
        proj_sum, second_out = proj_sum
        mlp_grad = jnp.stack([gate_sum, up_sum, down_sum[0]], 1)
    else:
        (dn1,) = team_sum(ctxs, 4, pairs, "sum_one")
        dqkv = jnp.concatenate([dq, dk, dv], 1)
        qkv_part = mm(dqkv, normed, 0, 0).astype(BF)
        mlp_grad = [plane_reduce([p[0]], planes)[0] for p in (gate_part, up_part, down_part)]
        mlp_grad = jnp.stack(mlp_grad, 1)
        if whole_heads:
            attn_part = qkv_part.reshape(3, planes, arows, D)
            attn_grad = plane_reduce([attn_part[i] for i in range(3)], planes)
            proj_grad = plane_reduce([proj_part[0]], planes)[0].reshape(ctxs, arows, D)
            proj_grad = line_reduce(proj_grad, ctxs)
        else:
            padded = lax.dynamic_update_slice_in_dim(
                jnp.zeros((3, D, D), BF), qkv_part.reshape(3, feats, D), me * feats, 1
            )
            attn_grad = lax.psum_scatter(padded, ALL, scatter_dimension=1, tiled=True)
            attn_grad = attn_grad.astype(F32)
            proj_grad = lax.psum_scatter(
                proj_part.reshape(D, D), ALL, scatter_dimension=0, tiled=True
            ).astype(F32)
        attn_grad = jnp.moveaxis(jnp.concatenate([attn_grad, proj_grad[None]], 0), 0, 1)

    source = tokens.astype(F32)
    source_part, gain_one_grad = norm_back(dn1, source, norm_scale(source), gains[0])
    grad_input = grad_middle + source_part
    gain_part = jnp.stack([gain_one_grad, gain_two_grad], 0).reshape(2, planes, team, gcols)
    gain_part = gain_part.transpose(1, 2, 0, 3)
    gain_part = jnp.pad(gain_part, ((0, 0), (0, 0), (0, 6), (0, 128 - gcols)))
    gain_grad = small_sum(planes, ctxs, gain_part)
    if square:
        gain_grad, proj_sum = lax.optimization_barrier((gain_grad, proj_sum))
        proj_sum = line_reduce(proj_sum.reshape(ctxs, arows, D), ctxs)
        proj_sum, last_out = lax.optimization_barrier((proj_sum, joined[2]))
        output = middle_own + joined[3].astype(F32) + first_out.astype(F32)
        output = output + second_out.astype(F32) + shifted(last_out, "ctx", 4, 3).astype(F32)
        output = output.astype(BF)
        attn_grad = jnp.stack(attn_sums + [proj_sum], 1)
    gain_grad = gain_grad[0:2, 0:gcols]

    attn_rate = (
        RATE_FACTOR
        * D ** (-0.5)
        * jnp.array([1.0, 1.0, 1.0, OUTPUT_BOOST], jnp.float32).reshape(1, 4, 1)
    )
    mlp_rate = RATE_FACTOR * jnp.array(
        [D ** (-0.5), D ** (-0.5), FF ** (-0.5)], jnp.float32
    ).reshape(1, 3, 1)
    attn_new = adam_update(attn_weight, attn_first, attn_second, attn_grad, attn_rate, WEIGHT_DECAY)
    mlp_new = adam_update(mlp_weight, mlp_first, mlp_second, mlp_grad, mlp_rate, WEIGHT_DECAY)
    gain_new = adam_update(gain_weight, gain_first, gain_second, gain_grad, GAIN_RATE, 0.0)
    return (
        output,
        grad_input,
        attn_new[0],
        attn_new[1][:, :3, :],
        attn_new[1][:, 3, :],
        attn_new[2],
        mlp_new[0],
        mlp_new[1],
        mlp_new[2],
        gain_new[0],
        gain_new[1],
        gain_new[2],
    )


def solution(mesh):
    dp, ctxs = mesh.shape["dp"], mesh.shape["ctx"]
    planes = dp // 2
    inner = Mesh(mesh.devices.reshape(planes, 2, ctxs), ALL)
    rows = P(ALL, None)
    cube = P(ALL, None, None)
    gain = P(None, ALL)

    def step(*args):
        return local(planes, ctxs, *args)

    return jax.shard_map(
        step,
        mesh=inner,
        in_specs=(rows, rows, P(ALL)) + (cube,) * 6 + (gain,) * 3,
        out_specs=(rows, rows, cube, cube, rows) + (cube,) * 4 + (gain,) * 3,
        check_vma=False,
    )
```

```python
import functools

import jax
import jax.numpy as jnp
import numpy as np
from jax import lax
from jax.experimental import pallas as pl
from jax.experimental.pallas import tpu as pltpu
from jax.sharding import Mesh
from jax.sharding import PartitionSpec as P

D = 2048
HEADS = 32
HD = 64
FF = 8192
STEP = 10


NORM_EPS = 1e-05
ROPE_BASE = 130000.0
BETA_ONE = 0.9
BETA_TWO = 0.95
ADAM_EPS = 1e-08
WEIGHT_DECAY = 0.1
RATE_FACTOR = 1.5
GAIN_RATE = 0.6
OUTPUT_BOOST = 12.0
MASKED = -1e30
BF = jnp.bfloat16
F32 = jnp.float32
ALL = ("plane", "core", "ctx")
TEAM = ("core", "ctx")


BLOCK = 256
CHUNKS = 2
VMEM_LIMIT = 60 * 1024 * 1024
MESH_ID = pl.DeviceIdType.MESH


def params(semantics=1, **more):
    return pltpu.CompilerParams(
        dimension_semantics=("arbitrary",) * semantics, vmem_limit_bytes=VMEM_LIMIT, **more
    )


def rope_tables(length):
    halved = HD // 2
    frequency = (ROPE_BASE ** (-(np.arange(halved) * 2.0 / HD))).astype(np.float32)
    angle = np.arange(length, dtype=np.float32)[:, None] * frequency[None, :]
    cosine, sine = np.cos(angle).astype(np.float32), np.sin(angle).astype(np.float32)
    zero = np.zeros_like(sine)
    return (
        jnp.asarray(np.concatenate([cosine] * 4, 1)),
        jnp.asarray(np.concatenate([-sine, zero] * 2, 1)),
        jnp.asarray(np.concatenate([zero, sine] * 2, 1)),
    )


def widen(table, feats):
    return jnp.concatenate([table] * (feats // 128), 1) if feats > 128 else table


def rope(values, cosine, low_sine, high_sine):
    width = values.shape[-1]
    ahead = pltpu.roll(values, width - HD // 2, 1)
    behind = pltpu.roll(values, HD // 2, 1)
    return values * cosine + ahead * low_sine + behind * high_sine


def rope_back(values, cosine, low_sine, high_sine):
    width = values.shape[-1]
    ahead = pltpu.roll(values, width - HD // 2, 1)
    behind = pltpu.roll(values, HD // 2, 1)
    return values * cosine - ahead * low_sine - behind * high_sine


def mm(a, b, ca, cb):
    return lax.dot_general(a, b, (((ca,), (cb,)), ((), ())), preferred_element_type=F32)


def norm_scale(values):
    return lax.rsqrt(jnp.mean(values * values, -1, keepdims=True) + NORM_EPS)


def norm_back(grad_normed, values, scale, gain):
    weighted = grad_normed * gain
    grad_values = scale * (
        weighted - values * scale * scale * jnp.mean(weighted * values, -1, keepdims=True)
    )
    return (grad_values, jnp.sum(grad_normed * values * scale, 0))


def adam_update(master, first, second, grad, rate, decay):
    first_new = BETA_ONE * first + (1.0 - BETA_ONE) * grad
    second_new = BETA_TWO * second + (1.0 - BETA_TWO) * grad * grad
    direction = (
        first_new
        / (1.0 - BETA_ONE**STEP)
        / (jnp.sqrt(second_new / (1.0 - BETA_TWO**STEP)) + ADAM_EPS)
    )
    return (first_new, second_new, master - rate * (direction + decay * master))


def greet_all(peers):
    barrier = pltpu.get_barrier_semaphore()
    for peer in peers:
        pl.semaphore_signal(barrier, inc=1, device_id=peer, device_id_type=MESH_ID)
    pl.semaphore_wait(barrier, len(peers))


def neighbours(planes, ctxs):
    plane, core, ctx = lax.axis_index("plane"), lax.axis_index("core"), lax.axis_index("ctx")
    column = [lax.rem(plane + k, planes) for k in range(1, planes)]
    group = [
        (core if dc == 0 else 1 - core, lax.rem(ctx + dz, ctxs))
        for dc in range(2)
        for dz in range(ctxs)
        if dc + dz > 0
    ]
    return plane, core, ctx, column, group


def gather_kernel(planes, ctxs, lines, boards, inputs, refs):
    ins, outs = refs[:inputs], refs[inputs : inputs + len(lines) + len(boards)]
    line_send, line_recv, side_send, side_recv, board_send, board_recv, pass_send, pass_recv, here = refs[
        inputs + len(lines) + len(boards) :
    ]
    plane, core, ctx = lax.axis_index("plane"), lax.axis_index("core"), lax.axis_index("ctx")
    last = ctxs - 1
    column = [lax.rem(plane + k, planes) for k in range(1, planes)]
    greet_all(
        [(p, core, ctx) for p in column]
        + [(plane, core, lax.rem(ctx + k, ctxs)) for k in range(1, ctxs)]
        + [(plane, 1 - core, ctx)]
    )
    other = (plane, 1 - core, ctx)
    pieces = []
    for source, target, chunks in lines:
        rows = ins[source].shape[0] // chunks
        for chunk in range(chunks):
            pieces.append((ins[source], outs[target], pl.ds(chunk * rows, rows)))

    def remote(source, target, send, recv, peer):
        return pltpu.make_async_remote_copy(
            src_ref=source,
            dst_ref=target,
            send_sem=send,
            recv_sem=recv,
            device_id=peer,
            device_id_type=MESH_ID,
        )

    def line(index, way, hop, block, peer_ctx, own):
        value, out, rows = pieces[index]
        slot = out.at[core * ctxs + block, rows]
        return remote(
            value.at[rows] if own else slot,
            slot,
            line_send.at[index, way, hop],
            line_recv.at[index, way, hop],
            (plane, core, peer_ctx),
        )

    def side(index, order, side_core, block, own):
        value, out, rows = pieces[index]
        slot = out.at[side_core * ctxs + block, rows]
        return remote(
            value.at[rows] if own else slot,
            slot,
            side_send.at[index, order],
            side_recv.at[index, order],
            other,
        )

    square = planes == 4
    near_x = plane + 1 - 2 * lax.rem(plane, 2)
    near_y = lax.rem(plane + 2, 4)
    far = 3 - plane

    def board_refs(index, home, half=None, own=True):
        kind, source, target = boards[index]
        value, out = source(ins, outs), outs[target]
        if kind in ("block", "late"):
            size = value.shape[0]
            part = pl.ds(0, size) if half is None else pl.ds(half * (size // 2), size // 2)
            slot = out.at[home, part]
            return (value.at[part] if own else slot), slot
        if kind == "slots":
            size = value.shape[1]
            part = pl.ds(0, size) if half is None else pl.ds(half * (size // 2), size // 2)
            slot = out.at[:, home, part]
            return (value.at[:, part] if own else slot), slot
        size = ctxs if half is None else ctxs // 2
        part = pl.ds(core * ctxs + (0 if half is None else half * size), size)
        slot = out.at[part, home]
        return (value.at[part] if own else slot), slot

    def board(index, k, home, peer):
        value, slot = board_refs(index, home)
        return remote(
            value, slot, board_send.at[index, k], board_recv.at[index, k], (peer, core, ctx)
        )

    sent = [(plane, 0, near_x), (plane, 1, near_x), (plane, 0, near_y), (plane, 1, near_y)]
    sent += [(near_y, 0, near_x), (near_x, 1, near_y)]
    landed = [near_x, near_x, near_y, near_y, far, far]

    def relay(index, k, arriving=False):
        home, half, peer = sent[k]
        value, slot = board_refs(index, landed[k] if arriving else home, half, k < 4)
        return remote(
            value, slot, board_send.at[index, k], board_recv.at[index, k], (peer, core, ctx)
        )

    def relayed(index):
        return square and boards[index][0] != "late"

    def board_start(index):
        if relayed(index):
            for k in (1, 2, 0, 3):
                relay(index, k).start()
            return
        for k, peer in enumerate(column):
            board(index, k, plane, peer).start()

    def board_pass(index):
        if relayed(index):
            relay(index, 2, True).wait_recv()
            relay(index, 4).start()
            relay(index, 1, True).wait_recv()
            relay(index, 5).start()

    def sources(index):
        if relayed(index):
            return [near_x, near_y, far]
        return [lax.rem(plane + planes - 1 - k, planes) for k in range(planes - 1)]

    def share(index, k, home):
        _, slot = board_refs(index, home)
        return remote(slot, slot, pass_send.at[index, k], pass_recv.at[index, k], other)

    def board_finish(index):
        if relayed(index):
            for k in (0, 3, 4, 5):
                relay(index, k, True).wait_recv()
        for k, home in enumerate(sources(index)):
            if not relayed(index):
                board(index, k, home, home).wait_recv()
            if boards[index][0] == "half":
                share(index, k, home).start()

    def board_close(index):
        if relayed(index):
            for k in range(6):
                relay(index, k).wait_send()
        else:
            for k, peer in enumerate(column):
                board(index, k, plane, peer).wait_send()
        if boards[index][0] == "half":
            out = outs[boards[index][2]]
            for k, home in enumerate(sources(index)):
                share(index, k, home).wait_send()
                slot = out.at[pl.ds((1 - core) * ctxs, ctxs), home]
                remote(
                    slot, slot, pass_send.at[index, k], pass_recv.at[index, k], other
                ).wait_recv()

    count = len(pieces)
    late = [i for i in range(len(boards)) if boards[i][0] == "late"]
    early = [i for i in range(len(boards)) if boards[i][0] != "late"]
    board_start(early[0]) if early else None

    @pl.when(ctx < last)
    def _():
        for i in range(count):
            line(i, 0, 1, ctx, ctx + 1, True).start()

    @pl.when(ctx > 0)
    def _():
        for i in range(count):
            line(i, 1, 1, ctx, ctx - 1, True).start()

    for i in range(count):
        side(i, 0, core, ctx, True).start()
    copies = []
    for i, (value, out, rows) in enumerate(pieces):
        copies.append(
            pltpu.make_async_copy(value.at[rows], out.at[core * ctxs + ctx, rows], here.at[i])
        )
    for i in early:
        kind, source, target = boards[i]
        slot = outs[target].at[plane] if kind == "block" else outs[target].at[:, plane]
        copies.append(pltpu.make_async_copy(source(ins, outs), slot, here.at[count + i]))
    for copy in copies:
        copy.start()

    passed = 0
    board_pass(early[0])
    if len(early) > 1:
        board_start(early[1])
    for hop in range(1, ctxs):

        @pl.when(ctx >= hop)
        def _():
            block = ctx - hop
            for i in range(count):
                line(i, 0, hop, block, ctx - 1, False).wait_recv()

                @pl.when(ctx < last)
                def _():
                    line(i, 0, hop + 1, block, ctx + 1, False).start()

                side(i, hop, core, block, False).start()

        @pl.when(ctx + hop <= last)
        def _():
            block = ctx + hop
            for i in range(count):
                line(i, 1, hop, block, ctx + 1, False).wait_recv()

                @pl.when(ctx > 0)
                def _():
                    line(i, 1, hop + 1, block, ctx - 1, False).start()

                side(i, last + hop, core, block, False).start()

        if passed + 1 < len(early):
            passed += 1
            board_pass(early[passed])
            if passed + 1 < len(early):
                board_start(early[passed + 1])
    for i in early:
        board_finish(i)

    for i in range(count):
        side(i, 0, 1 - core, ctx, False).wait_recv()
    for hop in range(1, ctxs):

        @pl.when(ctx >= hop)
        def _():
            for i in range(count):
                side(i, hop, 1 - core, ctx - hop, False).wait_recv()

        @pl.when(ctx + hop <= last)
        def _():
            for i in range(count):
                side(i, last + hop, 1 - core, ctx + hop, False).wait_recv()

    for copy in copies:
        copy.wait()
    for i in late:
        board_start(i)
        kind, source, target = boards[i]
        copy = pltpu.make_async_copy(source(ins, outs), outs[target].at[plane], here.at[count + i])
        copy.start()
        copy.wait()
    for i in late:
        board_finish(i)

    for i in range(len(boards)):
        board_close(i)
    for i in range(count):
        side(i, 0, core, ctx, True).wait_send()
    for hop in range(1, ctxs):

        @pl.when(ctx >= hop)
        def _():
            for i in range(count):
                side(i, hop, core, ctx - hop, False).wait_send()

        @pl.when(ctx + hop <= last)
        def _():
            for i in range(count):
                side(i, last + hop, core, ctx + hop, False).wait_send()

        @pl.when((ctx < last) & (ctx >= hop - 1))
        def _():
            for i in range(count):
                line(i, 0, hop, ctx - hop + 1, ctx + 1, False).wait_send()

        @pl.when((ctx > 0) & (ctx + hop - 1 <= last))
        def _():
            for i in range(count):
                line(i, 1, hop, ctx + hop - 1, ctx - 1, False).wait_send()


def gather_call(planes, ctxs, number, inputs, lines, boards, shapes, name):
    pieces = sum(chunks for _, _, chunks in lines)
    dma = pltpu.SemaphoreType.DMA

    def kernel(*refs):
        gather_kernel(planes, ctxs, lines, boards, len(inputs), refs)

    return pl.pallas_call(
        kernel,
        out_shape=tuple(jax.ShapeDtypeStruct(shape, dtype) for shape, dtype in shapes),
        in_specs=[pl.BlockSpec(memory_space=pl.ANY)] * len(inputs),
        out_specs=tuple(pl.BlockSpec(memory_space=pl.ANY) for _ in shapes),
        scratch_shapes=[
            dma((pieces, 2, ctxs + 1)),
            dma((pieces, 2, ctxs + 1)),
            dma((pieces, 2 * ctxs)),
            dma((pieces, 2 * ctxs)),
            dma((len(boards), max(planes, 6))),
            dma((len(boards), max(planes, 6))),
            dma((len(boards), planes)),
            dma((len(boards), planes)),
            dma((pieces + len(boards),)),
        ],
        compiler_params=pltpu.CompilerParams(collective_id=number, has_side_effects=True),
        name=name,
    )(*inputs)


def small_sum_kernel(planes, ctxs, value_ref, out_ref, got_one, middle, got_two, sems):
    plane, core, ctx, column, group = neighbours(planes, ctxs)
    greet_all([(p, core, ctx) for p in column] + [(plane, c, z) for c, z in group])

    def hop(index, source, target, peer):
        return pltpu.make_async_remote_copy(
            src_ref=source,
            dst_ref=target,
            send_sem=sems.at[0, index],
            recv_sem=sems.at[1, index],
            device_id=peer,
            device_id_type=MESH_ID,
        )

    first = [
        hop(i, value_ref.at[p], got_one.at[i], (p, core, ctx)) for i, p in enumerate(column)
    ]
    for copy in first:
        copy.start()
    total = value_ref[plane]
    for i, copy in enumerate(first):
        copy.wait_recv()
        total = total + got_one[i]
    middle[...] = total
    base = len(column)
    second = [
        hop(base + i, middle.at[c * ctxs + z], got_two.at[i], (plane, c, z))
        for i, (c, z) in enumerate(group)
    ]
    for copy in second:
        copy.start()
    total = middle[core * ctxs + ctx]
    for i, copy in enumerate(second):
        copy.wait_recv()
        total = total + got_two[i]
    out_ref[...] = total
    for copy in first + second:
        copy.wait_send()


def small_sum(planes, ctxs, value):
    hops = planes + 2 * ctxs - 2
    tile = value.shape[2:]
    return pl.pallas_call(
        functools.partial(small_sum_kernel, planes, ctxs),
        out_shape=jax.ShapeDtypeStruct(tile, F32),
        in_specs=[pl.BlockSpec(memory_space=pltpu.VMEM)],
        out_specs=pl.BlockSpec(memory_space=pltpu.VMEM),
        scratch_shapes=[
            pltpu.VMEM((planes - 1, 2 * ctxs) + tile, F32),
            pltpu.VMEM((2 * ctxs,) + tile, F32),
            pltpu.VMEM((2 * ctxs - 1,) + tile, F32),
            pltpu.SemaphoreType.DMA((2, hops)),
        ],
        compiler_params=pltpu.CompilerParams(collective_id=1, has_side_effects=True),
        name="small_sum",
    )(value)


class Gather:
    def __init__(self, ctxs, pieces, boards, sems):
        self.ctxs, self.pieces, self.boards = ctxs, pieces, boards
        self.line_sem, self.side_sem, self.board_sem, self.pass_sem = sems
        self.plane, self.core, self.ctx = (
            lax.axis_index("plane"),
            lax.axis_index("core"),
            lax.axis_index("ctx"),
        )
        self.last = ctxs - 1
        self.near_x = self.plane + 1 - 2 * lax.rem(self.plane, 2)
        self.near_y = lax.rem(self.plane + 2, 4)
        self.far = 3 - self.plane

    @staticmethod
    def scratch(ctxs, pieces, boards):
        dma = pltpu.SemaphoreType.DMA
        return [
            dma((2, pieces, 2, ctxs + 1)),
            dma((2, pieces, 2 * ctxs)),
            dma((2, boards, 6)),
            dma((2, boards, 3)),
        ]

    def peers(self):
        plane, core, ctx, ctxs = self.plane, self.core, self.ctx, self.ctxs
        return (
            [(plane, core, lax.rem(ctx + k, ctxs)) for k in range(1, ctxs)]
            + [(plane, 1 - core, ctx)]
            + [(near, core, ctx) for near in (self.near_x, self.near_y)]
        )

    def remote(self, slot, sem, index, peer):
        return pltpu.make_async_remote_copy(
            src_ref=slot,
            dst_ref=slot,
            send_sem=sem.at[(0,) + index],
            recv_sem=sem.at[(1,) + index],
            device_id=peer,
            device_id_type=MESH_ID,
        )

    def line(self, i, way, hop, block):
        buffer, rows = self.pieces[i]
        slot = buffer.at[self.core * self.ctxs + block, rows]
        away = 1 if way == 0 else self.ctxs - 1
        peer = (self.plane, self.core, lax.rem(self.ctx + away, self.ctxs))
        return self.remote(slot, self.line_sem, (i, way, hop), peer)

    def side(self, i, order, core, block):
        buffer, rows = self.pieces[i]
        slot = buffer.at[core * self.ctxs + block, rows]
        return self.remote(slot, self.side_sem, (i, order), (self.plane, 1 - self.core, self.ctx))

    def send_own(self, items):
        @pl.when(self.ctx < self.last)
        def _():
            for i in items:
                self.line(i, 0, 1, self.ctx).start()

        @pl.when(self.ctx > 0)
        def _():
            for i in items:
                self.line(i, 1, 1, self.ctx).start()

        for i in items:
            self.side(i, 0, self.core, self.ctx).start()

    def hop(self, k, items):
        ctx, last = self.ctx, self.last

        for i in items:

            @pl.when(ctx >= k)
            def _():
                self.line(i, 0, k, ctx - k).wait_recv()

                @pl.when(ctx < last)
                def _():
                    self.line(i, 0, k + 1, ctx - k).start()

                self.side(i, k, self.core, ctx - k).start()

            @pl.when(ctx + k <= last)
            def _():
                self.line(i, 1, k, ctx + k).wait_recv()

                @pl.when(ctx > 0)
                def _():
                    self.line(i, 1, k + 1, ctx + k).start()

                self.side(i, last + k, self.core, ctx + k).start()

    def side_arrive(self, k, items):
        ctx, last = self.ctx, self.last
        if k == 0:
            for i in items:
                self.side(i, 0, 1 - self.core, ctx).wait_recv()
            return

        @pl.when(ctx >= k)
        def _():
            for i in items:
                self.side(i, k, 1 - self.core, ctx - k).wait_recv()

        @pl.when(ctx + k <= last)
        def _():
            for i in items:
                self.side(i, last + k, 1 - self.core, ctx + k).wait_recv()

    def distant(self, k, action):
        ctx, last = self.ctx, self.last
        behind = (ctx >= k).astype(jnp.int32)
        ahead = (ctx + k <= last).astype(jnp.int32)

        def body(i, carry):
            action(jnp.where((behind == 1) & (i == 0), ctx - k, ctx + k))
            return carry

        lax.fori_loop(0, behind + ahead, body, 0)

    def board_slot(self, index, home, half):
        kind, buffer = self.boards[index]
        if kind == "block":
            size = buffer.shape[1] // 2
            return buffer.at[home, pl.ds(half * size, size)]
        if kind == "slots":
            size = buffer.shape[2] // 2
            return buffer.at[:, home, pl.ds(half * size, size)]
        size = self.ctxs // 2
        return buffer.at[pl.ds(self.core * self.ctxs + half * size, size), home]

    def relay(self, index, k, arriving=False):
        plane, near_x, near_y, far = self.plane, self.near_x, self.near_y, self.far
        sent = [(plane, 0, near_x), (plane, 1, near_x), (plane, 0, near_y), (plane, 1, near_y)]
        home, half, peer = (sent + [(near_y, 0, near_x), (near_x, 1, near_y)])[k]
        if arriving:
            home = [near_x, near_x, near_y, near_y, far, far][k]
        slot = self.board_slot(index, home, half)
        return self.remote(slot, self.board_sem, (index, k), (peer, self.core, self.ctx))

    def board_start(self, index):
        for k in (1, 2, 0, 3):
            self.relay(index, k).start()

    def board_pass(self, index):
        self.relay(index, 2, True).wait_recv()
        self.relay(index, 4).start()
        self.relay(index, 1, True).wait_recv()
        self.relay(index, 5).start()

    def share(self, index, k, core):
        buffer = self.boards[index][1]
        home = [self.near_x, self.near_y, self.far][k]
        slot = buffer.at[pl.ds(core * self.ctxs, self.ctxs), home]
        return self.remote(
            slot, self.pass_sem, (index, k), (self.plane, 1 - self.core, self.ctx)
        )

    def board_finish(self, index):
        for k in (0, 3, 4, 5):
            self.relay(index, k, True).wait_recv()
        if self.boards[index][0] == "half":
            for k in range(3):
                self.share(index, k, self.core).start()

    def board_shared(self, index):
        for k in range(3):
            self.share(index, k, 1 - self.core).wait_recv()

    def close(self):
        ctx, last = self.ctx, self.last
        items = range(len(self.pieces))
        for index in range(len(self.boards)):
            for k in range(6):
                self.relay(index, k).wait_send()
            if self.boards[index][0] == "half":
                for k in range(3):
                    self.share(index, k, self.core).wait_send()
        for i in items:
            self.side(i, 0, self.core, ctx).wait_send()
        for k in range(1, self.ctxs):

            @pl.when(ctx >= k)
            def _():
                for i in items:
                    self.side(i, k, self.core, ctx - k).wait_send()

            @pl.when(ctx + k <= last)
            def _():
                for i in items:
                    self.side(i, last + k, self.core, ctx + k).wait_send()

            @pl.when((ctx < last) & (ctx >= k - 1))
            def _():
                for i in items:
                    self.line(i, 0, k, ctx - k + 1).wait_send()

            @pl.when((ctx > 0) & (ctx + k - 1 <= last))
            def _():
                for i in items:
                    self.line(i, 1, k, ctx + k - 1).wait_send()


def front_kernel(ctxs, refs):
    tokens, qkv, mlp, packed, c_ref, a_ref, b_ref = refs[:7]
    x_out, n_out, q_out, k_out, v_out, w_out, g_out, small = refs[7:15]
    xs, ns, qs, ks, vs, ws, gs, wide, load, store, small_sem = refs[15:26]
    own = tokens.shape[0]
    half = own // 2
    pieces = [(xs, pl.ds(0, half)), (xs, pl.ds(half, half))]
    boards = [("slots", ws), ("block", gs)]
    net = Gather(ctxs, pieces, boards, refs[26:])
    plane, core, ctx = net.plane, net.core, net.ctx
    me = core * ctxs + ctx
    loads = [
        pltpu.make_async_copy(qkv, ws.at[:, plane], load.at[0]),
        pltpu.make_async_copy(tokens, xs.at[me], load.at[1]),
        pltpu.make_async_copy(mlp.at[0], wide, load.at[2]),
    ]
    for copy in loads:
        copy.start()
    others = [
        (core if dc == 0 else 1 - core, lax.rem(ctx + dz, ctxs))
        for dc in range(2)
        for dz in range(ctxs)
        if dc + dz > 0
    ]
    column = [lax.rem(plane + k, 4) for k in range(1, 4)]
    greet_all([(plane, c, z) for c, z in others] + [(p, core, ctx) for p in column])

    def tiny(index, source, target, peer):
        return pltpu.make_async_remote_copy(
            src_ref=source,
            dst_ref=target,
            send_sem=small_sem.at[0, index],
            recv_sem=small_sem.at[1, index],
            device_id=peer,
            device_id_type=MESH_ID,
        )

    small[plane, me] = packed[...]
    one = [
        tiny(i, packed, small.at[plane, me], (plane, c, z)) for i, (c, z) in enumerate(others)
    ]
    for copy in one:
        copy.start()
    for copy in loads[:2]:
        copy.wait()
    net.board_start(0)
    net.send_own([0, 1])
    i = 0
    for dc in range(2):
        for dz in range(ctxs):
            if dc + dz > 0:
                c, z = core if dc == 0 else 1 - core, lax.rem(ctx + ctxs - dz, ctxs)
                tiny(i, packed, small.at[plane, c * ctxs + z], (plane, c, z)).wait_recv()
                i += 1
    two = [
        tiny(i + k, small.at[plane], small.at[plane], (p, core, ctx))
        for k, p in enumerate(column)
    ]
    for copy in two:
        copy.start()
    loads[2].wait()

    def narrow(g, carry):
        part = pl.ds(pl.multiple_of(g * 16, 16), 16)
        gs[plane, part, :] = wide[part, :].astype(BF)
        return carry

    lax.fori_loop(0, wide.shape[0] // 16, narrow, 0)
    net.board_pass(0)
    net.board_start(1)
    for k in range(3):
        home = lax.rem(plane + 3 - k, 4)
        tiny(i + k, small.at[plane], small.at[home], (home, core, ctx)).wait_recv()
    tiles = [
        small[p, 2 * j][0:1] + small[p, 2 * j + 1][0:1] for p in range(4) for j in range(ctxs)
    ]
    gain = jnp.concatenate(tiles, 1)
    feats = q_out.shape[-1]
    stores = []

    blocks = [(xs, x_out), (ns, n_out), (qs, q_out), (ks, k_out), (vs, v_out)]

    def put(source, target, index):
        return pltpu.make_async_copy(source, target, store.at[index])

    def compute(side_core):
        def action(block):
            b = side_core * ctxs + block
            values = xs[b].astype(F32)
            normed = (values * norm_scale(values) * gain).astype(BF)
            ns[b] = normed
            rows = pl.ds(pl.multiple_of(block * own, own), own)
            cosine, low_sine, high_sine = [
                widen(ref[rows, :], feats) for ref in (c_ref, a_ref, b_ref)
            ]
            q = mm(normed, ws[0].reshape(feats, D), 1, 1)
            qs[b] = rope(q, cosine, low_sine, high_sine).astype(BF)
            k = mm(normed, ws[1].reshape(feats, D), 1, 1)
            ks[b] = rope(k, cosine, low_sine, high_sine).astype(BF)
            vs[b] = mm(normed, ws[2].reshape(feats, D), 1, 1).astype(BF)
            for i, (source, target) in enumerate(blocks):
                put(source.at[b], target.at[b], 5 * b + i).start()

        return action

    base = 10 * ctxs
    parts = [0, 1]
    stores = [put(s, t, base + i) for i, (s, t) in enumerate([(ws, w_out), (gs, g_out)])]
    net.hop(1, parts)
    net.board_finish(0)
    stores[0].start()
    compute(core)(ctx)
    net.side_arrive(0, parts)
    compute(1 - core)(ctx)
    net.board_pass(1)
    for k in range(1, ctxs):
        net.distant(k, compute(core))
        if k + 1 < ctxs:
            net.hop(k + 1, parts)
        net.side_arrive(k, parts)
        net.distant(k, compute(1 - core))
        if k == min(2, ctxs - 1):
            net.board_finish(1)
            stores[1].start()
    net.close()
    for copy in one + two:
        copy.wait_send()
    for copy in stores:
        copy.wait()
    for b in range(2 * ctxs):
        for i, (source, target) in enumerate(blocks):
            put(source.at[b], target.at[b], 5 * b + i).wait()


def front_call(ctxs, tokens, qkv, mlp, packed, tables):
    team = 2 * ctxs
    own, arows, frows = tokens.shape[0], qkv.shape[1], mlp.shape[1]
    feats = 4 * arows
    block, part = (team, own, D), (team, own, feats)
    shapes = [block, block, part, part, part, (3, 4, arows, D)]
    shapes += [(4, frows, D)]
    dma = pltpu.SemaphoreType.DMA
    hbm, vmem = pl.BlockSpec(memory_space=pl.ANY), pl.BlockSpec(memory_space=pltpu.VMEM)

    def kernel(*refs):
        front_kernel(ctxs, refs)

    return pl.pallas_call(
        kernel,
        out_shape=[jax.ShapeDtypeStruct(shape, BF) for shape in shapes]
        + [jax.ShapeDtypeStruct((4, team, 8, 128), F32)],
        in_specs=[hbm] * 3 + [vmem] * 4,
        out_specs=[hbm] * len(shapes) + [vmem],
        scratch_shapes=[pltpu.VMEM(shape, BF) for shape in shapes]
        + [pltpu.VMEM((frows, D), F32)]
        + [dma((3,)), dma((5 * team + 2,)), dma((2, team + 2))]
        + Gather.scratch(ctxs, 2, 2),
        compiler_params=pltpu.CompilerParams(
            collective_id=0, has_side_effects=True, vmem_limit_bytes=VMEM_LIMIT
        ),
        cost_estimate=pl.CostEstimate(
            flops=6 * team * own * D * feats, bytes_accessed=40 * own * D, transcendentals=0
        ),
        name="front",
    )(tokens, qkv, mlp, packed, *tables)


def attend_part(
    q_ref, k_ref, v_ref, col_ref, row_ref, l_ref, put, start, begin, end, pair, unit
):
    lanes = pl.ds(pl.multiple_of(pair * 128, 128), 128)
    for first in range(begin, end, BLOCK):
        keys = first + BLOCK
        rows = pl.ds(pl.multiple_of(start + first, BLOCK), BLOCK)
        past = pl.ds(pl.multiple_of(start, BLOCK), keys)
        same = col_ref[rows, :] == row_ref[:, 0:keys]
        query_place = first + lax.broadcasted_iota(jnp.int32, (BLOCK, keys), 0)
        key_place = lax.broadcasted_iota(jnp.int32, (BLOCK, keys), 1)
        allowed = same & (key_place <= query_place)
        query, key, value = q_ref[rows, lanes], k_ref[past, lanes], v_ref[past, lanes]
        parts = []
        for head in range(128 // HD):
            cut = slice(head * HD, (head + 1) * HD)
            scores = mm(query[:, cut] * HD ** (-0.5), key[:, cut], 1, 1)
            scores = jnp.where(allowed, scores, MASKED)
            highest = jnp.max(scores, -1, keepdims=True)
            shifted = jnp.exp(scores - highest)
            totals = jnp.sum(shifted, -1, keepdims=True)
            weights = (shifted * (1.0 / totals)).astype(BF)
            parts.append(mm(weights, value[:, cut], 1, 0))
            l_ref[unit + head, first:keys, :] = highest + jnp.log(totals)
        put(rows, lanes, jnp.concatenate(parts, 1).astype(BF))


def second_kernel(ctxs, refs):
    q_ref, k_ref, v_ref, col_ref, row_ref, proj, mlp = refs[:7]
    o_out, p_out, d_out, l_ref = refs[7:11]
    outs, ps, ds_, wide, load, store = refs[11:17]
    count, feats = q_ref.shape
    seq = count // 2
    pairs = feats // 128
    plane = lax.axis_index("plane")
    half = seq // 2
    pieces = [(outs, pl.ds(i * half, half)) for i in range(4)] + [(ps, plane)]
    parts, rows_piece = [0, 1, 2, 3], [4]
    net = Gather(ctxs, pieces, [("block", ds_), ("half", ps)], refs[17:])
    core, ctx = net.core, net.ctx
    me = core * ctxs + ctx
    loads = [
        pltpu.make_async_copy(proj, ps.at[me, plane], load.at[0]),
        pltpu.make_async_copy(mlp.at[1], wide, load.at[1]),
    ]
    for copy in loads:
        copy.start()
    greet_all(net.peers())
    loads[0].wait()
    net.send_own(rows_piece)
    loads[1].wait()

    def narrow(g, carry):
        part = pl.ds(pl.multiple_of(g * 16, 16), 16)
        ds_[plane, part, :] = wide[part, :].astype(BF)
        return carry

    lax.fori_loop(0, wide.shape[0] // 16, narrow, 0)
    net.board_start(0)

    def put(rows, lanes, values):
        outs[me, rows, lanes] = values

    hops = list(range(1, ctxs))
    for part in parts:
        s, begin = part // 2, (part % 2) * half
        for pair in range(pairs):
            attend_part(
                q_ref, k_ref, v_ref, col_ref, row_ref.at[s], l_ref, put,
                s * seq, begin, begin + half, pair, (s * pairs + pair) * (128 // HD),
            )
        net.send_own([part])
        if hops:
            net.hop(hops.pop(0), rows_piece)
            if not hops:
                net.board_start(1)
        if part == 1:
            net.board_pass(0)
    for k in hops:
        net.hop(k, rows_piece)
    if hops:
        net.board_start(1)

    def copy_out(b):
        return pltpu.make_async_copy(outs.at[b], o_out.at[b], store.at[b])

    copy_out(me).start()
    for k in range(1, ctxs):
        net.hop(k, parts[:2])
        if k == 2 or ctxs == 2:
            net.board_pass(1)
        net.hop(k, parts[2:])
        net.distant(k, lambda block: copy_out(core * ctxs + block).start())
        net.side_arrive(k - 1, parts)
        if k == 1:
            copy_out((1 - core) * ctxs + ctx).start()
            net.board_finish(0)
        else:
            net.distant(k - 1, lambda block: copy_out((1 - core) * ctxs + block).start())
    tail = [
        pltpu.make_async_copy(ds_, d_out, store.at[2 * ctxs]),
        pltpu.make_async_copy(ps, p_out, store.at[2 * ctxs + 1]),
    ]
    tail[0].start()
    for k in range(ctxs):
        net.side_arrive(k, rows_piece)
    net.board_finish(1)
    net.board_shared(1)
    tail[1].start()
    net.side_arrive(ctxs - 1, parts)
    net.distant(ctxs - 1, lambda block: copy_out((1 - core) * ctxs + block).start())
    net.close()
    for copy in tail:
        copy.wait()
    for b in range(2 * ctxs):
        copy_out(b).wait()


def second_call(ctxs, query, key, value, col, row, proj, mlp):
    team = 2 * ctxs
    count, feats = query.shape
    seq = count // 2
    arows, frows = proj.shape[0], mlp.shape[1]
    shapes = [(team, count, feats), (team, 4, arows, D), (4, frows, D)]
    dma = pltpu.SemaphoreType.DMA
    hbm, vmem = pl.BlockSpec(memory_space=pl.ANY), pl.BlockSpec(memory_space=pltpu.VMEM)

    def kernel(*refs):
        second_kernel(ctxs, refs)

    return pl.pallas_call(
        kernel,
        out_shape=[jax.ShapeDtypeStruct(shape, BF) for shape in shapes]
        + [jax.ShapeDtypeStruct((2 * feats // HD, seq, 1), F32)],
        in_specs=[vmem] * 5 + [hbm] * 2,
        out_specs=[hbm] * 3 + [vmem],
        scratch_shapes=[pltpu.VMEM(shape, BF) for shape in shapes]
        + [pltpu.VMEM((frows, D), F32)]
        + [dma((2,)), dma((team + 2,))]
        + Gather.scratch(ctxs, 5, 2),
        compiler_params=pltpu.CompilerParams(
            collective_id=2, has_side_effects=True, vmem_limit_bytes=VMEM_LIMIT
        ),
        cost_estimate=pl.CostEstimate(
            flops=4 * count * seq * feats, bytes_accessed=24 * count * feats, transcendentals=0
        ),
        name="second",
    )(query, key, value, col, row, proj, mlp)


def third_kernel(ctxs, refs):
    att, proj, x_all, gain, gate, up, mlp, dy = refs[:8]
    m_out, a_out, n_out, o_out, g_out, u_out, d_out = refs[8:15]
    pv, gv, uv, dv, ys, hs, gs, us, ob, xb, nb, sb, narrowed = refs[15:28]
    load, block_sem, store, late = refs[28:32]
    team, own = ys.shape[0], ys.shape[1]
    wide = gv.shape[0]
    pieces = [(ys, pl.ds(0, own // 2)), (ys, pl.ds(own // 2, own // 2))]
    net = Gather(ctxs, pieces, [("block", dv)], refs[32:])
    plane, core, ctx = net.plane, net.core, net.ctx
    me = core * ctxs + ctx
    loads = [
        pltpu.make_async_copy(dy, ys.at[me], load.at[0]),
        pltpu.make_async_copy(mlp.at[2], narrowed, load.at[1]),
        pltpu.make_async_copy(proj, pv, load.at[2]),
        pltpu.make_async_copy(gate, gv, load.at[3]),
        pltpu.make_async_copy(up, uv, load.at[4]),
    ]

    def fetch(i):
        slot = lax.rem(i, 2)
        rows = pl.ds(pl.multiple_of(i * own, own), own)
        size = att.shape[2]
        copies = [
            pltpu.make_async_copy(
                att.at[t, rows], ob.at[slot, :, pl.ds(t * size, size)], block_sem.at[t, slot]
            )
            for t in range(team)
        ]
        return copies + [pltpu.make_async_copy(x_all.at[i], xb.at[slot], block_sem.at[team, slot])]

    def n_store(i):
        return pltpu.make_async_copy(nb.at[lax.rem(i, 2)], n_out.at[i], store.at[0, lax.rem(i, 2)])

    def s_store(i, out):
        return pltpu.make_async_copy(sb.at[lax.rem(i, 2)], out.at[i], store.at[1, lax.rem(i, 2)])

    for copy in loads:
        copy.start()
    for copy in fetch(0):
        copy.start()
    greet_all(net.peers())
    loads[0].wait()
    net.send_own([0, 1])
    loads[1].wait()

    def narrow(g, carry):
        part = pl.ds(pl.multiple_of(g * 16, 16), 16)
        dv[plane, part, :] = narrowed[part, :].astype(BF)
        return carry

    lax.fori_loop(0, narrowed.shape[0] // 16, narrow, 0)
    net.board_start(0)
    for copy in loads[2:]:
        copy.wait()

    steps = [(hop, chunk) for hop in range(1, ctxs) for chunk in range(2)]
    stages = []
    for i, step in enumerate(steps[: 2 * (ctxs - 2)] if ctxs > 2 else []):
        stages.append((min(2 * i + 1, team - 1), step))

    def forward(i, carry):
        slot = lax.rem(i, 2)
        for copy in fetch(i):
            copy.wait()

        @pl.when(i + 1 < team)
        def _():
            for copy in fetch(i + 1):
                copy.start()

        total = xb[slot].astype(F32)
        total = total + mm(ob[slot], pv[...].reshape(ob.shape[2], D), 1, 0)

        @pl.when(i >= 2)
        def _():
            n_store(i - 2).wait()

        nb[slot] = (total * norm_scale(total) * gain[...]).astype(BF)
        n_store(i).start()

        @pl.when(i == me)
        def _():
            m_out[...] = total
            keep = pltpu.make_async_copy(ob.at[slot], a_out, late.at[0])
            keep.start()
            keep.wait()

        normed = nb[slot]
        for first in range(0, wide, 512):
            part = slice(first, first + 512)
            g = mm(normed, gv[part, :], 1, 1)
            u = mm(normed, uv[part, :], 1, 1)
            sig = 1.0 / (1.0 + jnp.exp(-g))
            lit = g * sig
            hs[i, :, part] = (lit * u).astype(BF)
            gs[i, :, part] = (u * sig * (1.0 + g * (1.0 - sig))).astype(BF)
            us[i, :, part] = lit.astype(BF)
        for at, (hop, chunk) in stages:

            @pl.when(i == at)
            def _():
                net.hop(hop, [chunk])

        @pl.when(i == 1)
        def _():
            net.board_pass(0)

        return carry

    lax.fori_loop(0, team, forward, 0)
    n_store(team - 2).wait()
    n_store(team - 1).wait()
    net.board_finish(0)

    def pair_store(i, out):
        return pltpu.make_async_copy(sb, out.at[pl.ds(2 * i, 2)], store.at[1, 0])

    def outward(i, carry):
        both = hs[pl.ds(2 * i, 2)].reshape(2 * own, wide)
        result = mm(both, dv[...].reshape(wide, D), 1, 0).astype(BF)

        @pl.when(i >= 1)
        def _():
            pair_store(i - 1, o_out).wait()

        sb[...] = result.reshape(2, own, D)
        pair_store(i, o_out).start()
        return carry

    def backward(side_core):
        def action(block):
            b = side_core * ctxs + block
            for p in range(4):
                cols = slice(p * (wide // 4), (p + 1) * (wide // 4))
                dh = mm(ys[b], dv[p], 1, 1)
                gs[b, :, cols] = (dh * gs[b, :, cols].astype(F32)).astype(BF)
                us[b, :, cols] = (dh * us[b, :, cols].astype(F32)).astype(BF)
            pltpu.make_async_copy(gs.at[b], g_out.at[b], late.at[1 + b]).start()
            pltpu.make_async_copy(us.at[b], u_out.at[b], late.at[1 + team + b]).start()

        return action

    backward(core)(ctx)
    net.side_arrive(0, [0, 1])
    backward(1 - core)(ctx)
    for k in range(1, ctxs - 1):
        if k == ctxs - 2:
            net.hop(ctxs - 1, [0])
        net.distant(k, backward(core))
        net.side_arrive(k, [0, 1])
        net.distant(k, backward(1 - core))
    lax.fori_loop(0, team // 2, outward, 0)
    pair_store(team // 2 - 1, o_out).wait()
    net.hop(ctxs - 1, [1])
    net.distant(ctxs - 1, backward(core))
    net.side_arrive(ctxs - 1, [0, 1])
    net.distant(ctxs - 1, backward(1 - core))
    for p in range(4):
        if p >= 2:
            s_store(p - 2, d_out).wait()
        hidden = hs[:, :, p * (wide // 4) : (p + 1) * (wide // 4)].reshape(team * own, wide // 4)
        sb[p % 2] = mm(hidden, ys[...].reshape(team * own, D), 0, 0).astype(BF)
        s_store(p, d_out).start()
    s_store(2, d_out).wait()
    s_store(3, d_out).wait()
    net.close()
    for b in range(team):
        pltpu.make_async_copy(gs.at[b], g_out.at[b], late.at[1 + b]).wait()
        pltpu.make_async_copy(us.at[b], u_out.at[b], late.at[1 + team + b]).wait()


def third_call(ctxs, att, proj, x_all, gain, gate, up, mlp, dy):
    team, own, wide = 2 * ctxs, dy.shape[0], gate.shape[0]
    feats = proj.shape[1]
    block, hidden = (team, own, D), (team, own, wide)
    shapes = [(own, team * feats), block, block, hidden, hidden, (4, wide // 4, D)]
    dma = pltpu.SemaphoreType.DMA
    hbm, vmem = pl.BlockSpec(memory_space=pl.ANY), pl.BlockSpec(memory_space=pltpu.VMEM)
    held = [proj.shape, gate.shape, up.shape, (4, wide // 4, D), block, hidden, hidden, hidden]
    held += [(2, own, team * feats), (2, own, D), (2, own, D), (2, own, D)]

    def kernel(*refs):
        third_kernel(ctxs, refs)

    return pl.pallas_call(
        kernel,
        out_shape=[jax.ShapeDtypeStruct((own, D), F32)]
        + [jax.ShapeDtypeStruct(shape, BF) for shape in shapes],
        in_specs=[hbm] * 3 + [vmem] + [hbm] * 4,
        out_specs=[vmem] + [hbm] * len(shapes),
        scratch_shapes=[pltpu.VMEM(shape, BF) for shape in held]
        + [pltpu.VMEM((wide // 4, D), F32)]
        + [dma((5,)), dma((team + 1, 2)), dma((2, 2)), dma((2 * team + 1,))]
        + Gather.scratch(ctxs, 2, 1),
        compiler_params=pltpu.CompilerParams(
            collective_id=6, has_side_effects=True, vmem_limit_bytes=VMEM_LIMIT
        ),
        cost_estimate=pl.CostEstimate(
            flops=2 * team * own * D * (D + 5 * wide),
            bytes_accessed=30 * own * D,
            transcendentals=0,
        ),
        name="third",
    )(att, proj, x_all, gain, gate, up, mlp, dy)


class Cargo:
    def __init__(self, arrays, refs):
        refs = list(refs)
        self.parts = []
        for array in arrays:
            ref = None if Cargo.made(array) else refs.pop(0)
            self.parts += [None if ref is None else ref.at[i] for i in range(array.shape[0])]
        count = len(self.parts)
        self.sums, refs = refs[:count], refs[count:]
        self.kept, refs = refs[:count], refs[count:]
        self.got, refs = refs[:count], refs[count:]
        self.last, refs = refs[:count], refs[count:]
        self.load, self.one, self.two = refs
        self.plane, self.core, self.ctx = (
            lax.axis_index("plane"),
            lax.axis_index("core"),
            lax.axis_index("ctx"),
        )
        self.near = (
            self.plane + 1 - 2 * lax.rem(self.plane, 2),
            lax.rem(self.plane + 2, 4),
        )

    @staticmethod
    def made(array):
        return isinstance(array, jax.ShapeDtypeStruct)

    @staticmethod
    def given(arrays):
        return [array for array in arrays if not Cargo.made(array)]

    def peers(self):
        return [(near, self.core, self.ctx) for near in self.near]

    def rows(self, s, half):
        size = self.kept[s].shape[1] // 2
        return pl.ds(half * size, size)

    def remote(self, source, target, sems, index, near):
        return pltpu.make_async_remote_copy(
            src_ref=source,
            dst_ref=target,
            send_sem=sems.at[(0,) + index],
            recv_sem=sems.at[(1,) + index],
            device_id=(near, self.core, self.ctx),
            device_id_type=MESH_ID,
        )

    def first(self, half, s, b):
        block = self.near[half] if b == 0 else 3 - self.plane
        source = self.kept[s].at[block, self.rows(s, half)]
        target = self.got[s].at[half, b]
        return self.remote(source, target, self.one, (half, s, b), self.near[half])

    def fetch(self, s):
        return pltpu.make_async_copy(self.parts[s], self.kept[s], self.load.at[s])

    def second(self, half, s):
        source = self.kept[s].at[self.near[1 - half], self.rows(s, half)]
        target = self.last[s].at[half]
        return self.remote(source, target, self.two, (half, s), self.near[1 - half])

    def begin(self):
        for s in range(len(self.parts)):
            if self.parts[s] is not None:
                self.fetch(s).start()

    def start(self, slots=None):
        for s in range(len(self.parts)) if slots is None else slots:
            if self.parts[s] is not None:
                self.fetch(s).wait()
            for b in (1, 0):
                for half in range(2):
                    self.first(half, s, b).start()

    def middle(self, s):
        kept, got = self.kept[s], self.got[s]
        size = got.shape[2]
        for half in range(2):
            block = self.near[1 - half]
            self.first(half, s, 1).wait_recv()

            def group(g, carry):
                part = pl.ds(pl.multiple_of(g * 16, 16), 16)
                rows = pl.ds(pl.multiple_of(half * size + g * 16, 16), 16)
                total = kept[block, rows, :].astype(F32) + got[half, 1, part, :].astype(F32)
                kept[block, rows, :] = total.astype(BF)
                return carry

            lax.fori_loop(0, size // 16, group, 0)
            self.second(half, s).start()

    def end(self):
        for s in range(len(self.parts)):
            kept, got, last, sums = self.kept[s], self.got[s], self.last[s], self.sums[s]
            size = got.shape[2]
            for half in range(2):
                self.first(half, s, 0).wait_recv()
                self.second(half, s).wait_recv()

                def group(g, carry):
                    part = pl.ds(pl.multiple_of(g * 16, 16), 16)
                    rows = pl.ds(pl.multiple_of(half * size + g * 16, 16), 16)
                    total = kept[self.plane, rows, :].astype(F32)
                    total = total + got[half, 0, part, :].astype(F32)
                    total = total + last[half, part, :].astype(F32)
                    sums[rows, :] = total
                    return carry

                lax.fori_loop(0, size // 16, group, 0)
        for s in range(len(self.parts)):
            for half in range(2):
                self.first(half, s, 0).wait_send()
                self.first(half, s, 1).wait_send()
                self.second(half, s).wait_send()

    @staticmethod
    def rows_of(arrays):
        return [array.shape[2] for array in arrays for _ in range(array.shape[0])]

    @staticmethod
    def out_shapes(arrays):
        return [jax.ShapeDtypeStruct((rows, D), F32) for rows in Cargo.rows_of(arrays)]

    @staticmethod
    def scratch(arrays):
        rows = Cargo.rows_of(arrays)
        if not rows:
            return []
        dma = pltpu.SemaphoreType.DMA
        return (
            [pltpu.VMEM((4, r, D), BF) for r in rows]
            + [pltpu.VMEM((2, 2, r // 2, D), BF) for r in rows]
            + [pltpu.VMEM((2, r // 2, D), BF) for r in rows]
            + [dma((len(rows),)), dma((2, 2, len(rows), 2)), dma((2, 2, len(rows)))]
        )


def team_sum_kernel(ctxs, pairs, refs, cargo, more):
    lhs, rhs, out_ref = refs[:pairs], refs[pairs : 2 * pairs], refs[2 * pairs]
    refs = refs[2 * pairs + 1 :]
    lhs_v, rhs_v = refs[:pairs], refs[pairs : 2 * pairs]
    staged, theirs, mine, from_left, from_right, load, side, hops = refs[2 * pairs :]
    plane, core, ctx = lax.axis_index("plane"), lax.axis_index("core"), lax.axis_index("ctx")
    last = ctxs - 1
    away = last - ctx
    own = out_ref.shape[0]
    rows = own // CHUNKS
    other = (plane, 1 - core, ctx)
    loads = [pltpu.make_async_copy(rhs[i], rhs_v[i], load.at[2 * ctxs, i]) for i in range(pairs)]
    for copy in loads:
        copy.start()

    def lhs_load(block, i):
        where = pl.ds(pl.multiple_of(block * own, own), own)
        return pltpu.make_async_copy(lhs[i].at[where], lhs_v[i].at[where], load.at[block, i])

    order = []
    for i in range((ctxs + 1) // 2):
        order += [last - i, i] if last - i != i else [i]
    order = [jnp.where(2 * ctx >= ctxs, last - place, place) for place in order]
    for index in order:
        for side_core in (1 - core, core):
            for i in range(pairs):
                lhs_load(side_core * ctxs + index, i).start()
    if cargo:
        cargo.begin()
    greet_all(
        [other]
        + [(plane, core, lax.rem(ctx + k, ctxs)) for k in range(1, ctxs)]
        + (cargo.peers() if cargo else [])
    )
    pending = list(range(len(cargo.parts))) if cargo else []
    ready = [i for i in pending if cargo.parts[i] is not None]
    if cargo:
        cargo.start(ready)
    for copy in loads:
        copy.wait()
    fills = []
    if more:
        other_in, other_v, made, tiles, sems = more
        other_copy = pltpu.make_async_copy(other_in, other_v, sems.at[2])
        other_copy.start()
        if made:

            def store(i, p):
                slot = (4 * i + p) % 2
                return pltpu.make_async_copy(tiles.at[slot], made[i].at[0, p], sems.at[slot])

            def tile(i, p):
                size = lhs_v[i].shape[1] // 4
                index = 4 * i + p
                if index >= 2:
                    store((index - 2) // 4, (index - 2) % 4).wait()
                part = lhs_v[i][:, p * size : (p + 1) * size]
                tiles[index % 2] = mm(part, other_v[...], 0, 0).astype(BF)
                store(i, p).start()

            fills = [functools.partial(tile, i, p) for i in range(len(made)) for p in range(4)]

    def produce(block, target):
        where = pl.ds(pl.multiple_of(block * own, own), own)
        for i in range(pairs):
            lhs_load(block, i).wait()

        def tile(t, carry):
            cols = pl.ds(pl.multiple_of(t * 512, 512), 512)
            total = mm(lhs_v[0][where, :], rhs_v[0][:, cols], 1, 0)
            for i in range(1, pairs):
                total = total + mm(lhs_v[i][where, :], rhs_v[i][:, cols], 1, 0)
            target[:, cols] = total.astype(BF)
            return carry

        lax.fori_loop(0, D // 512, tile, 0)

    def add(index, chunk, extra, slot):
        def group(g, carry):
            part = pl.ds(pl.multiple_of(chunk * rows + g * 16, 16), 16)
            total = mine[index, part, :].astype(F32) + theirs[index, part, :].astype(F32)
            if extra is not None:
                total = total + extra[slot, part, :].astype(F32)
            mine[index, part, :] = total.astype(BF)
            return carry

        lax.fori_loop(0, rows // 16, group, 0)

    def share(index):
        return pltpu.make_async_remote_copy(
            src_ref=staged.at[index],
            dst_ref=theirs.at[index],
            send_sem=side.at[0, index],
            recv_sem=side.at[1, index],
            device_id=other,
            device_id_type=MESH_ID,
        )

    def hop(way, slot, chunk, index):
        part = pl.ds(chunk * rows, rows)
        inbox = from_left if way == 0 else from_right
        return pltpu.make_async_remote_copy(
            src_ref=mine.at[index, part],
            dst_ref=inbox.at[slot, part],
            send_sem=hops.at[0, way, slot, chunk],
            recv_sem=hops.at[1, way, slot, chunk],
            device_id=(plane, core, lax.rem(ctx + (1 if way == 0 else last), ctxs)),
            device_id_type=MESH_ID,
        )

    places = []
    for i in range((ctxs + 1) // 2):
        places += [last - i, i] if last - i != i else [i]
    for place, index in zip(places, order):
        produce((1 - core) * ctxs + index, staged.at[index])
        share(index).start()
        produce(core * ctxs + index, mine.at[index])

        if place > 0:

            @pl.when(ctx == 0)
            def _():
                share(place).wait_recv()
                for chunk in range(CHUNKS):
                    add(place, chunk, None, 0)
                    hop(0, ctxs - place, chunk, place).start()

            @pl.when(ctx == last)
            def _():
                share(last - place).wait_recv()
                for chunk in range(CHUNKS):
                    add(last - place, chunk, None, 0)
                    hop(1, ctxs - place, chunk, last - place).start()

    if more:
        other_copy.wait()
        if not made:
            fresh = [i for i in pending if cargo.parts[i] is None]
            for i, slot in enumerate(fresh):
                size = lhs_v[i].shape[1]
                product = mm(lhs_v[i][...], other_v[...], 0, 0).astype(BF)
                cargo.kept[slot][...] = product.reshape(4, size // 4, D)
                cargo.start([slot])

    for step in range(1, last):

        @pl.when((ctx > 0) & (step >= ctx))
        def _():
            index = last + ctx - step
            share(index).wait_recv()
            for chunk in range(CHUNKS):
                hop(0, step, chunk, index).wait_recv()
                add(index, chunk, from_left, step)

                @pl.when(ctx < last)
                def _():
                    hop(0, step + 1, chunk, index).start()

        @pl.when((away > 0) & (step >= away))
        def _():
            index = step - away
            share(index).wait_recv()
            for chunk in range(CHUNKS):
                hop(1, step, chunk, index).wait_recv()
                add(index, chunk, from_right, step)

                @pl.when(ctx > 0)
                def _():
                    hop(1, step + 1, chunk, index).start()

        for fill in fills[:3]:
            fill()
        fills = fills[3:]
        if pending:
            cargo.middle(pending.pop(0))
    for fill in fills:
        fill()
    for s in pending:
        cargo.middle(s)
    if more and made:
        store(len(made) - 1, 2).wait()
        store(len(made) - 1, 3).wait()
    if cargo:
        cargo.end()

    share(ctx).wait_recv()

    def close(way):
        for chunk in range(CHUNKS):
            hop(way, last, chunk, ctx).wait_recv()

    def finish(inboxes):
        def group(g, carry):
            part = pl.ds(pl.multiple_of(g * 16, 16), 16)
            total = mine[ctx, part, :].astype(F32) + theirs[ctx, part, :].astype(F32)
            for inbox in inboxes:
                total = total + inbox[last, part, :].astype(F32)
            out_ref[part, :] = total
            return carry

        lax.fori_loop(0, own // 16, group, 0)

    @pl.when(ctx == 0)
    def _():
        close(1)
        finish([from_right])

    @pl.when(ctx == last)
    def _():
        close(0)
        finish([from_left])

    @pl.when((ctx > 0) & (ctx < last))
    def _():
        close(0)
        close(1)
        finish([from_left, from_right])

    for index in range(ctxs):
        share(index).wait_send()
    for slot in range(1, ctxs):

        @pl.when((ctx < last) & (slot >= ctx + 1))
        def _():
            for chunk in range(CHUNKS):
                hop(0, slot, chunk, ctxs + ctx - slot).wait_send()

        @pl.when((ctx > 0) & (slot >= away + 1))
        def _():
            for chunk in range(CHUNKS):
                hop(1, slot, chunk, slot - 1 - away).wait_send()


def team_sum(ctxs, number, pairs, name, freight=(), other=None, outer=False):
    count = pairs[0][0].shape[0]
    own = count // (2 * ctxs)
    lhs, rhs = [a for a, _ in pairs], [b for _, b in pairs]
    dma = pltpu.SemaphoreType.DMA

    inputs = 2 * len(pairs)
    given = Cargo.given(freight)
    outputs = 1 + len(Cargo.rows_of(freight))
    scratch = [pltpu.VMEM(a.shape, BF) for a in lhs + rhs]
    scratch += [pltpu.VMEM((ctxs, own, D), BF)] * 5
    scratch += [dma((2 * ctxs + 1, len(pairs))), dma((2, ctxs)), dma((2, 2, ctxs, CHUNKS))]
    made = [(1, 4, a.shape[1] // 4, D) for a in lhs] if outer else []
    extra = [other] if other is not None else []
    held = [pltpu.VMEM(a.shape, BF) for a in extra]
    held += [pltpu.VMEM((2,) + made[0][2:], BF)] if made else []
    held += [dma((3,))] if extra else []

    def kernel(*refs):
        ins, refs = refs[:inputs], refs[inputs:]
        parts, refs = refs[: len(given)], refs[len(given) :]
        more, refs = refs[: len(extra)], refs[len(extra) :]
        outs, refs = refs[:outputs], refs[outputs:]
        products, refs = refs[: len(made)], refs[len(made) :]
        mine, refs = refs[: len(scratch)], refs[len(scratch) :]
        spare, buffers = refs[: len(refs) - len(held)], refs[len(refs) - len(held) :]
        cargo = Cargo(freight, parts + outs[1:] + spare) if freight else None
        if more:
            tiles = buffers[1] if made else None
            more = (more[0], buffers[0], products, tiles, buffers[-1])
        team_sum_kernel(ctxs, len(pairs), ins + outs[:1] + mine, cargo, more)

    depth = sum(b.shape[0] for b in rhs)
    return pl.pallas_call(
        kernel,
        out_shape=[jax.ShapeDtypeStruct((own, D), F32)]
        + Cargo.out_shapes(freight)
        + [jax.ShapeDtypeStruct(shape, BF) for shape in made],
        in_specs=[pl.BlockSpec(memory_space=pl.ANY)] * (inputs + len(given) + len(extra)),
        out_specs=[pl.BlockSpec(memory_space=pltpu.VMEM)] * outputs
        + [pl.BlockSpec(memory_space=pl.ANY)] * len(made),
        scratch_shapes=scratch + Cargo.scratch(freight) + held,
        compiler_params=pltpu.CompilerParams(
            collective_id=number, has_side_effects=True, vmem_limit_bytes=VMEM_LIMIT
        ),
        cost_estimate=pl.CostEstimate(
            flops=2 * count * depth * D,
            bytes_accessed=2 * (count + D) * depth + 4 * own * D,
            transcendentals=0,
        ),
        name=name,
    )(*lhs, *rhs, *given, *extra)


def middle_kernel(ctxs, refs, freight):
    da, att, proj, out_part = refs[:4]
    refs = refs[4:]
    part, grad, joined, outs = refs[0], refs[1], refs[2], refs[3 : 3 + ctxs]
    first, sums, refs = refs[3 + ctxs], refs[4 + ctxs], refs[5 + ctxs :]
    pv, ov, sent, staged, mine, theirs, others, load, swap, side, shift = refs[:11]
    cargo = Cargo(freight, [part, sums] + list(refs[11:]))
    plane, core, ctx = cargo.plane, cargo.core, cargo.ctx
    me = core * ctxs + ctx
    loads = [
        pltpu.make_async_copy(proj, pv, load.at[0]),
        pltpu.make_async_copy(out_part, ov, load.at[1]),
    ]
    loads[1].start()
    loads[0].start()
    cargo.begin()
    partners = [
        (dc, dz) for dz in range(ctxs - 1, -1, -1) for dc in range(2) if dc + dz > 0
    ]

    def partner(dc, dz):
        return (core if dc == 0 else 1 - core, lax.rem(ctx + dz, ctxs))

    greet_all([(plane,) + partner(*step) for step in partners] + cargo.peers())

    def remote(source, target, sems, index, peer):
        return pltpu.make_async_remote_copy(
            src_ref=source,
            dst_ref=target,
            send_sem=sems.at[(0,) + index],
            recv_sem=sems.at[(1,) + index],
            device_id=(plane,) + peer,
            device_id_type=MESH_ID,
        )

    def piece(i, c, z, home):
        return remote(sent.at[c * ctxs + z], grad.at[home], swap, (i,), (c, z))

    def share(kind, z):
        source = ov.at[(1 - core) * ctxs + z] if kind == 0 else staged.at[z]
        target = others.at[z] if kind == 0 else theirs.at[z]
        return remote(source, target, side, (kind, z), (1 - core, ctx))

    loads[1].wait()
    for k in list(range(1, ctxs)) + [0]:
        share(0, lax.rem(ctx + k, ctxs)).start()
    loads[0].wait()
    for i, step in enumerate(partners):
        c, z = partner(*step)
        sent[c * ctxs + z] = mm(da[...], pv[c * ctxs + z], 1, 1).astype(BF)
        piece(i, c, z, me).start()
    cargo.start()

    def join(k):
        z = lax.rem(ctx + k, ctxs)
        share(0, z).wait_recv()
        target = outs[k - 1]

        def group(g, carry):
            part_ = pl.ds(pl.multiple_of(g * 16, 16), 16)
            total = ov[core * ctxs + z, part_, :].astype(F32) + others[z, part_, :].astype(F32)
            target[part_, :] = total.astype(BF)
            return carry

        lax.fori_loop(0, target.shape[0] // 16, group, 0)

    join(1)
    pass_on = remote(outs[0], first, shift, (0,), (core, lax.rem(ctx + 1, ctxs)))
    pass_on.start()
    grad[me] = mm(da[...], pv[me], 1, 1).astype(BF)
    width = grad.shape[2]

    def heads(t):
        return att[:, pl.ds(pl.multiple_of(t * width, width), width)]

    for z in range(ctxs):
        staged[z] = mm(heads((1 - core) * ctxs + z), da[...], 0, 0).astype(BF)
        share(1, z).start()
    for z in range(ctxs):
        mine[z] = mm(heads(core * ctxs + z), da[...], 0, 0).astype(BF)
    size = pv.shape[1]
    for k in list(range(2, ctxs)) + [0]:
        join(k)
    cargo.middle(0)
    for z in range(ctxs):
        share(1, z).wait_recv()
        for p in range(4):

            def group(g, carry):
                rows = pl.ds(pl.multiple_of(p * (size // 4) + g * 16, 16), 16)
                total = mine[z, rows, :].astype(F32) + theirs[z, rows, :].astype(F32)
                joined[p, z, pl.ds(pl.multiple_of(g * 16, 16), 16), :] = total.astype(BF)
                return carry

            lax.fori_loop(0, size // 64, group, 0)
    cargo.end()
    for i, (dc, dz) in enumerate(partners):
        c, z = core if dc == 0 else 1 - core, lax.rem(ctx + ctxs - dz, ctxs)
        piece(i, c, z, c * ctxs + z).wait_recv()
    pass_on.wait()
    for i, step in enumerate(partners):
        c, z = partner(*step)
        piece(i, c, z, me).wait_send()
    for z in range(ctxs):
        share(0, z).wait_send()
        share(1, z).wait_send()


def middle_call(ctxs, da, att, proj, out_part, part):
    team, own = 2 * ctxs, da.shape[0]
    feats = proj.shape[1]
    freight = (part,)
    dma = pltpu.SemaphoreType.DMA
    hbm, vmem = pl.BlockSpec(memory_space=pl.ANY), pl.BlockSpec(memory_space=pltpu.VMEM)
    block = (ctxs, own, D)

    def kernel(*refs):
        middle_kernel(ctxs, refs, freight)

    return pl.pallas_call(
        kernel,
        out_shape=[
            jax.ShapeDtypeStruct((team, own, feats), BF),
            jax.ShapeDtypeStruct((4, ctxs, feats // 4, D), BF),
        ]
        + [jax.ShapeDtypeStruct((own, D), BF)] * (ctxs + 1)
        + Cargo.out_shapes(freight),
        in_specs=[vmem, vmem, hbm, hbm, hbm],
        out_specs=[vmem] * (4 + ctxs),
        scratch_shapes=[
            pltpu.VMEM(proj.shape, BF),
            pltpu.VMEM(out_part.shape, BF),
            pltpu.VMEM((team, own, feats), BF),
            pltpu.VMEM((ctxs, feats, D), BF),
            pltpu.VMEM((ctxs, feats, D), BF),
            pltpu.VMEM((ctxs, feats, D), BF),
            pltpu.VMEM(block, BF),
            dma((2,)),
            dma((2, team - 1)),
            dma((2, 2, ctxs)),
            dma((2, 1)),
        ]
        + Cargo.scratch(freight),
        compiler_params=pltpu.CompilerParams(
            collective_id=7, has_side_effects=True, vmem_limit_bytes=VMEM_LIMIT
        ),
        cost_estimate=pl.CostEstimate(
            flops=4 * own * D * D, bytes_accessed=60 * own * D, transcendentals=0
        ),
        name="middle",
    )(da, att, proj, out_part, part)


def qkv_kernel(feats, x_ref, gain_ref, w_ref, c_ref, a_ref, b_ref, n_ref, q_ref, k_ref, v_ref):
    values = x_ref[...].astype(F32)
    normed = (values * norm_scale(values) * gain_ref[...]).astype(BF)
    n_ref[...] = normed
    cosine, low_sine, high_sine = [widen(ref[...], feats) for ref in (c_ref, a_ref, b_ref)]
    q = mm(normed, w_ref[0:feats], 1, 1)
    q_ref[...] = rope(q, cosine, low_sine, high_sine).astype(BF)
    k = mm(normed, w_ref[feats : 2 * feats], 1, 1)
    k_ref[...] = rope(k, cosine, low_sine, high_sine).astype(BF)
    v_ref[...] = mm(normed, w_ref[2 * feats :], 1, 1).astype(BF)


def qkv_call(x_all, gain, weights, tables):
    count = x_all.shape[0]
    feats = weights.shape[0] // 3
    turns = tables[0].shape[0] // BLOCK
    rows = pl.BlockSpec((BLOCK, D), lambda i: (i, 0))
    part = pl.BlockSpec((BLOCK, feats), lambda i: (i, 0))
    table = pl.BlockSpec((BLOCK, 128), lambda i: (i % turns, 0))
    out = jax.ShapeDtypeStruct((count, feats), BF)
    return pl.pallas_call(
        functools.partial(qkv_kernel, feats),
        grid=(count // BLOCK,),
        out_shape=(jax.ShapeDtypeStruct((count, D), BF), out, out, out),
        in_specs=[
            rows,
            pl.BlockSpec((1, D), lambda i: (0, 0)),
            pl.BlockSpec((3 * feats, D), lambda i: (0, 0)),
            table,
            table,
            table,
        ],
        out_specs=(rows, part, part, part),
        compiler_params=params(),
        cost_estimate=pl.CostEstimate(
            flops=6 * count * D * feats, bytes_accessed=4 * count * D, transcendentals=0
        ),
        name="qkv",
    )(x_all, gain, weights, *tables)


def allowed_keys(col_ref, row_ref, first, size, keys):
    same = col_ref[first : first + size, :] == row_ref[:, 0:keys]
    query_place = first + lax.broadcasted_iota(jnp.int32, (size, keys), 0)
    key_place = lax.broadcasted_iota(jnp.int32, (size, keys), 1)
    return same & (key_place <= query_place)


def attend_kernel(q_ref, k_ref, v_ref, col_ref, row_ref, o_ref, l_ref):
    length = q_ref.shape[0]
    for first in range(0, length, BLOCK):
        keys = first + BLOCK
        allowed = allowed_keys(col_ref, row_ref, first, BLOCK, keys)
        parts = []
        for head in range(q_ref.shape[1] // HD):
            lanes = slice(head * HD, (head + 1) * HD)
            query = q_ref[first:keys, lanes] * HD ** (-0.5)
            scores = jnp.where(allowed, mm(query, k_ref[0:keys, lanes], 1, 1), MASKED)
            highest = jnp.max(scores, -1, keepdims=True)
            shifted = jnp.exp(scores - highest)
            totals = jnp.sum(shifted, -1, keepdims=True)
            weights = (shifted * (1.0 / totals)).astype(BF)
            parts.append(mm(weights, v_ref[0:keys, lanes], 1, 0))
            l_ref[head, first:keys, :] = highest + jnp.log(totals)
        o_ref[first:keys, :] = jnp.concatenate(parts, 1).astype(BF)


def attend_call(query, key, value, col, row, seq):
    count, feats = query.shape
    pairs = feats // 128
    part = pl.BlockSpec((seq, 128), lambda s, h: (s, h))
    each = 128 // HD
    return pl.pallas_call(
        attend_kernel,
        grid=(2, pairs),
        out_shape=(
            jax.ShapeDtypeStruct((count, feats), BF),
            jax.ShapeDtypeStruct((2 * pairs * each, seq, 1), F32),
        ),
        in_specs=[
            part,
            part,
            part,
            pl.BlockSpec((seq, 1), lambda s, h: (s, 0)),
            pl.BlockSpec((None, 1, seq), lambda s, h: (s, 0, 0)),
        ],
        out_specs=(part, pl.BlockSpec((each, seq, 1), lambda s, h: (s * pairs + h, 0, 0))),
        compiler_params=params(2),
        cost_estimate=pl.CostEstimate(
            flops=4 * count * seq * feats, bytes_accessed=8 * count * feats, transcendentals=0
        ),
        name="attend",
    )(query, key, value, col, row)


def attend_back_kernel(
    q_ref, k_ref, v_ref, g_ref, l_ref, col_ref, row_ref, c_ref, a_ref, b_ref,
    dq_ref, dk_ref, dv_ref, key_total, value_total, query_total,
):
    length = q_ref.shape[0]
    scale = HD ** (-0.5)
    key_total[...] = jnp.zeros_like(key_total)
    value_total[...] = jnp.zeros_like(value_total)
    for first in range(0, length, BLOCK):
        keys = first + BLOCK
        allowed = allowed_keys(col_ref, row_ref, first, BLOCK, keys)
        dq_parts, dk_parts, dv_parts = [], [], []
        for head in range(q_ref.shape[1] // HD):
            lanes = slice(head * HD, (head + 1) * HD)
            query = q_ref[first:keys, lanes] * scale
            key = k_ref[0:keys, lanes]
            grad = g_ref[first:keys, lanes]
            scores = jnp.where(allowed, mm(query, key, 1, 1), MASKED)
            probs = jnp.exp(scores - l_ref[head, first:keys, :])
            grad_probs = mm(grad, v_ref[0:keys, lanes], 1, 1)
            inner = jnp.sum(probs * grad_probs, -1, keepdims=True)
            grad_scores = (probs * (grad_probs - inner)).astype(BF)
            dq_parts.append(mm(grad_scores, key, 1, 0) * scale)
            dk_parts.append(mm(grad_scores, query, 0, 0))
            dv_parts.append(mm(probs.astype(BF), grad, 0, 0))
        query_total[first:keys, :] = jnp.concatenate(dq_parts, 1)
        key_total[0:keys, :] += jnp.concatenate(dk_parts, 1)
        value_total[0:keys, :] += jnp.concatenate(dv_parts, 1)
    cosine, low_sine, high_sine = c_ref[...], a_ref[...], b_ref[...]
    dq_ref[...] = rope_back(query_total[...], cosine, low_sine, high_sine).astype(BF)
    dk_ref[...] = rope_back(key_total[...], cosine, low_sine, high_sine).astype(BF)
    dv_ref[...] = value_total[...].astype(BF)


def attend_back_call(
    query, key, value, grad, log_sums, col, row, tables, seq, freight=(), rider=(), number=None
):
    count, feats = query.shape
    pairs = feats // 128
    part = pl.BlockSpec((seq, 128), lambda s, h: (s, h))
    table = pl.BlockSpec((seq, 128), lambda s, h: (0, 0))
    each = 128 // HD
    out = jax.ShapeDtypeStruct((count, feats), BF)
    outputs = len(Cargo.rows_of(freight))

    def kernel(*refs):
        ins, refs = refs[:10], refs[10:]
        parts, refs = refs[: len(freight)], refs[len(freight) :]
        riders, refs = refs[: len(rider)], refs[len(rider) :]
        outs, refs = refs[:3], refs[3:]
        sums, refs = refs[:outputs], refs[outputs:]
        landed, refs = refs[: len(rider)], refs[len(rider) :]
        mine, spare = refs[:3], refs[3:]
        step = pl.program_id(0) * pairs + pl.program_id(1)
        if rider:
            held, got, sems = spare[-3:]
            spare = spare[:-3]
            plane, core, ctx = [lax.axis_index(name) for name in ALL]
            across = (plane, core, lax.rem(ctx + 2, 4))
            fetch = pltpu.make_async_copy(riders[0], held, sems.at[0])
            ride = pltpu.make_async_remote_copy(
                src_ref=held,
                dst_ref=got,
                send_sem=sems.at[1],
                recv_sem=sems.at[2],
                device_id=across,
                device_id_type=MESH_ID,
            )
        cargo = Cargo(freight, parts + sums + spare) if freight else None
        if freight:

            @pl.when(step == 0)
            def _():
                cargo.begin()
                if rider:
                    fetch.start()
                greet_all(cargo.peers() + ([across] if rider else []))
                if rider:
                    fetch.wait()
                    ride.start()
                cargo.start()

            @pl.when(step == 2 * pairs - 1)
            def _():
                for s in range(outputs):
                    cargo.middle(s)

        attend_back_kernel(*ins, *outs, *mine)
        if freight:

            @pl.when(step == 2 * pairs - 1)
            def _():
                cargo.end()
                if rider:
                    ride.wait()
                    landed[0][...] = got[...]

    more = dict(collective_id=number, has_side_effects=True) if freight else {}
    return pl.pallas_call(
        kernel,
        grid=(2, pairs),
        out_shape=[out, out, out]
        + Cargo.out_shapes(freight)
        + [jax.ShapeDtypeStruct(array.shape, BF) for array in rider],
        in_specs=[
            part,
            part,
            part,
            part,
            pl.BlockSpec((each, seq, 1), lambda s, h: (s * pairs + h, 0, 0)),
            pl.BlockSpec((seq, 1), lambda s, h: (s, 0)),
            pl.BlockSpec((None, 1, seq), lambda s, h: (s, 0, 0)),
            table,
            table,
            table,
        ]
        + [pl.BlockSpec(memory_space=pl.ANY)] * (len(freight) + len(rider)),
        out_specs=[part, part, part]
        + [pl.BlockSpec((rows, D), lambda s, h: (0, 0)) for rows in Cargo.rows_of(freight)]
        + [pl.BlockSpec(array.shape, lambda s, h: (0, 0)) for array in rider],
        scratch_shapes=[pltpu.VMEM((seq, 128), F32)] * 3
        + Cargo.scratch(freight)
        + ([pltpu.VMEM(rider[0].shape, BF)] * 2 + [pltpu.SemaphoreType.DMA((3,))] if rider else []),
        compiler_params=params(2, **more),
        cost_estimate=pl.CostEstimate(
            flops=10 * count * seq * feats, bytes_accessed=14 * count * feats, transcendentals=0
        ),
        name="attend_back",
    )(query, key, value, grad, log_sums, col, row, *tables, *freight, *rider)


def project_kernel(o_ref, w_ref, x_ref, gain_ref, m_ref, n_ref):
    total = x_ref[...].astype(F32)
    for index in range(o_ref.shape[0]):
        total = total + mm(o_ref[index], w_ref[index], 1, 0)
    m_ref[...] = total
    n_ref[...] = (total * norm_scale(total) * gain_ref[...]).astype(BF)


def project_call(attended, weights, x_all, gain):
    team, count, feats = attended.shape
    rows = pl.BlockSpec((BLOCK, D), lambda i: (i, 0))
    return pl.pallas_call(
        project_kernel,
        grid=(count // BLOCK,),
        out_shape=(
            jax.ShapeDtypeStruct((count, D), F32),
            jax.ShapeDtypeStruct((count, D), BF),
        ),
        in_specs=[
            pl.BlockSpec((team, BLOCK, feats), lambda i: (0, i, 0)),
            pl.BlockSpec((team, feats, D), lambda i: (0, 0, 0), pipeline_mode=pl.Buffered(1)),
            rows,
            pl.BlockSpec((1, D), lambda i: (0, 0)),
        ],
        out_specs=(rows, rows),
        compiler_params=params(),
        cost_estimate=pl.CostEstimate(
            flops=2 * count * D * D, bytes_accessed=10 * count * D, transcendentals=0
        ),
        name="project",
    )(attended, weights, x_all, gain)


def shifted(value, axis, size, step):
    return lax.ppermute(value, axis, [(i, (i + step) % size) for i in range(size)])


def plane_reduce(parts, planes):
    home = lax.axis_index("plane")
    rows = parts[0].shape[1]

    def block(index, first, size):
        return jnp.stack(
            [
                lax.dynamic_slice(part, (index, first, 0), (1, size, D))[0].astype(BF)
                for part in parts
            ],
            0,
        )

    if planes != 4:
        total = block(home, 0, rows).astype(F32)
        for k in range(1, planes):
            part = block(lax.rem(home + k, planes), 0, rows)
            total = total + shifted(part, "plane", planes, k).astype(F32)
        return total
    near_x, near_y = home + 1 - 2 * lax.rem(home, 2), lax.rem(home + 2, 4)
    far = 3 - home
    along = ([(0, 1), (1, 0), (2, 3), (3, 2)], [(0, 2), (2, 0), (1, 3), (3, 1)])
    size = rows // 2
    sums = []
    for half in range(2):
        one, two = (near_x, near_y) if half == 0 else (near_y, near_x)
        first = half * size
        sent = jnp.stack([block(one, first, size), block(far, first, size)], 0)
        got = lax.ppermute(sent, "plane", along[half]).astype(F32)
        kept = block(home, first, size).astype(F32) + got[0]
        passed = (block(two, first, size).astype(F32) + got[1]).astype(BF)
        sums.append(kept + lax.ppermute(passed, "plane", along[1 - half]).astype(F32))
    return jnp.concatenate(sums, 1)


def core_join(parts, ctxs):
    core = lax.axis_index("core")
    parts = parts.reshape((2, ctxs) + parts.shape[1:])
    got = shifted(lax.dynamic_index_in_dim(parts, 1 - core, 0, False), "core", 2, 1)
    kept = lax.dynamic_index_in_dim(parts, core, 0, False)
    joined = (kept.astype(F32) + got.astype(F32)).astype(BF)
    return jnp.moveaxis(joined, 1, 0)


def line_reduce(parts, ctxs):
    ctx = lax.axis_index("ctx")
    total = lax.dynamic_index_in_dim(parts, ctx, 0, False)
    for k in range(1, ctxs):
        part = lax.dynamic_index_in_dim(parts, lax.rem(ctx + k, ctxs), 0, False)
        total = total + shifted(part.astype(BF), "ctx", ctxs, k).astype(F32)
    return total


def after(value, *others):
    return lax.optimization_barrier((value,) + others)[0]


def team_join(parts, ctxs):
    core, ctx = lax.axis_index("core"), lax.axis_index("ctx")
    own = parts.shape[0] // (2 * ctxs)
    parts = parts.reshape(2 * ctxs, own, D)

    def block(which, k):
        return lax.dynamic_index_in_dim(parts, which * ctxs + (ctx + k) % ctxs, 0, False)

    joined = []
    for k in list(range(1, ctxs)) + [0]:
        got = shifted(block(1 - core, k), "core", 2, 1)
        both = block(core, k).astype(F32) + got.astype(F32)
        joined.append(both.astype(BF) if k > 0 else both)
    return joined


def team_finish(joined, ctxs):
    total = joined[-1].astype(F32)
    for k in range(1, ctxs):
        total = total + shifted(joined[k - 1], "ctx", ctxs, k).astype(F32)
    return total


def local(
    planes,
    ctxs,
    tokens,
    cotangent,
    segments,
    attn_weight,
    attn_first,
    attn_second,
    mlp_weight,
    mlp_first,
    mlp_second,
    gain_weight,
    gain_first,
    gain_second,
):
    team = 2 * ctxs
    devices = planes * team
    own = tokens.shape[0]
    seq = ctxs * own
    count = 2 * seq
    arows = attn_weight.shape[0]
    frows = mlp_weight.shape[0]
    gcols = gain_weight.shape[1]
    feats = planes * arows
    hidden_count = planes * frows
    whole_heads = arows % HD == 0
    me = lax.axis_index(TEAM)

    lines_seg = own // 128
    square = planes == 4 and ctxs == 4 and whole_heads and gcols == 64
    packed = jnp.zeros((8, 128), F32)
    own_gain = lax.reduce_precision(gain_weight, 8, 7)
    if square:
        side = lax.rem(lax.axis_index("ctx"), 2)
        packed = lax.dynamic_update_slice(packed, own_gain, (0, side * gcols))
    else:
        packed = packed.at[0:2, 0:gcols].set(own_gain)
    packed = packed.at[2 : 2 + lines_seg].set(segments.astype(F32).reshape(lines_seg, 128))
    attn_low = attn_weight.astype(BF)
    qkv_low = jnp.moveaxis(attn_low[:, :3], 1, 0)
    proj_low = attn_low[:, 3]
    gate_low, up_low, down_low = [mlp_weight[:, i].astype(BF) for i in range(3)]
    tables = rope_tables(seq)
    if square:
        mlp_slots = jnp.moveaxis(mlp_weight, 1, 0)
        x_all, normed, query, key, value, qkv, gate_w, small = front_call(
            ctxs, tokens, qkv_low, mlp_slots, packed, tables
        )
        normed = normed.reshape(count, D)
        query, key, value = [part.reshape(count, feats) for part in (query, key, value)]
        qkv = qkv.reshape(3 * feats, D)
        gate_w = gate_w.reshape(hidden_count, D)
        gains = small.reshape(planes, ctxs, 2, 8, 128)[:, :, :, 0:2].sum(2)
        gains = gains.transpose(2, 0, 1, 3).reshape(2, D)
        team_small = lax.dynamic_index_in_dim(small, lax.axis_index("plane"), 0, False)
        seg = team_small[:, 2 : 2 + lines_seg].reshape(count)
        seg_col, seg_row = seg.reshape(count, 1), seg.reshape(2, 1, seq)
        att_all, proj, up_w, log_sums = second_call(
            ctxs, query, key, value, seg_col, seg_row, proj_low, mlp_slots
        )
        proj = proj.reshape(team, feats, D)
        up_w = up_w.reshape(hidden_count, D)
        middle_own, att_own, normed_two, out_part, dgate, dup, down_part = third_call(
            ctxs, att_all, proj, x_all, gains[1:2], gate_w, up_w, mlp_slots, cotangent
        )
        normed_two, out_part = normed_two.reshape(count, D), out_part.reshape(count, D)
        dgate, dup = dgate.reshape(count, hidden_count), dup.reshape(count, hidden_count)
        down_part = down_part.reshape(1, planes, frows, D)
    else:
        inputs = [tokens, packed, gate_low, up_low]
        lines = [(0, 0, 2), (1, 1, 1)]
        shapes = [((team, own, D), BF), ((team, 8, 128), F32)]
        boards = []
        if whole_heads:
            inputs += [proj_low, qkv_low]
            lines.append((4, 2, 1))
            shapes.append(((team, arows, D), BF))
            boards.append(("slots", lambda ins, outs: ins[5], len(shapes)))
            shapes.append(((3, planes, arows, D), BF))
        boards.append(("block", lambda ins, outs: ins[2], len(shapes)))
        shapes.append(((planes, frows, D), BF))
        boards.append(("block", lambda ins, outs: ins[3], len(shapes)))
        shapes.append(((planes, frows, D), BF))
        boards.append(("late", lambda ins, outs: outs[1], len(shapes)))
        shapes.append(((planes, team, 8, 128), F32))
        gathered = gather_call(planes, ctxs, 0, inputs, lines, boards, shapes, "gather_first")
        x_all = gathered[0].reshape(count, D)
        small = gathered[-1]
        gate_w = gathered[-3].reshape(hidden_count, D)
        up_w = gathered[-2].reshape(hidden_count, D)
        gains = small[:, :, 0:2, 0:gcols].transpose(2, 0, 1, 3).reshape(2, D)
        seg = gathered[1][:, 2 : 2 + lines_seg].reshape(count)
        seg_col, seg_row = seg.reshape(count, 1), seg.reshape(2, 1, seq)
        if whole_heads:
            qkv = gathered[3].reshape(3 * feats, D)
        else:
            qkv = lax.all_gather(qkv_low, ALL, axis=1, tiled=True)
            qkv = lax.dynamic_slice_in_dim(qkv, me * feats, feats, 1).reshape(3 * feats, D)
            proj = lax.all_gather(proj_low, ALL, axis=0, tiled=True).reshape(team, feats, D)

        normed, query, key, value = qkv_call(x_all, gains[0:1], qkv, tables)
        attended, log_sums = attend_call(query, key, value, seg_col, seg_row, seq)

        inputs = [attended, down_low]
        lines = [(0, 0, 2)]
        shapes = [((team, count, feats), BF)]
        boards = []
        if whole_heads:
            inputs.append(gathered[2])
            boards.append(("half", lambda ins, outs: ins[2], len(shapes)))
            shapes.append(((team, planes, arows, D), BF))
        boards.append(("block", lambda ins, outs: ins[1], len(shapes)))
        shapes.append(((planes, frows, D), BF))
        gathered = gather_call(planes, ctxs, 2, inputs, lines, boards, shapes, "gather_second")
        att_all = gathered[0]
        down_w = gathered[-1].reshape(hidden_count, D)
        if whole_heads:
            proj = gathered[1].reshape(team, feats, D)
        dy_all = lax.all_gather(after(cotangent, att_all), TEAM, axis=0, tiled=True)
        middle, normed_two = project_call(att_all, proj, x_all, gains[1:2])
        mlp_w = (gate_w, up_w, down_w)

        gate = mm(normed_two, mlp_w[0], 1, 1)
        up = mm(normed_two, mlp_w[1], 1, 1)
        hidden = (jax.nn.silu(gate) * up).astype(BF)
        out_part = mm(hidden, mlp_w[2], 1, 0).astype(BF)
        grad_hidden = mm(after(dy_all, out_part), mlp_w[2], 1, 1)
        sig = jax.nn.sigmoid(gate)
        dgate = (grad_hidden * up * sig * (1.0 + gate * (1.0 - sig))).astype(BF)
        dup = (grad_hidden * gate * sig).astype(BF)
        down_part = mm(hidden, dy_all, 0, 0).astype(BF).reshape(1, planes, frows, D)
        middle_own = lax.dynamic_slice_in_dim(middle, me * own, own, 0)
        att_own = lax.dynamic_slice_in_dim(att_all, me * own, own, 1)
    if square:
        dn2, *down_sum, gate_part, up_part = team_sum(
            ctxs,
            3,
            [(dgate, gate_w), (dup, up_w)],
            "sum_two",
            (down_part,),
            normed_two,
            True,
        )
    else:
        (dn2,) = team_sum(ctxs, 3, [(dgate, gate_w), (dup, up_w)], "sum_two")
        gate_part = mm(dgate, normed_two, 0, 0).astype(BF).reshape(1, planes, frows, D)
        up_part = mm(dup, normed_two, 0, 0).astype(BF).reshape(1, planes, frows, D)

    middle_part, gain_two_grad = norm_back(dn2, middle_own, norm_scale(middle_own), gains[1])
    grad_middle = cotangent.astype(F32) + middle_part
    grad_branch = grad_middle.astype(BF)
    freight, rider = (), ()
    if square:
        grad_att, proj_part, *rest = middle_call(
            ctxs, grad_branch, att_own, proj, out_part.reshape(team, own, D), gate_part
        )
        joined, first_out, gate_sum = rest[:ctxs], rest[ctxs], rest[ctxs + 1]
        rider = (joined[1],)
        freight = (proj_part.reshape(1, planes, ctxs * arows, D),)
    else:
        grad_att = jnp.einsum("td,sfd->stf", grad_branch, proj, preferred_element_type=F32)
        grad_att = lax.all_to_all(
            grad_att.astype(BF), TEAM, split_axis=0, concat_axis=0, tiled=True
        )
        output = (middle_own + team_finish(team_join(out_part, ctxs), ctxs)).astype(BF)
        proj_part = jnp.einsum("tsf,sd->tfd", att_own, grad_branch, preferred_element_type=F32)
        proj_part = proj_part.astype(BF)
        if whole_heads:
            proj_part = core_join(proj_part.reshape(team, planes, arows, D), ctxs)
            proj_part = proj_part.reshape(1, planes, ctxs * arows, D)
        else:
            proj_grad = lax.psum_scatter(
                proj_part.reshape(D, D), ALL, scatter_dimension=0, tiled=True
            ).astype(F32)

    dq, dk, dv, *proj_sum = attend_back_call(
        query,
        key,
        value,
        grad_att.reshape(count, feats),
        log_sums,
        seg_col,
        seg_row,
        tables,
        seq,
        freight,
        rider,
        5,
    )
    pairs = [(dq, qkv[0:feats]), (dk, qkv[feats : 2 * feats]), (dv, qkv[2 * feats :])]
    if square:
        freight = (up_part, jax.ShapeDtypeStruct((3, planes, arows, D), BF))
        dn1, up_sum, *attn_sums = team_sum(ctxs, 4, pairs, "sum_one", freight, normed)
        proj_sum, second_out = proj_sum
        mlp_grad = jnp.stack([gate_sum, up_sum, down_sum[0]], 1)
    else:
        (dn1,) = team_sum(ctxs, 4, pairs, "sum_one")
        dqkv = jnp.concatenate([dq, dk, dv], 1)
        qkv_part = mm(dqkv, normed, 0, 0).astype(BF)
        mlp_grad = [plane_reduce([p[0]], planes)[0] for p in (gate_part, up_part, down_part)]
        mlp_grad = jnp.stack(mlp_grad, 1)
        if whole_heads:
            attn_part = qkv_part.reshape(3, planes, arows, D)
            attn_grad = plane_reduce([attn_part[i] for i in range(3)], planes)
            proj_grad = plane_reduce([proj_part[0]], planes)[0].reshape(ctxs, arows, D)
            proj_grad = line_reduce(proj_grad, ctxs)
        else:
            padded = lax.dynamic_update_slice_in_dim(
                jnp.zeros((3, D, D), BF), qkv_part.reshape(3, feats, D), me * feats, 1
            )
            attn_grad = lax.psum_scatter(padded, ALL, scatter_dimension=1, tiled=True)
            attn_grad = attn_grad.astype(F32)
            proj_grad = lax.psum_scatter(
                proj_part.reshape(D, D), ALL, scatter_dimension=0, tiled=True
            ).astype(F32)
        attn_grad = jnp.moveaxis(jnp.concatenate([attn_grad, proj_grad[None]], 0), 0, 1)

    source = tokens.astype(F32)
    source_part, gain_one_grad = norm_back(dn1, source, norm_scale(source), gains[0])
    grad_input = grad_middle + source_part
    gain_part = jnp.stack([gain_one_grad, gain_two_grad], 0).reshape(2, planes, team, gcols)
    gain_part = gain_part.transpose(1, 2, 0, 3)
    gain_part = jnp.pad(gain_part, ((0, 0), (0, 0), (0, 6), (0, 128 - gcols)))
    gain_grad = small_sum(planes, ctxs, gain_part)
    if square:
        gain_grad, last_out, proj_sum = lax.optimization_barrier((gain_grad, joined[2], proj_sum))
        proj_sum = line_reduce(proj_sum.reshape(ctxs, arows, D), ctxs)
        output = middle_own + joined[3].astype(F32) + first_out.astype(F32)
        output = output + second_out.astype(F32) + shifted(last_out, "ctx", 4, 3).astype(F32)
        output = output.astype(BF)
        attn_grad = jnp.stack(attn_sums + [proj_sum], 1)
    gain_grad = gain_grad[0:2, 0:gcols]

    attn_rate = (
        RATE_FACTOR
        * D ** (-0.5)
        * jnp.array([1.0, 1.0, 1.0, OUTPUT_BOOST], jnp.float32).reshape(1, 4, 1)
    )
    mlp_rate = RATE_FACTOR * jnp.array(
        [D ** (-0.5), D ** (-0.5), FF ** (-0.5)], jnp.float32
    ).reshape(1, 3, 1)
    attn_new = adam_update(attn_weight, attn_first, attn_second, attn_grad, attn_rate, WEIGHT_DECAY)
    mlp_new = adam_update(mlp_weight, mlp_first, mlp_second, mlp_grad, mlp_rate, WEIGHT_DECAY)
    gain_new = adam_update(gain_weight, gain_first, gain_second, gain_grad, GAIN_RATE, 0.0)
    return (
        output,
        grad_input,
        attn_new[0],
        attn_new[1][:, :3, :],
        attn_new[1][:, 3, :],
        attn_new[2],
        mlp_new[0],
        mlp_new[1],
        mlp_new[2],
        gain_new[0],
        gain_new[1],
        gain_new[2],
    )


def solution(mesh):
    dp, ctxs = mesh.shape["dp"], mesh.shape["ctx"]
    planes = dp // 2
    inner = Mesh(mesh.devices.reshape(planes, 2, ctxs), ALL)
    rows = P(ALL, None)
    cube = P(ALL, None, None)
    gain = P(None, ALL)

    def step(*args):
        return local(planes, ctxs, *args)

    return jax.shard_map(
        step,
        mesh=inner,
        in_specs=(rows, rows, P(ALL)) + (cube,) * 6 + (gain,) * 3,
        out_specs=(rows, rows, cube, cube, rows) + (cube,) * 4 + (gain,) * 3,
        check_vma=False,
    )
```
